32 devices in a mesh: grp: 2 (over y), seq: 4 (over z), rep: 4 (over x, core).
Axes of the slice: x: 2, y: 2, z: 4, core: 2. Of those that a mesh axis runs over, the one named last changes fastest.
Arguments:
- patches: bfloat16 [16, 384, 1024], P(('grp', 'rep'), 'seq'), parts along dimension 0, may hold values from -14 to 14, as said below
- kept_index: int32 [16, 384], P(('grp', 'rep'), 'seq'), parts along dimension 0, may hold values from 0 to 1023, as said below
- kept_count: int32 [16, 4], P(('grp', 'rep'), 'seq'), parts along dimension 0, may hold values from 48 to 96, as said below
- cotangent: bfloat16 [16, 384, 1024], P(('grp', 'rep'), 'seq'), parts along dimension 0, may hold values from -6 to 6
- w_qkv: bfloat16 [1024, 3072], replicated, may hold values from -1.3 to 1.3
- w_out: bfloat16 [1024, 1024], replicated, may hold values from -0.1875 to 0.1875
- gain: float32 [1024], replicated, may hold values from 0.1 to 1.9
Outputs:
- encoded: bfloat16 [16, 384, 1024], P(('grp', 'rep'), 'seq'), parts along dimension 0
- d_patches: bfloat16 [16, 384, 1024], P(('grp', 'rep'), 'seq'), parts along dimension 0
- d_w_qkv: float32 [2048, 3072], P('grp', 'seq'), parts along dimension 0
- d_w_out: float32 [2048, 1024], P('grp', 'seq'), parts along dimension 0
The draws below stay inside these ranges and needn't reach their ends.
There are 2 independent parts, one for each index of `grp`. The reference program is written for one: setup_inputs(seed, part) draws one part's arguments, and reference() takes and returns one part's arrays. A program takes and returns all parts, laid end to end along the dimension named above; an argument that names none is the same for every part. Nothing has to cross between parts.
Inputs may be any that keep to these rules, and one draw needn't show every extreme that they name: `kept_count`: each shard keeps between half of its 96 slots and all of them; in every sample some shard fills all 96 slots. `kept_index`: slots of shard j hold distinct positions from j * 256 to (j + 1) * 256 - 1, ascending over the first kept_count slots; later slots hold unused positions of the shard. `patches`: slots past a shard's kept count hold arbitrary values.
All inputs are finite; a program needn't handle non-finite values.
Results may differ from the reference program's by a relative error of at most 0.007.
Values may be sent and summed in bfloat16 or wider, within the bound.
No kernel may reach another device: no remote copies, remote signals or barrier semaphores. Data moves between devices by JAX's collectives and lax.ppermute only.
A program may use at most 128 MiB of HBM per device.

```python
import math
import jax
import jax.numpy as jnp
from jax import lax

D = 1024
HEADS = 16
SHARD = 256
GRID_COLS = 512
CAP = 96
SAMPLES = 8
ROWS = 384
N_SEQ = 4


def kept_layout(key):
    key = jax.random.fold_in(key, 5)
    count_key, pick_key, order_key, edge_key = jax.random.split(key, 4)
    counts = jax.random.randint(count_key, (SAMPLES, N_SEQ), CAP // 2, CAP + 1)
    full_shard = jax.random.randint(pick_key, (SAMPLES, 1), 0, N_SEQ)
    counts = jnp.where(jnp.arange(N_SEQ, dtype=jnp.int32)[None, :] == full_shard, CAP, counts).astype(jnp.int32)
    places = jnp.arange(SHARD, dtype=jnp.int32)
    scores = jax.random.randint(order_key, (SAMPLES, N_SEQ, SHARD), 0, 1 << 20) * SHARD + places
    edge_sample = jax.random.randint(edge_key, (), 0, SAMPLES)
    sample_ids = jnp.arange(SAMPLES, dtype=jnp.int32)[:, None, None]
    shard_ids = jnp.arange(N_SEQ, dtype=jnp.int32)[None, :, None]
    place_ids = places[None, None, :]
    first_end = (shard_ids == 0) & (place_ids == 0)
    last_end = (shard_ids == N_SEQ - 1) & (place_ids == SHARD - 1)
    forced = (sample_ids == edge_sample) & (first_end | last_end)
    scores = jnp.where(forced, -1, scores)
    order = jnp.argsort(scores, axis=2)
    ranks = jnp.argsort(order, axis=2)
    chosen = jnp.where(ranks < counts[:, :, None], places, SHARD + places)
    picked = jnp.sort(chosen, axis=2)[:, :, :CAP] % SHARD
    position = picked + (jnp.arange(N_SEQ, dtype=jnp.int32) * SHARD)[None, :, None]
    return (counts, position.reshape(SAMPLES, N_SEQ * CAP).astype(jnp.int32))


def draw_kept_index(key, part):
    return kept_layout(key)[1]


def draw_kept_count(key, part):
    return kept_layout(key)[0]


def draw_patches(key, part):
    key = jax.random.fold_in(key, 11)
    base_key = jax.random.fold_in(key, 0)
    values = jnp.clip(jax.random.normal(base_key, (SAMPLES, ROWS, D), jnp.float32), -6.0, 6.0)
    return values.astype(jnp.bfloat16)


def draw_w_qkv(key, part):
    key = jax.random.fold_in(key, 23)
    noise_key = jax.random.fold_in(key, 0)
    root = math.sqrt(D)
    values = jnp.clip(jax.random.normal(noise_key, (D, 3 * D), jnp.float32), -6.0, 6.0) / root
    return values.astype(jnp.bfloat16)


def spiked(entries, own_key, source, target, parts, factor):
    owner, partner = [(jnp.arange(entries.shape[axis_at]) // (entries.shape[axis_at] // parts)).reshape([-1 if axis == axis_at else 1 for axis in range(entries.ndim)]) for axis_at in (source, target)]
    chosen = jax.random.permutation(own_key, parts)[partner]
    strong = (owner == chosen) | (owner == (partner + parts // 2) % parts)
    return jnp.where(strong, factor * entries, entries)


def shard_levels(key, shape, shards, smallest, high):
    level = 1.0
    for dim, shards_of in shards:
        heights = jax.random.uniform(jax.random.fold_in(jax.random.fold_in(key, 6), dim), (shards_of,), jnp.float32, smallest / len(shards), high / len(shards))
        level = level * jnp.repeat(jnp.exp(heights), shape[dim] // shards_of).reshape((-1,) + (1,) * (len(shape) - 1 - dim))
    return level


def centred(stream_key, extent, scale, most, cuts=(), held_as=jnp.bfloat16):
    result = jax.random.normal(stream_key, extent, jnp.float32) * scale
    if len(cuts) > 0:
        result = shard_levels(stream_key, extent, cuts, -0.22, 0.18) * result
    return jnp.clip(result, min=-most, max=most).astype(held_as)


def heavy_noise(key, extent, width, most, cuts, heavy, kind=jnp.bfloat16):
    drawn = width * jax.random.normal(key, extent, jnp.float32)
    if cuts:
        drawn = drawn * shard_levels(key, extent, cuts, -0.22, 0.18)
    return jnp.clip(spiked(drawn, jax.random.fold_in(key, 3), *heavy), -most, most).astype(kind)


def setup_inputs(seed: int = 0, part: int = 0) -> dict:
    splits = jax.random.split(jax.random.key(seed), 8)
    part_keys = jax.random.split(jax.random.fold_in(splits[7], part), 8)
    return {
        "patches": draw_patches(jax.random.fold_in(jax.random.fold_in(splits[7], part), 71), part),
        "kept_index": draw_kept_index(jax.random.fold_in(jax.random.fold_in(splits[7], part), 71), part),
        "kept_count": draw_kept_count(jax.random.fold_in(jax.random.fold_in(splits[7], part), 71), part),
        "cotangent": heavy_noise(part_keys[3], (SAMPLES, ROWS, D), 1.0, 6.0, ((0, 4), (1, 4)), (1, 2, 4, 2.0)),
        "w_qkv": draw_w_qkv(jax.random.fold_in(splits[7], 71), part),
        "w_out": centred(splits[5], (D, D), D ** -0.5, 0.1875),
        "gain": jnp.clip(1.0 + 0.18 * jax.random.normal(splits[6], (D,), jnp.float32), 0.1, 1.9),
    }


epsilon = 1e-06

def position_table(position, model_width):
    quarter = model_width // 4
    frequency = jnp.exp(-jnp.log(10000.0) * jnp.arange(quarter, dtype=jnp.float32) / quarter)
    grid_row = (position // GRID_COLS).astype(jnp.float32)
    grid_col = (position % GRID_COLS).astype(jnp.float32)
    row_phase = grid_row[..., None] * frequency
    col_phase = grid_col[..., None] * frequency
    return jnp.concatenate([jnp.sin(row_phase), jnp.cos(row_phase), jnp.sin(col_phase), jnp.cos(col_phase)], axis=-1)

def normalize(hidden, gain):
    center = hidden - lax.optimization_barrier(jnp.mean(hidden, axis=-1, keepdims=True))
    spread = lax.optimization_barrier(jnp.mean(center * center, axis=-1, keepdims=True))
    inv_std = lax.rsqrt(spread + epsilon)
    unit_rows = center * inv_std
    return ((unit_rows * gain).astype(jnp.bfloat16), unit_rows, inv_std)

def norm_backward(d_normed, gain, unit_rows, inv_std):
    scaled = d_normed * gain
    return inv_std * (scaled - lax.optimization_barrier(jnp.mean(scaled, axis=-1, keepdims=True)) - unit_rows * lax.optimization_barrier(jnp.mean(scaled * unit_rows, axis=-1, keepdims=True)))

def head_block(query_rows, grad_rows, key_rows, value_rows, live_keys, score_scale):
    scores = jnp.dot(query_rows, key_rows.T, preferred_element_type=jnp.float32) * score_scale
    scores = jnp.where(live_keys[None, :], scores, -1e+30)
    top_score = lax.optimization_barrier(jnp.max(scores, axis=1, keepdims=True))
    raised = jnp.exp(scores - top_score)
    probability = raised / lax.optimization_barrier(jnp.sum(raised, axis=1, keepdims=True))
    rounded = probability.astype(jnp.bfloat16)
    attended = jnp.dot(rounded, value_rows, preferred_element_type=jnp.float32).astype(jnp.bfloat16)
    d_value = jnp.dot(rounded.T, grad_rows, preferred_element_type=jnp.float32)
    d_prob = jnp.dot(grad_rows, value_rows.T, preferred_element_type=jnp.float32)
    d_score = (probability * (d_prob - lax.optimization_barrier(jnp.sum(probability * d_prob, axis=1, keepdims=True))) * score_scale).astype(jnp.bfloat16)
    d_query = jnp.dot(d_score, key_rows, preferred_element_type=jnp.float32)
    d_key = jnp.dot(d_score.T, query_rows, preferred_element_type=jnp.float32)
    return (attended, d_query, d_key, d_value)

def attend(query_rows, grad_rows, key_rows, value_rows, live_keys, score_scale):
    row_count = query_rows.shape[0]
    blocks = max(1, row_count // 512)
    while row_count % blocks:
        blocks -= 1
    block_rows = row_count // blocks
    query_blocks = query_rows.reshape(blocks, block_rows, query_rows.shape[1])
    grad_blocks = grad_rows.reshape(blocks, block_rows, grad_rows.shape[1])

    def block_step(carry, pieces):
        key_total, value_total = carry
        attended, d_query, d_key, d_value = head_block(pieces[0], pieces[1], key_rows, value_rows, live_keys, score_scale)
        return ((key_total + d_key, value_total + d_value), (attended, d_query))
    empty = jnp.zeros(key_rows.shape, jnp.float32)
    (key_total, value_total), (attended, d_query) = lax.scan(block_step, (empty, empty), (query_blocks, grad_blocks))
    return (attended.reshape(row_count, -1), d_query.reshape(row_count, -1), key_total, value_total)

def one_sample(inputs, w_qkv, w_out, gain):
    patch_rows, position, shard_kept, grad_out = inputs
    model_width = patch_rows.shape[1]
    head_size = model_width // HEADS
    slot_ids = jnp.arange(ROWS, dtype=jnp.int32)
    live_slots = slot_ids % CAP < jnp.repeat(shard_kept, CAP, total_repeat_length=ROWS)
    hidden = patch_rows.astype(jnp.float32) + position_table(position, model_width)
    normed, unit_rows, inv_std = normalize(hidden, gain)
    packed = jnp.dot(normed, w_qkv, preferred_element_type=jnp.float32).astype(jnp.bfloat16)
    live_grad = jnp.where(live_slots[:, None], grad_out, jnp.zeros_like(grad_out))
    d_attended = jnp.dot(live_grad, w_out.T, preferred_element_type=jnp.float32).astype(jnp.bfloat16)

    def split_heads(tensor_block):
        return tensor_block.reshape(ROWS, HEADS, head_size).transpose(1, 0, 2)

    def merge_heads(tensor_block):
        return tensor_block.transpose(1, 0, 2).reshape(ROWS, model_width)
    query_heads = split_heads(packed[:, :model_width])
    key_heads = split_heads(packed[:, model_width:2 * model_width])
    value_heads = split_heads(packed[:, 2 * model_width:])
    grad_heads = split_heads(d_attended)

    def one_head(pieces):
        return attend(pieces[0], pieces[1], pieces[2], pieces[3], live_slots, head_size ** (-0.5))
    outputs, d_query, d_key, d_value = lax.map(one_head, (query_heads, grad_heads, key_heads, value_heads))
    attended = merge_heads(outputs)
    projected = jnp.dot(attended, w_out, preferred_element_type=jnp.float32)
    encoded = jnp.where(live_slots[:, None], hidden + projected, 0.0).astype(jnp.bfloat16)
    out_grad = jnp.dot(attended.T, live_grad, preferred_element_type=jnp.float32)
    d_packed = jnp.concatenate([merge_heads(d_query), merge_heads(d_key), merge_heads(d_value)], axis=1).astype(jnp.bfloat16)
    qkv_grad = jnp.dot(normed.T, d_packed, preferred_element_type=jnp.float32)
    d_normed = jnp.dot(d_packed, w_qkv.T, preferred_element_type=jnp.float32)
    d_hidden = norm_backward(d_normed, gain, unit_rows, inv_std)
    d_patch = jnp.where(live_slots[:, None], live_grad.astype(jnp.float32) + d_hidden, 0.0).astype(jnp.bfloat16)
    return (encoded, d_patch, qkv_grad, out_grad)

def reference(patches, kept_index, kept_count, cotangent, w_qkv, w_out, gain):

    def per_sample(inputs):
        return one_sample(inputs, w_qkv, w_out, gain)
    encoded, d_patches, qkv_terms, out_terms = lax.map(per_sample, (patches, kept_index, kept_count, cotangent))
    return (encoded, d_patches, lax.optimization_barrier(jnp.sum(qkv_terms, axis=0)), lax.optimization_barrier(jnp.sum(out_terms, axis=0)))
```

```python
import functools

import jax
import jax.numpy as jnp
import numpy as np
from jax import lax
from jax.experimental import pallas as pl
from jax.experimental.pallas import tpu as pltpu
from jax.sharding import PartitionSpec as P

HEADS = 16
GRID_COLS = 512


epsilon = 1e-06


def position_table(position, model_width):
    quarter = model_width // 4
    frequency = jnp.exp(-jnp.log(10000.0) * jnp.arange(quarter, dtype=jnp.float32) / quarter)
    grid_row = (position // GRID_COLS).astype(jnp.float32)
    grid_col = (position % GRID_COLS).astype(jnp.float32)
    row_phase = grid_row[..., None] * frequency
    col_phase = grid_col[..., None] * frequency
    return jnp.concatenate(
        [jnp.sin(row_phase), jnp.cos(row_phase), jnp.sin(col_phase), jnp.cos(col_phase)], axis=-1
    )


def normalize(hidden, gain):
    center = hidden - jnp.mean(hidden, axis=-1, keepdims=True)
    spread = jnp.mean(center * center, axis=-1, keepdims=True)
    inv_std = lax.rsqrt(spread + epsilon)
    unit_rows = center * inv_std
    return ((unit_rows * gain).astype(jnp.bfloat16), unit_rows, inv_std)


def norm_backward(d_normed, gain, unit_rows, inv_std):
    scaled = d_normed * gain
    return inv_std * (
        scaled
        - jnp.mean(scaled, axis=-1, keepdims=True)
        - unit_rows * jnp.mean(scaled * unit_rows, axis=-1, keepdims=True)
    )


def head_block(query_rows, grad_rows, key_rows, value_rows, live_keys, score_scale):
    scores = jnp.dot(query_rows, key_rows.T, preferred_element_type=jnp.float32) * score_scale
    scores = jnp.where(live_keys[None, :], scores, -1e30)
    top_score = jnp.max(scores, axis=1, keepdims=True)
    raised = jnp.exp(scores - top_score)
    probability = raised / jnp.sum(raised, axis=1, keepdims=True)
    rounded = probability.astype(jnp.bfloat16)
    attended = jnp.dot(rounded, value_rows, preferred_element_type=jnp.float32).astype(jnp.bfloat16)
    d_value = jnp.dot(rounded.T, grad_rows, preferred_element_type=jnp.float32)
    d_prob = jnp.dot(grad_rows, value_rows.T, preferred_element_type=jnp.float32)
    d_score = (
        probability * (d_prob - jnp.sum(probability * d_prob, axis=1, keepdims=True)) * score_scale
    ).astype(jnp.bfloat16)
    d_query = jnp.dot(d_score, key_rows, preferred_element_type=jnp.float32)
    d_key = jnp.dot(d_score.T, query_rows, preferred_element_type=jnp.float32)
    return (attended, d_query, d_key, d_value)


def attend(query_rows, grad_rows, key_rows, value_rows, live_keys, score_scale):
    row_count = query_rows.shape[0]
    blocks = max(1, row_count // 512)
    while row_count % blocks:
        blocks -= 1
    block_rows = row_count // blocks
    query_blocks = query_rows.reshape(blocks, block_rows, query_rows.shape[1])
    grad_blocks = grad_rows.reshape(blocks, block_rows, grad_rows.shape[1])

    def block_step(carry, pieces):
        key_total, value_total = carry
        attended, d_query, d_key, d_value = head_block(
            pieces[0], pieces[1], key_rows, value_rows, live_keys, score_scale
        )
        return ((key_total + d_key, value_total + d_value), (attended, d_query))

    empty = jnp.zeros(key_rows.shape, jnp.float32)
    (key_total, value_total), (attended, d_query) = lax.scan(
        block_step, (empty, empty), (query_blocks, grad_blocks)
    )
    return (attended.reshape(row_count, -1), d_query.reshape(row_count, -1), key_total, value_total)


def shards(patches, kept_index, kept_count, cotangent, w_qkv, w_out, gain):
    groups = lax.axis_size("seq")
    samples, slot_count, model_width = patches.shape
    head_size = model_width // HEADS
    per_device = max(1, HEADS // groups)
    splits = max(1, groups // HEADS)
    head_groups = groups // splits
    band_width = per_device * head_size
    part_rows = slot_count // splits
    slot_ids = jnp.arange(slot_count, dtype=jnp.int32)
    live_slots = slot_ids[None, :] < kept_count
    hidden = patches.astype(jnp.float32) + position_table(kept_index, model_width)
    normed, unit_rows, inv_std = normalize(hidden, gain)
    flat_normed = normed.reshape(samples * slot_count, model_width)
    packed = jnp.dot(flat_normed, w_qkv, preferred_element_type=jnp.float32).astype(jnp.bfloat16)
    packed = packed.reshape(samples, slot_count, 3 * model_width)
    live_grad = jnp.where(live_slots[:, :, None], cotangent, jnp.zeros_like(cotangent))
    flat_grad = live_grad.reshape(samples * slot_count, model_width)
    d_attended = jnp.dot(flat_grad, w_out.T, preferred_element_type=jnp.float32).astype(
        jnp.bfloat16
    )
    d_attended = d_attended.reshape(samples, slot_count, model_width)

    def to_owners(tensor_block):
        arranged = tensor_block.reshape(samples, splits, part_rows, head_groups, band_width)
        return arranged.transpose(3, 1, 0, 2, 4).reshape(groups, samples, part_rows, band_width)

    key_value_send = jnp.concatenate(
        [
            packed[:, :, model_width : 2 * model_width].reshape(
                samples, slot_count, head_groups, band_width
            ),
            packed[:, :, 2 * model_width :].reshape(samples, slot_count, head_groups, band_width),
        ],
        axis=3,
    )
    key_value_send = key_value_send.transpose(2, 0, 1, 3)
    key_value_send = jnp.broadcast_to(
        key_value_send[:, None], (head_groups, splits, samples, slot_count, 2 * band_width)
    )
    key_value_send = key_value_send.reshape(groups, samples, slot_count, 2 * band_width)
    got_query, got_grad, got_pair = (
        lax.all_to_all(
            to_owners(packed[:, :, :model_width]), "seq", split_axis=0, concat_axis=0, tiled=True
        ),
        lax.all_to_all(to_owners(d_attended), "seq", split_axis=0, concat_axis=0, tiled=True),
        lax.all_to_all(key_value_send, "seq", split_axis=0, concat_axis=0, tiled=True),
    )
    all_counts = lax.all_gather(kept_count, "seq", axis=1, tiled=True)
    live_keys = (slot_ids[None, None, :] < all_counts[:, :, None]).reshape(
        samples, groups * slot_count
    )

    def rows_by_head(tensor_block, row_count):
        arranged = tensor_block.transpose(1, 0, 2, 3).reshape(
            samples, groups * row_count, per_device, head_size
        )
        return arranged.transpose(0, 2, 1, 3)

    query_heads = rows_by_head(got_query, part_rows)
    grad_heads = rows_by_head(got_grad, part_rows)
    key_heads = rows_by_head(got_pair[..., :band_width], slot_count)
    value_heads = rows_by_head(got_pair[..., band_width:], slot_count)
    score_scale = head_size ** (-0.5)

    def one_head(query_rows, grad_rows, key_rows, value_rows, key_live):
        return attend(query_rows, grad_rows, key_rows, value_rows, key_live, score_scale)

    per_head = jax.vmap(one_head, in_axes=(0, 0, 0, 0, None))
    outputs, d_query, d_key, d_value = jax.vmap(per_head)(
        query_heads, grad_heads, key_heads, value_heads, live_keys
    )

    def back_to_sources(tensor_block, row_count):
        arranged = tensor_block.transpose(0, 2, 1, 3).reshape(
            samples, groups, row_count, band_width
        )
        return arranged.transpose(1, 0, 2, 3)

    query_send = back_to_sources(d_query, part_rows).astype(jnp.bfloat16)
    back_out, back_query = (
        lax.all_to_all(
            back_to_sources(outputs, part_rows), "seq", split_axis=0, concat_axis=0, tiled=True
        ),
        lax.all_to_all(query_send, "seq", split_axis=0, concat_axis=0, tiled=True),
    )
    key_value_grad = jnp.concatenate(
        [back_to_sources(d_key, slot_count), back_to_sources(d_value, slot_count)], axis=3
    )
    back_pair = lax.all_to_all(
        key_value_grad.astype(jnp.bfloat16), "seq", split_axis=0, concat_axis=0, tiled=True
    ).astype(key_value_grad.dtype)

    def from_owners(tensor_block):
        arranged = tensor_block.reshape(head_groups, splits, samples, part_rows, band_width)
        return arranged.transpose(2, 1, 3, 0, 4).reshape(samples, slot_count, model_width)

    attended = from_owners(back_out)
    summed_pair = jnp.sum(
        back_pair.reshape(head_groups, splits, samples, slot_count, 2 * band_width), axis=1
    )
    summed_pair = summed_pair.transpose(1, 2, 0, 3)
    key_grad_rows = (
        summed_pair[..., :band_width].reshape(samples, slot_count, model_width).astype(jnp.bfloat16)
    )
    value_grad_rows = (
        summed_pair[..., band_width:].reshape(samples, slot_count, model_width).astype(jnp.bfloat16)
    )
    d_packed = jnp.concatenate([from_owners(back_query), key_grad_rows, value_grad_rows], axis=2)
    flat_attended = attended.reshape(samples * slot_count, model_width)
    projected = jnp.dot(flat_attended, w_out, preferred_element_type=jnp.float32).reshape(
        samples, slot_count, model_width
    )
    encoded = jnp.where(live_slots[:, :, None], hidden + projected, 0.0).astype(jnp.bfloat16)
    flat_packed = d_packed.reshape(samples * slot_count, 3 * model_width)
    d_normed = jnp.dot(flat_packed, w_qkv.T, preferred_element_type=jnp.float32).reshape(
        samples, slot_count, model_width
    )
    d_hidden = norm_backward(d_normed, gain, unit_rows, inv_std)
    d_patches = jnp.where(
        live_slots[:, :, None], live_grad.astype(jnp.float32) + d_hidden, 0.0
    ).astype(jnp.bfloat16)
    columns = flat_grad
    out_part = lax.psum_scatter(
        jnp.dot(columns.T, flat_attended, preferred_element_type=jnp.float32),
        "seq",
        scatter_dimension=0,
        tiled=True,
    ).T
    my_columns = lax.all_to_all(flat_packed, "seq", split_axis=1, concat_axis=0, tiled=True)
    columns = my_columns
    qkv_part = jnp.dot(
        lax.all_gather(flat_normed, "seq", axis=0, tiled=True).T,
        columns,
        preferred_element_type=jnp.float32,
    )
    qkv_grad, out_grad = lax.psum((qkv_part, out_part), "rep")
    return (encoded, d_patches, qkv_grad, out_grad)


AXES = ("seq", "rep")
MARK = 1024.0
VMEM = 40 * 1024 * 1024


def line_perm(move, reps):
    pairs = []
    for z in range(4):
        for rep in range(reps):
            x, c = rep // 2, rep % 2
            to_x, to_c, to_z = move(x, c, z)
            pairs.append((z * reps + rep, to_z * reps + 2 * to_x + to_c))
    return pairs


def sine_cosine(phase):
    turns = jnp.floor(phase * np.float32(2.0 / np.pi) + 0.5)
    rest = phase - turns * np.float32(1.5703125)
    rest = rest - turns * np.float32(4.837512969970703125e-4)
    rest = rest - turns * np.float32(7.54978995489188216e-8)
    square = rest * rest
    sine = rest + rest * square * (
        np.float32(-1.6666654611e-1)
        + square * (np.float32(8.3321608736e-3) + square * np.float32(-1.9515295891e-4))
    )
    cosine = (
        1.0
        - 0.5 * square
        + square
        * square
        * (
            np.float32(4.166664568298827e-2)
            + square * (np.float32(-1.388731625493765e-3) + square * np.float32(2.443315711809948e-5))
        )
    )
    quadrant = turns.astype(jnp.int32) & 3
    swap = (quadrant & 1) == 1
    first = jnp.where(swap, cosine, sine)
    second = jnp.where(swap, sine, cosine)
    first = jnp.where(quadrant >= 2, -first, first)
    second = jnp.where((quadrant == 1) | (quadrant == 2), -second, second)
    return first, second


def live_column(count, rows):
    return lax.broadcasted_iota(jnp.int32, (rows, 1), 0) < count


def grad_kernel(place, count_ref, cot_ref, *grad_refs):
    par = place[0]
    for k in range(2):
        s = k ^ par
        live = live_column(count_ref[s, 0], cot_ref.shape[1])
        grad = cot_ref[s]
        grad_refs[k][...] = jnp.where(live, grad, jnp.zeros_like(grad))


def norm_kernel(place, count_ref, patch_ref, index_ref, freq_ref, gain_ref, n0_ref, n1_ref, hidden_ref):
    par = place[0]
    rows = patch_ref.shape[1]
    width = patch_ref.shape[2]
    freq = freq_ref[...]
    for k, out_ref in enumerate((n0_ref, n1_ref)):
        s = k ^ par
        position = index_ref[s]
        grid_row = (position // GRID_COLS).astype(jnp.float32)
        grid_col = (position % GRID_COLS).astype(jnp.float32)
        pieces = sine_cosine(grid_row * freq) + sine_cosine(grid_col * freq)
        table = jnp.concatenate(pieces, axis=1)
        hidden = patch_ref[s].astype(jnp.float32) + table
        hidden_ref[k] = hidden
        center = hidden - jnp.mean(hidden, axis=-1, keepdims=True)
        spread = jnp.mean(center * center, axis=-1, keepdims=True)
        normed = center * lax.rsqrt(spread + epsilon) * gain_ref[...]
        live = live_column(count_ref[s, 0], rows)
        out_ref[...] = jnp.where(live, normed, MARK).astype(out_ref.dtype)


def dot_nn(a, b):
    return jnp.dot(a, b, preferred_element_type=jnp.float32)


def dot_nt(a, b):
    return lax.dot_general(a, b, (((1,), (1,)), ((), ())), preferred_element_type=jnp.float32)


def dot_tn(a, b):
    return lax.dot_general(a, b, (((0,), (0,)), ((), ())), preferred_element_type=jnp.float32)


def attend_kernel(
    place, n0, n1, n2, n3, g0, g1, g2, g3, wq, wk, wv, wo,
    att_own, att_oth, dp_own, dp_oth, dwo_send, dwo_keep,
    norm_s, grad_s, bias_s,
):
    step = pl.program_id(0)
    block = n0.shape[0]
    rows = 4 * block
    half = 2 * block

    @pl.when(step == 0)
    def _():
        for i, (n_ref, g_ref) in enumerate(((n0, g0), (n1, g1), (n2, g2), (n3, g3))):
            at = pl.ds(i * block, block)
            value = n_ref[...]
            live = value[:, 0:1].astype(jnp.float32) < MARK
            norm_s[at, :] = jnp.where(live, value, jnp.zeros_like(value))
            bias_s[at, :] = jnp.where(live, 0.0, -1e30) + jnp.zeros((block, 128), jnp.float32)
            grad_s[at, :] = g_ref[...]

    normed = norm_s[...]
    grads = grad_s[...]
    bias = bias_s[:, 0:1]
    queries = dot_nn(normed, wq[...]).astype(jnp.bfloat16)
    keys = dot_nn(normed, wk[...]).astype(jnp.bfloat16)
    values = dot_nn(normed, wv[...]).astype(jnp.bfloat16)
    d_att = dot_nt(grads, wo[...]).astype(jnp.bfloat16)
    low = lax.broadcasted_iota(jnp.int32, (rows, 128), 1) < 64
    scale = jnp.bfloat16(0.125)
    zero = jnp.zeros((rows, 128), jnp.bfloat16)
    for pair in range(wq.shape[1] // 128):
        cols = slice(128 * pair, 128 * pair + 128)
        q = queries[:, cols] * scale
        k = keys[:, cols]
        v = values[:, cols]
        g = d_att[:, cols]
        v_t = v.T
        k_t = (k * scale).T
        att_t, dq_t, dk, dv = [], [], [], []
        for h in range(2):
            mine = low if h == 0 else jnp.logical_not(low)
            scores = dot_nt(k, jnp.where(mine, q, zero)) + bias
            raised = jnp.exp(scores - jnp.max(scores, axis=0, keepdims=True))
            prob = raised * (1.0 / jnp.sum(raised, axis=0, keepdims=True))
            weights = prob.astype(jnp.bfloat16)
            part = slice(64 * h, 64 * h + 64)
            att_t.append(dot_nn(v_t[part], weights))
            dv.append(dot_nn(weights, g))
            d_prob = dot_nt(v, jnp.where(mine, g, zero))
            total = jnp.sum(prob * d_prob, axis=0, keepdims=True)
            d_score = (prob * (d_prob - total)).astype(jnp.bfloat16)
            dq_t.append(dot_nn(k_t[part], d_score))
            dk.append(dot_nn(d_score, q))
        att_pair_t = jnp.concatenate(att_t, axis=0).astype(jnp.bfloat16)
        att_pair = att_pair_t.T
        dq_pair = jnp.concatenate(dq_t, axis=0).astype(jnp.bfloat16).T
        dk_pair = jnp.where(low, dk[0], dk[1]).astype(jnp.bfloat16)
        dv_pair = jnp.where(low, dv[0], dv[1]).astype(jnp.bfloat16)
        att_own[:, cols] = att_pair[:half]
        att_oth[:, cols] = att_pair[half:]
        for t, piece in enumerate((dq_pair, dk_pair, dv_pair)):
            dp_own[t, :, cols] = piece[:half]
            dp_oth[t, :, cols] = piece[half:]
        d_out = dot_nn(att_pair_t, grads).astype(jnp.bfloat16)

        @pl.when(step == 0)
        def _():
            dwo_send[cols, :] = d_out

        @pl.when(step == 1)
        def _():
            dwo_keep[cols, :] = d_out


def pack_kernel(place, own, got, s0, s1, s2, s3, rows_ref):
    c, z = place[1], place[2]
    width = own.shape[2]
    mine_low = c == 0
    for t in range(3):
        a, b = own[t], got[t]
        rows_ref[:, 2 * t * width : (2 * t + 1) * width] = jnp.where(mine_low, a, b)
        rows_ref[:, (2 * t + 1) * width : (2 * t + 2) * width] = jnp.where(mine_low, b, a)
    slab = s0.shape[1]
    for k, out in enumerate((s0, s1, s2, s3)):
        out[...] = rows_ref[:, pl.ds(pl.multiple_of((z ^ k) * slab, 128), slab)]


def d_normed_kernel(rows_ref, w_ref, o0, o1, total):
    step = pl.program_id(0)
    term = dot_nt(rows_ref[...], w_ref[...])

    @pl.when(step == 0)
    def _():
        total[...] = term

    @pl.when(step > 0)
    def _():
        total[...] += term

    @pl.when(step == pl.num_programs(0) - 1)
    def _():
        half = o0.shape[0]
        o0[...] = total[:half].astype(o0.dtype)
        o1[...] = total[half:].astype(o1.dtype)


def encode_kernel(place, count_ref, a0, a1, b0, b1, w_ref, hidden_ref, out_ref):
    par, half = place[0], place[2] // 2
    width = a0.shape[1]
    w_own = w_ref[pl.ds(pl.multiple_of(half * width, width), width), :]
    w_oth = w_ref[pl.ds(pl.multiple_of((1 - half) * width, width), width), :]
    for k, (a, b) in enumerate(((a0, b0), (a1, b1))):
        s = k ^ par
        projected = dot_nn(a[...], w_own) + dot_nn(b[...], w_oth)
        live = live_column(count_ref[s, 0], a.shape[0])
        out_ref[s] = jnp.where(live, hidden_ref[k] + projected, 0.0).astype(out_ref.dtype)


def patch_grad_kernel(place, count_ref, d0, d1, g0, g1, hidden_ref, gain_ref, out_ref):
    par = place[0]
    for k, (d_ref, g_ref) in enumerate(((d0, g0), (d1, g1))):
        s = k ^ par
        hidden = hidden_ref[k]
        center = hidden - jnp.mean(hidden, axis=-1, keepdims=True)
        spread = jnp.mean(center * center, axis=-1, keepdims=True)
        inv_std = lax.rsqrt(spread + epsilon)
        unit = center * inv_std
        d_hidden = norm_backward(d_ref[...].astype(jnp.float32), gain_ref[...], unit, inv_std)
        live = live_column(count_ref[s, 0], hidden.shape[0])
        value = g_ref[...].astype(jnp.float32) + d_hidden
        out_ref[s] = jnp.where(live, value, 0.0).astype(out_ref.dtype)


def weight_kernel(place, normed_ref, s0, s1, s2, s3, send_ref, pass_ref, keep_ref, total):
    step = pl.program_id(0)
    z = place[2]
    rows = s0.shape[0]
    total[...] = jnp.zeros_like(total)
    for k, slab in enumerate((s0, s1, s2, s3)):
        total[...] += dot_tn(normed_ref[z ^ k], slab[...])

    @pl.when(step == 0)
    def _():
        send_ref[0] = total[...].astype(send_ref.dtype)

    @pl.when(step == 1)
    def _():
        send_ref[1] = total[...].astype(send_ref.dtype)

    @pl.when(step == 2)
    def _():
        pass_ref[...] = total[...]

    @pl.when(step == 3)
    def _():
        keep_ref[...] = total[...]


def finish_kernel(place, a, b, c, d, out_ref):
    step = pl.program_id(0)
    for i, ref in enumerate((a, b, c, d)):

        @pl.when(step == i)
        def _():
            out_ref[...] = ref[...].astype(out_ref.dtype)


def whole(shape):
    return pl.BlockSpec(shape, lambda *_: (0,) * len(shape))


def call(kernel, place, args, specs, outs, out_specs, grid=(1,), scratch=(), cost=None):
    return pl.pallas_call(
        kernel,
        out_shape=outs,
        grid_spec=pltpu.PrefetchScalarGridSpec(
            num_scalar_prefetch=1,
            grid=grid,
            in_specs=specs,
            out_specs=out_specs,
            scratch_shapes=list(scratch),
        ),
        compiler_params=pltpu.CompilerParams(vmem_limit_bytes=VMEM),
        cost_estimate=cost,
    )(place, *args)


SMEM_SPEC = pl.BlockSpec(memory_space=pltpu.SMEM)


def struct(shape, dtype):
    return jax.ShapeDtypeStruct(shape, dtype)


def chip_shards(patches, kept_index, kept_count, cotangent, w_qkv, w_out, gain):
    bf16, f32 = jnp.bfloat16, jnp.float32
    samples, slots, width = patches.shape
    reps = lax.axis_size("rep")
    rep = lax.axis_index("rep")
    z = lax.axis_index("seq")
    c, x = rep % 2, rep // 2
    place = jnp.stack([z % 2, c, z, x]).astype(jnp.int32)
    own_width = width // 2
    quarter = width // 4
    slab = 3 * width // 4

    def send(value, move):
        return lax.ppermute(value, AXES, line_perm(move, reps))

    def to_core(value):
        return send(value, lambda x, c, z: (x, 1 - c, z))

    def to_x(value):
        return send(value, lambda x, c, z: (1 - x, c, z))

    def to_chip(value, k):
        return send(value, lambda x, c, z: (x, z >> 1, 2 * c + (k ^ (z & 1))))

    def to_rows(value, k, other):
        return send(value, lambda x, c, z: (x, z >> 1, 2 * (c ^ other) + (k ^ (z & 1))))

    def along(value, k):
        return send(value, lambda x, c, z: (x, c, z ^ k))

    block = (slots, width)
    block_spec = whole(block)
    block_out = struct(block, bf16)
    all_spec = whole((samples, slots, width))

    grad = call(
        grad_kernel, place, (kept_count, cotangent), [SMEM_SPEC, all_spec], [block_out] * 2, [block_spec] * 2
    )
    frequency = jnp.exp(-jnp.log(10000.0) * jnp.arange(width // 4, dtype=f32) / (width // 4))
    gain_row = gain.reshape(1, width)
    n0, n1, hidden = call(
        norm_kernel,
        place,
        (kept_count, patches, kept_index.reshape(samples, slots, 1), frequency.reshape(1, -1), gain_row),
        [SMEM_SPEC, all_spec, whole((samples, slots, 1)), whole((1, width // 4)), whole((1, width))],
        [block_out, block_out, struct(patches.shape, f32)],
        [block_spec, block_spec, all_spec],
    )
    got_g = [to_chip(grad[k], k) for k in range(2)]
    got_n = [to_chip(n, k) for k, n in enumerate((n0, n1))]
    oth_g = [to_core(v) for v in got_g]
    oth_n = [to_core(v) for v in got_n]

    heads = quarter

    def head_block(step, place):
        return 2 * place[1] + (place[3] ^ (1 - step))

    def col_block(step, place):
        return place[3] ^ (1 - step)

    w_specs = [
        pl.BlockSpec((width, heads), lambda i, p, t=t: (0, 4 * t + head_block(i, p))) for t in range(3)
    ] + [pl.BlockSpec((heads, width), lambda i, p: (head_block(i, p), 0))]
    rows2 = 2 * slots
    att_spec = pl.BlockSpec((rows2, heads), lambda i, p: (0, col_block(i, p)))
    dp_spec = pl.BlockSpec((3, rows2, heads), lambda i, p: (0, 0, col_block(i, p)))
    att_out = struct((rows2, own_width), bf16)
    dp_out = struct((3, rows2, own_width), bf16)
    dwo_out = struct((heads, width), bf16)
    att_own, att_oth, dp_own, dp_oth, dwo_send, dwo_keep = call(
        attend_kernel,
        place,
        (*got_n, *oth_n, *got_g, *oth_g, w_qkv, w_qkv, w_qkv, w_out),
        [block_spec] * 8 + w_specs,
        [att_out, att_out, dp_out, dp_out, dwo_out, dwo_out],
        [att_spec, att_spec, dp_spec, dp_spec, whole((heads, width)), whole((heads, width))],
        grid=(2,),
        scratch=[
            pltpu.VMEM((4 * slots, width), bf16),
            pltpu.VMEM((4 * slots, width), bf16),
            pltpu.VMEM((4 * slots, 128), f32),
        ],
        cost=pl.CostEstimate(flops=5_000_000_000, bytes_accessed=8_000_000, transcendentals=1_200_000),
    )
    dp_got = to_core(dp_oth)
    normed_all = lax.all_gather(jnp.concatenate(got_n, axis=0), "seq", axis=0, tiled=False)

    slab_out = struct((rows2, slab), bf16)
    *slabs, dp_rows = call(
        pack_kernel,
        place,
        (dp_own, dp_got),
        [whole((3, rows2, own_width))] * 2,
        [slab_out] * 4 + [struct((rows2, 3 * width), bf16)],
        [whole((rows2, slab))] * 4 + [whole((rows2, 3 * width))],
    )
    slabs = [slabs[0]] + [along(slabs[k], k) for k in range(1, 4)]

    back_own = [to_rows(att_own[k * slots : (k + 1) * slots], k, 0) for k in range(2)]
    back_oth = [to_rows(att_oth[k * slots : (k + 1) * slots], k, 1) for k in range(2)]

    dn = pl.pallas_call(
        d_normed_kernel,
        grid=(3,),
        in_specs=[pl.BlockSpec((rows2, width), lambda i: (0, i)), pl.BlockSpec((width, width), lambda i: (0, i))],
        out_specs=[pl.BlockSpec(block, lambda i: (0, 0))] * 2,
        out_shape=[block_out] * 2,
        scratch_shapes=[pltpu.VMEM((rows2, width), f32)],
        compiler_params=pltpu.CompilerParams(vmem_limit_bytes=VMEM),
    )(dp_rows, w_qkv)
    back_dn = [to_rows(dn[k], k, 0) for k in range(2)]

    dwo_sum = dwo_keep.astype(f32) + to_x(dwo_send).astype(f32)
    dwo_sum = dwo_sum.astype(bf16).reshape(heads, 4, quarter)

    def columns_of(k):
        return lax.dynamic_index_in_dim(dwo_sum, z ^ k, 1, keepdims=False)

    dwo = columns_of(0).astype(f32)
    for k in range(1, 4):
        dwo = dwo + along(columns_of(k), k).astype(f32)
    dwo = dwo.astype(bf16)

    encoded = call(
        encode_kernel,
        place,
        (kept_count, *back_own, *back_oth, w_out, hidden),
        [SMEM_SPEC] + [whole((slots, own_width))] * 4 + [whole((width, width)), all_spec],
        struct(patches.shape, bf16),
        all_spec,
    )

    def quarter_of(step, place):
        core = place[1] ^ (1 - step // 2)
        return 2 * core + (place[3] ^ (1 - step % 2))

    part = (quarter, slab)
    w_send, w_pass, w_keep = call(
        weight_kernel,
        place,
        (normed_all, *slabs),
        [pl.BlockSpec((4, rows2, quarter), lambda i, p: (0, 0, quarter_of(i, p)))] + [whole((rows2, slab))] * 4,
        [struct((2,) + part, bf16), struct(part, f32), struct(part, f32)],
        [whole((2,) + part), whole(part), whole(part)],
        grid=(4,),
        scratch=[pltpu.VMEM(part, f32)],
    )
    w_got = to_core(w_send)
    w_got_x = to_x((w_pass + w_got[0].astype(f32)).astype(bf16))
    dwq = (w_keep + w_got[1].astype(f32) + w_got_x.astype(f32)).astype(bf16)

    d_patches = call(
        patch_grad_kernel,
        place,
        (kept_count, *back_dn, *grad, hidden, gain_row),
        [SMEM_SPEC] + [block_spec] * 4 + [all_spec, whole((1, width))],
        struct(patches.shape, bf16),
        all_spec,
    )

    def spread(value, columns):
        by_x = to_x(value)
        by_core = to_core(value)
        by_both = to_core(by_x)

        def at(i, p):
            core = p[1] ^ (i // 2)
            return (2 * core + (p[3] ^ (i % 2)), 0)

        return call(
            finish_kernel,
            place,
            (value, by_x, by_core, by_both),
            [whole((quarter, columns))] * 4,
            struct((width, columns), f32),
            pl.BlockSpec((quarter, columns), at),
            grid=(4,),
        )

    return (encoded, d_patches, spread(dwq, slab), spread(dwo, quarter))


def solution(mesh):
    in_specs = (
        P(("grp", "rep"), "seq", None),
        P(("grp", "rep"), "seq"),
        P(("grp", "rep"), "seq"),
        P(("grp", "rep"), "seq", None),
        P(),
        P(),
        P(),
    )
    out_specs = (
        P(("grp", "rep"), "seq", None),
        P(("grp", "rep"), "seq", None),
        P("grp", "seq"),
        P("grp", "seq"),
    )
    chips = mesh.shape["seq"] == 4 and mesh.shape["rep"] % 2 == 0 and HEADS % 8 == 0

    def run(patches, *rest):
        per_device = patches.shape[0] // (mesh.shape["grp"] * mesh.shape["rep"])
        body = chip_shards if chips and per_device == 2 else shards
        inner = jax.shard_map(body, mesh=mesh, in_specs=in_specs, out_specs=out_specs, check_vma=False)
        return inner(patches, *rest)

    return run
```

```python
import functools

import jax
import jax.numpy as jnp
import numpy as np
from jax import lax
from jax.experimental import pallas as pl
from jax.experimental.pallas import tpu as pltpu
from jax.sharding import PartitionSpec as P

HEADS = 16
GRID_COLS = 512


epsilon = 1e-06


def position_table(position, model_width):
    quarter = model_width // 4
    frequency = jnp.exp(-jnp.log(10000.0) * jnp.arange(quarter, dtype=jnp.float32) / quarter)
    grid_row = (position // GRID_COLS).astype(jnp.float32)
    grid_col = (position % GRID_COLS).astype(jnp.float32)
    row_phase = grid_row[..., None] * frequency
    col_phase = grid_col[..., None] * frequency
    return jnp.concatenate(
        [jnp.sin(row_phase), jnp.cos(row_phase), jnp.sin(col_phase), jnp.cos(col_phase)], axis=-1
    )


def normalize(hidden, gain):
    center = hidden - jnp.mean(hidden, axis=-1, keepdims=True)
    spread = jnp.mean(center * center, axis=-1, keepdims=True)
    inv_std = lax.rsqrt(spread + epsilon)
    unit_rows = center * inv_std
    return ((unit_rows * gain).astype(jnp.bfloat16), unit_rows, inv_std)


def norm_backward(d_normed, gain, unit_rows, inv_std):
    scaled = d_normed * gain
    return inv_std * (
        scaled
        - jnp.mean(scaled, axis=-1, keepdims=True)
        - unit_rows * jnp.mean(scaled * unit_rows, axis=-1, keepdims=True)
    )


def head_block(query_rows, grad_rows, key_rows, value_rows, live_keys, score_scale):
    scores = jnp.dot(query_rows, key_rows.T, preferred_element_type=jnp.float32) * score_scale
    scores = jnp.where(live_keys[None, :], scores, -1e30)
    top_score = jnp.max(scores, axis=1, keepdims=True)
    raised = jnp.exp(scores - top_score)
    probability = raised / jnp.sum(raised, axis=1, keepdims=True)
    rounded = probability.astype(jnp.bfloat16)
    attended = jnp.dot(rounded, value_rows, preferred_element_type=jnp.float32).astype(jnp.bfloat16)
    d_value = jnp.dot(rounded.T, grad_rows, preferred_element_type=jnp.float32)
    d_prob = jnp.dot(grad_rows, value_rows.T, preferred_element_type=jnp.float32)
    d_score = (
        probability * (d_prob - jnp.sum(probability * d_prob, axis=1, keepdims=True)) * score_scale
    ).astype(jnp.bfloat16)
    d_query = jnp.dot(d_score, key_rows, preferred_element_type=jnp.float32)
    d_key = jnp.dot(d_score.T, query_rows, preferred_element_type=jnp.float32)
    return (attended, d_query, d_key, d_value)


def attend(query_rows, grad_rows, key_rows, value_rows, live_keys, score_scale):
    row_count = query_rows.shape[0]
    blocks = max(1, row_count // 512)
    while row_count % blocks:
        blocks -= 1
    block_rows = row_count // blocks
    query_blocks = query_rows.reshape(blocks, block_rows, query_rows.shape[1])
    grad_blocks = grad_rows.reshape(blocks, block_rows, grad_rows.shape[1])

    def block_step(carry, pieces):
        key_total, value_total = carry
        attended, d_query, d_key, d_value = head_block(
            pieces[0], pieces[1], key_rows, value_rows, live_keys, score_scale
        )
        return ((key_total + d_key, value_total + d_value), (attended, d_query))

    empty = jnp.zeros(key_rows.shape, jnp.float32)
    (key_total, value_total), (attended, d_query) = lax.scan(
        block_step, (empty, empty), (query_blocks, grad_blocks)
    )
    return (attended.reshape(row_count, -1), d_query.reshape(row_count, -1), key_total, value_total)


def shards(patches, kept_index, kept_count, cotangent, w_qkv, w_out, gain):
    groups = lax.axis_size("seq")
    samples, slot_count, model_width = patches.shape
    head_size = model_width // HEADS
    per_device = max(1, HEADS // groups)
    splits = max(1, groups // HEADS)
    head_groups = groups // splits
    band_width = per_device * head_size
    part_rows = slot_count // splits
    slot_ids = jnp.arange(slot_count, dtype=jnp.int32)
    live_slots = slot_ids[None, :] < kept_count
    hidden = patches.astype(jnp.float32) + position_table(kept_index, model_width)
    normed, unit_rows, inv_std = normalize(hidden, gain)
    flat_normed = normed.reshape(samples * slot_count, model_width)
    packed = jnp.dot(flat_normed, w_qkv, preferred_element_type=jnp.float32).astype(jnp.bfloat16)
    packed = packed.reshape(samples, slot_count, 3 * model_width)
    live_grad = jnp.where(live_slots[:, :, None], cotangent, jnp.zeros_like(cotangent))
    flat_grad = live_grad.reshape(samples * slot_count, model_width)
    d_attended = jnp.dot(flat_grad, w_out.T, preferred_element_type=jnp.float32).astype(
        jnp.bfloat16
    )
    d_attended = d_attended.reshape(samples, slot_count, model_width)

    def to_owners(tensor_block):
        arranged = tensor_block.reshape(samples, splits, part_rows, head_groups, band_width)
        return arranged.transpose(3, 1, 0, 2, 4).reshape(groups, samples, part_rows, band_width)

    key_value_send = jnp.concatenate(
        [
            packed[:, :, model_width : 2 * model_width].reshape(
                samples, slot_count, head_groups, band_width
            ),
            packed[:, :, 2 * model_width :].reshape(samples, slot_count, head_groups, band_width),
        ],
        axis=3,
    )
    key_value_send = key_value_send.transpose(2, 0, 1, 3)
    key_value_send = jnp.broadcast_to(
        key_value_send[:, None], (head_groups, splits, samples, slot_count, 2 * band_width)
    )
    key_value_send = key_value_send.reshape(groups, samples, slot_count, 2 * band_width)
    got_query, got_grad, got_pair = (
        lax.all_to_all(
            to_owners(packed[:, :, :model_width]), "seq", split_axis=0, concat_axis=0, tiled=True
        ),
        lax.all_to_all(to_owners(d_attended), "seq", split_axis=0, concat_axis=0, tiled=True),
        lax.all_to_all(key_value_send, "seq", split_axis=0, concat_axis=0, tiled=True),
    )
    all_counts = lax.all_gather(kept_count, "seq", axis=1, tiled=True)
    live_keys = (slot_ids[None, None, :] < all_counts[:, :, None]).reshape(
        samples, groups * slot_count
    )

    def rows_by_head(tensor_block, row_count):
        arranged = tensor_block.transpose(1, 0, 2, 3).reshape(
            samples, groups * row_count, per_device, head_size
        )
        return arranged.transpose(0, 2, 1, 3)

    query_heads = rows_by_head(got_query, part_rows)
    grad_heads = rows_by_head(got_grad, part_rows)
    key_heads = rows_by_head(got_pair[..., :band_width], slot_count)
    value_heads = rows_by_head(got_pair[..., band_width:], slot_count)
    score_scale = head_size ** (-0.5)

    def one_head(query_rows, grad_rows, key_rows, value_rows, key_live):
        return attend(query_rows, grad_rows, key_rows, value_rows, key_live, score_scale)

    per_head = jax.vmap(one_head, in_axes=(0, 0, 0, 0, None))
    outputs, d_query, d_key, d_value = jax.vmap(per_head)(
        query_heads, grad_heads, key_heads, value_heads, live_keys
    )

    def back_to_sources(tensor_block, row_count):
        arranged = tensor_block.transpose(0, 2, 1, 3).reshape(
            samples, groups, row_count, band_width
        )
        return arranged.transpose(1, 0, 2, 3)

    query_send = back_to_sources(d_query, part_rows).astype(jnp.bfloat16)
    back_out, back_query = (
        lax.all_to_all(
            back_to_sources(outputs, part_rows), "seq", split_axis=0, concat_axis=0, tiled=True
        ),
        lax.all_to_all(query_send, "seq", split_axis=0, concat_axis=0, tiled=True),
    )
    key_value_grad = jnp.concatenate(
        [back_to_sources(d_key, slot_count), back_to_sources(d_value, slot_count)], axis=3
    )
    back_pair = lax.all_to_all(
        key_value_grad.astype(jnp.bfloat16), "seq", split_axis=0, concat_axis=0, tiled=True
    ).astype(key_value_grad.dtype)

    def from_owners(tensor_block):
        arranged = tensor_block.reshape(head_groups, splits, samples, part_rows, band_width)
        return arranged.transpose(2, 1, 3, 0, 4).reshape(samples, slot_count, model_width)

    attended = from_owners(back_out)
    summed_pair = jnp.sum(
        back_pair.reshape(head_groups, splits, samples, slot_count, 2 * band_width), axis=1
    )
    summed_pair = summed_pair.transpose(1, 2, 0, 3)
    key_grad_rows = (
        summed_pair[..., :band_width].reshape(samples, slot_count, model_width).astype(jnp.bfloat16)
    )
    value_grad_rows = (
        summed_pair[..., band_width:].reshape(samples, slot_count, model_width).astype(jnp.bfloat16)
    )
    d_packed = jnp.concatenate([from_owners(back_query), key_grad_rows, value_grad_rows], axis=2)
    flat_attended = attended.reshape(samples * slot_count, model_width)
    projected = jnp.dot(flat_attended, w_out, preferred_element_type=jnp.float32).reshape(
        samples, slot_count, model_width
    )
    encoded = jnp.where(live_slots[:, :, None], hidden + projected, 0.0).astype(jnp.bfloat16)
    flat_packed = d_packed.reshape(samples * slot_count, 3 * model_width)
    d_normed = jnp.dot(flat_packed, w_qkv.T, preferred_element_type=jnp.float32).reshape(
        samples, slot_count, model_width
    )
    d_hidden = norm_backward(d_normed, gain, unit_rows, inv_std)
    d_patches = jnp.where(
        live_slots[:, :, None], live_grad.astype(jnp.float32) + d_hidden, 0.0
    ).astype(jnp.bfloat16)
    columns = flat_grad
    out_part = lax.psum_scatter(
        jnp.dot(columns.T, flat_attended, preferred_element_type=jnp.float32),
        "seq",
        scatter_dimension=0,
        tiled=True,
    ).T
    my_columns = lax.all_to_all(flat_packed, "seq", split_axis=1, concat_axis=0, tiled=True)
    columns = my_columns
    qkv_part = jnp.dot(
        lax.all_gather(flat_normed, "seq", axis=0, tiled=True).T,
        columns,
        preferred_element_type=jnp.float32,
    )
    qkv_grad, out_grad = lax.psum((qkv_part, out_part), "rep")
    return (encoded, d_patches, qkv_grad, out_grad)


AXES = ("seq", "rep")
MARK = 1024.0
MIB = 1024 * 1024


def line_perm(move, reps):
    pairs = []
    for z in range(4):
        for rep in range(reps):
            x, c = rep // 2, rep % 2
            to_x, to_c, to_z = move(x, c, z)
            pairs.append((z * reps + rep, to_z * reps + 2 * to_x + to_c))
    return pairs


def sine_cosine(phase):
    turns = jnp.floor(phase * np.float32(2.0 / np.pi) + 0.5)
    rest = phase - turns * np.float32(1.5703125)
    rest = rest - turns * np.float32(4.837512969970703125e-4)
    rest = rest - turns * np.float32(7.54978995489188216e-8)
    square = rest * rest
    sine = rest + rest * square * (
        np.float32(-1.6666654611e-1)
        + square * (np.float32(8.3321608736e-3) + square * np.float32(-1.9515295891e-4))
    )
    cosine = (
        1.0
        - 0.5 * square
        + square
        * square
        * (
            np.float32(4.166664568298827e-2)
            + square * (np.float32(-1.388731625493765e-3) + square * np.float32(2.443315711809948e-5))
        )
    )
    quadrant = turns.astype(jnp.int32) & 3
    swap = (quadrant & 1) == 1
    first = jnp.where(swap, cosine, sine)
    second = jnp.where(swap, sine, cosine)
    first = jnp.where(quadrant >= 2, -first, first)
    second = jnp.where((quadrant == 1) | (quadrant == 2), -second, second)
    return first, second


def live_column(count, rows):
    return lax.broadcasted_iota(jnp.int32, (rows, 1), 0) < count


def dot_nn(a, b):
    return jnp.dot(a, b, preferred_element_type=jnp.float32)


def dot_nt(a, b):
    return lax.dot_general(a, b, (((1,), (1,)), ((), ())), preferred_element_type=jnp.float32)


PAR, CORE, LINE, SIDE, KEPT = range(5)


def norm_kernel(place, patch_ref, cot_ref, index_ref, gain_ref, p0_ref, p1_ref, hidden_ref):
    par = place[PAR]
    rows, width = patch_ref.shape[1:]
    quarter = width // 4
    order = lax.broadcasted_iota(jnp.int32, (1, quarter), 1).astype(jnp.float32)
    freq = jnp.exp(-np.log(np.float32(10000.0)) * order / quarter)
    diagonal = lax.broadcasted_iota(jnp.int32, (rows, rows), 0) == lax.broadcasted_iota(
        jnp.int32, (rows, rows), 1
    )
    for k, out_ref in enumerate((p0_ref, p1_ref)):
        s = k ^ par
        live = live_column(place[KEPT + s], rows)
        position = index_ref[pl.ds(s, 1), :]
        grid_row = (position // GRID_COLS).astype(jnp.float32)
        grid_col = (position % GRID_COLS).astype(jnp.float32)
        grid_row = jnp.sum(jnp.where(diagonal, grid_row, 0.0), axis=1, keepdims=True)
        grid_col = jnp.sum(jnp.where(diagonal, grid_col, 0.0), axis=1, keepdims=True)
        pieces = sine_cosine(grid_row * freq) + sine_cosine(grid_col * freq)
        hidden = patch_ref[s].astype(jnp.float32) + jnp.concatenate(pieces, axis=1)
        hidden_ref[k] = hidden
        center = hidden - jnp.mean(hidden, axis=-1, keepdims=True)
        spread = jnp.mean(center * center, axis=-1, keepdims=True)
        normed = center * lax.rsqrt(spread + epsilon) * gain_ref[...]
        out_ref[:rows, :] = jnp.where(live, normed, MARK).astype(out_ref.dtype)
        grad = cot_ref[s]
        out_ref[rows:, :] = jnp.where(live, grad, jnp.zeros_like(grad))


def stage_kernel(place, q_in, k_in, v_in, o_in, q_out, k_out, v_out, o_out):
    q_out[...] = q_in[...]
    k_out[...] = k_in[...]
    v_out[...] = v_in[...]
    o_out[...] = o_in[...]


def attend_kernel(
    place, p0, p1, p2, p3, wq, wk, wv, wo,
    att0, att1, att2, att3, dp_own, dp_oth, att_send, att_keep, dp_send, dp_keep,
    norm_s, grad_s,
):
    block = p0.shape[0] // 2
    rows = 4 * block
    half = 2 * block
    biases = []
    for i, ref in enumerate((p0, p1, p2, p3)):
        at = slice(i * block, (i + 1) * block)
        value = ref[:block, :]
        live = value[:, 0:1].astype(jnp.float32) < MARK
        norm_s[at, :] = jnp.where(live, value, jnp.zeros_like(value))
        grad_s[at, :] = ref[block:, :]
        biases.append(jnp.where(live, 0.0, -1e30))
    bias = jnp.concatenate(biases, axis=0)
    low = lax.broadcasted_iota(jnp.int32, (rows, 128), 1) < 64
    scale = jnp.bfloat16(0.125)
    zero = jnp.zeros((rows, 128), jnp.bfloat16)
    first = place[SIDE] == 0
    for j in range(wq.shape[1] // 128):
        cols = slice(128 * j, 128 * j + 128)
        if j % 2 == 0:
            two = slice(128 * j, 128 * j + 256)
            normed = norm_s[...]
            queries = dot_nn(normed, wq[:, two]).astype(jnp.bfloat16)
            keys = dot_nn(normed, wk[:, two]).astype(jnp.bfloat16)
            values = dot_nn(normed, wv[:, two]).astype(jnp.bfloat16)
            d_att = dot_nt(grad_s[...], wo[two, :]).astype(jnp.bfloat16)
        here = slice(128 * (j % 2), 128 * (j % 2) + 128)
        q = queries[:, here] * scale
        k = keys[:, here]
        v = values[:, here]
        g = d_att[:, here]
        v_t = v.T
        k_t = (k * scale).T
        att_t, dq_t, dk, dv = [], [], [], []
        for h in range(2):
            mine = low if h == 0 else jnp.logical_not(low)
            scores = dot_nt(k, jnp.where(mine, q, zero)) + bias
            raised = jnp.exp(scores - jnp.max(scores, axis=0, keepdims=True))
            prob = raised * (1.0 / jnp.sum(raised, axis=0, keepdims=True))
            weights = prob.astype(jnp.bfloat16)
            part = slice(64 * h, 64 * h + 64)
            att_t.append(dot_nn(v_t[part], weights))
            dv.append(dot_nn(weights, g))
            d_prob = dot_nt(v, jnp.where(mine, g, zero))
            total = jnp.sum(prob * d_prob, axis=0, keepdims=True)
            d_score = (prob * (d_prob - total)).astype(jnp.bfloat16)
            dq_t.append(dot_nn(k_t[part], d_score))
            dk.append(dot_nn(d_score, q))
        att_pair_t = jnp.concatenate(att_t, axis=0).astype(jnp.bfloat16)
        att_pair = att_pair_t.T
        dq_pair_t = jnp.concatenate(dq_t, axis=0).astype(jnp.bfloat16)
        dk_pair = jnp.where(low, dk[0], dk[1]).astype(jnp.bfloat16)
        dv_pair = jnp.where(low, dv[0], dv[1]).astype(jnp.bfloat16)
        for i, out in enumerate((att0, att1, att2, att3)):
            out[:, cols] = att_pair[i * block : (i + 1) * block]
        for t, piece in enumerate((dq_pair_t.T, dk_pair, dv_pair)):
            dp_own[t, :, cols] = piece[:half]
            dp_oth[t, :, cols] = piece[half:]
        at = slice(64 * j, 64 * j + 64)
        att_keep[at, :] = jnp.where(first, att_pair_t[:64], att_pair_t[64:])
        att_send[at, :] = jnp.where(first, att_pair_t[64:], att_pair_t[:64])
        for t, piece in enumerate((dq_pair_t, dk_pair.T, dv_pair.T)):
            at = slice(64 * (4 * t + j), 64 * (4 * t + j) + 64)
            dp_keep[at, :] = jnp.where(first, piece[:64], piece[64:])
            dp_send[at, :] = jnp.where(first, piece[64:], piece[:64])


def in_order(place, own, got):
    pieces = []
    low = place == 0
    for j in range(own.shape[1] // 128):
        a, b = own[:, 128 * j : 128 * j + 128], got[:, 128 * j : 128 * j + 128]
        pieces += [jnp.where(low, a, b), jnp.where(low, b, a)]
    return jnp.concatenate(pieces, axis=1)


def d_normed_kernel(place, own, got, w_ref, o0, o1, total):
    step = pl.program_id(0)
    term = dot_nt(in_order(place[CORE], own[step], got[step]), w_ref[...])

    @pl.when(step == 0)
    def _():
        total[...] = term

    @pl.when(step > 0)
    def _():
        total[...] += term

    @pl.when(step == pl.num_programs(0) - 1)
    def _():
        half = o0.shape[0]
        o0[...] = total[:half].astype(o0.dtype)
        o1[...] = total[half:].astype(o1.dtype)


def out_weight_kernel(place, keep, got, p0, p1, p2, p3, r0, r1, r2, r3, o0, o1, o2, o3, tokens, total):
    block = p0.shape[0] // 2
    rows = 4 * block
    for i, ref in enumerate((p0, p1, p2, p3, r0, r1, r2, r3)):
        tokens[i * block : (i + 1) * block, :] = ref[block:, :]
    total[...] = dot_nn(keep[...], tokens[:rows, :]) + dot_nn(got[...], tokens[rows:, :])
    columns = o0.shape[1]
    for k, out in enumerate((o0, o1, o2, o3)):
        at = pl.multiple_of((place[LINE] ^ k) * columns, 128)
        out[...] = total[:, pl.ds(at, columns)].astype(out.dtype)


def weight_kernel(place, keep, got, p0, p1, p2, p3, r0, r1, r2, r3, o0, o1, o2, o3, tokens):
    block = p0.shape[0] // 2
    rows = 4 * block
    for i, ref in enumerate((p0, p1, p2, p3, r0, r1, r2, r3)):
        tokens[i * block : (i + 1) * block, :] = ref[:block, :]
    count = o0.shape[0]
    for k, out in enumerate((o0, o1, o2, o3)):
        at = pl.ds(pl.multiple_of((place[LINE] ^ k) * count, 16), count)
        value = dot_nn(keep[at, :], tokens[:rows, :]) + dot_nn(got[at, :], tokens[rows:, :])
        out[...] = value.astype(out.dtype)


def sum_kernel(a0, a1, a2, a3, b0, b1, b2, b3, out):
    f32 = jnp.float32
    count = a0.shape[0]
    value = (a0[...].astype(f32) + a1[...].astype(f32)) + (a2[...].astype(f32) + a3[...].astype(f32))
    out[:count, :] = value.astype(out.dtype)
    value = (b0[...].astype(f32) + b1[...].astype(f32)) + (b2[...].astype(f32) + b3[...].astype(f32))
    value = value.astype(out.dtype)
    columns = b0.shape[1]
    for j in range(4):
        out[count:, columns * j : columns * j + columns] = value[64 * j : 64 * j + 64, :]


def finish_kernel(place, own, by_x, by_core, by_both, wide, narrow):
    core_low, side_low = place[CORE] == 0, place[SIDE] == 0
    count = own.shape[0] - 64
    columns = narrow.shape[1]

    def pick(at, c, x, part):
        a = jnp.where(side_low == (x == 0), own[at, part], by_x[at, part])
        b = jnp.where(side_low == (x == 0), by_core[at, part], by_both[at, part])
        return jnp.where(core_low == (c == 0), a, b)

    for c in range(2):
        for i in range(count // 64):
            at = slice(64 * i, 64 * i + 64)
            both = jnp.concatenate([pick(at, c, x, slice(None)) for x in range(2)], axis=0)
            col = 128 * (2 * i + c)
            wide[:, col : col + 128] = both.T.astype(wide.dtype)
        for j in range(4):
            for x in range(2):
                row = 128 * (2 * j + c) + 64 * x
                part = slice(columns * j, columns * j + columns)
                narrow[row : row + 64, :] = pick(slice(count, None), c, x, part).astype(narrow.dtype)


def encode_kernel(place, a0, a1, b0, b1, w_ref, hidden_ref, out_ref):
    par, core = place[PAR], place[LINE] // 2
    for k, (a, b) in enumerate(((a0, b0), (a1, b1))):
        s = k ^ par
        projected = dot_nn(in_order(core, a[...], b[...]), w_ref[...])
        live = live_column(place[KEPT + s], a.shape[0])
        out_ref[s] = jnp.where(live, hidden_ref[k] + projected, 0.0).astype(out_ref.dtype)


def patch_grad_kernel(place, d0, d1, p0, p1, hidden_ref, gain_ref, out_ref):
    par = place[PAR]
    rows = d0.shape[0]
    for k, (d_ref, p_ref) in enumerate(((d0, p0), (d1, p1))):
        s = k ^ par
        hidden = hidden_ref[k]
        center = hidden - jnp.mean(hidden, axis=-1, keepdims=True)
        spread = jnp.mean(center * center, axis=-1, keepdims=True)
        inv_std = lax.rsqrt(spread + epsilon)
        unit = center * inv_std
        d_hidden = norm_backward(d_ref[...].astype(jnp.float32), gain_ref[...], unit, inv_std)
        live = live_column(place[KEPT + s], rows)
        value = p_ref[rows:, :].astype(jnp.float32) + d_hidden
        out_ref[s] = jnp.where(live, value, 0.0).astype(out_ref.dtype)


SMEM_SPEC = pl.BlockSpec(memory_space=pltpu.SMEM)
VMEM_SPEC = pl.BlockSpec(memory_space=pltpu.VMEM)


def struct(shape, dtype=jnp.bfloat16):
    return jax.ShapeDtypeStruct(shape, dtype)


def call(kernel, args, outs, limit, place=None, scratch=(), flops=0, moved=1_000_000):
    specs = [VMEM_SPEC] * len(args)
    if place is not None:
        args, specs = (place, *args), [SMEM_SPEC] + specs
    single = not isinstance(outs, list)
    return pl.pallas_call(
        kernel,
        in_specs=specs,
        out_specs=VMEM_SPEC if single else [VMEM_SPEC] * len(outs),
        out_shape=outs,
        scratch_shapes=list(scratch),
        compiler_params=pltpu.CompilerParams(vmem_limit_bytes=limit * MIB),
        cost_estimate=pl.CostEstimate(flops=flops, bytes_accessed=moved, transcendentals=0),
    )(*args)


def chip_shards(patches, kept_index, kept_count, cotangent, w_qkv, w_out, gain):
    bf16, f32 = jnp.bfloat16, jnp.float32
    samples, slots, width = patches.shape
    reps = lax.axis_size("rep")
    rep = lax.axis_index("rep")
    z = lax.axis_index("seq")
    core, x = rep & 1, rep >> 1
    place = jnp.concatenate(
        [jnp.stack([z & 1, core, z, x]).astype(jnp.int32), kept_count.reshape(samples)]
    )
    own_width = width // 2
    quarter = width // 4
    rows = 4 * slots

    def send(value, move):
        return lax.ppermute(value, AXES, line_perm(move, reps))

    def to_core(value):
        return send(value, lambda x, c, z: (x, 1 - c, z))

    def to_x(value):
        return send(value, lambda x, c, z: (1 - x, c, z))

    def to_chip(value, k):
        return send(value, lambda x, c, z: (x, z >> 1, 2 * c + (k ^ (z & 1))))

    def to_rows(value, k, other):
        return send(value, lambda x, c, z: (x, z >> 1, 2 * (c ^ other) + (k ^ (z & 1))))

    def along(value, k):
        return send(value, lambda x, c, z: (x, c, z ^ k))

    gain_row = gain.reshape(1, width)
    pay = struct((2 * slots, width))
    *mine, hidden = call(
        norm_kernel,
        (patches, cotangent, kept_index, gain_row),
        [pay, pay, struct(patches.shape, f32)],
        16,
        place,
        moved=4_000_000,
    )
    got = [to_chip(mine[k], k) for k in range(2)]

    wide, tall = (width, 128), (128, width)
    blocks = own_width // 128
    staged = pl.pallas_call(
        stage_kernel,
        grid_spec=pltpu.PrefetchScalarGridSpec(
            num_scalar_prefetch=1,
            grid=(blocks,),
            in_specs=[
                pl.BlockSpec(wide, lambda j, p, t=t: (0, (width // 128) * t + 2 * j + p[CORE])) for t in range(3)
            ]
            + [pl.BlockSpec(tall, lambda j, p: (2 * j + p[CORE], 0))],
            out_specs=[pl.BlockSpec(wide, lambda j, p: (0, j))] * 3 + [pl.BlockSpec(tall, lambda j, p: (j, 0))],
        ),
        out_shape=[struct((width, own_width))] * 3 + [struct((own_width, width))],
        compiler_params=pltpu.CompilerParams(vmem_limit_bytes=8 * MIB),
        cost_estimate=pl.CostEstimate(flops=0, bytes_accessed=8_000_000, transcendentals=0),
    )(place, w_qkv, w_qkv, w_qkv, w_out)

    here = got + [to_core(v) for v in got]
    from_x = [to_x(v) for v in got]
    there = from_x + [to_core(v) for v in from_x]

    att = struct((slots, own_width))
    d_rows = struct((3, 2 * slots, own_width))
    att_t = struct((quarter, rows))
    dp_t = struct((3 * quarter, rows))
    *atts, dp_own, dp_oth, att_send, att_keep, dp_send, dp_keep = call(
        attend_kernel,
        (*here, *staged),
        [att] * 4 + [d_rows] * 2 + [att_t] * 2 + [dp_t] * 2,
        32,
        place,
        scratch=[pltpu.VMEM((rows, width), bf16)] * 2,
        flops=6_000_000_000,
        moved=20_000_000,
    )
    att_got = to_x(att_send)
    dp_got = to_x(dp_send)
    dp_core = to_core(dp_oth)
    back_att = [to_rows(atts[k], k, 0) for k in range(2)] + [to_rows(atts[2 + k], k, 1) for k in range(2)]

    d_normed = pl.pallas_call(
        d_normed_kernel,
        grid_spec=pltpu.PrefetchScalarGridSpec(
            num_scalar_prefetch=1,
            grid=(3,),
            in_specs=[pl.BlockSpec(d_rows.shape, lambda i, p: (0, 0, 0))] * 2
            + [pl.BlockSpec((width, width), lambda i, p: (0, i))],
            out_specs=[pl.BlockSpec((slots, width), lambda i, p: (0, 0))] * 2,
            scratch_shapes=[pltpu.VMEM((2 * slots, width), f32)],
        ),
        out_shape=[struct((slots, width))] * 2,
        compiler_params=pltpu.CompilerParams(vmem_limit_bytes=16 * MIB),
        cost_estimate=pl.CostEstimate(flops=1_200_000_000, bytes_accessed=8_000_000, transcendentals=0),
    )(place, dp_own, dp_core, w_qkv)
    back_dn = [to_rows(d_normed[k], k, 0) for k in range(2)]

    out_part = struct((quarter, quarter))
    dwo = call(
        out_weight_kernel,
        (att_keep, att_got, *here, *there),
        [out_part] * 4,
        12,
        place,
        scratch=[pltpu.VMEM((2 * rows, width), bf16), pltpu.VMEM((quarter, width), f32)],
        flops=400_000_000,
        moved=4_000_000,
    )
    dwo = [dwo[0]] + [along(dwo[k], k) for k in range(1, 4)]
    in_part = struct((3 * quarter // 4, width))
    dwq = call(
        weight_kernel,
        (dp_keep, dp_got, *here, *there),
        [in_part] * 4,
        12,
        place,
        scratch=[pltpu.VMEM((2 * rows, width), bf16)],
        flops=1_200_000_000,
        moved=6_000_000,
    )
    dwq = [dwq[0]] + [along(dwq[k], k) for k in range(1, 4)]

    encoded = call(
        encode_kernel,
        (*back_att, w_out, hidden),
        struct(patches.shape),
        12,
        place,
        flops=400_000_000,
        moved=5_000_000,
    )
    d_patches = call(
        patch_grad_kernel,
        (*back_dn, *mine, hidden, gain_row),
        struct(patches.shape),
        8,
        place,
        moved=4_000_000,
    )
    sums = call(sum_kernel, (*dwq, *dwo), struct((quarter, width)), 8, moved=2_500_000)
    by_x = to_x(sums)
    by_core = to_core(sums)
    by_both = to_core(by_x)
    qkv_grad, out_grad = call(
        finish_kernel,
        (sums, by_x, by_core, by_both),
        [struct((width, 3 * quarter), f32), struct((width, quarter), f32)],
        12,
        place,
        moved=6_000_000,
    )
    return (encoded, d_patches, qkv_grad, out_grad)


def solution(mesh):
    in_specs = (
        P(("grp", "rep"), "seq", None),
        P(("grp", "rep"), "seq"),
        P(("grp", "rep"), "seq"),
        P(("grp", "rep"), "seq", None),
        P(),
        P(),
        P(),
    )
    out_specs = (
        P(("grp", "rep"), "seq", None),
        P(("grp", "rep"), "seq", None),
        P("grp", "seq"),
        P("grp", "seq"),
    )
    chips = mesh.shape["seq"] == 4 and mesh.shape["rep"] % 2 == 0 and HEADS % 8 == 0

    def run(patches, *rest):
        per_device = patches.shape[0] // (mesh.shape["grp"] * mesh.shape["rep"])
        body = chip_shards if chips and per_device == 2 else shards
        inner = jax.shard_map(body, mesh=mesh, in_specs=in_specs, out_specs=out_specs, check_vma=False)
        return inner(patches, *rest)

    return run
```

```python
import functools

import jax
import jax.numpy as jnp
import numpy as np
from jax import lax
from jax.experimental import pallas as pl
from jax.experimental.pallas import tpu as pltpu
from jax.sharding import PartitionSpec as P

HEADS = 16
GRID_COLS = 512


epsilon = 1e-06


def position_table(position, model_width):
    quarter = model_width // 4
    frequency = jnp.exp(-jnp.log(10000.0) * jnp.arange(quarter, dtype=jnp.float32) / quarter)
    grid_row = (position // GRID_COLS).astype(jnp.float32)
    grid_col = (position % GRID_COLS).astype(jnp.float32)
    row_phase = grid_row[..., None] * frequency
    col_phase = grid_col[..., None] * frequency
    return jnp.concatenate(
        [jnp.sin(row_phase), jnp.cos(row_phase), jnp.sin(col_phase), jnp.cos(col_phase)], axis=-1
    )


def normalize(hidden, gain):
    center = hidden - jnp.mean(hidden, axis=-1, keepdims=True)
    spread = jnp.mean(center * center, axis=-1, keepdims=True)
    inv_std = lax.rsqrt(spread + epsilon)
    unit_rows = center * inv_std
    return ((unit_rows * gain).astype(jnp.bfloat16), unit_rows, inv_std)


def norm_backward(d_normed, gain, unit_rows, inv_std):
    scaled = d_normed * gain
    return inv_std * (
        scaled
        - jnp.mean(scaled, axis=-1, keepdims=True)
        - unit_rows * jnp.mean(scaled * unit_rows, axis=-1, keepdims=True)
    )


def head_block(query_rows, grad_rows, key_rows, value_rows, live_keys, score_scale):
    scores = jnp.dot(query_rows, key_rows.T, preferred_element_type=jnp.float32) * score_scale
    scores = jnp.where(live_keys[None, :], scores, -1e30)
    top_score = jnp.max(scores, axis=1, keepdims=True)
    raised = jnp.exp(scores - top_score)
    probability = raised / jnp.sum(raised, axis=1, keepdims=True)
    rounded = probability.astype(jnp.bfloat16)
    attended = jnp.dot(rounded, value_rows, preferred_element_type=jnp.float32).astype(jnp.bfloat16)
    d_value = jnp.dot(rounded.T, grad_rows, preferred_element_type=jnp.float32)
    d_prob = jnp.dot(grad_rows, value_rows.T, preferred_element_type=jnp.float32)
    d_score = (
        probability * (d_prob - jnp.sum(probability * d_prob, axis=1, keepdims=True)) * score_scale
    ).astype(jnp.bfloat16)
    d_query = jnp.dot(d_score, key_rows, preferred_element_type=jnp.float32)
    d_key = jnp.dot(d_score.T, query_rows, preferred_element_type=jnp.float32)
    return (attended, d_query, d_key, d_value)


def attend(query_rows, grad_rows, key_rows, value_rows, live_keys, score_scale):
    row_count = query_rows.shape[0]
    blocks = max(1, row_count // 512)
    while row_count % blocks:
        blocks -= 1
    block_rows = row_count // blocks
    query_blocks = query_rows.reshape(blocks, block_rows, query_rows.shape[1])
    grad_blocks = grad_rows.reshape(blocks, block_rows, grad_rows.shape[1])

    def block_step(carry, pieces):
        key_total, value_total = carry
        attended, d_query, d_key, d_value = head_block(
            pieces[0], pieces[1], key_rows, value_rows, live_keys, score_scale
        )
        return ((key_total + d_key, value_total + d_value), (attended, d_query))

    empty = jnp.zeros(key_rows.shape, jnp.float32)
    (key_total, value_total), (attended, d_query) = lax.scan(
        block_step, (empty, empty), (query_blocks, grad_blocks)
    )
    return (attended.reshape(row_count, -1), d_query.reshape(row_count, -1), key_total, value_total)


def shards(patches, kept_index, kept_count, cotangent, w_qkv, w_out, gain):
    groups = lax.axis_size("seq")
    samples, slot_count, model_width = patches.shape
    head_size = model_width // HEADS
    per_device = max(1, HEADS // groups)
    splits = max(1, groups // HEADS)
    head_groups = groups // splits
    band_width = per_device * head_size
    part_rows = slot_count // splits
    slot_ids = jnp.arange(slot_count, dtype=jnp.int32)
    live_slots = slot_ids[None, :] < kept_count
    hidden = patches.astype(jnp.float32) + position_table(kept_index, model_width)
    normed, unit_rows, inv_std = normalize(hidden, gain)
    flat_normed = normed.reshape(samples * slot_count, model_width)
    packed = jnp.dot(flat_normed, w_qkv, preferred_element_type=jnp.float32).astype(jnp.bfloat16)
    packed = packed.reshape(samples, slot_count, 3 * model_width)
    live_grad = jnp.where(live_slots[:, :, None], cotangent, jnp.zeros_like(cotangent))
    flat_grad = live_grad.reshape(samples * slot_count, model_width)
    d_attended = jnp.dot(flat_grad, w_out.T, preferred_element_type=jnp.float32).astype(
        jnp.bfloat16
    )
    d_attended = d_attended.reshape(samples, slot_count, model_width)

    def to_owners(tensor_block):
        arranged = tensor_block.reshape(samples, splits, part_rows, head_groups, band_width)
        return arranged.transpose(3, 1, 0, 2, 4).reshape(groups, samples, part_rows, band_width)

    key_value_send = jnp.concatenate(
        [
            packed[:, :, model_width : 2 * model_width].reshape(
                samples, slot_count, head_groups, band_width
            ),
            packed[:, :, 2 * model_width :].reshape(samples, slot_count, head_groups, band_width),
        ],
        axis=3,
    )
    key_value_send = key_value_send.transpose(2, 0, 1, 3)
    key_value_send = jnp.broadcast_to(
        key_value_send[:, None], (head_groups, splits, samples, slot_count, 2 * band_width)
    )
    key_value_send = key_value_send.reshape(groups, samples, slot_count, 2 * band_width)
    got_query, got_grad, got_pair = (
        lax.all_to_all(
            to_owners(packed[:, :, :model_width]), "seq", split_axis=0, concat_axis=0, tiled=True
        ),
        lax.all_to_all(to_owners(d_attended), "seq", split_axis=0, concat_axis=0, tiled=True),
        lax.all_to_all(key_value_send, "seq", split_axis=0, concat_axis=0, tiled=True),
    )
    all_counts = lax.all_gather(kept_count, "seq", axis=1, tiled=True)
    live_keys = (slot_ids[None, None, :] < all_counts[:, :, None]).reshape(
        samples, groups * slot_count
    )

    def rows_by_head(tensor_block, row_count):
        arranged = tensor_block.transpose(1, 0, 2, 3).reshape(
            samples, groups * row_count, per_device, head_size
        )
        return arranged.transpose(0, 2, 1, 3)

    query_heads = rows_by_head(got_query, part_rows)
    grad_heads = rows_by_head(got_grad, part_rows)
    key_heads = rows_by_head(got_pair[..., :band_width], slot_count)
    value_heads = rows_by_head(got_pair[..., band_width:], slot_count)
    score_scale = head_size ** (-0.5)

    def one_head(query_rows, grad_rows, key_rows, value_rows, key_live):
        return attend(query_rows, grad_rows, key_rows, value_rows, key_live, score_scale)

    per_head = jax.vmap(one_head, in_axes=(0, 0, 0, 0, None))
    outputs, d_query, d_key, d_value = jax.vmap(per_head)(
        query_heads, grad_heads, key_heads, value_heads, live_keys
    )

    def back_to_sources(tensor_block, row_count):
        arranged = tensor_block.transpose(0, 2, 1, 3).reshape(
            samples, groups, row_count, band_width
        )
        return arranged.transpose(1, 0, 2, 3)

    query_send = back_to_sources(d_query, part_rows).astype(jnp.bfloat16)
    back_out, back_query = (
        lax.all_to_all(
            back_to_sources(outputs, part_rows), "seq", split_axis=0, concat_axis=0, tiled=True
        ),
        lax.all_to_all(query_send, "seq", split_axis=0, concat_axis=0, tiled=True),
    )
    key_value_grad = jnp.concatenate(
        [back_to_sources(d_key, slot_count), back_to_sources(d_value, slot_count)], axis=3
    )
    back_pair = lax.all_to_all(
        key_value_grad.astype(jnp.bfloat16), "seq", split_axis=0, concat_axis=0, tiled=True
    ).astype(key_value_grad.dtype)

    def from_owners(tensor_block):
        arranged = tensor_block.reshape(head_groups, splits, samples, part_rows, band_width)
        return arranged.transpose(2, 1, 3, 0, 4).reshape(samples, slot_count, model_width)

    attended = from_owners(back_out)
    summed_pair = jnp.sum(
        back_pair.reshape(head_groups, splits, samples, slot_count, 2 * band_width), axis=1
    )
    summed_pair = summed_pair.transpose(1, 2, 0, 3)
    key_grad_rows = (
        summed_pair[..., :band_width].reshape(samples, slot_count, model_width).astype(jnp.bfloat16)
    )
    value_grad_rows = (
        summed_pair[..., band_width:].reshape(samples, slot_count, model_width).astype(jnp.bfloat16)
    )
    d_packed = jnp.concatenate([from_owners(back_query), key_grad_rows, value_grad_rows], axis=2)
    flat_attended = attended.reshape(samples * slot_count, model_width)
    projected = jnp.dot(flat_attended, w_out, preferred_element_type=jnp.float32).reshape(
        samples, slot_count, model_width
    )
    encoded = jnp.where(live_slots[:, :, None], hidden + projected, 0.0).astype(jnp.bfloat16)
    flat_packed = d_packed.reshape(samples * slot_count, 3 * model_width)
    d_normed = jnp.dot(flat_packed, w_qkv.T, preferred_element_type=jnp.float32).reshape(
        samples, slot_count, model_width
    )
    d_hidden = norm_backward(d_normed, gain, unit_rows, inv_std)
    d_patches = jnp.where(
        live_slots[:, :, None], live_grad.astype(jnp.float32) + d_hidden, 0.0
    ).astype(jnp.bfloat16)
    columns = flat_grad
    out_part = lax.psum_scatter(
        jnp.dot(columns.T, flat_attended, preferred_element_type=jnp.float32),
        "seq",
        scatter_dimension=0,
        tiled=True,
    ).T
    my_columns = lax.all_to_all(flat_packed, "seq", split_axis=1, concat_axis=0, tiled=True)
    columns = my_columns
    qkv_part = jnp.dot(
        lax.all_gather(flat_normed, "seq", axis=0, tiled=True).T,
        columns,
        preferred_element_type=jnp.float32,
    )
    qkv_grad, out_grad = lax.psum((qkv_part, out_part), "rep")
    return (encoded, d_patches, qkv_grad, out_grad)


AXES = ("seq", "rep")
MARK = 1024.0
MIB = 1024 * 1024


def line_perm(move, reps):
    pairs = []
    for z in range(4):
        for rep in range(reps):
            x, c = rep // 2, rep % 2
            to_x, to_c, to_z = move(x, c, z)
            pairs.append((z * reps + rep, to_z * reps + 2 * to_x + to_c))
    return pairs


def sine_cosine(phase):
    turns = jnp.floor(phase * np.float32(2.0 / np.pi) + 0.5)
    rest = phase - turns * np.float32(1.5703125)
    rest = rest - turns * np.float32(4.837512969970703125e-4)
    rest = rest - turns * np.float32(7.54978995489188216e-8)
    square = rest * rest
    sine = rest + rest * square * (
        np.float32(-1.6666654611e-1)
        + square * (np.float32(8.3321608736e-3) + square * np.float32(-1.9515295891e-4))
    )
    cosine = (
        1.0
        - 0.5 * square
        + square
        * square
        * (
            np.float32(4.166664568298827e-2)
            + square * (np.float32(-1.388731625493765e-3) + square * np.float32(2.443315711809948e-5))
        )
    )
    quadrant = turns.astype(jnp.int32) & 3
    swap = (quadrant & 1) == 1
    first = jnp.where(swap, cosine, sine)
    second = jnp.where(swap, sine, cosine)
    first = jnp.where(quadrant >= 2, -first, first)
    second = jnp.where((quadrant == 1) | (quadrant == 2), -second, second)
    return first, second


def live_column(count, rows):
    return lax.broadcasted_iota(jnp.int32, (rows, 1), 0) < count


def dot_nn(a, b):
    return jnp.dot(a, b, preferred_element_type=jnp.float32)


def dot_nt(a, b):
    return lax.dot_general(a, b, (((1,), (1,)), ((), ())), preferred_element_type=jnp.float32)


PAR, CORE, LINE, SIDE, KEPT = range(5)


def norm_kernel(
    place, patch_hbm, cot_hbm, index_hbm, gain_hbm, p0_ref, p1_ref, hidden_ref,
    patch_ref, cot_ref, index_ref, gain_ref, sems,
):
    par = place[PAR]
    rows, width = patch_ref.shape[1:]
    quarter = width // 4
    copies = [
        pltpu.make_async_copy(src, dst, sems.at[i])
        for i, (src, dst) in enumerate(
            ((index_hbm, index_ref), (patch_hbm, patch_ref), (gain_hbm, gain_ref), (cot_hbm, cot_ref))
        )
    ]
    for copy in copies:
        copy.start()
    order = lax.broadcasted_iota(jnp.int32, (1, quarter), 1).astype(jnp.float32)
    freq = jnp.exp(-np.log(np.float32(10000.0)) * order / quarter)
    diagonal = lax.broadcasted_iota(jnp.int32, (rows, rows), 0) == lax.broadcasted_iota(
        jnp.int32, (rows, rows), 1
    )
    copies[0].wait()
    tables = []
    for k in range(2):
        position = index_ref[pl.ds(k ^ par, 1), :]
        grid_row = (position // GRID_COLS).astype(jnp.float32)
        grid_col = (position % GRID_COLS).astype(jnp.float32)
        grid_row = jnp.sum(jnp.where(diagonal, grid_row, 0.0), axis=1, keepdims=True)
        grid_col = jnp.sum(jnp.where(diagonal, grid_col, 0.0), axis=1, keepdims=True)
        pieces = sine_cosine(grid_row * freq) + sine_cosine(grid_col * freq)
        tables.append(jnp.concatenate(pieces, axis=1))
    copies[1].wait()
    copies[2].wait()
    for k, out_ref in enumerate((p0_ref, p1_ref)):
        s = k ^ par
        hidden = patch_ref[s].astype(jnp.float32) + tables[k]
        hidden_ref[k] = hidden
        center = hidden - jnp.mean(hidden, axis=-1, keepdims=True)
        spread = jnp.mean(center * center, axis=-1, keepdims=True)
        normed = center * lax.rsqrt(spread + epsilon) * gain_ref[...]
        live = live_column(place[KEPT + s], rows)
        out_ref[:rows, :] = jnp.where(live, normed, MARK).astype(out_ref.dtype)
    copies[3].wait()
    for k, out_ref in enumerate((p0_ref, p1_ref)):
        s = k ^ par
        live = live_column(place[KEPT + s], rows)
        grad = cot_ref[s]
        out_ref[rows:, :] = jnp.where(live, grad, jnp.zeros_like(grad))


def attend_kernel(
    place, p0, p1, p2, p3, w_in_hbm, w_out_hbm,
    att0, att1, att2, att3, dp_own, dp_oth, send_t, keep_t,
    norm_s, grad_s, wq, wk, wv, wo, sems,
):
    core = place[CORE]
    width = p0.shape[1]
    copies = []
    for j in range(width // 256):
        to = pl.ds(128 * j, 128)
        row = pl.multiple_of(256 * j + 128 * core, 128)
        pairs = [(w_out_hbm.at[pl.ds(row, 128), :], wo.at[to, :])]
        for t, out in enumerate((wq, wk, wv)):
            at = pl.multiple_of(t * width + 256 * j + 128 * core, 128)
            pairs.append((w_in_hbm.at[:, pl.ds(at, 128)], out.at[:, to]))
        copies += [pltpu.make_async_copy(a, b, sems.at[4 * j + i]) for i, (a, b) in enumerate(pairs)]
    for copy in copies:
        copy.start()
    block = p0.shape[0] // 2
    rows = 4 * block
    half = 2 * block
    biases = []
    for i, ref in enumerate((p0, p1, p2, p3)):
        at = slice(i * block, (i + 1) * block)
        value = ref[:block, :]
        live = value[:, 0:1].astype(jnp.float32) < MARK
        norm_s[at, :] = jnp.where(live, value, jnp.zeros_like(value))
        grad_s[at, :] = ref[block:, :]
        biases.append(jnp.where(live, 0.0, -1e30))
    bias = jnp.concatenate(biases, axis=0)
    low = lax.broadcasted_iota(jnp.int32, (rows, 128), 1) < 64
    scale = jnp.bfloat16(0.125)
    zero = jnp.zeros((rows, 128), jnp.bfloat16)
    first = place[SIDE] == 0
    for j in range(width // 256):
        cols = slice(128 * j, 128 * j + 128)
        if j % 2 == 0:
            two = slice(128 * j, 128 * j + 256)
            for copy in copies[4 * j : 4 * j + 8]:
                copy.wait()
            normed = norm_s[...]
            queries = dot_nn(normed, wq[:, two]).astype(jnp.bfloat16)
            keys = dot_nn(normed, wk[:, two]).astype(jnp.bfloat16)
            values = dot_nn(normed, wv[:, two]).astype(jnp.bfloat16)
            d_att = dot_nt(grad_s[...], wo[two, :]).astype(jnp.bfloat16)
        here = slice(128 * (j % 2), 128 * (j % 2) + 128)
        q = queries[:, here] * scale
        k = keys[:, here]
        v = values[:, here]
        g = d_att[:, here]
        v_t = v.T
        k_t = (k * scale).T
        att_t, dq_t, dk, dv = [], [], [], []
        for h in range(2):
            mine = low if h == 0 else jnp.logical_not(low)
            scores = dot_nt(k, jnp.where(mine, q, zero)) + bias
            raised = jnp.exp(scores - jnp.max(scores, axis=0, keepdims=True))
            prob = raised * (1.0 / jnp.sum(raised, axis=0, keepdims=True))
            weights = prob.astype(jnp.bfloat16)
            part = slice(64 * h, 64 * h + 64)
            att_t.append(dot_nn(v_t[part], weights))
            dv.append(dot_nn(weights, g))
            d_prob = dot_nt(v, jnp.where(mine, g, zero))
            total = jnp.sum(prob * d_prob, axis=0, keepdims=True)
            d_score = (prob * (d_prob - total)).astype(jnp.bfloat16)
            dq_t.append(dot_nn(k_t[part], d_score))
            dk.append(dot_nn(d_score, q))
        att_pair_t = jnp.concatenate(att_t, axis=0).astype(jnp.bfloat16)
        att_pair = att_pair_t.T
        dq_pair_t = jnp.concatenate(dq_t, axis=0).astype(jnp.bfloat16)
        dk_pair = jnp.where(low, dk[0], dk[1]).astype(jnp.bfloat16)
        dv_pair = jnp.where(low, dv[0], dv[1]).astype(jnp.bfloat16)
        for i, out in enumerate((att0, att1, att2, att3)):
            out[:, cols] = att_pair[i * block : (i + 1) * block]
        for t, piece in enumerate((dq_pair_t.T, dk_pair, dv_pair)):
            dp_own[t, :, cols] = piece[:half]
            dp_oth[t, :, cols] = piece[half:]
        for t, piece in enumerate((dq_pair_t, dk_pair.T, dv_pair.T, att_pair_t)):
            at = slice(64 * (4 * t + j), 64 * (4 * t + j) + 64)
            keep_t[at, :] = jnp.where(first, piece[:64], piece[64:])
            send_t[at, :] = jnp.where(first, piece[64:], piece[:64])


def in_order(place, own, got):
    pieces = []
    low = place == 0
    for j in range(own.shape[1] // 128):
        a, b = own[:, 128 * j : 128 * j + 128], got[:, 128 * j : 128 * j + 128]
        pieces += [jnp.where(low, a, b), jnp.where(low, b, a)]
    return jnp.concatenate(pieces, axis=1)


def d_normed_kernel(place, own, got, w_ref, o0, o1, total):
    step = pl.program_id(0)
    term = dot_nt(in_order(place[CORE], own[step], got[step]), w_ref[...])

    @pl.when(step == 0)
    def _():
        total[...] = term

    @pl.when(step > 0)
    def _():
        total[...] += term

    @pl.when(step == pl.num_programs(0) - 1)
    def _():
        half = o0.shape[0]
        o0[...] = total[:half].astype(o0.dtype)
        o1[...] = total[half:].astype(o1.dtype)


def encode(place, a0, a1, b0, b1, w_ref, hidden_ref, out_ref):
    par, core = place[PAR], place[LINE] // 2
    for k, (a, b) in enumerate(((a0, b0), (a1, b1))):
        s = k ^ par
        projected = dot_nn(in_order(core, a[...], b[...]), w_ref[...])
        live = live_column(place[KEPT + s], a.shape[0])
        out_ref[s] = jnp.where(live, hidden_ref[k] + projected, 0.0).astype(out_ref.dtype)


def patch_grad(place, d0, d1, p0, p1, hidden_ref, gain_ref, out_ref):
    par = place[PAR]
    rows = d0.shape[0]
    for k, (d_ref, p_ref) in enumerate(((d0, p0), (d1, p1))):
        s = k ^ par
        hidden = hidden_ref[k]
        center = hidden - jnp.mean(hidden, axis=-1, keepdims=True)
        spread = jnp.mean(center * center, axis=-1, keepdims=True)
        inv_std = lax.rsqrt(spread + epsilon)
        unit = center * inv_std
        d_hidden = norm_backward(d_ref[...].astype(jnp.float32), gain_ref[...], unit, inv_std)
        live = live_column(place[KEPT + s], rows)
        value = p_ref[rows:, :].astype(jnp.float32) + d_hidden
        out_ref[s] = jnp.where(live, value, 0.0).astype(out_ref.dtype)


def return_kernel(place, a0, a1, b0, b1, w_ref, hidden_ref, d0, d1, m0, m1, gain_ref, encoded, d_patches):
    encode(place, a0, a1, b0, b1, w_ref, hidden_ref, encoded)
    patch_grad(place, d0, d1, m0, m1, hidden_ref, gain_ref, d_patches)


def weight_kernel(
    place, keep, got, p0, p1, p2, p3, r0, r1, r2, r3, d0, d1, a0, a1, b0, b1,
    o0, o1, o2, o3, tokens, total,
):
    del d0, d1, a0, a1, b0, b1
    block = p0.shape[0] // 2
    rows = 4 * block
    columns = o0.shape[0]
    count = 3 * columns // 4
    for i, ref in enumerate((p0, p1, p2, p3, r0, r1, r2, r3)):
        tokens[i * block : (i + 1) * block, :] = ref[block:, :]
    at = slice(4 * count, None)
    total[...] = dot_nn(keep[at, :], tokens[:rows, :]) + dot_nn(got[at, :], tokens[rows:, :])
    for k, out in enumerate((o0, o1, o2, o3)):
        at = pl.multiple_of((place[LINE] ^ k) * columns, 128)
        value = total[:, pl.ds(at, columns)].astype(out.dtype)
        for j in range(4):
            out[count:, columns * j : columns * j + columns] = value[64 * j : 64 * j + 64, :]
    for i, ref in enumerate((p0, p1, p2, p3, r0, r1, r2, r3)):
        tokens[i * block : (i + 1) * block, :] = ref[:block, :]
    for k, out in enumerate((o0, o1, o2, o3)):
        at = pl.ds(pl.multiple_of((place[LINE] ^ k) * count, 16), count)
        value = dot_nn(keep[at, :], tokens[:rows, :]) + dot_nn(got[at, :], tokens[rows:, :])
        out[:count, :] = value.astype(out.dtype)


def sum_kernel(a0, a1, a2, a3, out):
    f32 = jnp.float32
    value = (a0[...].astype(f32) + a1[...].astype(f32)) + (a2[...].astype(f32) + a3[...].astype(f32))
    out[...] = value.astype(out.dtype)


def finish_kernel(place, own, by_x, by_core, by_both, wide, narrow):
    core_low, side_low = place[CORE] == 0, place[SIDE] == 0
    count = own.shape[0] - 64
    columns = narrow.shape[1]

    def pick(at, c, x, part):
        a = jnp.where(side_low == (x == 0), own[at, part], by_x[at, part])
        b = jnp.where(side_low == (x == 0), by_core[at, part], by_both[at, part])
        return jnp.where(core_low == (c == 0), a, b)

    for c in range(2):
        for i in range(count // 64):
            at = slice(64 * i, 64 * i + 64)
            both = jnp.concatenate([pick(at, c, x, slice(None)) for x in range(2)], axis=0)
            col = 128 * (2 * i + c)
            wide[:, col : col + 128] = both.T.astype(wide.dtype)
        for j in range(4):
            for x in range(2):
                row = 128 * (2 * j + c) + 64 * x
                part = slice(columns * j, columns * j + columns)
                narrow[row : row + 64, :] = pick(slice(count, None), c, x, part).astype(narrow.dtype)


SMEM_SPEC = pl.BlockSpec(memory_space=pltpu.SMEM)
VMEM_SPEC = pl.BlockSpec(memory_space=pltpu.VMEM)


def struct(shape, dtype=jnp.bfloat16):
    return jax.ShapeDtypeStruct(shape, dtype)


COST = pl.CostEstimate(flops=1000, bytes_accessed=1000, transcendentals=0)


def in_hbm(value):
    return pltpu.with_memory_space_constraint(value, pltpu.HBM)


def call(kernel, args, outs, limit, place=None, scratch=(), specs=None):
    specs = specs or [VMEM_SPEC] * len(args)
    if place is not None:
        args, specs = (place, *args), [SMEM_SPEC] + specs
    single = not isinstance(outs, list)
    return pl.pallas_call(
        kernel,
        in_specs=specs,
        out_specs=VMEM_SPEC if single else [VMEM_SPEC] * len(outs),
        out_shape=outs,
        scratch_shapes=list(scratch),
        compiler_params=pltpu.CompilerParams(vmem_limit_bytes=limit * MIB),
        cost_estimate=COST,
    )(*args)


def chip_shards(patches, kept_index, kept_count, cotangent, w_qkv, w_out, gain):
    bf16, f32 = jnp.bfloat16, jnp.float32
    samples, slots, width = patches.shape
    reps = lax.axis_size("rep")
    rep = lax.axis_index("rep")
    z = lax.axis_index("seq")
    core, x = rep & 1, rep >> 1
    place = jnp.concatenate(
        [jnp.stack([z & 1, core, z, x]).astype(jnp.int32), kept_count.reshape(samples)]
    )
    own_width = width // 2
    quarter = width // 4
    rows = 4 * slots

    def send(value, move):
        return lax.ppermute(value, AXES, line_perm(move, reps))

    def to_core(value):
        return send(value, lambda x, c, z: (x, 1 - c, z))

    def to_x(value):
        return send(value, lambda x, c, z: (1 - x, c, z))

    def to_chip(value, k):
        return send(value, lambda x, c, z: (x, z >> 1, 2 * c + (k ^ (z & 1))))

    def to_rows(value, k, other):
        return send(value, lambda x, c, z: (x, z >> 1, 2 * (c ^ other) + (k ^ (z & 1))))

    def along(value, k):
        return send(value, lambda x, c, z: (x, c, z ^ k))

    gain_row = gain.reshape(1, width)
    pay = struct((2 * slots, width))
    hbm = pl.BlockSpec(memory_space=pl.ANY)
    *mine, hidden = call(
        norm_kernel,
        tuple(in_hbm(v) for v in (patches, cotangent, kept_index, gain_row)),
        [pay, pay, struct(patches.shape, f32)],
        24,
        place,
        scratch=[
            pltpu.VMEM(patches.shape, bf16),
            pltpu.VMEM(patches.shape, bf16),
            pltpu.VMEM(kept_index.shape, jnp.int32),
            pltpu.VMEM(gain_row.shape, f32),
            pltpu.SemaphoreType.DMA((4,)),
        ],
        specs=[hbm] * 4,
    )
    got = [to_chip(mine[k], k) for k in range(2)]
    here = got + [to_core(v) for v in got]
    from_x = [to_x(v) for v in got]
    there = from_x + [to_core(v) for v in from_x]

    att = struct((slots, own_width))
    d_rows = struct((3, 2 * slots, own_width))
    half_t = struct((width, rows))
    *atts, dp_own, dp_oth, send_t, keep_t = call(
        attend_kernel,
        (*here, in_hbm(w_qkv), in_hbm(w_out)),
        [att] * 4 + [d_rows] * 2 + [half_t] * 2,
        36,
        place,
        scratch=[pltpu.VMEM((rows, width), bf16)] * 2
        + [pltpu.VMEM((width, own_width), bf16)] * 3
        + [pltpu.VMEM((own_width, width), bf16), pltpu.SemaphoreType.DMA((4 * (width // 256),))],
        specs=[VMEM_SPEC] * 4 + [hbm] * 2,
    )
    got_t = to_x(send_t)
    dp_core = to_core(dp_oth)
    back_att = [to_rows(atts[k], k, 0) for k in range(2)] + [to_rows(atts[2 + k], k, 1) for k in range(2)]

    d_normed = pl.pallas_call(
        d_normed_kernel,
        grid_spec=pltpu.PrefetchScalarGridSpec(
            num_scalar_prefetch=1,
            grid=(3,),
            in_specs=[pl.BlockSpec(d_rows.shape, lambda i, p: (0, 0, 0))] * 2
            + [pl.BlockSpec((width, width), lambda i, p: (0, i))],
            out_specs=[pl.BlockSpec((slots, width), lambda i, p: (0, 0))] * 2,
            scratch_shapes=[pltpu.VMEM((2 * slots, width), f32)],
        ),
        out_shape=[struct((slots, width))] * 2,
        compiler_params=pltpu.CompilerParams(vmem_limit_bytes=16 * MIB),
        cost_estimate=COST,
    )(place, dp_own, dp_core, in_hbm(w_qkv))
    back_dn = [to_rows(d_normed[k], k, 0) for k in range(2)]

    part = struct((quarter, width))
    dw = call(
        weight_kernel,
        (keep_t, got_t, *here, *there, *back_dn, *back_att),
        [part] * 4,
        16,
        place,
        scratch=[pltpu.VMEM((2 * rows, width), bf16), pltpu.VMEM((quarter, width), f32)],
        specs=[VMEM_SPEC] * 10 + [pl.BlockSpec(memory_space=pl.ANY)] * 6,
    )
    dw = [dw[0]] + [along(dw[k], k) for k in range(1, 4)]
    encoded, d_patches = call(
        return_kernel,
        (*back_att, w_out, hidden, *back_dn, *mine, gain_row),
        [struct(patches.shape)] * 2,
        12,
        place,
    )
    sums = call(sum_kernel, dw, part, 8)
    by_x = to_x(sums)
    by_core = to_core(sums)
    by_both = to_core(by_x)
    qkv_grad, out_grad = call(
        finish_kernel,
        (sums, by_x, by_core, by_both),
        [struct((width, 3 * quarter), f32), struct((width, quarter), f32)],
        12,
        place,
    )
    return (encoded, d_patches, qkv_grad, out_grad)


def solution(mesh):
    in_specs = (
        P(("grp", "rep"), "seq", None),
        P(("grp", "rep"), "seq"),
        P(("grp", "rep"), "seq"),
        P(("grp", "rep"), "seq", None),
        P(),
        P(),
        P(),
    )
    out_specs = (
        P(("grp", "rep"), "seq", None),
        P(("grp", "rep"), "seq", None),
        P("grp", "seq"),
        P("grp", "seq"),
    )
    chips = mesh.shape["seq"] == 4 and mesh.shape["rep"] % 2 == 0 and HEADS % 8 == 0

    def run(patches, *rest):
        per_device = patches.shape[0] // (mesh.shape["grp"] * mesh.shape["rep"])
        body = chip_shards if chips and per_device == 2 else shards
        inner = jax.shard_map(body, mesh=mesh, in_specs=in_specs, out_specs=out_specs, check_vma=False)
        return inner(patches, *rest)

    return run
```

```python
import functools

import jax
import jax.numpy as jnp
import numpy as np
from jax import lax
from jax.experimental import pallas as pl
from jax.experimental.pallas import tpu as pltpu
from jax.sharding import PartitionSpec as P

HEADS = 16
GRID_COLS = 512


epsilon = 1e-06


def position_table(position, model_width):
    quarter = model_width // 4
    frequency = jnp.exp(-jnp.log(10000.0) * jnp.arange(quarter, dtype=jnp.float32) / quarter)
    grid_row = (position // GRID_COLS).astype(jnp.float32)
    grid_col = (position % GRID_COLS).astype(jnp.float32)
    row_phase = grid_row[..., None] * frequency
    col_phase = grid_col[..., None] * frequency
    return jnp.concatenate(
        [jnp.sin(row_phase), jnp.cos(row_phase), jnp.sin(col_phase), jnp.cos(col_phase)], axis=-1
    )


def normalize(hidden, gain):
    center = hidden - jnp.mean(hidden, axis=-1, keepdims=True)
    spread = jnp.mean(center * center, axis=-1, keepdims=True)
    inv_std = lax.rsqrt(spread + epsilon)
    unit_rows = center * inv_std
    return ((unit_rows * gain).astype(jnp.bfloat16), unit_rows, inv_std)


def norm_backward(d_normed, gain, unit_rows, inv_std):
    scaled = d_normed * gain
    return inv_std * (
        scaled
        - jnp.mean(scaled, axis=-1, keepdims=True)
        - unit_rows * jnp.mean(scaled * unit_rows, axis=-1, keepdims=True)
    )


def head_block(query_rows, grad_rows, key_rows, value_rows, live_keys, score_scale):
    scores = jnp.dot(query_rows, key_rows.T, preferred_element_type=jnp.float32) * score_scale
    scores = jnp.where(live_keys[None, :], scores, -1e30)
    top_score = jnp.max(scores, axis=1, keepdims=True)
    raised = jnp.exp(scores - top_score)
    probability = raised / jnp.sum(raised, axis=1, keepdims=True)
    rounded = probability.astype(jnp.bfloat16)
    attended = jnp.dot(rounded, value_rows, preferred_element_type=jnp.float32).astype(jnp.bfloat16)
    d_value = jnp.dot(rounded.T, grad_rows, preferred_element_type=jnp.float32)
    d_prob = jnp.dot(grad_rows, value_rows.T, preferred_element_type=jnp.float32)
    d_score = (
        probability * (d_prob - jnp.sum(probability * d_prob, axis=1, keepdims=True)) * score_scale
    ).astype(jnp.bfloat16)
    d_query = jnp.dot(d_score, key_rows, preferred_element_type=jnp.float32)
    d_key = jnp.dot(d_score.T, query_rows, preferred_element_type=jnp.float32)
    return (attended, d_query, d_key, d_value)


def attend(query_rows, grad_rows, key_rows, value_rows, live_keys, score_scale):
    row_count = query_rows.shape[0]
    blocks = max(1, row_count // 512)
    while row_count % blocks:
        blocks -= 1
    block_rows = row_count // blocks
    query_blocks = query_rows.reshape(blocks, block_rows, query_rows.shape[1])
    grad_blocks = grad_rows.reshape(blocks, block_rows, grad_rows.shape[1])

    def block_step(carry, pieces):
        key_total, value_total = carry
        attended, d_query, d_key, d_value = head_block(
            pieces[0], pieces[1], key_rows, value_rows, live_keys, score_scale
        )
        return ((key_total + d_key, value_total + d_value), (attended, d_query))

    empty = jnp.zeros(key_rows.shape, jnp.float32)
    (key_total, value_total), (attended, d_query) = lax.scan(
        block_step, (empty, empty), (query_blocks, grad_blocks)
    )
    return (attended.reshape(row_count, -1), d_query.reshape(row_count, -1), key_total, value_total)


def shards(patches, kept_index, kept_count, cotangent, w_qkv, w_out, gain):
    groups = lax.axis_size("seq")
    samples, slot_count, model_width = patches.shape
    head_size = model_width // HEADS
    per_device = max(1, HEADS // groups)
    splits = max(1, groups // HEADS)
    head_groups = groups // splits
    band_width = per_device * head_size
    part_rows = slot_count // splits
    slot_ids = jnp.arange(slot_count, dtype=jnp.int32)
    live_slots = slot_ids[None, :] < kept_count
    hidden = patches.astype(jnp.float32) + position_table(kept_index, model_width)
    normed, unit_rows, inv_std = normalize(hidden, gain)
    flat_normed = normed.reshape(samples * slot_count, model_width)
    packed = jnp.dot(flat_normed, w_qkv, preferred_element_type=jnp.float32).astype(jnp.bfloat16)
    packed = packed.reshape(samples, slot_count, 3 * model_width)
    live_grad = jnp.where(live_slots[:, :, None], cotangent, jnp.zeros_like(cotangent))
    flat_grad = live_grad.reshape(samples * slot_count, model_width)
    d_attended = jnp.dot(flat_grad, w_out.T, preferred_element_type=jnp.float32).astype(
        jnp.bfloat16
    )
    d_attended = d_attended.reshape(samples, slot_count, model_width)

    def to_owners(tensor_block):
        arranged = tensor_block.reshape(samples, splits, part_rows, head_groups, band_width)
        return arranged.transpose(3, 1, 0, 2, 4).reshape(groups, samples, part_rows, band_width)

    key_value_send = jnp.concatenate(
        [
            packed[:, :, model_width : 2 * model_width].reshape(
                samples, slot_count, head_groups, band_width
            ),
            packed[:, :, 2 * model_width :].reshape(samples, slot_count, head_groups, band_width),
        ],
        axis=3,
    )
    key_value_send = key_value_send.transpose(2, 0, 1, 3)
    key_value_send = jnp.broadcast_to(
        key_value_send[:, None], (head_groups, splits, samples, slot_count, 2 * band_width)
    )
    key_value_send = key_value_send.reshape(groups, samples, slot_count, 2 * band_width)
    got_query, got_grad, got_pair = (
        lax.all_to_all(
            to_owners(packed[:, :, :model_width]), "seq", split_axis=0, concat_axis=0, tiled=True
        ),
        lax.all_to_all(to_owners(d_attended), "seq", split_axis=0, concat_axis=0, tiled=True),
        lax.all_to_all(key_value_send, "seq", split_axis=0, concat_axis=0, tiled=True),
    )
    all_counts = lax.all_gather(kept_count, "seq", axis=1, tiled=True)
    live_keys = (slot_ids[None, None, :] < all_counts[:, :, None]).reshape(
        samples, groups * slot_count
    )

    def rows_by_head(tensor_block, row_count):
        arranged = tensor_block.transpose(1, 0, 2, 3).reshape(
            samples, groups * row_count, per_device, head_size
        )
        return arranged.transpose(0, 2, 1, 3)

    query_heads = rows_by_head(got_query, part_rows)
    grad_heads = rows_by_head(got_grad, part_rows)
    key_heads = rows_by_head(got_pair[..., :band_width], slot_count)
    value_heads = rows_by_head(got_pair[..., band_width:], slot_count)
    score_scale = head_size ** (-0.5)

    def one_head(query_rows, grad_rows, key_rows, value_rows, key_live):
        return attend(query_rows, grad_rows, key_rows, value_rows, key_live, score_scale)

    per_head = jax.vmap(one_head, in_axes=(0, 0, 0, 0, None))
    outputs, d_query, d_key, d_value = jax.vmap(per_head)(
        query_heads, grad_heads, key_heads, value_heads, live_keys
    )

    def back_to_sources(tensor_block, row_count):
        arranged = tensor_block.transpose(0, 2, 1, 3).reshape(
            samples, groups, row_count, band_width
        )
        return arranged.transpose(1, 0, 2, 3)

    query_send = back_to_sources(d_query, part_rows).astype(jnp.bfloat16)
    back_out, back_query = (
        lax.all_to_all(
            back_to_sources(outputs, part_rows), "seq", split_axis=0, concat_axis=0, tiled=True
        ),
        lax.all_to_all(query_send, "seq", split_axis=0, concat_axis=0, tiled=True),
    )
    key_value_grad = jnp.concatenate(
        [back_to_sources(d_key, slot_count), back_to_sources(d_value, slot_count)], axis=3
    )
    back_pair = lax.all_to_all(
        key_value_grad.astype(jnp.bfloat16), "seq", split_axis=0, concat_axis=0, tiled=True
    ).astype(key_value_grad.dtype)

    def from_owners(tensor_block):
        arranged = tensor_block.reshape(head_groups, splits, samples, part_rows, band_width)
        return arranged.transpose(2, 1, 3, 0, 4).reshape(samples, slot_count, model_width)

    attended = from_owners(back_out)
    summed_pair = jnp.sum(
        back_pair.reshape(head_groups, splits, samples, slot_count, 2 * band_width), axis=1
    )
    summed_pair = summed_pair.transpose(1, 2, 0, 3)
    key_grad_rows = (
        summed_pair[..., :band_width].reshape(samples, slot_count, model_width).astype(jnp.bfloat16)
    )
    value_grad_rows = (
        summed_pair[..., band_width:].reshape(samples, slot_count, model_width).astype(jnp.bfloat16)
    )
    d_packed = jnp.concatenate([from_owners(back_query), key_grad_rows, value_grad_rows], axis=2)
    flat_attended = attended.reshape(samples * slot_count, model_width)
    projected = jnp.dot(flat_attended, w_out, preferred_element_type=jnp.float32).reshape(
        samples, slot_count, model_width
    )
    encoded = jnp.where(live_slots[:, :, None], hidden + projected, 0.0).astype(jnp.bfloat16)
    flat_packed = d_packed.reshape(samples * slot_count, 3 * model_width)
    d_normed = jnp.dot(flat_packed, w_qkv.T, preferred_element_type=jnp.float32).reshape(
        samples, slot_count, model_width
    )
    d_hidden = norm_backward(d_normed, gain, unit_rows, inv_std)
    d_patches = jnp.where(
        live_slots[:, :, None], live_grad.astype(jnp.float32) + d_hidden, 0.0
    ).astype(jnp.bfloat16)
    columns = flat_grad
    out_part = lax.psum_scatter(
        jnp.dot(columns.T, flat_attended, preferred_element_type=jnp.float32),
        "seq",
        scatter_dimension=0,
        tiled=True,
    ).T
    my_columns = lax.all_to_all(flat_packed, "seq", split_axis=1, concat_axis=0, tiled=True)
    columns = my_columns
    qkv_part = jnp.dot(
        lax.all_gather(flat_normed, "seq", axis=0, tiled=True).T,
        columns,
        preferred_element_type=jnp.float32,
    )
    qkv_grad, out_grad = lax.psum((qkv_part, out_part), "rep")
    return (encoded, d_patches, qkv_grad, out_grad)


AXES = ("seq", "rep")
MARK = 1024.0
MIB = 1024 * 1024


def line_perm(move, reps):
    pairs = []
    for z in range(4):
        for rep in range(reps):
            x, c = rep // 2, rep % 2
            to_x, to_c, to_z = move(x, c, z)
            pairs.append((z * reps + rep, to_z * reps + 2 * to_x + to_c))
    return pairs


def sine_cosine(phase):
    turns = jnp.floor(phase * np.float32(2.0 / np.pi) + 0.5)
    rest = phase - turns * np.float32(1.5703125)
    rest = rest - turns * np.float32(4.837512969970703125e-4)
    rest = rest - turns * np.float32(7.54978995489188216e-8)
    square = rest * rest
    sine = rest + rest * square * (
        np.float32(-1.6666654611e-1)
        + square * (np.float32(8.3321608736e-3) + square * np.float32(-1.9515295891e-4))
    )
    cosine = (
        1.0
        - 0.5 * square
        + square
        * square
        * (
            np.float32(4.166664568298827e-2)
            + square * (np.float32(-1.388731625493765e-3) + square * np.float32(2.443315711809948e-5))
        )
    )
    quadrant = turns.astype(jnp.int32) & 3
    swap = (quadrant & 1) == 1
    first = jnp.where(swap, cosine, sine)
    second = jnp.where(swap, sine, cosine)
    first = jnp.where(quadrant >= 2, -first, first)
    second = jnp.where((quadrant == 1) | (quadrant == 2), -second, second)
    return first, second


def live_column(count, rows):
    return lax.broadcasted_iota(jnp.int32, (rows, 1), 0) < count


def dot_nn(a, b):
    return jnp.dot(a, b, preferred_element_type=jnp.float32)


def dot_nt(a, b):
    return lax.dot_general(a, b, (((1,), (1,)), ((), ())), preferred_element_type=jnp.float32)


PAR, CORE, LINE, SIDE, KEPT = range(5)


def norm_kernel(
    place, patch_hbm, cot_hbm, index_hbm, gain_hbm, p0_ref, p1_ref, hidden_ref,
    patch_ref, cot_ref, index_ref, gain_ref, sems,
):
    par = place[PAR]
    rows, width = patch_ref.shape[1:]
    quarter = width // 4
    copies = [
        pltpu.make_async_copy(src, dst, sems.at[i])
        for i, (src, dst) in enumerate(
            ((index_hbm, index_ref), (patch_hbm, patch_ref), (gain_hbm, gain_ref), (cot_hbm, cot_ref))
        )
    ]
    for copy in copies:
        copy.start()
    order = lax.broadcasted_iota(jnp.int32, (1, quarter), 1).astype(jnp.float32)
    freq = jnp.exp(-np.log(np.float32(10000.0)) * order / quarter)
    diagonal = lax.broadcasted_iota(jnp.int32, (rows, rows), 0) == lax.broadcasted_iota(
        jnp.int32, (rows, rows), 1
    )
    copies[0].wait()
    tables = []
    for k in range(2):
        position = index_ref[pl.ds(k ^ par, 1), :]
        grid_row = (position // GRID_COLS).astype(jnp.float32)
        grid_col = (position % GRID_COLS).astype(jnp.float32)
        grid_row = jnp.sum(jnp.where(diagonal, grid_row, 0.0), axis=1, keepdims=True)
        grid_col = jnp.sum(jnp.where(diagonal, grid_col, 0.0), axis=1, keepdims=True)
        pieces = sine_cosine(grid_row * freq) + sine_cosine(grid_col * freq)
        tables.append(jnp.concatenate(pieces, axis=1))
    copies[1].wait()
    copies[2].wait()
    for k, out_ref in enumerate((p0_ref, p1_ref)):
        s = k ^ par
        hidden = patch_ref[s].astype(jnp.float32) + tables[k]
        hidden_ref[k] = hidden
        center = hidden - jnp.mean(hidden, axis=-1, keepdims=True)
        spread = jnp.mean(center * center, axis=-1, keepdims=True)
        normed = center * lax.rsqrt(spread + epsilon) * gain_ref[...]
        live = live_column(place[KEPT + s], rows)
        out_ref[:rows, :] = jnp.where(live, normed, MARK).astype(out_ref.dtype)
    copies[3].wait()
    for k, out_ref in enumerate((p0_ref, p1_ref)):
        s = k ^ par
        live = live_column(place[KEPT + s], rows)
        grad = cot_ref[s]
        out_ref[rows:, :] = jnp.where(live, grad, jnp.zeros_like(grad))


def load_weights(core, first_pair, w_in_hbm, w_out_hbm, wq, wk, wv, wo, sems):
    width = w_out_hbm.shape[0]
    copies = []
    for j in range(wq.shape[1] // 128):
        to = pl.ds(128 * j, 128)
        row = pl.multiple_of(256 * (first_pair + j) + 128 * core, 128)
        pairs = [(w_out_hbm.at[pl.ds(row, 128), :], wo.at[to, :])]
        for t, out in enumerate((wq, wk, wv)):
            at = pl.multiple_of(t * width + row, 128)
            pairs.append((w_in_hbm.at[:, pl.ds(at, 128)], out.at[:, to]))
        copies += [pltpu.make_async_copy(a, b, sems.at[4 * j + i]) for i, (a, b) in enumerate(pairs)]
    for copy in copies:
        copy.start()
    return copies


def attend_pairs(
    place, first_pair, payloads, w_in_hbm, w_out_hbm, own, oth, keep_t, out_keep, send,
    norm_s, grad_s, att_s, wq, wk, wv, wo, sems,
):
    copies = load_weights(place[CORE], first_pair, w_in_hbm, w_out_hbm, wq, wk, wv, wo, sems)
    block = payloads[0].shape[0] // 2
    rows = 4 * block
    half = 2 * block
    biases = []
    for i, ref in enumerate(payloads):
        at = slice(i * block, (i + 1) * block)
        value = ref[:block, :]
        live = value[:, 0:1].astype(jnp.float32) < MARK
        norm_s[at, :] = jnp.where(live, value, jnp.zeros_like(value))
        grad_s[at, :] = ref[block:, :]
        biases.append(jnp.where(live, 0.0, -1e30))
    bias = jnp.concatenate(biases, axis=0)
    low = lax.broadcasted_iota(jnp.int32, (rows, 128), 1) < 64
    scale = jnp.bfloat16(0.125)
    zero = jnp.zeros((rows, 128), jnp.bfloat16)
    first = place[SIDE] == 0
    count = wq.shape[1] // 128
    for copy in copies:
        copy.wait()
    normed = norm_s[...]
    queries = dot_nn(normed, wq[...]).astype(jnp.bfloat16)
    keys = dot_nn(normed, wk[...]).astype(jnp.bfloat16)
    values = dot_nn(normed, wv[...]).astype(jnp.bfloat16)
    d_att = dot_nt(grad_s[...], wo[...]).astype(jnp.bfloat16)
    for j in range(count):
        cols = slice(128 * j, 128 * j + 128)
        q = queries[:, cols] * scale
        k = keys[:, cols]
        v = values[:, cols]
        g = d_att[:, cols]
        v_t = v.T
        k_t = (k * scale).T
        att_t, dq_t, dk, dv = [], [], [], []
        for h in range(2):
            mine = low if h == 0 else jnp.logical_not(low)
            scores = dot_nt(k, jnp.where(mine, q, zero)) + bias
            raised = jnp.exp(scores - jnp.max(scores, axis=0, keepdims=True))
            prob = raised * (1.0 / jnp.sum(raised, axis=0, keepdims=True))
            weights = prob.astype(jnp.bfloat16)
            part = slice(64 * h, 64 * h + 64)
            att_t.append(dot_nn(v_t[part], weights))
            dv.append(dot_nn(weights, g))
            d_prob = dot_nt(v, jnp.where(mine, g, zero))
            total = jnp.sum(prob * d_prob, axis=0, keepdims=True)
            d_score = (prob * (d_prob - total)).astype(jnp.bfloat16)
            dq_t.append(dot_nn(k_t[part], d_score))
            dk.append(dot_nn(d_score, q))
        att_pair_t = jnp.concatenate(att_t, axis=0).astype(jnp.bfloat16)
        dq_pair_t = jnp.concatenate(dq_t, axis=0).astype(jnp.bfloat16)
        dk_pair = jnp.where(low, dk[0], dk[1]).astype(jnp.bfloat16)
        dv_pair = jnp.where(low, dv[0], dv[1]).astype(jnp.bfloat16)
        for t, piece in enumerate((dq_pair_t.T, dk_pair, dv_pair, att_pair_t.T)):
            own[t, :, cols] = piece[:half]
            oth[t, :, cols] = piece[half:]
        for t, piece in enumerate((dq_pair_t, dk_pair.T, dv_pair.T)):
            at = slice(64 * j, 64 * j + 64)
            part = slice(rows * t, rows * t + rows)
            keep_t[at, part] = jnp.where(first, piece[:64], piece[64:])
            send[at, part] = jnp.where(first, piece[64:], piece[:64])
        at = slice(64 * j, 64 * j + 64)
        att_s[0, at, :] = jnp.where(first, att_pair_t[:64], att_pair_t[64:])
        att_s[1, at, :] = jnp.where(first, att_pair_t[64:], att_pair_t[:64])
    out_keep[...] = dot_nn(att_s[0], grad_s[...])
    send[:, 3 * rows :] = dot_nn(att_s[1], grad_s[...]).astype(send.dtype)


def attend_first(place, p0, p1, p2, p3, *refs):
    attend_pairs(place, 0, (p0, p1, p2, p3), *refs)


def attend_second(place, p0, p1, p2, p3, w_in_hbm, w_out_hbm, after, *refs):
    del after
    attend_pairs(place, 2, (p0, p1, p2, p3), w_in_hbm, w_out_hbm, *refs)


def in_order(place, own, got):
    pieces = []
    low = place == 0
    for j in range(own.shape[1] // 128):
        a, b = own[:, 128 * j : 128 * j + 128], got[:, 128 * j : 128 * j + 128]
        pieces += [jnp.where(low, a, b), jnp.where(low, b, a)]
    return jnp.concatenate(pieces, axis=1)


def rows_kernel(place, own_a, got_a, own_b, got_b, w_ref, after, before, o0, o1, total):
    del after, before
    step = pl.program_id(0)
    core = place[CORE]
    block = o0.shape[0] // 2

    def rows_of(t):
        return jnp.concatenate([in_order(core, own_a[t], got_a[t]), in_order(core, own_b[t], got_b[t])], axis=1)

    term = dot_nt(rows_of(step), w_ref[...])

    @pl.when(step == 0)
    def _():
        total[...] = term
        att = rows_of(3)
        o0[:block, :] = att[:block]
        o1[:block, :] = att[block:]

    @pl.when(step > 0)
    def _():
        total[...] += term

    @pl.when(step == pl.num_programs(0) - 1)
    def _():
        o0[block:, :] = total[:block].astype(o0.dtype)
        o1[block:, :] = total[block:].astype(o1.dtype)


def return_kernel(place, r0, r1, w_ref, hidden_ref, m0, m1, gain_ref, encoded, d_patches):
    par = place[PAR]
    rows = r0.shape[0] // 2
    for k, (r_ref, m_ref) in enumerate(((r0, m0), (r1, m1))):
        s = k ^ par
        live = live_column(place[KEPT + s], rows)
        hidden = hidden_ref[k]
        projected = dot_nn(r_ref[:rows, :], w_ref[...])
        encoded[s] = jnp.where(live, hidden + projected, 0.0).astype(encoded.dtype)
        center = hidden - jnp.mean(hidden, axis=-1, keepdims=True)
        spread = jnp.mean(center * center, axis=-1, keepdims=True)
        inv_std = lax.rsqrt(spread + epsilon)
        unit = center * inv_std
        d_hidden = norm_backward(r_ref[rows:, :].astype(jnp.float32), gain_ref[...], unit, inv_std)
        value = m_ref[rows:, :].astype(jnp.float32) + d_hidden
        d_patches[s] = jnp.where(live, value, 0.0).astype(d_patches.dtype)


def put_out_part(place, out_keep, got, outs, total):
    total[...] = out_keep[...] + got[:, got.shape[1] - total.shape[1] :].astype(jnp.float32)
    columns = total.shape[1] // 4
    tall = total.shape[0] // 4
    for k, out in enumerate(outs):
        at = pl.multiple_of((place[LINE] ^ k) * columns, 128)
        value = total[:, pl.ds(at, columns)].astype(out.dtype)
        base = out.shape[0] - tall
        for j in range(4):
            out[base:, columns * j : columns * j + columns] = value[tall * j : tall * j + tall, :]


def piece_of(ref, at, rows):
    t, j = at // 2, at % 2
    return ref[64 * j : 64 * j + 64, rows * t : rows * t + rows]


def weight_first(
    place, keep, out_keep, got, p0, p1, p2, p3, n0, n1,
    o0, o1, o2, o3, tokens, left, total, out_total,
):
    block = p0.shape[0] // 2
    rows = 4 * block
    for i, ref in enumerate((p0, p1, p2, p3)):
        tokens[i * block : (i + 1) * block, :] = ref[:block, :]
    tokens[rows : rows + 2 * block, :] = n0[...]
    tokens[rows + 2 * block :, :] = n1[...]
    for side, ref in enumerate((keep, got)):
        for i, at in enumerate((0, 2, 4, 5)):
            left[side, 64 * i : 64 * i + 64, :] = piece_of(ref, at, rows)
    total[...] = dot_nn(left[0], tokens[:rows, :]) + dot_nn(left[1], tokens[rows:, :])
    for k, out in enumerate((o0, o1, o2, o3)):
        at = pl.multiple_of((place[LINE] ^ k) * 64, 64)
        out[:64, :] = total[pl.ds(at, 64), :].astype(out.dtype)
    put_out_part(place, out_keep, got, (o0, o1, o2, o3), out_total)


def weight_second(
    place, keep_a, got_a, keep_b, out_keep, got_b, p0, p1, p2, p3, n0, n1, after,
    o0, o1, o2, o3, tokens, left, total, out_total,
):
    del after
    block = p0.shape[0] // 2
    rows = 4 * block
    for i, ref in enumerate((p0, p1, p2, p3)):
        tokens[i * block : (i + 1) * block, :] = ref[:block, :]
    tokens[rows : rows + 2 * block, :] = n0[...]
    tokens[rows + 2 * block :, :] = n1[...]
    for side, (a, b) in enumerate(((keep_a, keep_b), (got_a, got_b))):
        for i, (ref, at) in enumerate(
            ((a, 1), (b, 0), (b, 1), (a, 3), (b, 2), (b, 3), (b, 4), (b, 5))
        ):
            left[side, 64 * i : 64 * i + 64, :] = piece_of(ref, at, rows)
    total[...] = dot_nn(left[0], tokens[:rows, :]) + dot_nn(left[1], tokens[rows:, :])
    for k, out in enumerate((o0, o1, o2, o3)):
        at = pl.multiple_of((place[LINE] ^ k) * 128, 128)
        out[:128, :] = total[pl.ds(at, 128), :].astype(out.dtype)
    put_out_part(place, out_keep, got_b, (o0, o1, o2, o3), out_total)


def sum_kernel(a0, a1, a2, a3, *refs):
    out = refs[-1]
    f32 = jnp.float32
    value = (a0[...].astype(f32) + a1[...].astype(f32)) + (a2[...].astype(f32) + a3[...].astype(f32))
    out[...] = value.astype(out.dtype)


def finish_kernel(place, a0, a1, a2, a3, b0, b1, b2, b3, wide, narrow):
    core_low, side_low = place[CORE] == 0, place[SIDE] == 0
    slab = place[LINE]
    columns = narrow.shape[1]
    spot = jnp.where(slab == 3, 0, slab)
    spots = (spot, jnp.where(spot == 0, 1, 0), jnp.where(spot == 2, 1, 2))

    def pick(refs, c, x, at, part):
        own, by_x, by_core, by_both = refs
        near = jnp.where(side_low == (x == 0), own[at, part], by_x[at, part])
        far = jnp.where(side_low == (x == 0), by_core[at, part], by_both[at, part])
        return jnp.where(core_low == (c == 0), near, far)

    every = slice(None)
    first, second = (a0, a1, a2, a3), (b0, b1, b2, b3)
    for c in range(2):
        for i, (refs, row) in enumerate(((first, 0), (second, 0), (second, 64))):
            at = slice(row, row + 64)
            both = jnp.concatenate([pick(refs, c, x, at, every) for x in range(2)], axis=0)
            col = pl.multiple_of(128 * (2 * spots[i] + c), 128)
            wide[:, pl.ds(col, 128)] = both.T.astype(wide.dtype)
        for half, (refs, base) in enumerate(((first, 64), (second, 128))):
            for j in range(4):
                at = slice(base, base + 32)
                part = slice(columns * j, columns * j + columns)
                for x in range(2):
                    pair, row = 2 * half + j // 2, 32 * (j % 2)
                    row += 128 * (2 * pair + c) + 64 * x
                    narrow[row : row + 32, :] = pick(refs, c, x, at, part).astype(narrow.dtype)


SMEM_SPEC = pl.BlockSpec(memory_space=pltpu.SMEM)
VMEM_SPEC = pl.BlockSpec(memory_space=pltpu.VMEM)


def struct(shape, dtype=jnp.bfloat16):
    return jax.ShapeDtypeStruct(shape, dtype)


COST = pl.CostEstimate(flops=1000, bytes_accessed=1000, transcendentals=0)


def in_hbm(value):
    return pltpu.with_memory_space_constraint(value, pltpu.HBM)


def call(kernel, args, outs, limit, place=None, scratch=(), specs=None):
    specs = specs or [VMEM_SPEC] * len(args)
    if place is not None:
        args, specs = (place, *args), [SMEM_SPEC] + specs
    single = not isinstance(outs, list)
    return pl.pallas_call(
        kernel,
        in_specs=specs,
        out_specs=VMEM_SPEC if single else [VMEM_SPEC] * len(outs),
        out_shape=outs,
        scratch_shapes=list(scratch),
        compiler_params=pltpu.CompilerParams(vmem_limit_bytes=limit * MIB),
        cost_estimate=COST,
    )(*args)


def chip_shards(patches, kept_index, kept_count, cotangent, w_qkv, w_out, gain):
    bf16, f32 = jnp.bfloat16, jnp.float32
    samples, slots, width = patches.shape
    reps = lax.axis_size("rep")
    rep = lax.axis_index("rep")
    z = lax.axis_index("seq")
    core, x = rep & 1, rep >> 1
    place = jnp.concatenate(
        [jnp.stack([z & 1, core, z, x]).astype(jnp.int32), kept_count.reshape(samples)]
    )
    own_width = width // 2
    quarter = width // 4
    rows = 4 * slots

    def send(value, move):
        return lax.ppermute(value, AXES, line_perm(move, reps))

    def to_core(value):
        return send(value, lambda x, c, z: (x, 1 - c, z))

    def to_x(value):
        return send(value, lambda x, c, z: (1 - x, c, z))

    def to_chip(value, k):
        return send(value, lambda x, c, z: (x, z >> 1, 2 * c + (k ^ (z & 1))))

    def to_rows(value, k, other):
        return send(value, lambda x, c, z: (x, z >> 1, 2 * (c ^ other) + (k ^ (z & 1))))

    def along(value, k):
        return send(value, lambda x, c, z: (x, c, z ^ k))

    gain_row = gain.reshape(1, width)
    pay = struct((2 * slots, width))
    hbm = pl.BlockSpec(memory_space=pl.ANY)
    *mine, hidden = call(
        norm_kernel,
        tuple(in_hbm(v) for v in (patches, cotangent, kept_index, gain_row)),
        [pay, pay, struct(patches.shape, f32)],
        24,
        place,
        scratch=[
            pltpu.VMEM(patches.shape, bf16),
            pltpu.VMEM(patches.shape, bf16),
            pltpu.VMEM(kept_index.shape, jnp.int32),
            pltpu.VMEM(gain_row.shape, f32),
            pltpu.SemaphoreType.DMA((4,)),
        ],
        specs=[hbm] * 4,
    )
    got = [to_chip(mine[k], k) for k in range(2)]
    here = got + [to_core(v) for v in got]
    from_x = to_x(jnp.concatenate([v[:slots] for v in got], axis=0))
    there = (from_x, to_core(from_x))

    any_spec = pl.BlockSpec(memory_space=pl.ANY)
    pairs = width // 512
    half_rows = struct((4, 2 * slots, 128 * pairs))
    out_half = (64 * pairs, width)
    half_t = struct((64 * pairs, 3 * rows))
    half_send = struct((64 * pairs, 3 * rows + width))

    def attend(kernel, extra):
        return call(
            kernel,
            (*here, in_hbm(w_qkv), in_hbm(w_out), *extra),
            [half_rows] * 2 + [half_t, struct(out_half, f32), half_send],
            32,
            place,
            scratch=[pltpu.VMEM((rows, width), bf16)] * 2
            + [pltpu.VMEM((2, 64 * pairs, rows), bf16)]
            + [pltpu.VMEM((width, 128 * pairs), bf16)] * 3
            + [pltpu.VMEM((128 * pairs, width), bf16), pltpu.SemaphoreType.DMA((4 * pairs,))],
            specs=[VMEM_SPEC] * 4 + [any_spec] * (2 + len(extra)),
        )

    own_a, oth_a, keep_a, out_keep_a, send_a = attend(attend_first, ())
    got_a = to_x(send_a)
    core_a = to_core(oth_a)
    own_b, oth_b, keep_b, out_keep_b, send_b = attend(attend_second, (from_x,))
    got_b = to_x(send_b)
    core_b = to_core(oth_b)

    def exchange(kernel, args, tall, scratch, after=()):
        outs = call(
            kernel,
            (*args, *here, *there, *after),
            [struct((tall, width))] * 4,
            16,
            place,
            scratch=[pltpu.VMEM((2 * rows, width), bf16)] + scratch + [pltpu.VMEM(out_half, f32)],
            specs=[VMEM_SPEC] * (len(args) + 6) + [any_spec] * len(after),
        )
        return [outs[0]] + [along(outs[k], k) for k in range(1, 4)]

    def spread(parts, after=()):
        sums = call(
            sum_kernel,
            (*parts, *after),
            struct(parts[0].shape),
            8,
            specs=[VMEM_SPEC] * 4 + [any_spec] * len(after),
        )
        by_x = to_x(sums)
        return (sums, by_x, to_core(sums), to_core(by_x))

    parts = exchange(
        weight_first,
        (keep_a, out_keep_a, got_a),
        96,
        [pltpu.VMEM((2, 256, rows), bf16), pltpu.VMEM((256, width), f32)],
    )
    first = spread(parts)
    parts = exchange(
        weight_second,
        (keep_a, got_a, keep_b, out_keep_b, got_b),
        160,
        [pltpu.VMEM((2, 512, rows), bf16), pltpu.VMEM((512, width), f32)],
        (first[0],),
    )
    back = pl.pallas_call(
        rows_kernel,
        grid_spec=pltpu.PrefetchScalarGridSpec(
            num_scalar_prefetch=1,
            grid=(3,),
            in_specs=[pl.BlockSpec(half_rows.shape, lambda i, p: (0, 0, 0))] * 4
            + [pl.BlockSpec((width, width), lambda i, p: (0, i)), any_spec, any_spec],
            out_specs=[pl.BlockSpec(pay.shape, lambda i, p: (0, 0))] * 2,
            scratch_shapes=[pltpu.VMEM((2 * slots, width), f32)],
        ),
        out_shape=[pay] * 2,
        compiler_params=pltpu.CompilerParams(vmem_limit_bytes=20 * MIB),
        cost_estimate=COST,
    )(place, own_a, core_a, own_b, core_b, in_hbm(w_qkv), parts[0], first[1])
    second = spread(parts, (back[0],))
    back = [to_rows(back[k], k, 0) for k in range(2)]
    encoded, d_patches = call(
        return_kernel,
        (*back, w_out, hidden, *mine, gain_row),
        [struct(patches.shape)] * 2,
        12,
        place,
    )
    qkv_grad, out_grad = call(
        finish_kernel,
        (*first, *second),
        [struct((width, 3 * quarter), f32), struct((width, quarter), f32)],
        12,
        place,
    )
    return (encoded, d_patches, qkv_grad, out_grad)


def solution(mesh):
    in_specs = (
        P(("grp", "rep"), "seq", None),
        P(("grp", "rep"), "seq"),
        P(("grp", "rep"), "seq"),
        P(("grp", "rep"), "seq", None),
        P(),
        P(),
        P(),
    )
    out_specs = (
        P(("grp", "rep"), "seq", None),
        P(("grp", "rep"), "seq", None),
        P("grp", "seq"),
        P("grp", "seq"),
    )
    chips = mesh.shape["seq"] == 4 and mesh.shape["rep"] % 2 == 0 and HEADS % 8 == 0

    def run(patches, *rest):
        per_device = patches.shape[0] // (mesh.shape["grp"] * mesh.shape["rep"])
        body = chip_shards if chips and per_device == 2 else shards
        inner = jax.shard_map(body, mesh=mesh, in_specs=in_specs, out_specs=out_specs, check_vma=False)
        return inner(patches, *rest)

    return run
```

```python
import functools

import jax
import jax.numpy as jnp
import numpy as np
from jax import lax
from jax.experimental import pallas as pl
from jax.experimental.pallas import tpu as pltpu
from jax.sharding import PartitionSpec as P

HEADS = 16
GRID_COLS = 512


epsilon = 1e-06


def position_table(position, model_width):
    quarter = model_width // 4
    frequency = jnp.exp(-jnp.log(10000.0) * jnp.arange(quarter, dtype=jnp.float32) / quarter)
    grid_row = (position // GRID_COLS).astype(jnp.float32)
    grid_col = (position % GRID_COLS).astype(jnp.float32)
    row_phase = grid_row[..., None] * frequency
    col_phase = grid_col[..., None] * frequency
    return jnp.concatenate(
        [jnp.sin(row_phase), jnp.cos(row_phase), jnp.sin(col_phase), jnp.cos(col_phase)], axis=-1
    )


def normalize(hidden, gain):
    center = hidden - jnp.mean(hidden, axis=-1, keepdims=True)
    spread = jnp.mean(center * center, axis=-1, keepdims=True)
    inv_std = lax.rsqrt(spread + epsilon)
    unit_rows = center * inv_std
    return ((unit_rows * gain).astype(jnp.bfloat16), unit_rows, inv_std)


def norm_backward(d_normed, gain, unit_rows, inv_std):
    scaled = d_normed * gain
    return inv_std * (
        scaled
        - jnp.mean(scaled, axis=-1, keepdims=True)
        - unit_rows * jnp.mean(scaled * unit_rows, axis=-1, keepdims=True)
    )


def head_block(query_rows, grad_rows, key_rows, value_rows, live_keys, score_scale):
    scores = jnp.dot(query_rows, key_rows.T, preferred_element_type=jnp.float32) * score_scale
    scores = jnp.where(live_keys[None, :], scores, -1e30)
    top_score = jnp.max(scores, axis=1, keepdims=True)
    raised = jnp.exp(scores - top_score)
    probability = raised / jnp.sum(raised, axis=1, keepdims=True)
    rounded = probability.astype(jnp.bfloat16)
    attended = jnp.dot(rounded, value_rows, preferred_element_type=jnp.float32).astype(jnp.bfloat16)
    d_value = jnp.dot(rounded.T, grad_rows, preferred_element_type=jnp.float32)
    d_prob = jnp.dot(grad_rows, value_rows.T, preferred_element_type=jnp.float32)
    d_score = (
        probability * (d_prob - jnp.sum(probability * d_prob, axis=1, keepdims=True)) * score_scale
    ).astype(jnp.bfloat16)
    d_query = jnp.dot(d_score, key_rows, preferred_element_type=jnp.float32)
    d_key = jnp.dot(d_score.T, query_rows, preferred_element_type=jnp.float32)
    return (attended, d_query, d_key, d_value)


def attend(query_rows, grad_rows, key_rows, value_rows, live_keys, score_scale):
    row_count = query_rows.shape[0]
    blocks = max(1, row_count // 512)
    while row_count % blocks:
        blocks -= 1
    block_rows = row_count // blocks
    query_blocks = query_rows.reshape(blocks, block_rows, query_rows.shape[1])
    grad_blocks = grad_rows.reshape(blocks, block_rows, grad_rows.shape[1])

    def block_step(carry, pieces):
        key_total, value_total = carry
        attended, d_query, d_key, d_value = head_block(
            pieces[0], pieces[1], key_rows, value_rows, live_keys, score_scale
        )
        return ((key_total + d_key, value_total + d_value), (attended, d_query))

    empty = jnp.zeros(key_rows.shape, jnp.float32)
    (key_total, value_total), (attended, d_query) = lax.scan(
        block_step, (empty, empty), (query_blocks, grad_blocks)
    )
    return (attended.reshape(row_count, -1), d_query.reshape(row_count, -1), key_total, value_total)


def shards(patches, kept_index, kept_count, cotangent, w_qkv, w_out, gain):
    groups = lax.axis_size("seq")
    samples, slot_count, model_width = patches.shape
    head_size = model_width // HEADS
    per_device = max(1, HEADS // groups)
    splits = max(1, groups // HEADS)
    head_groups = groups // splits
    band_width = per_device * head_size
    part_rows = slot_count // splits
    slot_ids = jnp.arange(slot_count, dtype=jnp.int32)
    live_slots = slot_ids[None, :] < kept_count
    hidden = patches.astype(jnp.float32) + position_table(kept_index, model_width)
    normed, unit_rows, inv_std = normalize(hidden, gain)
    flat_normed = normed.reshape(samples * slot_count, model_width)
    packed = jnp.dot(flat_normed, w_qkv, preferred_element_type=jnp.float32).astype(jnp.bfloat16)
    packed = packed.reshape(samples, slot_count, 3 * model_width)
    live_grad = jnp.where(live_slots[:, :, None], cotangent, jnp.zeros_like(cotangent))
    flat_grad = live_grad.reshape(samples * slot_count, model_width)
    d_attended = jnp.dot(flat_grad, w_out.T, preferred_element_type=jnp.float32).astype(
        jnp.bfloat16
    )
    d_attended = d_attended.reshape(samples, slot_count, model_width)

    def to_owners(tensor_block):
        arranged = tensor_block.reshape(samples, splits, part_rows, head_groups, band_width)
        return arranged.transpose(3, 1, 0, 2, 4).reshape(groups, samples, part_rows, band_width)

    key_value_send = jnp.concatenate(
        [
            packed[:, :, model_width : 2 * model_width].reshape(
                samples, slot_count, head_groups, band_width
            ),
            packed[:, :, 2 * model_width :].reshape(samples, slot_count, head_groups, band_width),
        ],
        axis=3,
    )
    key_value_send = key_value_send.transpose(2, 0, 1, 3)
    key_value_send = jnp.broadcast_to(
        key_value_send[:, None], (head_groups, splits, samples, slot_count, 2 * band_width)
    )
    key_value_send = key_value_send.reshape(groups, samples, slot_count, 2 * band_width)
    got_query, got_grad, got_pair = (
        lax.all_to_all(
            to_owners(packed[:, :, :model_width]), "seq", split_axis=0, concat_axis=0, tiled=True
        ),
        lax.all_to_all(to_owners(d_attended), "seq", split_axis=0, concat_axis=0, tiled=True),
        lax.all_to_all(key_value_send, "seq", split_axis=0, concat_axis=0, tiled=True),
    )
    all_counts = lax.all_gather(kept_count, "seq", axis=1, tiled=True)
    live_keys = (slot_ids[None, None, :] < all_counts[:, :, None]).reshape(
        samples, groups * slot_count
    )

    def rows_by_head(tensor_block, row_count):
        arranged = tensor_block.transpose(1, 0, 2, 3).reshape(
            samples, groups * row_count, per_device, head_size
        )
        return arranged.transpose(0, 2, 1, 3)

    query_heads = rows_by_head(got_query, part_rows)
    grad_heads = rows_by_head(got_grad, part_rows)
    key_heads = rows_by_head(got_pair[..., :band_width], slot_count)
    value_heads = rows_by_head(got_pair[..., band_width:], slot_count)
    score_scale = head_size ** (-0.5)

    def one_head(query_rows, grad_rows, key_rows, value_rows, key_live):
        return attend(query_rows, grad_rows, key_rows, value_rows, key_live, score_scale)

    per_head = jax.vmap(one_head, in_axes=(0, 0, 0, 0, None))
    outputs, d_query, d_key, d_value = jax.vmap(per_head)(
        query_heads, grad_heads, key_heads, value_heads, live_keys
    )

    def back_to_sources(tensor_block, row_count):
        arranged = tensor_block.transpose(0, 2, 1, 3).reshape(
            samples, groups, row_count, band_width
        )
        return arranged.transpose(1, 0, 2, 3)

    query_send = back_to_sources(d_query, part_rows).astype(jnp.bfloat16)
    back_out, back_query = (
        lax.all_to_all(
            back_to_sources(outputs, part_rows), "seq", split_axis=0, concat_axis=0, tiled=True
        ),
        lax.all_to_all(query_send, "seq", split_axis=0, concat_axis=0, tiled=True),
    )
    key_value_grad = jnp.concatenate(
        [back_to_sources(d_key, slot_count), back_to_sources(d_value, slot_count)], axis=3
    )
    back_pair = lax.all_to_all(
        key_value_grad.astype(jnp.bfloat16), "seq", split_axis=0, concat_axis=0, tiled=True
    ).astype(key_value_grad.dtype)

    def from_owners(tensor_block):
        arranged = tensor_block.reshape(head_groups, splits, samples, part_rows, band_width)
        return arranged.transpose(2, 1, 3, 0, 4).reshape(samples, slot_count, model_width)

    attended = from_owners(back_out)
    summed_pair = jnp.sum(
        back_pair.reshape(head_groups, splits, samples, slot_count, 2 * band_width), axis=1
    )
    summed_pair = summed_pair.transpose(1, 2, 0, 3)
    key_grad_rows = (
        summed_pair[..., :band_width].reshape(samples, slot_count, model_width).astype(jnp.bfloat16)
    )
    value_grad_rows = (
        summed_pair[..., band_width:].reshape(samples, slot_count, model_width).astype(jnp.bfloat16)
    )
    d_packed = jnp.concatenate([from_owners(back_query), key_grad_rows, value_grad_rows], axis=2)
    flat_attended = attended.reshape(samples * slot_count, model_width)
    projected = jnp.dot(flat_attended, w_out, preferred_element_type=jnp.float32).reshape(
        samples, slot_count, model_width
    )
    encoded = jnp.where(live_slots[:, :, None], hidden + projected, 0.0).astype(jnp.bfloat16)
    flat_packed = d_packed.reshape(samples * slot_count, 3 * model_width)
    d_normed = jnp.dot(flat_packed, w_qkv.T, preferred_element_type=jnp.float32).reshape(
        samples, slot_count, model_width
    )
    d_hidden = norm_backward(d_normed, gain, unit_rows, inv_std)
    d_patches = jnp.where(
        live_slots[:, :, None], live_grad.astype(jnp.float32) + d_hidden, 0.0
    ).astype(jnp.bfloat16)
    columns = flat_grad
    out_part = lax.psum_scatter(
        jnp.dot(columns.T, flat_attended, preferred_element_type=jnp.float32),
        "seq",
        scatter_dimension=0,
        tiled=True,
    ).T
    my_columns = lax.all_to_all(flat_packed, "seq", split_axis=1, concat_axis=0, tiled=True)
    columns = my_columns
    qkv_part = jnp.dot(
        lax.all_gather(flat_normed, "seq", axis=0, tiled=True).T,
        columns,
        preferred_element_type=jnp.float32,
    )
    qkv_grad, out_grad = lax.psum((qkv_part, out_part), "rep")
    return (encoded, d_patches, qkv_grad, out_grad)


AXES = ("seq", "rep")
MARK = 1024.0
MIB = 1024 * 1024


def line_perm(move, reps):
    pairs = []
    for z in range(4):
        for rep in range(reps):
            x, c = rep // 2, rep % 2
            to_x, to_c, to_z = move(x, c, z)
            pairs.append((z * reps + rep, to_z * reps + 2 * to_x + to_c))
    return pairs


def sine_cosine(phase):
    turns = jnp.floor(phase * np.float32(2.0 / np.pi) + 0.5)
    rest = phase - turns * np.float32(1.5703125)
    rest = rest - turns * np.float32(4.837512969970703125e-4)
    rest = rest - turns * np.float32(7.54978995489188216e-8)
    square = rest * rest
    sine = rest + rest * square * (
        np.float32(-1.6666654611e-1)
        + square * (np.float32(8.3321608736e-3) + square * np.float32(-1.9515295891e-4))
    )
    cosine = (
        1.0
        - 0.5 * square
        + square
        * square
        * (
            np.float32(4.166664568298827e-2)
            + square * (np.float32(-1.388731625493765e-3) + square * np.float32(2.443315711809948e-5))
        )
    )
    quadrant = turns.astype(jnp.int32) & 3
    swap = (quadrant & 1) == 1
    first = jnp.where(swap, cosine, sine)
    second = jnp.where(swap, sine, cosine)
    first = jnp.where(quadrant >= 2, -first, first)
    second = jnp.where((quadrant == 1) | (quadrant == 2), -second, second)
    return first, second


def live_column(count, rows):
    return lax.broadcasted_iota(jnp.int32, (rows, 1), 0) < count


def dot_nn(a, b):
    return jnp.dot(a, b, preferred_element_type=jnp.float32)


def dot_nt(a, b):
    return lax.dot_general(a, b, (((1,), (1,)), ((), ())), preferred_element_type=jnp.float32)


PAR, CORE, LINE, SIDE, KEPT = range(5)


def norm_kernel(
    place, patch_hbm, cot_hbm, index_hbm, gain_hbm, p0_ref, p1_ref, hidden_ref,
    patch_ref, cot_ref, index_ref, gain_ref, sems,
):
    par = place[PAR]
    rows, width = patch_ref.shape[1:]
    quarter = width // 4
    copies = [
        pltpu.make_async_copy(src, dst, sems.at[i])
        for i, (src, dst) in enumerate(
            ((index_hbm, index_ref), (patch_hbm, patch_ref), (gain_hbm, gain_ref), (cot_hbm, cot_ref))
        )
    ]
    for copy in copies:
        copy.start()
    order = lax.broadcasted_iota(jnp.int32, (1, quarter), 1).astype(jnp.float32)
    freq = jnp.exp(-np.log(np.float32(10000.0)) * order / quarter)
    diagonal = lax.broadcasted_iota(jnp.int32, (rows, rows), 0) == lax.broadcasted_iota(
        jnp.int32, (rows, rows), 1
    )
    copies[0].wait()
    tables = []
    for k in range(2):
        position = index_ref[pl.ds(k ^ par, 1), :]
        grid_row = (position // GRID_COLS).astype(jnp.float32)
        grid_col = (position % GRID_COLS).astype(jnp.float32)
        grid_row = jnp.sum(jnp.where(diagonal, grid_row, 0.0), axis=1, keepdims=True)
        grid_col = jnp.sum(jnp.where(diagonal, grid_col, 0.0), axis=1, keepdims=True)
        pieces = sine_cosine(grid_row * freq) + sine_cosine(grid_col * freq)
        tables.append(jnp.concatenate(pieces, axis=1))
    copies[1].wait()
    copies[2].wait()
    for k, out_ref in enumerate((p0_ref, p1_ref)):
        s = k ^ par
        hidden = patch_ref[s].astype(jnp.float32) + tables[k]
        hidden_ref[k] = hidden
        center = hidden - jnp.mean(hidden, axis=-1, keepdims=True)
        spread = jnp.mean(center * center, axis=-1, keepdims=True)
        normed = center * lax.rsqrt(spread + epsilon) * gain_ref[...]
        live = live_column(place[KEPT + s], rows)
        out_ref[:rows, :] = jnp.where(live, normed, MARK).astype(out_ref.dtype)
    copies[3].wait()
    for k, out_ref in enumerate((p0_ref, p1_ref)):
        s = k ^ par
        live = live_column(place[KEPT + s], rows)
        grad = cot_ref[s]
        out_ref[rows:, :] = jnp.where(live, grad, jnp.zeros_like(grad))


def load_weights(core, first_pair, w_in_hbm, w_out_hbm, wq, wk, wv, wo, sems):
    width = w_out_hbm.shape[0]
    copies = []
    for j in range(wq.shape[1] // 128):
        to = pl.ds(128 * j, 128)
        row = pl.multiple_of(256 * (first_pair + j) + 128 * core, 128)
        pairs = [(w_out_hbm.at[pl.ds(row, 128), :], wo.at[to, :])]
        for t, out in enumerate((wq, wk, wv)):
            at = pl.multiple_of(t * width + row, 128)
            pairs.append((w_in_hbm.at[:, pl.ds(at, 128)], out.at[:, to]))
        copies += [pltpu.make_async_copy(a, b, sems.at[4 * j + i]) for i, (a, b) in enumerate(pairs)]
    for copy in copies:
        copy.start()
    return copies


def attend_pairs(
    place, first_pair, payloads, w_in_hbm, w_out_hbm, own, oth, keep_t, out_keep, send,
    norm_s, grad_s, att_s, wq, wk, wv, wo, sems,
):
    copies = load_weights(place[CORE], first_pair, w_in_hbm, w_out_hbm, wq, wk, wv, wo, sems)
    block = payloads[0].shape[0] // 2
    rows = 4 * block
    half = 2 * block
    biases = []
    for i, ref in enumerate(payloads):
        at = slice(i * block, (i + 1) * block)
        value = ref[:block, :]
        live = value[:, 0:1].astype(jnp.float32) < MARK
        norm_s[at, :] = jnp.where(live, value, jnp.zeros_like(value))
        grad_s[at, :] = ref[block:, :]
        biases.append(jnp.where(live, 0.0, -1e30))
    bias = jnp.concatenate(biases, axis=0)
    low = lax.broadcasted_iota(jnp.int32, (rows, 128), 1) < 64
    scale = jnp.bfloat16(0.125)
    zero = jnp.zeros((rows, 128), jnp.bfloat16)
    first = place[SIDE] == 0
    count = wq.shape[1] // 128
    for copy in copies:
        copy.wait()
    normed = norm_s[...]
    queries = dot_nn(normed, wq[...]).astype(jnp.bfloat16)
    keys = dot_nn(normed, wk[...]).astype(jnp.bfloat16)
    values = dot_nn(normed, wv[...]).astype(jnp.bfloat16)
    d_att = dot_nt(grad_s[...], wo[...]).astype(jnp.bfloat16)
    for j in range(count):
        cols = slice(128 * j, 128 * j + 128)
        q = queries[:, cols] * scale
        k = keys[:, cols]
        v = values[:, cols]
        g = d_att[:, cols]
        v_t = v.T
        k_t = (k * scale).T
        att_t, dq_t, dk, dv = [], [], [], []
        for h in range(2):
            mine = low if h == 0 else jnp.logical_not(low)
            scores = dot_nt(k, jnp.where(mine, q, zero)) + bias
            raised = jnp.exp(scores - jnp.max(scores, axis=0, keepdims=True))
            prob = raised * (1.0 / jnp.sum(raised, axis=0, keepdims=True))
            weights = prob.astype(jnp.bfloat16)
            part = slice(64 * h, 64 * h + 64)
            att_t.append(dot_nn(v_t[part], weights))
            dv.append(dot_nn(weights, g))
            d_prob = dot_nt(v, jnp.where(mine, g, zero))
            total = jnp.sum(prob * d_prob, axis=0, keepdims=True)
            d_score = (prob * (d_prob - total)).astype(jnp.bfloat16)
            dq_t.append(dot_nn(k_t[part], d_score))
            dk.append(dot_nn(d_score, q))
        att_pair_t = jnp.concatenate(att_t, axis=0).astype(jnp.bfloat16)
        dq_pair_t = jnp.concatenate(dq_t, axis=0).astype(jnp.bfloat16)
        dk_pair = jnp.where(low, dk[0], dk[1]).astype(jnp.bfloat16)
        dv_pair = jnp.where(low, dv[0], dv[1]).astype(jnp.bfloat16)
        for t, piece in enumerate((dq_pair_t.T, dk_pair, dv_pair, att_pair_t.T)):
            own[t, :, cols] = piece[:half]
            oth[t, :, cols] = piece[half:]
        for t, piece in enumerate((dq_pair_t, dk_pair.T, dv_pair.T)):
            at = slice(64 * j, 64 * j + 64)
            part = slice(rows * t, rows * t + rows)
            keep_t[at, part] = jnp.where(first, piece[:64], piece[64:])
            send[at, part] = jnp.where(first, piece[64:], piece[:64])
        at = slice(64 * j, 64 * j + 64)
        att_s[0, at, :] = jnp.where(first, att_pair_t[:64], att_pair_t[64:])
        att_s[1, at, :] = jnp.where(first, att_pair_t[64:], att_pair_t[:64])
    out_keep[...] = dot_nn(att_s[0], grad_s[...])
    send[:, 3 * rows :] = dot_nn(att_s[1], grad_s[...]).astype(send.dtype)


def attend_first(place, p0, p1, p2, p3, *refs):
    attend_pairs(place, 0, (p0, p1, p2, p3), *refs)


def attend_second(place, p0, p1, p2, p3, w_in_hbm, w_out_hbm, after, *refs):
    del after
    attend_pairs(place, 2, (p0, p1, p2, p3), w_in_hbm, w_out_hbm, *refs)


def in_order(place, own, got):
    pieces = []
    low = place == 0
    for j in range(own.shape[1] // 128):
        a, b = own[:, 128 * j : 128 * j + 128], got[:, 128 * j : 128 * j + 128]
        pieces += [jnp.where(low, a, b), jnp.where(low, b, a)]
    return jnp.concatenate(pieces, axis=1)


def rows_kernel(place, own_a, got_a, own_b, got_b, w_ref, after, before, o0, o1, total):
    del after, before
    step = pl.program_id(0)
    core = place[CORE]
    block = o0.shape[0] // 2

    def rows_of(t):
        return jnp.concatenate([in_order(core, own_a[t], got_a[t]), in_order(core, own_b[t], got_b[t])], axis=1)

    term = dot_nt(rows_of(step), w_ref[...])

    @pl.when(step == 0)
    def _():
        total[...] = term
        att = rows_of(3)
        o0[:block, :] = att[:block]
        o1[:block, :] = att[block:]

    @pl.when(step > 0)
    def _():
        total[...] += term

    @pl.when(step == pl.num_programs(0) - 1)
    def _():
        o0[block:, :] = total[:block].astype(o0.dtype)
        o1[block:, :] = total[block:].astype(o1.dtype)


def return_kernel(place, r0, r1, w_ref, hidden_ref, m0, m1, gain_ref, encoded, d_patches):
    par = place[PAR]
    rows = r0.shape[0] // 2
    for k, (r_ref, m_ref) in enumerate(((r0, m0), (r1, m1))):
        s = k ^ par
        live = live_column(place[KEPT + s], rows)
        hidden = hidden_ref[k]
        projected = dot_nn(r_ref[:rows, :], w_ref[...])
        encoded[s] = jnp.where(live, hidden + projected, 0.0).astype(encoded.dtype)
        center = hidden - jnp.mean(hidden, axis=-1, keepdims=True)
        spread = jnp.mean(center * center, axis=-1, keepdims=True)
        inv_std = lax.rsqrt(spread + epsilon)
        unit = center * inv_std
        d_hidden = norm_backward(r_ref[rows:, :].astype(jnp.float32), gain_ref[...], unit, inv_std)
        value = m_ref[rows:, :].astype(jnp.float32) + d_hidden
        d_patches[s] = jnp.where(live, value, 0.0).astype(d_patches.dtype)


def put_parts(place, total, out_keep, got, keep, send, out_total):
    out_total[...] = out_keep[...] + got[:, got.shape[1] - out_total.shape[1] :].astype(jnp.float32)
    columns = out_total.shape[1] // 4
    tall = out_total.shape[0] // 4
    count = total.shape[0] // 4
    for k in range(4):
        ref, spot = (keep, send)[k % 2], k // 2
        at = pl.multiple_of((place[LINE] ^ k) * count, 64)
        ref[spot, :count, :] = total[pl.ds(at, count), :].astype(ref.dtype)
        at = pl.multiple_of((place[LINE] ^ k) * columns, 128)
        value = out_total[:, pl.ds(at, columns)].astype(ref.dtype)
        for j in range(4):
            ref[spot, count:, columns * j : columns * j + columns] = value[tall * j : tall * j + tall, :]


def piece_of(ref, at, rows):
    t, j = at // 2, at % 2
    return ref[64 * j : 64 * j + 64, rows * t : rows * t + rows]


def weight_first(
    place, keep, out_keep, got, p0, p1, p2, p3, n0, n1,
    part_keep, part_send, tokens, left, total, out_total,
):
    block = p0.shape[0] // 2
    rows = 4 * block
    for i, ref in enumerate((p0, p1, p2, p3)):
        tokens[i * block : (i + 1) * block, :] = ref[:block, :]
    tokens[rows : rows + 2 * block, :] = n0[...]
    tokens[rows + 2 * block :, :] = n1[...]
    for side, ref in enumerate((keep, got)):
        for i, at in enumerate((0, 2, 4, 5)):
            left[side, 64 * i : 64 * i + 64, :] = piece_of(ref, at, rows)
    total[...] = dot_nn(left[0], tokens[:rows, :]) + dot_nn(left[1], tokens[rows:, :])
    put_parts(place, total, out_keep, got, part_keep, part_send, out_total)


def weight_second(
    place, keep_a, got_a, keep_b, out_keep, got_b, p0, p1, p2, p3, n0, n1, after,
    part_keep, part_send, tokens, left, total, out_total,
):
    del after
    block = p0.shape[0] // 2
    rows = 4 * block
    for i, ref in enumerate((p0, p1, p2, p3)):
        tokens[i * block : (i + 1) * block, :] = ref[:block, :]
    tokens[rows : rows + 2 * block, :] = n0[...]
    tokens[rows + 2 * block :, :] = n1[...]
    for side, (a, b) in enumerate(((keep_a, keep_b), (got_a, got_b))):
        for i, (ref, at) in enumerate(
            ((a, 1), (b, 0), (b, 1), (a, 3), (b, 2), (b, 3), (b, 4), (b, 5))
        ):
            left[side, 64 * i : 64 * i + 64, :] = piece_of(ref, at, rows)
    total[...] = dot_nn(left[0], tokens[:rows, :]) + dot_nn(left[1], tokens[rows:, :])
    put_parts(place, total, out_keep, got_b, part_keep, part_send, out_total)


def pair_kernel(keep, got, mine, send):
    mine[...] = keep[0] + got[0].astype(jnp.float32)
    send[...] = (keep[1] + got[1].astype(jnp.float32)).astype(send.dtype)


def sum_kernel(mine, got, *refs):
    out = refs[-1]
    out[...] = (mine[...] + got[...].astype(jnp.float32)).astype(out.dtype)


def finish_kernel(place, a0, a1, a2, a3, b0, b1, b2, b3, wide, narrow):
    core_low, side_low = place[CORE] == 0, place[SIDE] == 0
    slab = place[LINE]
    columns = narrow.shape[1]
    spot = jnp.where(slab == 3, 0, slab)
    spots = (spot, jnp.where(spot == 0, 1, 0), jnp.where(spot == 2, 1, 2))

    def pick(refs, c, x, at, part):
        own, by_x, by_core, by_both = refs
        near = jnp.where(side_low == (x == 0), own[at, part], by_x[at, part])
        far = jnp.where(side_low == (x == 0), by_core[at, part], by_both[at, part])
        return jnp.where(core_low == (c == 0), near, far)

    every = slice(None)
    first, second = (a0, a1, a2, a3), (b0, b1, b2, b3)
    for c in range(2):
        for i, (refs, row) in enumerate(((first, 0), (second, 0), (second, 64))):
            at = slice(row, row + 64)
            both = jnp.concatenate([pick(refs, c, x, at, every) for x in range(2)], axis=0)
            col = pl.multiple_of(128 * (2 * spots[i] + c), 128)
            wide[:, pl.ds(col, 128)] = both.T.astype(wide.dtype)
        for half, (refs, base) in enumerate(((first, 64), (second, 128))):
            for j in range(4):
                at = slice(base, base + 32)
                part = slice(columns * j, columns * j + columns)
                for x in range(2):
                    pair, row = 2 * half + j // 2, 32 * (j % 2)
                    row += 128 * (2 * pair + c) + 64 * x
                    narrow[row : row + 32, :] = pick(refs, c, x, at, part).astype(narrow.dtype)


SMEM_SPEC = pl.BlockSpec(memory_space=pltpu.SMEM)
VMEM_SPEC = pl.BlockSpec(memory_space=pltpu.VMEM)


def struct(shape, dtype=jnp.bfloat16):
    return jax.ShapeDtypeStruct(shape, dtype)


COST = pl.CostEstimate(flops=1000, bytes_accessed=1000, transcendentals=0)


def in_hbm(value):
    return pltpu.with_memory_space_constraint(value, pltpu.HBM)


def call(kernel, args, outs, limit, place=None, scratch=(), specs=None):
    specs = specs or [VMEM_SPEC] * len(args)
    if place is not None:
        args, specs = (place, *args), [SMEM_SPEC] + specs
    single = not isinstance(outs, list)
    return pl.pallas_call(
        kernel,
        in_specs=specs,
        out_specs=VMEM_SPEC if single else [VMEM_SPEC] * len(outs),
        out_shape=outs,
        scratch_shapes=list(scratch),
        compiler_params=pltpu.CompilerParams(vmem_limit_bytes=limit * MIB),
        cost_estimate=COST,
    )(*args)


def chip_shards(patches, kept_index, kept_count, cotangent, w_qkv, w_out, gain):
    bf16, f32 = jnp.bfloat16, jnp.float32
    samples, slots, width = patches.shape
    reps = lax.axis_size("rep")
    rep = lax.axis_index("rep")
    z = lax.axis_index("seq")
    core, x = rep & 1, rep >> 1
    place = jnp.concatenate(
        [jnp.stack([z & 1, core, z, x]).astype(jnp.int32), kept_count.reshape(samples)]
    )
    own_width = width // 2
    quarter = width // 4
    rows = 4 * slots

    def send(value, move):
        return lax.ppermute(value, AXES, line_perm(move, reps))

    def to_core(value):
        return send(value, lambda x, c, z: (x, 1 - c, z))

    def to_x(value):
        return send(value, lambda x, c, z: (1 - x, c, z))

    def to_chip(value, k):
        return send(value, lambda x, c, z: (x, z >> 1, 2 * c + (k ^ (z & 1))))

    def to_rows(value, k, other):
        return send(value, lambda x, c, z: (x, z >> 1, 2 * (c ^ other) + (k ^ (z & 1))))

    def along(value, k):
        return send(value, lambda x, c, z: (x, c, z ^ k))

    gain_row = gain.reshape(1, width)
    pay = struct((2 * slots, width))
    hbm = pl.BlockSpec(memory_space=pl.ANY)
    *mine, hidden = call(
        norm_kernel,
        tuple(in_hbm(v) for v in (patches, cotangent, kept_index, gain_row)),
        [pay, pay, struct(patches.shape, f32)],
        24,
        place,
        scratch=[
            pltpu.VMEM(patches.shape, bf16),
            pltpu.VMEM(patches.shape, bf16),
            pltpu.VMEM(kept_index.shape, jnp.int32),
            pltpu.VMEM(gain_row.shape, f32),
            pltpu.SemaphoreType.DMA((4,)),
        ],
        specs=[hbm] * 4,
    )
    got = [to_chip(mine[k], k) for k in range(2)]
    here = got + [to_core(v) for v in got]
    from_x = to_x(jnp.concatenate([v[:slots] for v in got], axis=0))
    there = (from_x, to_core(from_x))

    any_spec = pl.BlockSpec(memory_space=pl.ANY)
    pairs = width // 512
    half_rows = struct((4, 2 * slots, 128 * pairs))
    out_half = (64 * pairs, width)
    half_t = struct((64 * pairs, 3 * rows))
    half_send = struct((64 * pairs, 3 * rows + width))

    def attend(kernel, extra):
        return call(
            kernel,
            (*here, in_hbm(w_qkv), in_hbm(w_out), *extra),
            [half_rows] * 2 + [half_t, struct(out_half, f32), half_send],
            32,
            place,
            scratch=[pltpu.VMEM((rows, width), bf16)] * 2
            + [pltpu.VMEM((2, 64 * pairs, rows), bf16)]
            + [pltpu.VMEM((width, 128 * pairs), bf16)] * 3
            + [pltpu.VMEM((128 * pairs, width), bf16), pltpu.SemaphoreType.DMA((4 * pairs,))],
            specs=[VMEM_SPEC] * 4 + [any_spec] * (2 + len(extra)),
        )

    own_a, oth_a, keep_a, out_keep_a, send_a = attend(attend_first, ())
    got_a = to_x(send_a)
    core_a = to_core(oth_a)
    own_b, oth_b, keep_b, out_keep_b, send_b = attend(attend_second, (from_x,))
    got_b = to_x(send_b)
    core_b = to_core(oth_b)

    def parts_of(kernel, args, tall, scratch, after=()):
        return call(
            kernel,
            (*args, *here, *there, *after),
            [struct((2, tall, width), f32), struct((2, tall, width))],
            16,
            place,
            scratch=[pltpu.VMEM((2 * rows, width), bf16)] + scratch + [pltpu.VMEM(out_half, f32)],
            specs=[VMEM_SPEC] * (len(args) + 6) + [any_spec] * len(after),
        )

    def pair_sums(keep, part):
        shape = keep.shape[1:]
        mine, part = call(pair_kernel, (keep, along(part, 1)), [struct(shape, f32), struct(shape)], 8)
        return mine, part, along(part, 2)

    def spread(mine, part, after=()):
        sums = call(
            sum_kernel,
            (mine, part, *after),
            struct(part.shape),
            8,
            specs=[VMEM_SPEC] * 2 + [any_spec] * len(after),
        )
        by_x = to_x(sums)
        return (sums, by_x, to_core(sums), to_core(by_x))

    keep, part = parts_of(
        weight_first,
        (keep_a, out_keep_a, got_a),
        96,
        [pltpu.VMEM((2, 256, rows), bf16), pltpu.VMEM((256, width), f32)],
    )
    first_sum, paired, first_got = pair_sums(keep, part)
    keep, part = parts_of(
        weight_second,
        (keep_a, got_a, keep_b, out_keep_b, got_b),
        160,
        [pltpu.VMEM((2, 512, rows), bf16), pltpu.VMEM((512, width), f32)],
        (paired,),
    )
    started = part
    second_sum, _, second_got = pair_sums(keep, part)
    first = spread(first_sum, first_got)
    back = pl.pallas_call(
        rows_kernel,
        grid_spec=pltpu.PrefetchScalarGridSpec(
            num_scalar_prefetch=1,
            grid=(3,),
            in_specs=[pl.BlockSpec(half_rows.shape, lambda i, p: (0, 0, 0))] * 4
            + [pl.BlockSpec((width, width), lambda i, p: (0, i)), any_spec, any_spec],
            out_specs=[pl.BlockSpec(pay.shape, lambda i, p: (0, 0))] * 2,
            scratch_shapes=[pltpu.VMEM((2 * slots, width), f32)],
        ),
        out_shape=[pay] * 2,
        compiler_params=pltpu.CompilerParams(vmem_limit_bytes=20 * MIB),
        cost_estimate=COST,
    )(place, own_a, core_a, own_b, core_b, in_hbm(w_qkv), started, first[1])
    second = spread(second_sum, second_got, (back[0],))
    back = [to_rows(back[k], k, 0) for k in range(2)]
    encoded, d_patches = call(
        return_kernel,
        (*back, w_out, hidden, *mine, gain_row),
        [struct(patches.shape)] * 2,
        12,
        place,
    )
    qkv_grad, out_grad = call(
        finish_kernel,
        (*first, *second),
        [struct((width, 3 * quarter), f32), struct((width, quarter), f32)],
        12,
        place,
    )
    return (encoded, d_patches, qkv_grad, out_grad)


def solution(mesh):
    in_specs = (
        P(("grp", "rep"), "seq", None),
        P(("grp", "rep"), "seq"),
        P(("grp", "rep"), "seq"),
        P(("grp", "rep"), "seq", None),
        P(),
        P(),
        P(),
    )
    out_specs = (
        P(("grp", "rep"), "seq", None),
        P(("grp", "rep"), "seq", None),
        P("grp", "seq"),
        P("grp", "seq"),
    )
    chips = mesh.shape["seq"] == 4 and mesh.shape["rep"] % 2 == 0 and HEADS % 8 == 0

    def run(patches, *rest):
        per_device = patches.shape[0] // (mesh.shape["grp"] * mesh.shape["rep"])
        body = chip_shards if chips and per_device == 2 else shards
        inner = jax.shard_map(body, mesh=mesh, in_specs=in_specs, out_specs=out_specs, check_vma=False)
        return inner(patches, *rest)

    return run
```

```python
import functools

import jax
import jax.numpy as jnp
import numpy as np
from jax import lax
from jax.experimental import pallas as pl
from jax.experimental.pallas import tpu as pltpu
from jax.sharding import PartitionSpec as P

HEADS = 16
GRID_COLS = 512


epsilon = 1e-06


def position_table(position, model_width):
    quarter = model_width // 4
    frequency = jnp.exp(-jnp.log(10000.0) * jnp.arange(quarter, dtype=jnp.float32) / quarter)
    grid_row = (position // GRID_COLS).astype(jnp.float32)
    grid_col = (position % GRID_COLS).astype(jnp.float32)
    row_phase = grid_row[..., None] * frequency
    col_phase = grid_col[..., None] * frequency
    return jnp.concatenate(
        [jnp.sin(row_phase), jnp.cos(row_phase), jnp.sin(col_phase), jnp.cos(col_phase)], axis=-1
    )


def normalize(hidden, gain):
    center = hidden - jnp.mean(hidden, axis=-1, keepdims=True)
    spread = jnp.mean(center * center, axis=-1, keepdims=True)
    inv_std = lax.rsqrt(spread + epsilon)
    unit_rows = center * inv_std
    return ((unit_rows * gain).astype(jnp.bfloat16), unit_rows, inv_std)


def norm_backward(d_normed, gain, unit_rows, inv_std):
    scaled = d_normed * gain
    return inv_std * (
        scaled
        - jnp.mean(scaled, axis=-1, keepdims=True)
        - unit_rows * jnp.mean(scaled * unit_rows, axis=-1, keepdims=True)
    )


def head_block(query_rows, grad_rows, key_rows, value_rows, live_keys, score_scale):
    scores = jnp.dot(query_rows, key_rows.T, preferred_element_type=jnp.float32) * score_scale
    scores = jnp.where(live_keys[None, :], scores, -1e30)
    top_score = jnp.max(scores, axis=1, keepdims=True)
    raised = jnp.exp(scores - top_score)
    probability = raised / jnp.sum(raised, axis=1, keepdims=True)
    rounded = probability.astype(jnp.bfloat16)
    attended = jnp.dot(rounded, value_rows, preferred_element_type=jnp.float32).astype(jnp.bfloat16)
    d_value = jnp.dot(rounded.T, grad_rows, preferred_element_type=jnp.float32)
    d_prob = jnp.dot(grad_rows, value_rows.T, preferred_element_type=jnp.float32)
    d_score = (
        probability * (d_prob - jnp.sum(probability * d_prob, axis=1, keepdims=True)) * score_scale
    ).astype(jnp.bfloat16)
    d_query = jnp.dot(d_score, key_rows, preferred_element_type=jnp.float32)
    d_key = jnp.dot(d_score.T, query_rows, preferred_element_type=jnp.float32)
    return (attended, d_query, d_key, d_value)


def attend(query_rows, grad_rows, key_rows, value_rows, live_keys, score_scale):
    row_count = query_rows.shape[0]
    blocks = max(1, row_count // 512)
    while row_count % blocks:
        blocks -= 1
    block_rows = row_count // blocks
    query_blocks = query_rows.reshape(blocks, block_rows, query_rows.shape[1])
    grad_blocks = grad_rows.reshape(blocks, block_rows, grad_rows.shape[1])

    def block_step(carry, pieces):
        key_total, value_total = carry
        attended, d_query, d_key, d_value = head_block(
            pieces[0], pieces[1], key_rows, value_rows, live_keys, score_scale
        )
        return ((key_total + d_key, value_total + d_value), (attended, d_query))

    empty = jnp.zeros(key_rows.shape, jnp.float32)
    (key_total, value_total), (attended, d_query) = lax.scan(
        block_step, (empty, empty), (query_blocks, grad_blocks)
    )
    return (attended.reshape(row_count, -1), d_query.reshape(row_count, -1), key_total, value_total)


def shards(patches, kept_index, kept_count, cotangent, w_qkv, w_out, gain):
    groups = lax.axis_size("seq")
    samples, slot_count, model_width = patches.shape
    head_size = model_width // HEADS
    per_device = max(1, HEADS // groups)
    splits = max(1, groups // HEADS)
    head_groups = groups // splits
    band_width = per_device * head_size
    part_rows = slot_count // splits
    slot_ids = jnp.arange(slot_count, dtype=jnp.int32)
    live_slots = slot_ids[None, :] < kept_count
    hidden = patches.astype(jnp.float32) + position_table(kept_index, model_width)
    normed, unit_rows, inv_std = normalize(hidden, gain)
    flat_normed = normed.reshape(samples * slot_count, model_width)
    packed = jnp.dot(flat_normed, w_qkv, preferred_element_type=jnp.float32).astype(jnp.bfloat16)
    packed = packed.reshape(samples, slot_count, 3 * model_width)
    live_grad = jnp.where(live_slots[:, :, None], cotangent, jnp.zeros_like(cotangent))
    flat_grad = live_grad.reshape(samples * slot_count, model_width)
    d_attended = jnp.dot(flat_grad, w_out.T, preferred_element_type=jnp.float32).astype(
        jnp.bfloat16
    )
    d_attended = d_attended.reshape(samples, slot_count, model_width)

    def to_owners(tensor_block):
        arranged = tensor_block.reshape(samples, splits, part_rows, head_groups, band_width)
        return arranged.transpose(3, 1, 0, 2, 4).reshape(groups, samples, part_rows, band_width)

    key_value_send = jnp.concatenate(
        [
            packed[:, :, model_width : 2 * model_width].reshape(
                samples, slot_count, head_groups, band_width
            ),
            packed[:, :, 2 * model_width :].reshape(samples, slot_count, head_groups, band_width),
        ],
        axis=3,
    )
    key_value_send = key_value_send.transpose(2, 0, 1, 3)
    key_value_send = jnp.broadcast_to(
        key_value_send[:, None], (head_groups, splits, samples, slot_count, 2 * band_width)
    )
    key_value_send = key_value_send.reshape(groups, samples, slot_count, 2 * band_width)
    got_query, got_grad, got_pair = (
        lax.all_to_all(
            to_owners(packed[:, :, :model_width]), "seq", split_axis=0, concat_axis=0, tiled=True
        ),
        lax.all_to_all(to_owners(d_attended), "seq", split_axis=0, concat_axis=0, tiled=True),
        lax.all_to_all(key_value_send, "seq", split_axis=0, concat_axis=0, tiled=True),
    )
    all_counts = lax.all_gather(kept_count, "seq", axis=1, tiled=True)
    live_keys = (slot_ids[None, None, :] < all_counts[:, :, None]).reshape(
        samples, groups * slot_count
    )

    def rows_by_head(tensor_block, row_count):
        arranged = tensor_block.transpose(1, 0, 2, 3).reshape(
            samples, groups * row_count, per_device, head_size
        )
        return arranged.transpose(0, 2, 1, 3)

    query_heads = rows_by_head(got_query, part_rows)
    grad_heads = rows_by_head(got_grad, part_rows)
    key_heads = rows_by_head(got_pair[..., :band_width], slot_count)
    value_heads = rows_by_head(got_pair[..., band_width:], slot_count)
    score_scale = head_size ** (-0.5)

    def one_head(query_rows, grad_rows, key_rows, value_rows, key_live):
        return attend(query_rows, grad_rows, key_rows, value_rows, key_live, score_scale)

    per_head = jax.vmap(one_head, in_axes=(0, 0, 0, 0, None))
    outputs, d_query, d_key, d_value = jax.vmap(per_head)(
        query_heads, grad_heads, key_heads, value_heads, live_keys
    )

    def back_to_sources(tensor_block, row_count):
        arranged = tensor_block.transpose(0, 2, 1, 3).reshape(
            samples, groups, row_count, band_width
        )
        return arranged.transpose(1, 0, 2, 3)

    query_send = back_to_sources(d_query, part_rows).astype(jnp.bfloat16)
    back_out, back_query = (
        lax.all_to_all(
            back_to_sources(outputs, part_rows), "seq", split_axis=0, concat_axis=0, tiled=True
        ),
        lax.all_to_all(query_send, "seq", split_axis=0, concat_axis=0, tiled=True),
    )
    key_value_grad = jnp.concatenate(
        [back_to_sources(d_key, slot_count), back_to_sources(d_value, slot_count)], axis=3
    )
    back_pair = lax.all_to_all(
        key_value_grad.astype(jnp.bfloat16), "seq", split_axis=0, concat_axis=0, tiled=True
    ).astype(key_value_grad.dtype)

    def from_owners(tensor_block):
        arranged = tensor_block.reshape(head_groups, splits, samples, part_rows, band_width)
        return arranged.transpose(2, 1, 3, 0, 4).reshape(samples, slot_count, model_width)

    attended = from_owners(back_out)
    summed_pair = jnp.sum(
        back_pair.reshape(head_groups, splits, samples, slot_count, 2 * band_width), axis=1
    )
    summed_pair = summed_pair.transpose(1, 2, 0, 3)
    key_grad_rows = (
        summed_pair[..., :band_width].reshape(samples, slot_count, model_width).astype(jnp.bfloat16)
    )
    value_grad_rows = (
        summed_pair[..., band_width:].reshape(samples, slot_count, model_width).astype(jnp.bfloat16)
    )
    d_packed = jnp.concatenate([from_owners(back_query), key_grad_rows, value_grad_rows], axis=2)
    flat_attended = attended.reshape(samples * slot_count, model_width)
    projected = jnp.dot(flat_attended, w_out, preferred_element_type=jnp.float32).reshape(
        samples, slot_count, model_width
    )
    encoded = jnp.where(live_slots[:, :, None], hidden + projected, 0.0).astype(jnp.bfloat16)
    flat_packed = d_packed.reshape(samples * slot_count, 3 * model_width)
    d_normed = jnp.dot(flat_packed, w_qkv.T, preferred_element_type=jnp.float32).reshape(
        samples, slot_count, model_width
    )
    d_hidden = norm_backward(d_normed, gain, unit_rows, inv_std)
    d_patches = jnp.where(
        live_slots[:, :, None], live_grad.astype(jnp.float32) + d_hidden, 0.0
    ).astype(jnp.bfloat16)
    columns = flat_grad
    out_part = lax.psum_scatter(
        jnp.dot(columns.T, flat_attended, preferred_element_type=jnp.float32),
        "seq",
        scatter_dimension=0,
        tiled=True,
    ).T
    my_columns = lax.all_to_all(flat_packed, "seq", split_axis=1, concat_axis=0, tiled=True)
    columns = my_columns
    qkv_part = jnp.dot(
        lax.all_gather(flat_normed, "seq", axis=0, tiled=True).T,
        columns,
        preferred_element_type=jnp.float32,
    )
    qkv_grad, out_grad = lax.psum((qkv_part, out_part), "rep")
    return (encoded, d_patches, qkv_grad, out_grad)


AXES = ("seq", "rep")
MARK = 1024.0
MIB = 1024 * 1024


def line_perm(move, reps):
    pairs = []
    for z in range(4):
        for rep in range(reps):
            x, c = rep // 2, rep % 2
            to_x, to_c, to_z = move(x, c, z)
            pairs.append((z * reps + rep, to_z * reps + 2 * to_x + to_c))
    return pairs


def sine_cosine(phase):
    turns = jnp.floor(phase * np.float32(2.0 / np.pi) + 0.5)
    rest = phase - turns * np.float32(1.5703125)
    rest = rest - turns * np.float32(4.837512969970703125e-4)
    rest = rest - turns * np.float32(7.54978995489188216e-8)
    square = rest * rest
    sine = rest + rest * square * (
        np.float32(-1.6666654611e-1)
        + square * (np.float32(8.3321608736e-3) + square * np.float32(-1.9515295891e-4))
    )
    cosine = (
        1.0
        - 0.5 * square
        + square
        * square
        * (
            np.float32(4.166664568298827e-2)
            + square * (np.float32(-1.388731625493765e-3) + square * np.float32(2.443315711809948e-5))
        )
    )
    quadrant = turns.astype(jnp.int32) & 3
    swap = (quadrant & 1) == 1
    first = jnp.where(swap, cosine, sine)
    second = jnp.where(swap, sine, cosine)
    first = jnp.where(quadrant >= 2, -first, first)
    second = jnp.where((quadrant == 1) | (quadrant == 2), -second, second)
    return first, second


def live_column(count, rows):
    return lax.broadcasted_iota(jnp.int32, (rows, 1), 0) < count


def dot_nn(a, b):
    return jnp.dot(a, b, preferred_element_type=jnp.float32)


def dot_nt(a, b):
    return lax.dot_general(a, b, (((1,), (1,)), ((), ())), preferred_element_type=jnp.float32)


PAR, CORE, LINE, SIDE, KEPT = range(5)


def norm_kernel(
    place, patch_hbm, index_hbm, gain_hbm, n0_ref, n1_ref, hidden_ref, patch_ref, index_ref, gain_ref, sems,
):
    par = place[PAR]
    rows, width = patch_ref.shape[1:]
    quarter = width // 4
    copies = [
        pltpu.make_async_copy(src, dst, sems.at[i])
        for i, (src, dst) in enumerate(
            ((index_hbm, index_ref), (patch_hbm, patch_ref), (gain_hbm, gain_ref))
        )
    ]
    for copy in copies:
        copy.start()
    order = lax.broadcasted_iota(jnp.int32, (1, quarter), 1).astype(jnp.float32)
    freq = jnp.exp(-np.log(np.float32(10000.0)) * order / quarter)
    diagonal = lax.broadcasted_iota(jnp.int32, (rows, rows), 0) == lax.broadcasted_iota(
        jnp.int32, (rows, rows), 1
    )
    copies[0].wait()
    tables = []
    for k in range(2):
        position = index_ref[pl.ds(k ^ par, 1), :]
        grid_row = (position // GRID_COLS).astype(jnp.float32)
        grid_col = (position % GRID_COLS).astype(jnp.float32)
        grid_row = jnp.sum(jnp.where(diagonal, grid_row, 0.0), axis=1, keepdims=True)
        grid_col = jnp.sum(jnp.where(diagonal, grid_col, 0.0), axis=1, keepdims=True)
        pieces = sine_cosine(grid_row * freq) + sine_cosine(grid_col * freq)
        tables.append(jnp.concatenate(pieces, axis=1))
    copies[1].wait()
    copies[2].wait()
    for k, out_ref in enumerate((n0_ref, n1_ref)):
        s = k ^ par
        hidden = patch_ref[s].astype(jnp.float32) + tables[k]
        hidden_ref[k] = hidden
        center = hidden - jnp.mean(hidden, axis=-1, keepdims=True)
        spread = jnp.mean(center * center, axis=-1, keepdims=True)
        normed = center * lax.rsqrt(spread + epsilon) * gain_ref[...]
        live = live_column(place[KEPT + s], rows)
        out_ref[...] = jnp.where(live, normed, MARK).astype(out_ref.dtype)


def grad_kernel(place, cot_hbm, after, g0_ref, g1_ref, cot_ref, sem):
    del after
    copy = pltpu.make_async_copy(cot_hbm, cot_ref, sem)
    copy.start()
    copy.wait()
    for k, out_ref in enumerate((g0_ref, g1_ref)):
        s = k ^ place[PAR]
        grad = cot_ref[s]
        live = live_column(place[KEPT + s], grad.shape[0])
        out_ref[...] = jnp.where(live, grad, jnp.zeros_like(grad))


def join_kernel(a, b, after, out):
    del after
    block = a.shape[0]
    out[:block, :] = a[...]
    out[block:, :] = b[...]


def forward_kernel(
    place, n0, n1, w_in_hbm, w_out_hbm, norm_out, q_out, k_out, v_out, wo, prob_out, att_out,
    wq, wk, wv, sems,
):
    block, width = n0.shape
    rows = 2 * block
    pairs = width // 256
    copies = []
    for j in range(pairs):
        to = pl.ds(128 * j, 128)
        row = pl.multiple_of(256 * j + 128 * place[CORE], 128)
        moves = [(w_out_hbm.at[pl.ds(row, 128), :], wo.at[to, :])]
        for t, out in enumerate((wq, wk, wv)):
            at = pl.multiple_of(t * width + row, 128)
            moves.append((w_in_hbm.at[:, pl.ds(at, 128)], out.at[:, to]))
        copies += [pltpu.make_async_copy(a, b, sems.at[4 * j + i]) for i, (a, b) in enumerate(moves)]
    for copy in copies:
        copy.start()
    biases = []
    for i, ref in enumerate((n0, n1)):
        value = ref[...]
        live = value[:, 0:1].astype(jnp.float32) < MARK
        norm_out[i * block : (i + 1) * block, :] = jnp.where(live, value, jnp.zeros_like(value))
        biases.append(jnp.where(live, 0.0, -1e30))
    bias = jnp.concatenate(biases, axis=0)
    for copy in copies:
        copy.wait()
    normed = norm_out[...]
    q_out[...] = dot_nn(normed, wq[...]).astype(jnp.bfloat16) * jnp.bfloat16(0.125)
    k_out[...] = dot_nn(normed, wk[...]).astype(jnp.bfloat16)
    v_out[...] = dot_nn(normed, wv[...]).astype(jnp.bfloat16)
    low = lax.broadcasted_iota(jnp.int32, (rows, 128), 1) < 64
    zero = jnp.zeros((rows, 128), jnp.bfloat16)
    for j in range(pairs):
        cols = slice(128 * j, 128 * j + 128)
        q = q_out[:, cols]
        k = k_out[:, cols]
        v_t = v_out[:, cols].T
        for h in range(2):
            mine = low if h == 0 else jnp.logical_not(low)
            scores = dot_nt(k, jnp.where(mine, q, zero)) + bias
            raised = jnp.exp(scores - jnp.max(scores, axis=0, keepdims=True))
            prob = raised * (1.0 / jnp.sum(raised, axis=0, keepdims=True))
            prob_out[2 * j + h] = prob
            part = slice(64 * h, 64 * h + 64)
            to = slice(128 * j + 64 * h, 128 * j + 64 * h + 64)
            att_out[to, :] = dot_nn(v_t[part], prob.astype(jnp.bfloat16)).astype(jnp.bfloat16)


def backward_pairs(
    place, first_pair, grads, q_in, k_in, v_in, wo, prob_in, att_in, own, oth, keep_t, out_keep, send,
    grad_s, att_s,
):
    half = grads[0].shape[0]
    rows = 2 * half
    for i, ref in enumerate(grads):
        grad_s[i * half : (i + 1) * half, :] = ref[...]
    low = lax.broadcasted_iota(jnp.int32, (rows, 128), 1) < 64
    scale = jnp.bfloat16(0.125)
    zero = jnp.zeros((rows, 128), jnp.bfloat16)
    first = place[SIDE] == 0
    count = own.shape[2] // 128
    mine_rows = slice(128 * first_pair, 128 * (first_pair + count))
    d_att = dot_nt(grad_s[...], wo[mine_rows, :]).astype(jnp.bfloat16)
    for j in range(count):
        cols = slice(128 * j, 128 * j + 128)
        pair = slice(128 * (first_pair + j), 128 * (first_pair + j) + 128)
        q = q_in[:, pair]
        k = k_in[:, pair]
        v = v_in[:, pair]
        g = d_att[:, cols]
        k_t = (k * scale).T
        dq_t, dk, dv = [], [], []
        for h in range(2):
            mine = low if h == 0 else jnp.logical_not(low)
            prob = prob_in[2 * (first_pair + j) + h]
            dv.append(dot_nn(prob.astype(jnp.bfloat16), g))
            d_prob = dot_nt(v, jnp.where(mine, g, zero))
            total = jnp.sum(prob * d_prob, axis=0, keepdims=True)
            d_score = (prob * (d_prob - total)).astype(jnp.bfloat16)
            dq_t.append(dot_nn(k_t[64 * h : 64 * h + 64], d_score))
            dk.append(dot_nn(d_score, q))
        att_pair_t = att_in[pair, :]
        dq_pair_t = jnp.concatenate(dq_t, axis=0).astype(jnp.bfloat16)
        dk_pair = jnp.where(low, dk[0], dk[1]).astype(jnp.bfloat16)
        dv_pair = jnp.where(low, dv[0], dv[1]).astype(jnp.bfloat16)
        for t, piece in enumerate((dq_pair_t.T, dk_pair, dv_pair, att_pair_t.T)):
            own[t, :, cols] = piece[:half]
            oth[t, :, cols] = piece[half:]
        at = slice(64 * j, 64 * j + 64)
        for t, piece in enumerate((dq_pair_t, dk_pair.T, dv_pair.T)):
            part = slice(rows * t, rows * t + rows)
            keep_t[at, part] = jnp.where(first, piece[:64], piece[64:])
            send[at, part] = jnp.where(first, piece[64:], piece[:64])
        att_s[0, at, :] = jnp.where(first, att_pair_t[:64], att_pair_t[64:])
        att_s[1, at, :] = jnp.where(first, att_pair_t[64:], att_pair_t[:64])
    out_keep[...] = dot_nn(att_s[0], grad_s[...])
    send[:, 3 * rows :] = dot_nn(att_s[1], grad_s[...]).astype(send.dtype)


def backward_second(place, g0, g1, *refs):
    backward_pairs(place, 2, (g0, g1), *refs)


def backward_first(place, g0, g1, q_in, k_in, v_in, wo, prob_in, att_in, after, *refs):
    del after
    backward_pairs(place, 0, (g0, g1), q_in, k_in, v_in, wo, prob_in, att_in, *refs)


def in_order(place, own, got):
    pieces = []
    low = place == 0
    for j in range(own.shape[1] // 128):
        a, b = own[:, 128 * j : 128 * j + 128], got[:, 128 * j : 128 * j + 128]
        pieces += [jnp.where(low, a, b), jnp.where(low, b, a)]
    return jnp.concatenate(pieces, axis=1)


def rows_kernel(place, own_a, got_a, own_b, got_b, w_ref, after, o0, o1, total):
    del after
    step = pl.program_id(0)
    core = place[CORE]
    block = o0.shape[0] // 2

    def rows_of(t):
        return jnp.concatenate([in_order(core, own_a[t], got_a[t]), in_order(core, own_b[t], got_b[t])], axis=1)

    term = dot_nt(rows_of(step), w_ref[...])

    @pl.when(step == 0)
    def _():
        total[...] = term
        att = rows_of(3)
        o0[:block, :] = att[:block]
        o1[:block, :] = att[block:]

    @pl.when(step > 0)
    def _():
        total[...] += term

    @pl.when(step == pl.num_programs(0) - 1)
    def _():
        o0[block:, :] = total[:block].astype(o0.dtype)
        o1[block:, :] = total[block:].astype(o1.dtype)


def return_kernel(place, r0, r1, w_ref, hidden_ref, m0, m1, gain_ref, encoded, d_patches):
    par = place[PAR]
    rows = r0.shape[0] // 2
    for k, (r_ref, m_ref) in enumerate(((r0, m0), (r1, m1))):
        s = k ^ par
        live = live_column(place[KEPT + s], rows)
        hidden = hidden_ref[k]
        projected = dot_nn(r_ref[:rows, :], w_ref[...])
        encoded[s] = jnp.where(live, hidden + projected, 0.0).astype(encoded.dtype)
        center = hidden - jnp.mean(hidden, axis=-1, keepdims=True)
        spread = jnp.mean(center * center, axis=-1, keepdims=True)
        inv_std = lax.rsqrt(spread + epsilon)
        unit = center * inv_std
        d_hidden = norm_backward(r_ref[rows:, :].astype(jnp.float32), gain_ref[...], unit, inv_std)
        value = m_ref[...].astype(jnp.float32) + d_hidden
        d_patches[s] = jnp.where(live, value, 0.0).astype(d_patches.dtype)


def put_parts(place, total, out_keep, got, keep, send, out_total):
    out_total[...] = out_keep[...] + got[:, got.shape[1] - out_total.shape[1] :].astype(jnp.float32)
    columns = out_total.shape[1] // 4
    tall = out_total.shape[0] // 4
    count = total.shape[0] // 4
    for k in range(4):
        ref, spot = (keep, send)[k % 2], k // 2
        at = pl.multiple_of((place[LINE] ^ k) * count, 64)
        ref[spot, :count, :] = total[pl.ds(at, count), :].astype(ref.dtype)
        at = pl.multiple_of((place[LINE] ^ k) * columns, 128)
        value = out_total[:, pl.ds(at, columns)].astype(ref.dtype)
        for j in range(4):
            ref[spot, count:, columns * j : columns * j + columns] = value[tall * j : tall * j + tall, :]


def piece_of(ref, at, rows):
    t, j = at // 2, at % 2
    return ref[64 * j : 64 * j + 64, rows * t : rows * t + rows]


def weight_first(
    place, keep, out_keep, got, normed, n0, n1,
    part_keep, part_send, tokens, left, total, out_total,
):
    rows, half = normed.shape[0], n0.shape[0]
    tokens[:half, :] = n0[...]
    tokens[half:, :] = n1[...]
    for side, ref in enumerate((keep, got)):
        for i, at in enumerate((0, 2, 4, 5)):
            left[side, 64 * i : 64 * i + 64, :] = piece_of(ref, at, rows)
    total[...] = dot_nn(left[0], normed[...]) + dot_nn(left[1], tokens[...])
    put_parts(place, total, out_keep, got, part_keep, part_send, out_total)


def weight_second(
    place, keep_a, got_a, keep_b, out_keep, got_b, normed, n0, n1, after, before,
    part_keep, part_send, tokens, left, total, out_total,
):
    del after, before
    rows, half = normed.shape[0], n0.shape[0]
    tokens[:half, :] = n0[...]
    tokens[half:, :] = n1[...]
    for side, (a, b) in enumerate(((keep_a, keep_b), (got_a, got_b))):
        for i, (ref, at) in enumerate(
            ((a, 1), (b, 0), (b, 1), (a, 3), (b, 2), (b, 3), (b, 4), (b, 5))
        ):
            left[side, 64 * i : 64 * i + 64, :] = piece_of(ref, at, rows)
    total[...] = dot_nn(left[0], normed[...]) + dot_nn(left[1], tokens[...])
    put_parts(place, total, out_keep, got_b, part_keep, part_send, out_total)


def pair_kernel(keep, got, *refs):
    mine, send = refs[-2:]
    mine[...] = keep[0] + got[0].astype(jnp.float32)
    send[...] = (keep[1] + got[1].astype(jnp.float32)).astype(send.dtype)


def sum_kernel(mine, got, *refs):
    out = refs[-1]
    out[...] = (mine[...] + got[...].astype(jnp.float32)).astype(out.dtype)


def finish_kernel(place, a0, a1, a2, a3, b0, b1, b2, b3, wide, narrow):
    core_low, side_low = place[CORE] == 0, place[SIDE] == 0
    slab = place[LINE]
    columns = narrow.shape[1]
    spot = jnp.where(slab == 3, 0, slab)
    spots = (spot, jnp.where(spot == 0, 1, 0), jnp.where(spot == 2, 1, 2))

    def pick(refs, c, x, at, part):
        own, by_x, by_core, by_both = refs
        near = jnp.where(side_low == (x == 0), own[at, part], by_x[at, part])
        far = jnp.where(side_low == (x == 0), by_core[at, part], by_both[at, part])
        return jnp.where(core_low == (c == 0), near, far)

    every = slice(None)
    first, second = (a0, a1, a2, a3), (b0, b1, b2, b3)
    for c in range(2):
        for i, (refs, row) in enumerate(((first, 0), (second, 0), (second, 64))):
            at = slice(row, row + 64)
            both = jnp.concatenate([pick(refs, c, x, at, every) for x in range(2)], axis=0)
            col = pl.multiple_of(128 * (2 * spots[i] + c), 128)
            wide[:, pl.ds(col, 128)] = both.T.astype(wide.dtype)
        for half, (refs, base) in enumerate(((first, 64), (second, 128))):
            for j in range(4):
                at = slice(base, base + 32)
                part = slice(columns * j, columns * j + columns)
                for x in range(2):
                    pair, row = 2 * half + j // 2, 32 * (j % 2)
                    row += 128 * (2 * pair + c) + 64 * x
                    narrow[row : row + 32, :] = pick(refs, c, x, at, part).astype(narrow.dtype)


SMEM_SPEC = pl.BlockSpec(memory_space=pltpu.SMEM)
VMEM_SPEC = pl.BlockSpec(memory_space=pltpu.VMEM)


def struct(shape, dtype=jnp.bfloat16):
    return jax.ShapeDtypeStruct(shape, dtype)


COST = pl.CostEstimate(flops=1000, bytes_accessed=1000, transcendentals=0)


def in_hbm(value):
    return pltpu.with_memory_space_constraint(value, pltpu.HBM)


def call(kernel, args, outs, limit, place=None, scratch=(), specs=None):
    specs = specs or [VMEM_SPEC] * len(args)
    if place is not None:
        args, specs = (place, *args), [SMEM_SPEC] + specs
    single = not isinstance(outs, list)
    return pl.pallas_call(
        kernel,
        in_specs=specs,
        out_specs=VMEM_SPEC if single else [VMEM_SPEC] * len(outs),
        out_shape=outs,
        scratch_shapes=list(scratch),
        compiler_params=pltpu.CompilerParams(vmem_limit_bytes=limit * MIB),
        cost_estimate=COST,
    )(*args)


def chip_shards(patches, kept_index, kept_count, cotangent, w_qkv, w_out, gain):
    bf16, f32 = jnp.bfloat16, jnp.float32
    samples, slots, width = patches.shape
    reps = lax.axis_size("rep")
    rep = lax.axis_index("rep")
    z = lax.axis_index("seq")
    core, x = rep & 1, rep >> 1
    place = jnp.concatenate(
        [jnp.stack([z & 1, core, z, x]).astype(jnp.int32), kept_count.reshape(samples)]
    )
    own_width = width // 2
    quarter = width // 4
    rows = 4 * slots

    def send(value, move):
        return lax.ppermute(value, AXES, line_perm(move, reps))

    def to_core(value):
        return send(value, lambda x, c, z: (x, 1 - c, z))

    def to_x(value):
        return send(value, lambda x, c, z: (1 - x, c, z))

    def to_chip(value, k):
        return send(value, lambda x, c, z: (x, z >> 1, 2 * c + (k ^ (z & 1))))

    def to_rows(value, k, other):
        return send(value, lambda x, c, z: (x, z >> 1, 2 * (c ^ other) + (k ^ (z & 1))))

    def along(value, k):
        return send(value, lambda x, c, z: (x, c, z ^ k))

    gain_row = gain.reshape(1, width)
    pay = struct((2 * slots, width))
    block = struct((slots, width))
    any_spec = pl.BlockSpec(memory_space=pl.ANY)
    *normed, hidden = call(
        norm_kernel,
        tuple(in_hbm(v) for v in (patches, kept_index, gain_row)),
        [block, block, struct(patches.shape, f32)],
        24,
        place,
        scratch=[
            pltpu.VMEM(patches.shape, bf16),
            pltpu.VMEM(kept_index.shape, jnp.int32),
            pltpu.VMEM(gain_row.shape, f32),
            pltpu.SemaphoreType.DMA((3,)),
        ],
        specs=[any_spec] * 3,
    )
    mine = call(
        grad_kernel,
        (in_hbm(cotangent), normed[0]),
        [block, block],
        8,
        place,
        scratch=[pltpu.VMEM(patches.shape, bf16), pltpu.SemaphoreType.DMA(())],
        specs=[any_spec] * 2,
    )
    got = [to_chip(normed[k], k) for k in range(2)]
    got_g = [to_chip(mine[k], k) for k in range(2)]
    joined = call(join_kernel, (*got, mine[0]), pay, 8, specs=[VMEM_SPEC] * 2 + [any_spec])
    here = (joined, to_core(joined))
    from_x = to_x(joined)
    there = (from_x, to_core(from_x))

    pairs = width // 512
    own_cols = struct((rows, own_width))
    normed, *saved = call(
        forward_kernel,
        (*here, in_hbm(w_qkv), in_hbm(w_out)),
        [struct((rows, width))]
        + [own_cols] * 3
        + [struct((own_width, width)), struct((4 * pairs, rows, rows), f32), struct((own_width, rows))],
        32,
        place,
        scratch=[pltpu.VMEM((width, own_width), bf16)] * 3 + [pltpu.SemaphoreType.DMA((8 * pairs,))],
        specs=[VMEM_SPEC] * 2 + [any_spec] * 2,
    )
    joined = call(join_kernel, (*got_g, saved[0]), pay, 8, specs=[VMEM_SPEC] * 2 + [any_spec])
    here_g = (joined, to_core(joined))
    half_rows = struct((4, 2 * slots, 128 * pairs))
    out_half = (64 * pairs, width)
    half_t = struct((64 * pairs, 3 * rows))
    half_send = struct((64 * pairs, 3 * rows + width))

    def backward(kernel, extra):
        return call(
            kernel,
            (*here_g, *saved, *extra),
            [half_rows] * 2 + [half_t, struct(out_half, f32), half_send],
            32,
            place,
            scratch=[pltpu.VMEM((rows, width), bf16), pltpu.VMEM((2, 64 * pairs, rows), bf16)],
            specs=[VMEM_SPEC] * 8 + [any_spec] * len(extra),
        )

    own_a, oth_a, keep_a, out_keep_a, send_a = backward(backward_first, (from_x,))
    got_a = to_x(send_a)
    core_a = to_core(oth_a)
    own_b, oth_b, keep_b, out_keep_b, send_b = backward(backward_second, ())
    got_b = to_x(send_b)
    core_b = to_core(oth_b)

    def parts_of(kernel, args, tall, scratch, after=()):
        return call(
            kernel,
            (*args, normed, *there, *after),
            [struct((2, tall, width), f32), struct((2, tall, width))],
            16,
            place,
            scratch=[pltpu.VMEM((rows, width), bf16)] + scratch + [pltpu.VMEM(out_half, f32)],
            specs=[VMEM_SPEC] * (len(args) + 3) + [any_spec] * len(after),
        )

    def pair_sums(keep, part, after=()):
        shape = keep.shape[1:]
        mine, part = call(
            pair_kernel,
            (keep, along(part, 1), *after),
            [struct(shape, f32), struct(shape)],
            8,
            specs=[VMEM_SPEC] * 2 + [any_spec] * len(after),
        )
        return mine, part, along(part, 2)

    def spread(mine, part, after=()):
        sums = call(
            sum_kernel,
            (mine, part, *after),
            struct(part.shape),
            8,
            specs=[VMEM_SPEC] * 2 + [any_spec] * len(after),
        )
        by_x = to_x(sums)
        return (sums, by_x, to_core(sums), to_core(by_x))

    keep, part = parts_of(
        weight_first,
        (keep_a, out_keep_a, got_a),
        96,
        [pltpu.VMEM((2, 256, rows), bf16), pltpu.VMEM((256, width), f32)],
    )
    first_sum, paired, first_got = pair_sums(keep, part)
    back = pl.pallas_call(
        rows_kernel,
        grid_spec=pltpu.PrefetchScalarGridSpec(
            num_scalar_prefetch=1,
            grid=(3,),
            in_specs=[pl.BlockSpec(half_rows.shape, lambda i, p: (0, 0, 0))] * 4
            + [pl.BlockSpec((width, width), lambda i, p: (0, i)), any_spec],
            out_specs=[pl.BlockSpec(pay.shape, lambda i, p: (0, 0))] * 2,
            scratch_shapes=[pltpu.VMEM((2 * slots, width), f32)],
        ),
        out_shape=[pay] * 2,
        compiler_params=pltpu.CompilerParams(vmem_limit_bytes=20 * MIB),
        cost_estimate=COST,
    )(place, own_a, core_a, own_b, core_b, in_hbm(w_qkv), part)
    keep, part = parts_of(
        weight_second,
        (keep_a, got_a, keep_b, out_keep_b, got_b),
        160,
        [pltpu.VMEM((2, 512, rows), bf16), pltpu.VMEM((512, width), f32)],
        (paired, back[0]),
    )
    back = [to_rows(back[k], k, 0) for k in range(2)]
    second_sum, _, second_got = pair_sums(keep, part, (back[0],))
    first = spread(first_sum, first_got)
    second = spread(second_sum, second_got, (back[1], first[1]))
    encoded, d_patches = call(
        return_kernel,
        (*back, w_out, hidden, *mine, gain_row),
        [struct(patches.shape)] * 2,
        12,
        place,
    )
    qkv_grad, out_grad = call(
        finish_kernel,
        (*first, *second),
        [struct((width, 3 * quarter), f32), struct((width, quarter), f32)],
        12,
        place,
    )
    return (encoded, d_patches, qkv_grad, out_grad)


def solution(mesh):
    in_specs = (
        P(("grp", "rep"), "seq", None),
        P(("grp", "rep"), "seq"),
        P(("grp", "rep"), "seq"),
        P(("grp", "rep"), "seq", None),
        P(),
        P(),
        P(),
    )
    out_specs = (
        P(("grp", "rep"), "seq", None),
        P(("grp", "rep"), "seq", None),
        P("grp", "seq"),
        P("grp", "seq"),
    )
    chips = mesh.shape["seq"] == 4 and mesh.shape["rep"] % 2 == 0 and HEADS % 8 == 0

    def run(patches, *rest):
        per_device = patches.shape[0] // (mesh.shape["grp"] * mesh.shape["rep"])
        body = chip_shards if chips and per_device == 2 else shards
        inner = jax.shard_map(body, mesh=mesh, in_specs=in_specs, out_specs=out_specs, check_vma=False)
        return inner(patches, *rest)

    return run
```

```python
import functools

import jax
import jax.numpy as jnp
import numpy as np
from jax import lax
from jax.experimental import pallas as pl
from jax.experimental.pallas import tpu as pltpu
from jax.sharding import PartitionSpec as P

HEADS = 16
GRID_COLS = 512


epsilon = 1e-06


def position_table(position, model_width):
    quarter = model_width // 4
    frequency = jnp.exp(-jnp.log(10000.0) * jnp.arange(quarter, dtype=jnp.float32) / quarter)
    grid_row = (position // GRID_COLS).astype(jnp.float32)
    grid_col = (position % GRID_COLS).astype(jnp.float32)
    row_phase = grid_row[..., None] * frequency
    col_phase = grid_col[..., None] * frequency
    return jnp.concatenate(
        [jnp.sin(row_phase), jnp.cos(row_phase), jnp.sin(col_phase), jnp.cos(col_phase)], axis=-1
    )


def normalize(hidden, gain):
    center = hidden - jnp.mean(hidden, axis=-1, keepdims=True)
    spread = jnp.mean(center * center, axis=-1, keepdims=True)
    inv_std = lax.rsqrt(spread + epsilon)
    unit_rows = center * inv_std
    return ((unit_rows * gain).astype(jnp.bfloat16), unit_rows, inv_std)


def norm_backward(d_normed, gain, unit_rows, inv_std):
    scaled = d_normed * gain
    return inv_std * (
        scaled
        - jnp.mean(scaled, axis=-1, keepdims=True)
        - unit_rows * jnp.mean(scaled * unit_rows, axis=-1, keepdims=True)
    )


def head_block(query_rows, grad_rows, key_rows, value_rows, live_keys, score_scale):
    scores = jnp.dot(query_rows, key_rows.T, preferred_element_type=jnp.float32) * score_scale
    scores = jnp.where(live_keys[None, :], scores, -1e30)
    top_score = jnp.max(scores, axis=1, keepdims=True)
    raised = jnp.exp(scores - top_score)
    probability = raised / jnp.sum(raised, axis=1, keepdims=True)
    rounded = probability.astype(jnp.bfloat16)
    attended = jnp.dot(rounded, value_rows, preferred_element_type=jnp.float32).astype(jnp.bfloat16)
    d_value = jnp.dot(rounded.T, grad_rows, preferred_element_type=jnp.float32)
    d_prob = jnp.dot(grad_rows, value_rows.T, preferred_element_type=jnp.float32)
    d_score = (
        probability * (d_prob - jnp.sum(probability * d_prob, axis=1, keepdims=True)) * score_scale
    ).astype(jnp.bfloat16)
    d_query = jnp.dot(d_score, key_rows, preferred_element_type=jnp.float32)
    d_key = jnp.dot(d_score.T, query_rows, preferred_element_type=jnp.float32)
    return (attended, d_query, d_key, d_value)


def attend(query_rows, grad_rows, key_rows, value_rows, live_keys, score_scale):
    row_count = query_rows.shape[0]
    blocks = max(1, row_count // 512)
    while row_count % blocks:
        blocks -= 1
    block_rows = row_count // blocks
    query_blocks = query_rows.reshape(blocks, block_rows, query_rows.shape[1])
    grad_blocks = grad_rows.reshape(blocks, block_rows, grad_rows.shape[1])

    def block_step(carry, pieces):
        key_total, value_total = carry
        attended, d_query, d_key, d_value = head_block(
            pieces[0], pieces[1], key_rows, value_rows, live_keys, score_scale
        )
        return ((key_total + d_key, value_total + d_value), (attended, d_query))

    empty = jnp.zeros(key_rows.shape, jnp.float32)
    (key_total, value_total), (attended, d_query) = lax.scan(
        block_step, (empty, empty), (query_blocks, grad_blocks)
    )
    return (attended.reshape(row_count, -1), d_query.reshape(row_count, -1), key_total, value_total)


def shards(patches, kept_index, kept_count, cotangent, w_qkv, w_out, gain):
    groups = lax.axis_size("seq")
    samples, slot_count, model_width = patches.shape
    head_size = model_width // HEADS
    per_device = max(1, HEADS // groups)
    splits = max(1, groups // HEADS)
    head_groups = groups // splits
    band_width = per_device * head_size
    part_rows = slot_count // splits
    slot_ids = jnp.arange(slot_count, dtype=jnp.int32)
    live_slots = slot_ids[None, :] < kept_count
    hidden = patches.astype(jnp.float32) + position_table(kept_index, model_width)
    normed, unit_rows, inv_std = normalize(hidden, gain)
    flat_normed = normed.reshape(samples * slot_count, model_width)
    packed = jnp.dot(flat_normed, w_qkv, preferred_element_type=jnp.float32).astype(jnp.bfloat16)
    packed = packed.reshape(samples, slot_count, 3 * model_width)
    live_grad = jnp.where(live_slots[:, :, None], cotangent, jnp.zeros_like(cotangent))
    flat_grad = live_grad.reshape(samples * slot_count, model_width)
    d_attended = jnp.dot(flat_grad, w_out.T, preferred_element_type=jnp.float32).astype(
        jnp.bfloat16
    )
    d_attended = d_attended.reshape(samples, slot_count, model_width)

    def to_owners(tensor_block):
        arranged = tensor_block.reshape(samples, splits, part_rows, head_groups, band_width)
        return arranged.transpose(3, 1, 0, 2, 4).reshape(groups, samples, part_rows, band_width)

    key_value_send = jnp.concatenate(
        [
            packed[:, :, model_width : 2 * model_width].reshape(
                samples, slot_count, head_groups, band_width
            ),
            packed[:, :, 2 * model_width :].reshape(samples, slot_count, head_groups, band_width),
        ],
        axis=3,
    )
    key_value_send = key_value_send.transpose(2, 0, 1, 3)
    key_value_send = jnp.broadcast_to(
        key_value_send[:, None], (head_groups, splits, samples, slot_count, 2 * band_width)
    )
    key_value_send = key_value_send.reshape(groups, samples, slot_count, 2 * band_width)
    got_query, got_grad, got_pair = (
        lax.all_to_all(
            to_owners(packed[:, :, :model_width]), "seq", split_axis=0, concat_axis=0, tiled=True
        ),
        lax.all_to_all(to_owners(d_attended), "seq", split_axis=0, concat_axis=0, tiled=True),
        lax.all_to_all(key_value_send, "seq", split_axis=0, concat_axis=0, tiled=True),
    )
    all_counts = lax.all_gather(kept_count, "seq", axis=1, tiled=True)
    live_keys = (slot_ids[None, None, :] < all_counts[:, :, None]).reshape(
        samples, groups * slot_count
    )

    def rows_by_head(tensor_block, row_count):
        arranged = tensor_block.transpose(1, 0, 2, 3).reshape(
            samples, groups * row_count, per_device, head_size
        )
        return arranged.transpose(0, 2, 1, 3)

    query_heads = rows_by_head(got_query, part_rows)
    grad_heads = rows_by_head(got_grad, part_rows)
    key_heads = rows_by_head(got_pair[..., :band_width], slot_count)
    value_heads = rows_by_head(got_pair[..., band_width:], slot_count)
    score_scale = head_size ** (-0.5)

    def one_head(query_rows, grad_rows, key_rows, value_rows, key_live):
        return attend(query_rows, grad_rows, key_rows, value_rows, key_live, score_scale)

    per_head = jax.vmap(one_head, in_axes=(0, 0, 0, 0, None))
    outputs, d_query, d_key, d_value = jax.vmap(per_head)(
        query_heads, grad_heads, key_heads, value_heads, live_keys
    )

    def back_to_sources(tensor_block, row_count):
        arranged = tensor_block.transpose(0, 2, 1, 3).reshape(
            samples, groups, row_count, band_width
        )
        return arranged.transpose(1, 0, 2, 3)

    query_send = back_to_sources(d_query, part_rows).astype(jnp.bfloat16)
    back_out, back_query = (
        lax.all_to_all(
            back_to_sources(outputs, part_rows), "seq", split_axis=0, concat_axis=0, tiled=True
        ),
        lax.all_to_all(query_send, "seq", split_axis=0, concat_axis=0, tiled=True),
    )
    key_value_grad = jnp.concatenate(
        [back_to_sources(d_key, slot_count), back_to_sources(d_value, slot_count)], axis=3
    )
    back_pair = lax.all_to_all(
        key_value_grad.astype(jnp.bfloat16), "seq", split_axis=0, concat_axis=0, tiled=True
    ).astype(key_value_grad.dtype)

    def from_owners(tensor_block):
        arranged = tensor_block.reshape(head_groups, splits, samples, part_rows, band_width)
        return arranged.transpose(2, 1, 3, 0, 4).reshape(samples, slot_count, model_width)

    attended = from_owners(back_out)
    summed_pair = jnp.sum(
        back_pair.reshape(head_groups, splits, samples, slot_count, 2 * band_width), axis=1
    )
    summed_pair = summed_pair.transpose(1, 2, 0, 3)
    key_grad_rows = (
        summed_pair[..., :band_width].reshape(samples, slot_count, model_width).astype(jnp.bfloat16)
    )
    value_grad_rows = (
        summed_pair[..., band_width:].reshape(samples, slot_count, model_width).astype(jnp.bfloat16)
    )
    d_packed = jnp.concatenate([from_owners(back_query), key_grad_rows, value_grad_rows], axis=2)
    flat_attended = attended.reshape(samples * slot_count, model_width)
    projected = jnp.dot(flat_attended, w_out, preferred_element_type=jnp.float32).reshape(
        samples, slot_count, model_width
    )
    encoded = jnp.where(live_slots[:, :, None], hidden + projected, 0.0).astype(jnp.bfloat16)
    flat_packed = d_packed.reshape(samples * slot_count, 3 * model_width)
    d_normed = jnp.dot(flat_packed, w_qkv.T, preferred_element_type=jnp.float32).reshape(
        samples, slot_count, model_width
    )
    d_hidden = norm_backward(d_normed, gain, unit_rows, inv_std)
    d_patches = jnp.where(
        live_slots[:, :, None], live_grad.astype(jnp.float32) + d_hidden, 0.0
    ).astype(jnp.bfloat16)
    columns = flat_grad
    out_part = lax.psum_scatter(
        jnp.dot(columns.T, flat_attended, preferred_element_type=jnp.float32),
        "seq",
        scatter_dimension=0,
        tiled=True,
    ).T
    my_columns = lax.all_to_all(flat_packed, "seq", split_axis=1, concat_axis=0, tiled=True)
    columns = my_columns
    qkv_part = jnp.dot(
        lax.all_gather(flat_normed, "seq", axis=0, tiled=True).T,
        columns,
        preferred_element_type=jnp.float32,
    )
    qkv_grad, out_grad = lax.psum((qkv_part, out_part), "rep")
    return (encoded, d_patches, qkv_grad, out_grad)


AXES = ("seq", "rep")
MARK = 1024.0
MIB = 1024 * 1024


def line_perm(move, reps):
    pairs = []
    for z in range(4):
        for rep in range(reps):
            x, c = rep // 2, rep % 2
            to_x, to_c, to_z = move(x, c, z)
            pairs.append((z * reps + rep, to_z * reps + 2 * to_x + to_c))
    return pairs


def sine_cosine(phase):
    turns = jnp.floor(phase * np.float32(2.0 / np.pi) + 0.5)
    rest = phase - turns * np.float32(1.5703125)
    rest = rest - turns * np.float32(4.837512969970703125e-4)
    rest = rest - turns * np.float32(7.54978995489188216e-8)
    square = rest * rest
    sine = rest + rest * square * (
        np.float32(-1.6666654611e-1)
        + square * (np.float32(8.3321608736e-3) + square * np.float32(-1.9515295891e-4))
    )
    cosine = (
        1.0
        - 0.5 * square
        + square
        * square
        * (
            np.float32(4.166664568298827e-2)
            + square * (np.float32(-1.388731625493765e-3) + square * np.float32(2.443315711809948e-5))
        )
    )
    quadrant = turns.astype(jnp.int32) & 3
    swap = (quadrant & 1) == 1
    first = jnp.where(swap, cosine, sine)
    second = jnp.where(swap, sine, cosine)
    first = jnp.where(quadrant >= 2, -first, first)
    second = jnp.where((quadrant == 1) | (quadrant == 2), -second, second)
    return first, second


def live_column(count, rows):
    return lax.broadcasted_iota(jnp.int32, (rows, 1), 0) < count


def dot_nn(a, b):
    return jnp.dot(a, b, preferred_element_type=jnp.float32)


def dot_nt(a, b):
    return lax.dot_general(a, b, (((1,), (1,)), ((), ())), preferred_element_type=jnp.float32)


PAR, CORE, LINE, SIDE, KEPT = range(5)


def norm_kernel(
    place, patch_hbm, cot_hbm, index_hbm, gain_hbm, p0_ref, p1_ref, hidden_ref,
    patch_ref, cot_ref, index_ref, gain_ref, sems,
):
    par = place[PAR]
    rows, width = patch_ref.shape[1:]
    quarter = width // 4
    copies = [
        pltpu.make_async_copy(src, dst, sems.at[i])
        for i, (src, dst) in enumerate(
            ((index_hbm, index_ref), (patch_hbm, patch_ref), (gain_hbm, gain_ref), (cot_hbm, cot_ref))
        )
    ]
    for copy in copies:
        copy.start()
    order = lax.broadcasted_iota(jnp.int32, (1, quarter), 1).astype(jnp.float32)
    freq = jnp.exp(-np.log(np.float32(10000.0)) * order / quarter)
    diagonal = lax.broadcasted_iota(jnp.int32, (rows, rows), 0) == lax.broadcasted_iota(
        jnp.int32, (rows, rows), 1
    )
    copies[0].wait()
    tables = []
    for k in range(2):
        position = index_ref[pl.ds(k ^ par, 1), :]
        grid_row = (position // GRID_COLS).astype(jnp.float32)
        grid_col = (position % GRID_COLS).astype(jnp.float32)
        grid_row = jnp.sum(jnp.where(diagonal, grid_row, 0.0), axis=1, keepdims=True)
        grid_col = jnp.sum(jnp.where(diagonal, grid_col, 0.0), axis=1, keepdims=True)
        pieces = sine_cosine(grid_row * freq) + sine_cosine(grid_col * freq)
        tables.append(jnp.concatenate(pieces, axis=1))
    copies[1].wait()
    copies[2].wait()
    for k, out_ref in enumerate((p0_ref, p1_ref)):
        s = k ^ par
        hidden = patch_ref[s].astype(jnp.float32) + tables[k]
        hidden_ref[k] = hidden
        center = hidden - jnp.mean(hidden, axis=-1, keepdims=True)
        spread = jnp.mean(center * center, axis=-1, keepdims=True)
        normed = center * lax.rsqrt(spread + epsilon) * gain_ref[...]
        live = live_column(place[KEPT + s], rows)
        out_ref[:rows, :] = jnp.where(live, normed, MARK).astype(out_ref.dtype)
    copies[3].wait()
    for k, out_ref in enumerate((p0_ref, p1_ref)):
        s = k ^ par
        live = live_column(place[KEPT + s], rows)
        grad = cot_ref[s]
        out_ref[rows:, :] = jnp.where(live, grad, jnp.zeros_like(grad))


def load_weights(core, first_pair, w_in_hbm, w_out_hbm, wq, wk, wv, wo, sems):
    width = w_out_hbm.shape[0]
    copies = []
    for j in range(wq.shape[1] // 128):
        to = pl.ds(128 * j, 128)
        row = pl.multiple_of(256 * (first_pair + j) + 128 * core, 128)
        pairs = [(w_out_hbm.at[pl.ds(row, 128), :], wo.at[to, :])]
        for t, out in enumerate((wq, wk, wv)):
            at = pl.multiple_of(t * width + row, 128)
            pairs.append((w_in_hbm.at[:, pl.ds(at, 128)], out.at[:, to]))
        copies += [pltpu.make_async_copy(a, b, sems.at[4 * j + i]) for i, (a, b) in enumerate(pairs)]
    for copy in copies:
        copy.start()
    return copies


def attend_pairs(
    place, first_pair, payloads, w_in_hbm, w_out_hbm, own, oth, att_own, att_oth, keep_t, out_keep, send,
    norm_s, grad_s, att_s, wq, wk, wv, wo, sems,
):
    copies = load_weights(place[CORE], first_pair, w_in_hbm, w_out_hbm, wq, wk, wv, wo, sems)
    block = payloads[0].shape[0] // 2
    rows = 4 * block
    half = 2 * block
    biases = []
    for i, ref in enumerate(payloads):
        at = slice(i * block, (i + 1) * block)
        value = ref[:block, :]
        live = value[:, 0:1].astype(jnp.float32) < MARK
        norm_s[at, :] = jnp.where(live, value, jnp.zeros_like(value))
        grad_s[at, :] = ref[block:, :]
        biases.append(jnp.where(live, 0.0, -1e30))
    bias = jnp.concatenate(biases, axis=0)
    low = lax.broadcasted_iota(jnp.int32, (rows, 128), 1) < 64
    scale = jnp.bfloat16(0.125)
    zero = jnp.zeros((rows, 128), jnp.bfloat16)
    first = place[SIDE] == 0
    count = wq.shape[1] // 128
    for copy in copies:
        copy.wait()
    normed = norm_s[...]
    queries = dot_nn(normed, wq[...]).astype(jnp.bfloat16)
    keys = dot_nn(normed, wk[...]).astype(jnp.bfloat16)
    values = dot_nn(normed, wv[...]).astype(jnp.bfloat16)
    d_att = dot_nt(grad_s[...], wo[...]).astype(jnp.bfloat16)
    for j in range(count):
        cols = slice(128 * j, 128 * j + 128)
        q = queries[:, cols] * scale
        k = keys[:, cols]
        v = values[:, cols]
        g = d_att[:, cols]
        v_t = v.T
        k_t = (k * scale).T
        att_t, dq_t, dk, dv = [], [], [], []
        for h in range(2):
            mine = low if h == 0 else jnp.logical_not(low)
            scores = dot_nt(k, jnp.where(mine, q, zero)) + bias
            raised = jnp.exp(scores - jnp.max(scores, axis=0, keepdims=True))
            prob = raised * (1.0 / jnp.sum(raised, axis=0, keepdims=True))
            weights = prob.astype(jnp.bfloat16)
            part = slice(64 * h, 64 * h + 64)
            att_t.append(dot_nn(v_t[part], weights))
            dv.append(dot_nn(weights, g))
            d_prob = dot_nt(v, jnp.where(mine, g, zero))
            total = jnp.sum(prob * d_prob, axis=0, keepdims=True)
            d_score = (prob * (d_prob - total)).astype(jnp.bfloat16)
            dq_t.append(dot_nn(k_t[part], d_score))
            dk.append(dot_nn(d_score, q))
        att_pair_t = jnp.concatenate(att_t, axis=0).astype(jnp.bfloat16)
        dq_pair_t = jnp.concatenate(dq_t, axis=0).astype(jnp.bfloat16)
        dk_pair = jnp.where(low, dk[0], dk[1]).astype(jnp.bfloat16)
        dv_pair = jnp.where(low, dv[0], dv[1]).astype(jnp.bfloat16)
        for t, piece in enumerate((dq_pair_t.T, dk_pair, dv_pair)):
            own[t, :, cols] = piece[:half]
            oth[t, :, cols] = piece[half:]
        att_pair = att_pair_t.T
        to = slice(128 * (first_pair + j), 128 * (first_pair + j) + 128)
        att_own[:, to] = att_pair[:half]
        att_oth[:, to] = att_pair[half:]
        for t, piece in enumerate((dq_pair_t, dk_pair.T, dv_pair.T)):
            at = slice(64 * j, 64 * j + 64)
            part = slice(rows * t, rows * t + rows)
            keep_t[at, part] = jnp.where(first, piece[:64], piece[64:])
            send[at, part] = jnp.where(first, piece[64:], piece[:64])
        at = slice(64 * j, 64 * j + 64)
        att_s[0, at, :] = jnp.where(first, att_pair_t[:64], att_pair_t[64:])
        att_s[1, at, :] = jnp.where(first, att_pair_t[64:], att_pair_t[:64])
    out_keep[...] = dot_nn(att_s[0], grad_s[...])
    send[:, 3 * rows :] = dot_nn(att_s[1], grad_s[...]).astype(send.dtype)


def attend_first(place, p0, p1, p2, p3, *refs):
    attend_pairs(place, 0, (p0, p1, p2, p3), *refs)


def attend_second(place, p0, p1, p2, p3, w_in_hbm, w_out_hbm, att_own, att_oth, after, own, oth, all_own, all_oth, *refs):
    del after
    width = att_own.shape[1] // 2
    all_own[:, :width] = att_own[:, :width]
    all_oth[:, :width] = att_oth[:, :width]
    attend_pairs(place, 2, (p0, p1, p2, p3), w_in_hbm, w_out_hbm, own, oth, all_own, all_oth, *refs)


def att_kernel(place, own, got, o0, o1):
    block = o0.shape[0]
    att = in_order(place[CORE], own[...], got[...])
    o0[...] = att[:block]
    o1[...] = att[block:]


def in_order(place, own, got):
    pieces = []
    low = place == 0
    for j in range(own.shape[1] // 128):
        a, b = own[:, 128 * j : 128 * j + 128], got[:, 128 * j : 128 * j + 128]
        pieces += [jnp.where(low, a, b), jnp.where(low, b, a)]
    return jnp.concatenate(pieces, axis=1)


def rows_kernel(place, own_a, got_a, own_b, got_b, w_ref, after, o0, o1, total):
    del after
    step = pl.program_id(0)
    core = place[CORE]
    block = o0.shape[0]

    def rows_of(t):
        return jnp.concatenate([in_order(core, own_a[t], got_a[t]), in_order(core, own_b[t], got_b[t])], axis=1)

    term = dot_nt(rows_of(step), w_ref[...])

    @pl.when(step == 0)
    def _():
        total[...] = term

    @pl.when(step > 0)
    def _():
        total[...] += term

    @pl.when(step == pl.num_programs(0) - 1)
    def _():
        o0[...] = total[:block].astype(o0.dtype)
        o1[...] = total[block:].astype(o1.dtype)


def encode_kernel(place, r0, r1, w_ref, hidden_ref, after, encoded):
    del after
    for k, ref in enumerate((r0, r1)):
        s = k ^ place[PAR]
        live = live_column(place[KEPT + s], ref.shape[0])
        projected = dot_nn(ref[...], w_ref[...])
        encoded[s] = jnp.where(live, hidden_ref[k] + projected, 0.0).astype(encoded.dtype)


def patch_grad_kernel(place, r0, r1, hidden_ref, m0, m1, gain_ref, d_patches):
    rows = r0.shape[0]
    for k, (r_ref, m_ref) in enumerate(((r0, m0), (r1, m1))):
        s = k ^ place[PAR]
        live = live_column(place[KEPT + s], rows)
        hidden = hidden_ref[k]
        center = hidden - jnp.mean(hidden, axis=-1, keepdims=True)
        spread = jnp.mean(center * center, axis=-1, keepdims=True)
        inv_std = lax.rsqrt(spread + epsilon)
        unit = center * inv_std
        d_hidden = norm_backward(r_ref[...].astype(jnp.float32), gain_ref[...], unit, inv_std)
        value = m_ref[rows:, :].astype(jnp.float32) + d_hidden
        d_patches[s] = jnp.where(live, value, 0.0).astype(d_patches.dtype)


def put_parts(place, total, first, out_total, out_first, keep, send):
    columns = out_total.shape[1] // 4
    count = 64
    tall = keep.shape[1] - count
    for k in range(4):
        ref, spot = (keep, send)[k % 2], k // 2
        slab = place[LINE] ^ k
        at = pl.multiple_of(first + slab * count, 64)
        ref[spot, :count, :] = total[pl.ds(at, count), :].astype(ref.dtype)
        at = pl.ds(pl.multiple_of(slab * columns, 128), columns)
        for j in range(4):
            rows = slice(out_first + tall * j, out_first + tall * j + tall)
            ref[spot, count:, columns * j : columns * j + columns] = out_total[rows, at].astype(ref.dtype)


def sum_out_part(out_keep, got, out_total):
    out_total[...] = out_keep[...] + got[:, got.shape[1] - out_total.shape[1] :].astype(jnp.float32)


def piece_of(ref, at, rows):
    t, j = at // 2, at % 2
    return ref[64 * j : 64 * j + 64, rows * t : rows * t + rows]


def weight_first(
    place, keep, out_keep, got, p0, p1, p2, p3, n0, n1, after,
    part_keep, part_send, tokens, left, total, out_total,
):
    del after
    block = p0.shape[0] // 2
    rows = 4 * block
    for i, ref in enumerate((p0, p1, p2, p3)):
        tokens[i * block : (i + 1) * block, :] = ref[:block, :]
    tokens[rows : rows + 2 * block, :] = n0[...]
    tokens[rows + 2 * block :, :] = n1[...]
    for side, ref in enumerate((keep, got)):
        for i, at in enumerate((0, 2, 4, 5)):
            left[side, 64 * i : 64 * i + 64, :] = piece_of(ref, at, rows)
    total[...] = dot_nn(left[0], tokens[:rows, :]) + dot_nn(left[1], tokens[rows:, :])
    sum_out_part(out_keep, got, out_total)
    put_parts(place, total, 0, out_total, 0, part_keep, part_send)


def weight_second(
    place, keep_a, got_a, keep_b, out_keep, got_b, p0, p1, p2, p3, n0, n1, after, before, early,
    part_keep, part_send, last_keep, last_send, tokens, left, total, out_total,
):
    del after, before, early
    block = p0.shape[0] // 2
    rows = 4 * block
    for i, ref in enumerate((p0, p1, p2, p3)):
        tokens[i * block : (i + 1) * block, :] = ref[:block, :]
    tokens[rows : rows + 2 * block, :] = n0[...]
    tokens[rows + 2 * block :, :] = n1[...]
    for side, (a, b) in enumerate(((keep_a, keep_b), (got_a, got_b))):
        for i, (ref, at) in enumerate(
            ((a, 1), (b, 1), (b, 2), (b, 4), (b, 0), (a, 3), (b, 3), (b, 5))
        ):
            left[side, 64 * i : 64 * i + 64, :] = piece_of(ref, at, rows)
    total[...] = dot_nn(left[0], tokens[:rows, :]) + dot_nn(left[1], tokens[rows:, :])
    sum_out_part(out_keep, got_b, out_total)
    put_parts(place, total, 0, out_total, 0, part_keep, part_send)
    put_parts(place, total, 256, out_total, 64, last_keep, last_send)


def pair_kernel(keep, got, *refs):
    mine, send = refs[-2:]
    mine[...] = keep[0] + got[0].astype(jnp.float32)
    send[...] = (keep[1] + got[1].astype(jnp.float32)).astype(send.dtype)


def sum_kernel(*refs):
    out = refs[-1]
    at = 0
    for mine, got in zip(refs[:-1:2], refs[1:-1:2]):
        count = mine.shape[0]
        out[at : at + count, :] = (mine[...] + got[...].astype(jnp.float32)).astype(out.dtype)
        at += count


def finish_kernel(place, a0, a1, a2, a3, b0, b1, b2, b3, wide, narrow):
    core_low, side_low = place[CORE] == 0, place[SIDE] == 0
    slab = place[LINE]
    columns = narrow.shape[1]
    spot = jnp.where(slab == 3, 0, slab)
    spots = (spot, jnp.where(spot == 0, 1, 0), jnp.where(spot == 2, 1, 2))

    def pick(refs, c, x, at, part):
        own, by_x, by_core, by_both = refs
        near = jnp.where(side_low == (x == 0), own[at, part], by_x[at, part])
        far = jnp.where(side_low == (x == 0), by_core[at, part], by_both[at, part])
        return jnp.where(core_low == (c == 0), near, far)

    every = slice(None)
    first, second = (a0, a1, a2, a3), (b0, b1, b2, b3)
    for c in range(2):
        for i, (refs, row) in enumerate(((first, 0), (first, 96), (second, 0))):
            at = slice(row, row + 64)
            both = jnp.concatenate([pick(refs, c, x, at, every) for x in range(2)], axis=0)
            col = pl.multiple_of(128 * (2 * spots[i] + c), 128)
            wide[:, pl.ds(col, 128)] = both.T.astype(wide.dtype)
        for refs, base, tall, pair in ((first, 64, 32, 0), (first, 160, 16, 2), (second, 64, 16, 3)):
            for j in range(4):
                at = slice(base, base + tall)
                part = slice(columns * j, columns * j + columns)
                for x in range(2):
                    row = 128 * (2 * (pair + tall * j // 64) + c) + 64 * x + tall * j % 64
                    narrow[row : row + tall, :] = pick(refs, c, x, at, part).astype(narrow.dtype)


SMEM_SPEC = pl.BlockSpec(memory_space=pltpu.SMEM)
VMEM_SPEC = pl.BlockSpec(memory_space=pltpu.VMEM)


def struct(shape, dtype=jnp.bfloat16):
    return jax.ShapeDtypeStruct(shape, dtype)


COST = pl.CostEstimate(flops=1000, bytes_accessed=1000, transcendentals=0)


def in_hbm(value):
    return pltpu.with_memory_space_constraint(value, pltpu.HBM)


def call(kernel, args, outs, limit, place=None, scratch=(), specs=None):
    specs = specs or [VMEM_SPEC] * len(args)
    if place is not None:
        args, specs = (place, *args), [SMEM_SPEC] + specs
    single = not isinstance(outs, list)
    return pl.pallas_call(
        kernel,
        in_specs=specs,
        out_specs=VMEM_SPEC if single else [VMEM_SPEC] * len(outs),
        out_shape=outs,
        scratch_shapes=list(scratch),
        compiler_params=pltpu.CompilerParams(vmem_limit_bytes=limit * MIB),
        cost_estimate=COST,
    )(*args)


def chip_shards(patches, kept_index, kept_count, cotangent, w_qkv, w_out, gain):
    bf16, f32 = jnp.bfloat16, jnp.float32
    samples, slots, width = patches.shape
    reps = lax.axis_size("rep")
    rep = lax.axis_index("rep")
    z = lax.axis_index("seq")
    core, x = rep & 1, rep >> 1
    place = jnp.concatenate(
        [jnp.stack([z & 1, core, z, x]).astype(jnp.int32), kept_count.reshape(samples)]
    )
    own_width = width // 2
    quarter = width // 4
    rows = 4 * slots

    def send(value, move):
        return lax.ppermute(value, AXES, line_perm(move, reps))

    def to_core(value):
        return send(value, lambda x, c, z: (x, 1 - c, z))

    def to_x(value):
        return send(value, lambda x, c, z: (1 - x, c, z))

    def to_chip(value, k):
        return send(value, lambda x, c, z: (x, z >> 1, 2 * c + (k ^ (z & 1))))

    def to_rows(value, k, other):
        return send(value, lambda x, c, z: (x, z >> 1, 2 * (c ^ other) + (k ^ (z & 1))))

    def along(value, k):
        return send(value, lambda x, c, z: (x, c, z ^ k))

    gain_row = gain.reshape(1, width)
    pay = struct((2 * slots, width))
    hbm = pl.BlockSpec(memory_space=pl.ANY)
    *mine, hidden = call(
        norm_kernel,
        tuple(in_hbm(v) for v in (patches, cotangent, kept_index, gain_row)),
        [pay, pay, struct(patches.shape, f32)],
        24,
        place,
        scratch=[
            pltpu.VMEM(patches.shape, bf16),
            pltpu.VMEM(patches.shape, bf16),
            pltpu.VMEM(kept_index.shape, jnp.int32),
            pltpu.VMEM(gain_row.shape, f32),
            pltpu.SemaphoreType.DMA((4,)),
        ],
        specs=[hbm] * 4,
    )
    got = [to_chip(mine[k], k) for k in range(2)]
    here = got + [to_core(v) for v in got]
    from_x = to_x(jnp.concatenate([v[:slots] for v in got], axis=0))
    there = (from_x, to_core(from_x))

    any_spec = pl.BlockSpec(memory_space=pl.ANY)
    pairs = width // 512
    half_rows = struct((3, 2 * slots, 128 * pairs))
    att_rows = struct((2 * slots, own_width))
    out_half = (64 * pairs, width)
    half_t = struct((64 * pairs, 3 * rows))
    half_send = struct((64 * pairs, 3 * rows + width))

    def attend(kernel, extra, specs=()):
        return call(
            kernel,
            (*here, in_hbm(w_qkv), in_hbm(w_out), *extra),
            [half_rows] * 2 + [att_rows] * 2 + [half_t, struct(out_half, f32), half_send],
            32,
            place,
            scratch=[pltpu.VMEM((rows, width), bf16)] * 2
            + [pltpu.VMEM((2, 64 * pairs, rows), bf16)]
            + [pltpu.VMEM((width, 128 * pairs), bf16)] * 3
            + [pltpu.VMEM((128 * pairs, width), bf16), pltpu.SemaphoreType.DMA((4 * pairs,))],
            specs=[VMEM_SPEC] * 4 + [any_spec] * 2 + list(specs),
        )

    own_a, oth_a, *att_a, keep_a, out_keep_a, send_a = attend(attend_first, ())
    got_a = to_x(send_a)
    core_a = to_core(oth_a)
    own_b, oth_b, att_own, att_oth, keep_b, out_keep_b, send_b = attend(
        attend_second, (*att_a, from_x), [VMEM_SPEC] * 2 + [any_spec]
    )
    got_b = to_x(send_b)
    core_b = to_core(oth_b)
    block = struct((slots, width))
    att = call(att_kernel, (att_own, to_core(att_oth)), [block] * 2, 8, place)
    back_att = [to_rows(att[k], k, 0) for k in range(2)]

    def parts_of(kernel, args, chunks, scratch, after=()):
        return call(
            kernel,
            (*args, *here, *there, *after),
            [struct((2, tall, width), kind) for tall in chunks for kind in (f32, bf16)],
            16,
            place,
            scratch=[pltpu.VMEM((2 * rows, width), bf16)] + scratch + [pltpu.VMEM(out_half, f32)],
            specs=[VMEM_SPEC] * (len(args) + 6) + [any_spec] * len(after),
        )

    def pair_sums(keep, part, after=()):
        shape = keep.shape[1:]
        mine, part = call(
            pair_kernel,
            (keep, along(part, 1), *after),
            [struct(shape, f32), struct(shape)],
            8,
            specs=[VMEM_SPEC] * 2 + [any_spec] * len(after),
        )
        return mine, part, along(part, 2)

    def spread(*parts):
        count = sum(part.shape[0] for part in parts[::2])
        sums = call(sum_kernel, parts, struct((count, width)), 8)
        by_x = to_x(sums)
        return (sums, by_x, to_core(sums), to_core(by_x))

    keep, part = parts_of(
        weight_first,
        (keep_a, out_keep_a, got_a),
        (96,),
        [pltpu.VMEM((2, 256, rows), bf16), pltpu.VMEM((256, width), f32)],
        (att[0],),
    )
    d_normed = pl.pallas_call(
        rows_kernel,
        grid_spec=pltpu.PrefetchScalarGridSpec(
            num_scalar_prefetch=1,
            grid=(3,),
            in_specs=[pl.BlockSpec(half_rows.shape, lambda i, p: (0, 0, 0))] * 4
            + [pl.BlockSpec((width, width), lambda i, p: (0, i)), any_spec],
            out_specs=[pl.BlockSpec(block.shape, lambda i, p: (0, 0))] * 2,
            scratch_shapes=[pltpu.VMEM((2 * slots, width), f32)],
        ),
        out_shape=[block] * 2,
        compiler_params=pltpu.CompilerParams(vmem_limit_bytes=20 * MIB),
        cost_estimate=COST,
    )(place, own_a, core_a, own_b, core_b, in_hbm(w_qkv), part)
    encoded = call(
        encode_kernel,
        (*back_att, w_out, hidden, d_normed[0]),
        struct(patches.shape),
        12,
        place,
        specs=[VMEM_SPEC] * 4 + [any_spec],
    )
    first_sum, paired, first_got = pair_sums(keep, part)
    keep, part, last_keep, last_part = parts_of(
        weight_second,
        (keep_a, got_a, keep_b, out_keep_b, got_b),
        (80, 80),
        [pltpu.VMEM((2, 512, rows), bf16), pltpu.VMEM((512, width), f32)],
        (paired, d_normed[0], encoded),
    )
    second_sum, paired, second_got = pair_sums(keep, part)
    last_sum, paired, last_got = pair_sums(last_keep, last_part)
    first = spread(first_sum, first_got, second_sum, second_got)
    second = spread(last_sum, last_got)
    back_dn = [to_rows(d_normed[k], k, 0) for k in range(2)]
    d_patches = call(
        patch_grad_kernel,
        (*back_dn, hidden, *mine, gain_row),
        struct(patches.shape),
        12,
        place,
    )
    qkv_grad, out_grad = call(
        finish_kernel,
        (*first, *second),
        [struct((width, 3 * quarter), f32), struct((width, quarter), f32)],
        12,
        place,
    )
    return (encoded, d_patches, qkv_grad, out_grad)


def solution(mesh):
    in_specs = (
        P(("grp", "rep"), "seq", None),
        P(("grp", "rep"), "seq"),
        P(("grp", "rep"), "seq"),
        P(("grp", "rep"), "seq", None),
        P(),
        P(),
        P(),
    )
    out_specs = (
        P(("grp", "rep"), "seq", None),
        P(("grp", "rep"), "seq", None),
        P("grp", "seq"),
        P("grp", "seq"),
    )
    chips = mesh.shape["seq"] == 4 and mesh.shape["rep"] % 2 == 0 and HEADS % 8 == 0

    def run(patches, *rest):
        per_device = patches.shape[0] // (mesh.shape["grp"] * mesh.shape["rep"])
        body = chip_shards if chips and per_device == 2 else shards
        inner = jax.shard_map(body, mesh=mesh, in_specs=in_specs, out_specs=out_specs, check_vma=False)
        return inner(patches, *rest)

    return run
```

```python
import functools

import jax
import jax.numpy as jnp
import numpy as np
from jax import lax
from jax.experimental import pallas as pl
from jax.experimental.pallas import tpu as pltpu
from jax.sharding import PartitionSpec as P

HEADS = 16
GRID_COLS = 512


epsilon = 1e-06


def position_table(position, model_width):
    quarter = model_width // 4
    frequency = jnp.exp(-jnp.log(10000.0) * jnp.arange(quarter, dtype=jnp.float32) / quarter)
    grid_row = (position // GRID_COLS).astype(jnp.float32)
    grid_col = (position % GRID_COLS).astype(jnp.float32)
    row_phase = grid_row[..., None] * frequency
    col_phase = grid_col[..., None] * frequency
    return jnp.concatenate(
        [jnp.sin(row_phase), jnp.cos(row_phase), jnp.sin(col_phase), jnp.cos(col_phase)], axis=-1
    )


def normalize(hidden, gain):
    center = hidden - jnp.mean(hidden, axis=-1, keepdims=True)
    spread = jnp.mean(center * center, axis=-1, keepdims=True)
    inv_std = lax.rsqrt(spread + epsilon)
    unit_rows = center * inv_std
    return ((unit_rows * gain).astype(jnp.bfloat16), unit_rows, inv_std)


def norm_backward(d_normed, gain, unit_rows, inv_std):
    scaled = d_normed * gain
    return inv_std * (
        scaled
        - jnp.mean(scaled, axis=-1, keepdims=True)
        - unit_rows * jnp.mean(scaled * unit_rows, axis=-1, keepdims=True)
    )


def head_block(query_rows, grad_rows, key_rows, value_rows, live_keys, score_scale):
    scores = jnp.dot(query_rows, key_rows.T, preferred_element_type=jnp.float32) * score_scale
    scores = jnp.where(live_keys[None, :], scores, -1e30)
    top_score = jnp.max(scores, axis=1, keepdims=True)
    raised = jnp.exp(scores - top_score)
    probability = raised / jnp.sum(raised, axis=1, keepdims=True)
    rounded = probability.astype(jnp.bfloat16)
    attended = jnp.dot(rounded, value_rows, preferred_element_type=jnp.float32).astype(jnp.bfloat16)
    d_value = jnp.dot(rounded.T, grad_rows, preferred_element_type=jnp.float32)
    d_prob = jnp.dot(grad_rows, value_rows.T, preferred_element_type=jnp.float32)
    d_score = (
        probability * (d_prob - jnp.sum(probability * d_prob, axis=1, keepdims=True)) * score_scale
    ).astype(jnp.bfloat16)
    d_query = jnp.dot(d_score, key_rows, preferred_element_type=jnp.float32)
    d_key = jnp.dot(d_score.T, query_rows, preferred_element_type=jnp.float32)
    return (attended, d_query, d_key, d_value)


def attend(query_rows, grad_rows, key_rows, value_rows, live_keys, score_scale):
    row_count = query_rows.shape[0]
    blocks = max(1, row_count // 512)
    while row_count % blocks:
        blocks -= 1
    block_rows = row_count // blocks
    query_blocks = query_rows.reshape(blocks, block_rows, query_rows.shape[1])
    grad_blocks = grad_rows.reshape(blocks, block_rows, grad_rows.shape[1])

    def block_step(carry, pieces):
        key_total, value_total = carry
        attended, d_query, d_key, d_value = head_block(
            pieces[0], pieces[1], key_rows, value_rows, live_keys, score_scale
        )
        return ((key_total + d_key, value_total + d_value), (attended, d_query))

    empty = jnp.zeros(key_rows.shape, jnp.float32)
    (key_total, value_total), (attended, d_query) = lax.scan(
        block_step, (empty, empty), (query_blocks, grad_blocks)
    )
    return (attended.reshape(row_count, -1), d_query.reshape(row_count, -1), key_total, value_total)


def shards(patches, kept_index, kept_count, cotangent, w_qkv, w_out, gain):
    groups = lax.axis_size("seq")
    samples, slot_count, model_width = patches.shape
    head_size = model_width // HEADS
    per_device = max(1, HEADS // groups)
    splits = max(1, groups // HEADS)
    head_groups = groups // splits
    band_width = per_device * head_size
    part_rows = slot_count // splits
    slot_ids = jnp.arange(slot_count, dtype=jnp.int32)
    live_slots = slot_ids[None, :] < kept_count
    hidden = patches.astype(jnp.float32) + position_table(kept_index, model_width)
    normed, unit_rows, inv_std = normalize(hidden, gain)
    flat_normed = normed.reshape(samples * slot_count, model_width)
    packed = jnp.dot(flat_normed, w_qkv, preferred_element_type=jnp.float32).astype(jnp.bfloat16)
    packed = packed.reshape(samples, slot_count, 3 * model_width)
    live_grad = jnp.where(live_slots[:, :, None], cotangent, jnp.zeros_like(cotangent))
    flat_grad = live_grad.reshape(samples * slot_count, model_width)
    d_attended = jnp.dot(flat_grad, w_out.T, preferred_element_type=jnp.float32).astype(
        jnp.bfloat16
    )
    d_attended = d_attended.reshape(samples, slot_count, model_width)

    def to_owners(tensor_block):
        arranged = tensor_block.reshape(samples, splits, part_rows, head_groups, band_width)
        return arranged.transpose(3, 1, 0, 2, 4).reshape(groups, samples, part_rows, band_width)

    key_value_send = jnp.concatenate(
        [
            packed[:, :, model_width : 2 * model_width].reshape(
                samples, slot_count, head_groups, band_width
            ),
            packed[:, :, 2 * model_width :].reshape(samples, slot_count, head_groups, band_width),
        ],
        axis=3,
    )
    key_value_send = key_value_send.transpose(2, 0, 1, 3)
    key_value_send = jnp.broadcast_to(
        key_value_send[:, None], (head_groups, splits, samples, slot_count, 2 * band_width)
    )
    key_value_send = key_value_send.reshape(groups, samples, slot_count, 2 * band_width)
    got_query, got_grad, got_pair = (
        lax.all_to_all(
            to_owners(packed[:, :, :model_width]), "seq", split_axis=0, concat_axis=0, tiled=True
        ),
        lax.all_to_all(to_owners(d_attended), "seq", split_axis=0, concat_axis=0, tiled=True),
        lax.all_to_all(key_value_send, "seq", split_axis=0, concat_axis=0, tiled=True),
    )
    all_counts = lax.all_gather(kept_count, "seq", axis=1, tiled=True)
    live_keys = (slot_ids[None, None, :] < all_counts[:, :, None]).reshape(
        samples, groups * slot_count
    )

    def rows_by_head(tensor_block, row_count):
        arranged = tensor_block.transpose(1, 0, 2, 3).reshape(
            samples, groups * row_count, per_device, head_size
        )
        return arranged.transpose(0, 2, 1, 3)

    query_heads = rows_by_head(got_query, part_rows)
    grad_heads = rows_by_head(got_grad, part_rows)
    key_heads = rows_by_head(got_pair[..., :band_width], slot_count)
    value_heads = rows_by_head(got_pair[..., band_width:], slot_count)
    score_scale = head_size ** (-0.5)

    def one_head(query_rows, grad_rows, key_rows, value_rows, key_live):
        return attend(query_rows, grad_rows, key_rows, value_rows, key_live, score_scale)

    per_head = jax.vmap(one_head, in_axes=(0, 0, 0, 0, None))
    outputs, d_query, d_key, d_value = jax.vmap(per_head)(
        query_heads, grad_heads, key_heads, value_heads, live_keys
    )

    def back_to_sources(tensor_block, row_count):
        arranged = tensor_block.transpose(0, 2, 1, 3).reshape(
            samples, groups, row_count, band_width
        )
        return arranged.transpose(1, 0, 2, 3)

    query_send = back_to_sources(d_query, part_rows).astype(jnp.bfloat16)
    back_out, back_query = (
        lax.all_to_all(
            back_to_sources(outputs, part_rows), "seq", split_axis=0, concat_axis=0, tiled=True
        ),
        lax.all_to_all(query_send, "seq", split_axis=0, concat_axis=0, tiled=True),
    )
    key_value_grad = jnp.concatenate(
        [back_to_sources(d_key, slot_count), back_to_sources(d_value, slot_count)], axis=3
    )
    back_pair = lax.all_to_all(
        key_value_grad.astype(jnp.bfloat16), "seq", split_axis=0, concat_axis=0, tiled=True
    ).astype(key_value_grad.dtype)

    def from_owners(tensor_block):
        arranged = tensor_block.reshape(head_groups, splits, samples, part_rows, band_width)
        return arranged.transpose(2, 1, 3, 0, 4).reshape(samples, slot_count, model_width)

    attended = from_owners(back_out)
    summed_pair = jnp.sum(
        back_pair.reshape(head_groups, splits, samples, slot_count, 2 * band_width), axis=1
    )
    summed_pair = summed_pair.transpose(1, 2, 0, 3)
    key_grad_rows = (
        summed_pair[..., :band_width].reshape(samples, slot_count, model_width).astype(jnp.bfloat16)
    )
    value_grad_rows = (
        summed_pair[..., band_width:].reshape(samples, slot_count, model_width).astype(jnp.bfloat16)
    )
    d_packed = jnp.concatenate([from_owners(back_query), key_grad_rows, value_grad_rows], axis=2)
    flat_attended = attended.reshape(samples * slot_count, model_width)
    projected = jnp.dot(flat_attended, w_out, preferred_element_type=jnp.float32).reshape(
        samples, slot_count, model_width
    )
    encoded = jnp.where(live_slots[:, :, None], hidden + projected, 0.0).astype(jnp.bfloat16)
    flat_packed = d_packed.reshape(samples * slot_count, 3 * model_width)
    d_normed = jnp.dot(flat_packed, w_qkv.T, preferred_element_type=jnp.float32).reshape(
        samples, slot_count, model_width
    )
    d_hidden = norm_backward(d_normed, gain, unit_rows, inv_std)
    d_patches = jnp.where(
        live_slots[:, :, None], live_grad.astype(jnp.float32) + d_hidden, 0.0
    ).astype(jnp.bfloat16)
    columns = flat_grad
    out_part = lax.psum_scatter(
        jnp.dot(columns.T, flat_attended, preferred_element_type=jnp.float32),
        "seq",
        scatter_dimension=0,
        tiled=True,
    ).T
    my_columns = lax.all_to_all(flat_packed, "seq", split_axis=1, concat_axis=0, tiled=True)
    columns = my_columns
    qkv_part = jnp.dot(
        lax.all_gather(flat_normed, "seq", axis=0, tiled=True).T,
        columns,
        preferred_element_type=jnp.float32,
    )
    qkv_grad, out_grad = lax.psum((qkv_part, out_part), "rep")
    return (encoded, d_patches, qkv_grad, out_grad)


AXES = ("seq", "rep")
MARK = 1024.0
MIB = 1024 * 1024


def line_perm(move, reps):
    pairs = []
    for z in range(4):
        for rep in range(reps):
            x, c = rep // 2, rep % 2
            to_x, to_c, to_z = move(x, c, z)
            pairs.append((z * reps + rep, to_z * reps + 2 * to_x + to_c))
    return pairs


def sine_cosine(phase):
    turns = jnp.floor(phase * np.float32(2.0 / np.pi) + 0.5)
    rest = phase - turns * np.float32(1.5703125)
    rest = rest - turns * np.float32(4.837512969970703125e-4)
    rest = rest - turns * np.float32(7.54978995489188216e-8)
    square = rest * rest
    sine = rest + rest * square * (
        np.float32(-1.6666654611e-1)
        + square * (np.float32(8.3321608736e-3) + square * np.float32(-1.9515295891e-4))
    )
    cosine = (
        1.0
        - 0.5 * square
        + square
        * square
        * (
            np.float32(4.166664568298827e-2)
            + square * (np.float32(-1.388731625493765e-3) + square * np.float32(2.443315711809948e-5))
        )
    )
    quadrant = turns.astype(jnp.int32) & 3
    swap = (quadrant & 1) == 1
    first = jnp.where(swap, cosine, sine)
    second = jnp.where(swap, sine, cosine)
    first = jnp.where(quadrant >= 2, -first, first)
    second = jnp.where((quadrant == 1) | (quadrant == 2), -second, second)
    return first, second


def live_column(count, rows):
    return lax.broadcasted_iota(jnp.int32, (rows, 1), 0) < count


def dot_nn(a, b):
    return jnp.dot(a, b, preferred_element_type=jnp.float32)


def dot_nt(a, b):
    return lax.dot_general(a, b, (((1,), (1,)), ((), ())), preferred_element_type=jnp.float32)


PAR, CORE, LINE, SIDE, KEPT = range(5)


def load_weights(core, w_in_hbm, w_out_hbm, wq, wk, wv, wo, sems):
    width = w_out_hbm.shape[0]
    copies = []
    for j in range(width // 256):
        to = pl.ds(128 * j, 128)
        row = pl.multiple_of(256 * j + 128 * core, 128)
        pairs = [(w_out_hbm.at[pl.ds(row, 128), :], wo.at[to, :])]
        for t, out in enumerate((wq, wk, wv)):
            at = pl.multiple_of(t * width + row, 128)
            pairs.append((w_in_hbm.at[:, pl.ds(at, 128)], out.at[:, to]))
        copies += [pltpu.make_async_copy(a, b, sems.at[4 + 4 * j + i]) for i, (a, b) in enumerate(pairs)]
    for copy in copies:
        copy.start()
    return copies


def norm_kernel(
    place, patch_hbm, cot_hbm, index_hbm, gain_hbm, w_in_hbm, w_out_hbm,
    p0_ref, p1_ref, hidden_ref, wq, wk, wv, wo,
    patch_ref, cot_ref, index_ref, gain_ref, sems,
):
    par = place[PAR]
    rows, width = patch_ref.shape[1:]
    quarter = width // 4
    copies = [
        pltpu.make_async_copy(src, dst, sems.at[i])
        for i, (src, dst) in enumerate(
            ((index_hbm, index_ref), (patch_hbm, patch_ref), (gain_hbm, gain_ref), (cot_hbm, cot_ref))
        )
    ]
    for copy in copies:
        copy.start()
    staged = load_weights(place[CORE], w_in_hbm, w_out_hbm, wq, wk, wv, wo, sems)
    order = lax.broadcasted_iota(jnp.int32, (1, quarter), 1).astype(jnp.float32)
    freq = jnp.exp(-np.log(np.float32(10000.0)) * order / quarter)
    diagonal = lax.broadcasted_iota(jnp.int32, (rows, rows), 0) == lax.broadcasted_iota(
        jnp.int32, (rows, rows), 1
    )
    copies[0].wait()
    tables = []
    for k in range(2):
        position = index_ref[pl.ds(k ^ par, 1), :]
        grid_row = (position // GRID_COLS).astype(jnp.float32)
        grid_col = (position % GRID_COLS).astype(jnp.float32)
        grid_row = jnp.sum(jnp.where(diagonal, grid_row, 0.0), axis=1, keepdims=True)
        grid_col = jnp.sum(jnp.where(diagonal, grid_col, 0.0), axis=1, keepdims=True)
        pieces = sine_cosine(grid_row * freq) + sine_cosine(grid_col * freq)
        tables.append(jnp.concatenate(pieces, axis=1))
    copies[1].wait()
    copies[2].wait()
    for k, out_ref in enumerate((p0_ref, p1_ref)):
        s = k ^ par
        hidden = patch_ref[s].astype(jnp.float32) + tables[k]
        hidden_ref[k] = hidden
        center = hidden - jnp.mean(hidden, axis=-1, keepdims=True)
        spread = jnp.mean(center * center, axis=-1, keepdims=True)
        normed = center * lax.rsqrt(spread + epsilon) * gain_ref[...]
        live = live_column(place[KEPT + s], rows)
        out_ref[:rows, :] = jnp.where(live, normed, MARK).astype(out_ref.dtype)
    copies[3].wait()
    for k, out_ref in enumerate((p0_ref, p1_ref)):
        s = k ^ par
        live = live_column(place[KEPT + s], rows)
        grad = cot_ref[s]
        out_ref[rows:, :] = jnp.where(live, grad, jnp.zeros_like(grad))
    for copy in staged:
        copy.wait()


def attend_pairs(
    place, first_pair, payloads, wq, wk, wv, wo, own, oth, att_own, att_oth, keep_t, out_keep, send,
    norm_s, grad_s, att_s,
):
    block = payloads[0].shape[0] // 2
    rows = 4 * block
    half = 2 * block
    biases = []
    for i, ref in enumerate(payloads):
        at = slice(i * block, (i + 1) * block)
        value = ref[:block, :]
        live = value[:, 0:1].astype(jnp.float32) < MARK
        norm_s[at, :] = jnp.where(live, value, jnp.zeros_like(value))
        grad_s[at, :] = ref[block:, :]
        biases.append(jnp.where(live, 0.0, -1e30))
    bias = jnp.concatenate(biases, axis=0)
    low = lax.broadcasted_iota(jnp.int32, (rows, 128), 1) < 64
    scale = jnp.bfloat16(0.125)
    zero = jnp.zeros((rows, 128), jnp.bfloat16)
    first = place[SIDE] == 0
    count = own.shape[2] // 128
    here = slice(128 * first_pair, 128 * (first_pair + count))
    normed = norm_s[...]
    queries = dot_nn(normed, wq[:, here]).astype(jnp.bfloat16)
    keys = dot_nn(normed, wk[:, here]).astype(jnp.bfloat16)
    values = dot_nn(normed, wv[:, here]).astype(jnp.bfloat16)
    d_att = dot_nt(grad_s[...], wo[here, :]).astype(jnp.bfloat16)
    for j in range(count):
        cols = slice(128 * j, 128 * j + 128)
        q = queries[:, cols] * scale
        k = keys[:, cols]
        v = values[:, cols]
        g = d_att[:, cols]
        v_t = v.T
        k_t = (k * scale).T
        att_t, dq_t, dk, dv = [], [], [], []
        for h in range(2):
            mine = low if h == 0 else jnp.logical_not(low)
            scores = dot_nt(k, jnp.where(mine, q, zero)) + bias
            raised = jnp.exp(scores - jnp.max(scores, axis=0, keepdims=True))
            prob = raised * (1.0 / jnp.sum(raised, axis=0, keepdims=True))
            weights = prob.astype(jnp.bfloat16)
            part = slice(64 * h, 64 * h + 64)
            att_t.append(dot_nn(v_t[part], weights))
            dv.append(dot_nn(weights, g))
            d_prob = dot_nt(v, jnp.where(mine, g, zero))
            total = jnp.sum(prob * d_prob, axis=0, keepdims=True)
            d_score = (prob * (d_prob - total)).astype(jnp.bfloat16)
            dq_t.append(dot_nn(k_t[part], d_score))
            dk.append(dot_nn(d_score, q))
        att_pair_t = jnp.concatenate(att_t, axis=0).astype(jnp.bfloat16)
        dq_pair_t = jnp.concatenate(dq_t, axis=0).astype(jnp.bfloat16)
        dk_pair = jnp.where(low, dk[0], dk[1]).astype(jnp.bfloat16)
        dv_pair = jnp.where(low, dv[0], dv[1]).astype(jnp.bfloat16)
        for t, piece in enumerate((dq_pair_t.T, dk_pair, dv_pair)):
            own[t, :, cols] = piece[:half]
            oth[t, :, cols] = piece[half:]
        att_pair = att_pair_t.T
        to = slice(128 * (first_pair + j), 128 * (first_pair + j) + 128)
        att_own[:, to] = att_pair[:half]
        att_oth[:, to] = att_pair[half:]
        for t, piece in enumerate((dq_pair_t, dk_pair.T, dv_pair.T)):
            at = slice(64 * j, 64 * j + 64)
            part = slice(rows * t, rows * t + rows)
            keep_t[at, part] = jnp.where(first, piece[:64], piece[64:])
            send[at, part] = jnp.where(first, piece[64:], piece[:64])
        at = slice(64 * j, 64 * j + 64)
        att_s[0, at, :] = jnp.where(first, att_pair_t[:64], att_pair_t[64:])
        att_s[1, at, :] = jnp.where(first, att_pair_t[64:], att_pair_t[:64])
    out_keep[...] = dot_nn(att_s[0], grad_s[...])
    send[:, 3 * rows :] = dot_nn(att_s[1], grad_s[...]).astype(send.dtype)


def attend_first(place, p0, p1, p2, p3, *refs):
    attend_pairs(place, 0, (p0, p1, p2, p3), *refs)


def attend_second(
    place, p0, p1, p2, p3, wq, wk, wv, wo, att_own, att_oth, after, own, oth, all_own, all_oth, *refs
):
    del after
    width = att_own.shape[1] // 2
    all_own[:, :width] = att_own[:, :width]
    all_oth[:, :width] = att_oth[:, :width]
    attend_pairs(place, 2, (p0, p1, p2, p3), wq, wk, wv, wo, own, oth, all_own, all_oth, *refs)


def att_kernel(place, own, got, o0, o1):
    block = o0.shape[0]
    att = in_order(place[CORE], own[...], got[...])
    o0[...] = att[:block]
    o1[...] = att[block:]


def in_order(place, own, got):
    pieces = []
    low = place == 0
    for j in range(own.shape[1] // 128):
        a, b = own[:, 128 * j : 128 * j + 128], got[:, 128 * j : 128 * j + 128]
        pieces += [jnp.where(low, a, b), jnp.where(low, b, a)]
    return jnp.concatenate(pieces, axis=1)


def rows_kernel(place, own_a, got_a, own_b, got_b, w_ref, after, o0, o1, total):
    del after
    step = pl.program_id(0)
    core = place[CORE]
    block = o0.shape[0]

    def rows_of(t):
        return jnp.concatenate([in_order(core, own_a[t], got_a[t]), in_order(core, own_b[t], got_b[t])], axis=1)

    term = dot_nt(rows_of(step), w_ref[...])

    @pl.when(step == 0)
    def _():
        total[...] = term

    @pl.when(step > 0)
    def _():
        total[...] += term

    @pl.when(step == pl.num_programs(0) - 1)
    def _():
        o0[...] = total[:block].astype(o0.dtype)
        o1[...] = total[block:].astype(o1.dtype)


def encode_kernel(place, r0, r1, w_ref, hidden_ref, encoded):
    for k, ref in enumerate((r0, r1)):
        s = k ^ place[PAR]
        live = live_column(place[KEPT + s], ref.shape[0])
        projected = dot_nn(ref[...], w_ref[...])
        encoded[s] = jnp.where(live, hidden_ref[k] + projected, 0.0).astype(encoded.dtype)


def patch_grad_kernel(place, r0, r1, hidden_ref, m0, m1, gain_ref, d_patches):
    rows = r0.shape[0]
    for k, (r_ref, m_ref) in enumerate(((r0, m0), (r1, m1))):
        s = k ^ place[PAR]
        live = live_column(place[KEPT + s], rows)
        hidden = hidden_ref[k]
        center = hidden - jnp.mean(hidden, axis=-1, keepdims=True)
        spread = jnp.mean(center * center, axis=-1, keepdims=True)
        inv_std = lax.rsqrt(spread + epsilon)
        unit = center * inv_std
        d_hidden = norm_backward(r_ref[...].astype(jnp.float32), gain_ref[...], unit, inv_std)
        value = m_ref[rows:, :].astype(jnp.float32) + d_hidden
        d_patches[s] = jnp.where(live, value, 0.0).astype(d_patches.dtype)


def put_parts(place, total, out_total, keep, send):
    columns = out_total.shape[1] // 4
    count = total.shape[0] // 4
    tall = out_total.shape[0] // 4
    for k in range(4):
        ref, spot = (keep, send)[k % 2], k // 2
        slab = place[LINE] ^ k
        at = pl.multiple_of(slab * count, 64)
        ref[spot, :count, :] = total[pl.ds(at, count), :].astype(ref.dtype)
        at = pl.ds(pl.multiple_of(slab * columns, 128), columns)
        for j in range(4):
            rows = slice(tall * j, tall * j + tall)
            ref[spot, count:, columns * j : columns * j + columns] = out_total[rows, at].astype(ref.dtype)


def sum_out_part(out_keep, got, out_total):
    out_total[...] = out_keep[...] + got[:, got.shape[1] - out_total.shape[1] :].astype(jnp.float32)


def piece_of(ref, at, rows):
    t, j = at // 2, at % 2
    return ref[64 * j : 64 * j + 64, rows * t : rows * t + rows]


def weight_first(
    place, keep, out_keep, got, p0, p1, p2, p3, n0, n1, after,
    part_keep, part_send, tokens, left, total, out_total,
):
    del after
    block = p0.shape[0] // 2
    rows = 4 * block
    for i, ref in enumerate((p0, p1, p2, p3)):
        tokens[i * block : (i + 1) * block, :] = ref[:block, :]
    tokens[rows : rows + 2 * block, :] = n0[...]
    tokens[rows + 2 * block :, :] = n1[...]
    for side, ref in enumerate((keep, got)):
        for i, at in enumerate((0, 2, 4, 5)):
            left[side, 64 * i : 64 * i + 64, :] = piece_of(ref, at, rows)
    total[...] = dot_nn(left[0], tokens[:rows, :]) + dot_nn(left[1], tokens[rows:, :])
    sum_out_part(out_keep, got, out_total)
    put_parts(place, total, out_total, part_keep, part_send)


def weight_second(
    place, keep_a, got_a, keep_b, out_keep, got_b, p0, p1, p2, p3, n0, n1, after, before,
    part_keep, part_send, tokens, left, total, out_total,
):
    del after, before
    block = p0.shape[0] // 2
    rows = 4 * block
    for i, ref in enumerate((p0, p1, p2, p3)):
        tokens[i * block : (i + 1) * block, :] = ref[:block, :]
    tokens[rows : rows + 2 * block, :] = n0[...]
    tokens[rows + 2 * block :, :] = n1[...]
    for side, (a, b) in enumerate(((keep_a, keep_b), (got_a, got_b))):
        for i, (ref, at) in enumerate(
            ((a, 1), (b, 0), (b, 1), (a, 3), (b, 2), (b, 3), (b, 4), (b, 5))
        ):
            left[side, 64 * i : 64 * i + 64, :] = piece_of(ref, at, rows)
    total[...] = dot_nn(left[0], tokens[:rows, :]) + dot_nn(left[1], tokens[rows:, :])
    sum_out_part(out_keep, got_b, out_total)
    put_parts(place, total, out_total, part_keep, part_send)


def pair_kernel(keep, got, *refs):
    mine, send = refs[-2:]
    mine[...] = keep[0] + got[0].astype(jnp.float32)
    send[...] = (keep[1] + got[1].astype(jnp.float32)).astype(send.dtype)


def sum_kernel(mine, got, *refs):
    out = refs[-1]
    out[...] = (mine[...] + got[...].astype(jnp.float32)).astype(out.dtype)


def finish_kernel(place, a0, a1, a2, a3, b0, b1, b2, b3, wide, narrow):
    core_low, side_low = place[CORE] == 0, place[SIDE] == 0
    slab = place[LINE]
    columns = narrow.shape[1]
    spot = jnp.where(slab == 3, 0, slab)
    spots = (spot, jnp.where(spot == 0, 1, 0), jnp.where(spot == 2, 1, 2))

    def pick(refs, c, x, at, part):
        own, by_x, by_core, by_both = refs
        near = jnp.where(side_low == (x == 0), own[at, part], by_x[at, part])
        far = jnp.where(side_low == (x == 0), by_core[at, part], by_both[at, part])
        return jnp.where(core_low == (c == 0), near, far)

    every = slice(None)
    first, second = (a0, a1, a2, a3), (b0, b1, b2, b3)
    for c in range(2):
        for i, (refs, row) in enumerate(((first, 0), (second, 0), (second, 64))):
            at = slice(row, row + 64)
            both = jnp.concatenate([pick(refs, c, x, at, every) for x in range(2)], axis=0)
            col = pl.multiple_of(128 * (2 * spots[i] + c), 128)
            wide[:, pl.ds(col, 128)] = both.T.astype(wide.dtype)
        for refs, base, tall, pair in ((first, 64, 32, 0), (second, 128, 32, 2)):
            for j in range(4):
                at = slice(base, base + tall)
                part = slice(columns * j, columns * j + columns)
                for x in range(2):
                    row = 128 * (2 * (pair + tall * j // 64) + c) + 64 * x + tall * j % 64
                    narrow[row : row + tall, :] = pick(refs, c, x, at, part).astype(narrow.dtype)


SMEM_SPEC = pl.BlockSpec(memory_space=pltpu.SMEM)
VMEM_SPEC = pl.BlockSpec(memory_space=pltpu.VMEM)


def struct(shape, dtype=jnp.bfloat16):
    return jax.ShapeDtypeStruct(shape, dtype)


COST = pl.CostEstimate(flops=1000, bytes_accessed=1000, transcendentals=0)


def in_hbm(value):
    return pltpu.with_memory_space_constraint(value, pltpu.HBM)


def call(kernel, args, outs, limit, place=None, scratch=(), specs=None):
    specs = specs or [VMEM_SPEC] * len(args)
    if place is not None:
        args, specs = (place, *args), [SMEM_SPEC] + specs
    single = not isinstance(outs, list)
    return pl.pallas_call(
        kernel,
        in_specs=specs,
        out_specs=VMEM_SPEC if single else [VMEM_SPEC] * len(outs),
        out_shape=outs,
        scratch_shapes=list(scratch),
        compiler_params=pltpu.CompilerParams(vmem_limit_bytes=limit * MIB),
        cost_estimate=COST,
    )(*args)


def chip_shards(patches, kept_index, kept_count, cotangent, w_qkv, w_out, gain):
    bf16, f32 = jnp.bfloat16, jnp.float32
    samples, slots, width = patches.shape
    reps = lax.axis_size("rep")
    rep = lax.axis_index("rep")
    z = lax.axis_index("seq")
    core, x = rep & 1, rep >> 1
    place = jnp.concatenate(
        [jnp.stack([z & 1, core, z, x]).astype(jnp.int32), kept_count.reshape(samples)]
    )
    own_width = width // 2
    quarter = width // 4
    rows = 4 * slots

    def send(value, move):
        return lax.ppermute(value, AXES, line_perm(move, reps))

    def to_core(value):
        return send(value, lambda x, c, z: (x, 1 - c, z))

    def to_x(value):
        return send(value, lambda x, c, z: (1 - x, c, z))

    def to_chip(value, k):
        return send(value, lambda x, c, z: (x, z >> 1, 2 * c + (k ^ (z & 1))))

    def to_rows(value, k, other):
        return send(value, lambda x, c, z: (x, z >> 1, 2 * (c ^ other) + (k ^ (z & 1))))

    def along(value, k):
        return send(value, lambda x, c, z: (x, c, z ^ k))

    gain_row = gain.reshape(1, width)
    pay = struct((2 * slots, width))
    hbm = pl.BlockSpec(memory_space=pl.ANY)
    any_spec = pl.BlockSpec(memory_space=pl.ANY)
    own_cols = struct((width, own_width))
    *outs, wq, wk, wv, wo = call(
        norm_kernel,
        tuple(in_hbm(v) for v in (patches, cotangent, kept_index, gain_row, w_qkv, w_out)),
        [pay, pay, struct(patches.shape, f32)] + [own_cols] * 3 + [struct((own_width, width))],
        24,
        place,
        scratch=[
            pltpu.VMEM(patches.shape, bf16),
            pltpu.VMEM(patches.shape, bf16),
            pltpu.VMEM(kept_index.shape, jnp.int32),
            pltpu.VMEM(gain_row.shape, f32),
            pltpu.SemaphoreType.DMA((4 + 4 * (width // 256),)),
        ],
        specs=[any_spec] * 6,
    )
    *mine, hidden = outs
    staged = (wq, wk, wv, wo)
    got = [to_chip(mine[k], k) for k in range(2)]
    here = got + [to_core(v) for v in got]
    from_x = to_x(jnp.concatenate([v[:slots] for v in got], axis=0))
    there = (from_x, to_core(from_x))

    any_spec = pl.BlockSpec(memory_space=pl.ANY)
    pairs = width // 512
    half_rows = struct((3, 2 * slots, 128 * pairs))
    att_rows = struct((2 * slots, own_width))
    out_half = (64 * pairs, width)
    half_t = struct((64 * pairs, 3 * rows))
    half_send = struct((64 * pairs, 3 * rows + width))

    def attend(kernel, extra, specs=()):
        return call(
            kernel,
            (*here, *staged, *extra),
            [half_rows] * 2 + [att_rows] * 2 + [half_t, struct(out_half, f32), half_send],
            32,
            place,
            scratch=[pltpu.VMEM((rows, width), bf16)] * 2
            + [pltpu.VMEM((2, 64 * pairs, rows), bf16)],
            specs=[VMEM_SPEC] * 8 + list(specs),
        )

    own_a, oth_a, *att_a, keep_a, out_keep_a, send_a = attend(attend_first, ())
    got_a = to_x(send_a)
    core_a = to_core(oth_a)
    own_b, oth_b, att_own, att_oth, keep_b, out_keep_b, send_b = attend(
        attend_second, (*att_a, from_x), [VMEM_SPEC] * 2 + [any_spec]
    )
    got_b = to_x(send_b)
    core_b = to_core(oth_b)
    block = struct((slots, width))
    att = call(att_kernel, (att_own, to_core(att_oth)), [block] * 2, 8, place)
    back_att = [to_rows(att[k], k, 0) for k in range(2)]

    def parts_of(kernel, args, chunks, scratch, after=()):
        return call(
            kernel,
            (*args, *here, *there, *after),
            [struct((2, tall, width), kind) for tall in chunks for kind in (f32, bf16)],
            16,
            place,
            scratch=[pltpu.VMEM((2 * rows, width), bf16)] + scratch + [pltpu.VMEM(out_half, f32)],
            specs=[VMEM_SPEC] * (len(args) + 6) + [any_spec] * len(after),
        )

    def pair_sums(keep, part, after=()):
        shape = keep.shape[1:]
        mine, part = call(
            pair_kernel,
            (keep, along(part, 1), *after),
            [struct(shape, f32), struct(shape)],
            8,
            specs=[VMEM_SPEC] * 2 + [any_spec] * len(after),
        )
        return mine, part, along(part, 2)

    def spread(mine, part, after=()):
        sums = call(
            sum_kernel,
            (mine, part, *after),
            struct(part.shape),
            8,
            specs=[VMEM_SPEC] * 2 + [any_spec] * len(after),
        )
        by_x = to_x(sums)
        return (sums, by_x, to_core(sums), to_core(by_x))

    keep, part = parts_of(
        weight_first,
        (keep_a, out_keep_a, got_a),
        (96,),
        [pltpu.VMEM((2, 256, rows), bf16), pltpu.VMEM((256, width), f32)],
        (att[0],),
    )
    d_normed = pl.pallas_call(
        rows_kernel,
        grid_spec=pltpu.PrefetchScalarGridSpec(
            num_scalar_prefetch=1,
            grid=(3,),
            in_specs=[pl.BlockSpec(half_rows.shape, lambda i, p: (0, 0, 0))] * 4
            + [pl.BlockSpec((width, width), lambda i, p: (0, i)), any_spec],
            out_specs=[pl.BlockSpec(block.shape, lambda i, p: (0, 0))] * 2,
            scratch_shapes=[pltpu.VMEM((2 * slots, width), f32)],
        ),
        out_shape=[block] * 2,
        compiler_params=pltpu.CompilerParams(vmem_limit_bytes=20 * MIB),
        cost_estimate=COST,
    )(place, own_a, core_a, own_b, core_b, in_hbm(w_qkv), part)
    first_sum, paired, first_got = pair_sums(keep, part)
    keep, part = parts_of(
        weight_second,
        (keep_a, got_a, keep_b, out_keep_b, got_b),
        (160,),
        [pltpu.VMEM((2, 512, rows), bf16), pltpu.VMEM((512, width), f32)],
        (paired, d_normed[0]),
    )
    second_sum, _, second_got = pair_sums(keep, part, back_att)
    first = spread(first_sum, first_got)
    encoded = call(
        encode_kernel,
        (*back_att, w_out, hidden),
        struct(patches.shape),
        12,
        place,
    )
    second = spread(second_sum, second_got, (*first[1:], encoded))
    back_dn = [to_rows(d_normed[k], k, 0) for k in range(2)]
    qkv_grad, out_grad = call(
        finish_kernel,
        (*first, *second),
        [struct((width, 3 * quarter), f32), struct((width, quarter), f32)],
        12,
        place,
    )
    d_patches = call(
        patch_grad_kernel,
        (*back_dn, hidden, *mine, gain_row),
        struct(patches.shape),
        12,
        place,
    )
    return (encoded, d_patches, qkv_grad, out_grad)


def solution(mesh):
    in_specs = (
        P(("grp", "rep"), "seq", None),
        P(("grp", "rep"), "seq"),
        P(("grp", "rep"), "seq"),
        P(("grp", "rep"), "seq", None),
        P(),
        P(),
        P(),
    )
    out_specs = (
        P(("grp", "rep"), "seq", None),
        P(("grp", "rep"), "seq", None),
        P("grp", "seq"),
        P("grp", "seq"),
    )
    chips = mesh.shape["seq"] == 4 and mesh.shape["rep"] % 2 == 0 and HEADS % 8 == 0

    def run(patches, *rest):
        per_device = patches.shape[0] // (mesh.shape["grp"] * mesh.shape["rep"])
        body = chip_shards if chips and per_device == 2 else shards
        inner = jax.shard_map(body, mesh=mesh, in_specs=in_specs, out_specs=out_specs, check_vma=False)
        return inner(patches, *rest)

    return run
```

```python
import functools

import jax
import jax.numpy as jnp
import numpy as np
from jax import lax
from jax.experimental import pallas as pl
from jax.experimental.pallas import tpu as pltpu
from jax.sharding import PartitionSpec as P

HEADS = 16
GRID_COLS = 512


epsilon = 1e-06


def position_table(position, model_width):
    quarter = model_width // 4
    frequency = jnp.exp(-jnp.log(10000.0) * jnp.arange(quarter, dtype=jnp.float32) / quarter)
    grid_row = (position // GRID_COLS).astype(jnp.float32)
    grid_col = (position % GRID_COLS).astype(jnp.float32)
    row_phase = grid_row[..., None] * frequency
    col_phase = grid_col[..., None] * frequency
    return jnp.concatenate(
        [jnp.sin(row_phase), jnp.cos(row_phase), jnp.sin(col_phase), jnp.cos(col_phase)], axis=-1
    )


def normalize(hidden, gain):
    center = hidden - jnp.mean(hidden, axis=-1, keepdims=True)
    spread = jnp.mean(center * center, axis=-1, keepdims=True)
    inv_std = lax.rsqrt(spread + epsilon)
    unit_rows = center * inv_std
    return ((unit_rows * gain).astype(jnp.bfloat16), unit_rows, inv_std)


def norm_backward(d_normed, gain, unit_rows, inv_std):
    scaled = d_normed * gain
    return inv_std * (
        scaled
        - jnp.mean(scaled, axis=-1, keepdims=True)
        - unit_rows * jnp.mean(scaled * unit_rows, axis=-1, keepdims=True)
    )


def head_block(query_rows, grad_rows, key_rows, value_rows, live_keys, score_scale):
    scores = jnp.dot(query_rows, key_rows.T, preferred_element_type=jnp.float32) * score_scale
    scores = jnp.where(live_keys[None, :], scores, -1e30)
    top_score = jnp.max(scores, axis=1, keepdims=True)
    raised = jnp.exp(scores - top_score)
    probability = raised / jnp.sum(raised, axis=1, keepdims=True)
    rounded = probability.astype(jnp.bfloat16)
    attended = jnp.dot(rounded, value_rows, preferred_element_type=jnp.float32).astype(jnp.bfloat16)
    d_value = jnp.dot(rounded.T, grad_rows, preferred_element_type=jnp.float32)
    d_prob = jnp.dot(grad_rows, value_rows.T, preferred_element_type=jnp.float32)
    d_score = (
        probability * (d_prob - jnp.sum(probability * d_prob, axis=1, keepdims=True)) * score_scale
    ).astype(jnp.bfloat16)
    d_query = jnp.dot(d_score, key_rows, preferred_element_type=jnp.float32)
    d_key = jnp.dot(d_score.T, query_rows, preferred_element_type=jnp.float32)
    return (attended, d_query, d_key, d_value)


def attend(query_rows, grad_rows, key_rows, value_rows, live_keys, score_scale):
    row_count = query_rows.shape[0]
    blocks = max(1, row_count // 512)
    while row_count % blocks:
        blocks -= 1
    block_rows = row_count // blocks
    query_blocks = query_rows.reshape(blocks, block_rows, query_rows.shape[1])
    grad_blocks = grad_rows.reshape(blocks, block_rows, grad_rows.shape[1])

    def block_step(carry, pieces):
        key_total, value_total = carry
        attended, d_query, d_key, d_value = head_block(
            pieces[0], pieces[1], key_rows, value_rows, live_keys, score_scale
        )
        return ((key_total + d_key, value_total + d_value), (attended, d_query))

    empty = jnp.zeros(key_rows.shape, jnp.float32)
    (key_total, value_total), (attended, d_query) = lax.scan(
        block_step, (empty, empty), (query_blocks, grad_blocks)
    )
    return (attended.reshape(row_count, -1), d_query.reshape(row_count, -1), key_total, value_total)


def shards(patches, kept_index, kept_count, cotangent, w_qkv, w_out, gain):
    groups = lax.axis_size("seq")
    samples, slot_count, model_width = patches.shape
    head_size = model_width // HEADS
    per_device = max(1, HEADS // groups)
    splits = max(1, groups // HEADS)
    head_groups = groups // splits
    band_width = per_device * head_size
    part_rows = slot_count // splits
    slot_ids = jnp.arange(slot_count, dtype=jnp.int32)
    live_slots = slot_ids[None, :] < kept_count
    hidden = patches.astype(jnp.float32) + position_table(kept_index, model_width)
    normed, unit_rows, inv_std = normalize(hidden, gain)
    flat_normed = normed.reshape(samples * slot_count, model_width)
    packed = jnp.dot(flat_normed, w_qkv, preferred_element_type=jnp.float32).astype(jnp.bfloat16)
    packed = packed.reshape(samples, slot_count, 3 * model_width)
    live_grad = jnp.where(live_slots[:, :, None], cotangent, jnp.zeros_like(cotangent))
    flat_grad = live_grad.reshape(samples * slot_count, model_width)
    d_attended = jnp.dot(flat_grad, w_out.T, preferred_element_type=jnp.float32).astype(
        jnp.bfloat16
    )
    d_attended = d_attended.reshape(samples, slot_count, model_width)

    def to_owners(tensor_block):
        arranged = tensor_block.reshape(samples, splits, part_rows, head_groups, band_width)
        return arranged.transpose(3, 1, 0, 2, 4).reshape(groups, samples, part_rows, band_width)

    key_value_send = jnp.concatenate(
        [
            packed[:, :, model_width : 2 * model_width].reshape(
                samples, slot_count, head_groups, band_width
            ),
            packed[:, :, 2 * model_width :].reshape(samples, slot_count, head_groups, band_width),
        ],
        axis=3,
    )
    key_value_send = key_value_send.transpose(2, 0, 1, 3)
    key_value_send = jnp.broadcast_to(
        key_value_send[:, None], (head_groups, splits, samples, slot_count, 2 * band_width)
    )
    key_value_send = key_value_send.reshape(groups, samples, slot_count, 2 * band_width)
    got_query, got_grad, got_pair = (
        lax.all_to_all(
            to_owners(packed[:, :, :model_width]), "seq", split_axis=0, concat_axis=0, tiled=True
        ),
        lax.all_to_all(to_owners(d_attended), "seq", split_axis=0, concat_axis=0, tiled=True),
        lax.all_to_all(key_value_send, "seq", split_axis=0, concat_axis=0, tiled=True),
    )
    all_counts = lax.all_gather(kept_count, "seq", axis=1, tiled=True)
    live_keys = (slot_ids[None, None, :] < all_counts[:, :, None]).reshape(
        samples, groups * slot_count
    )

    def rows_by_head(tensor_block, row_count):
        arranged = tensor_block.transpose(1, 0, 2, 3).reshape(
            samples, groups * row_count, per_device, head_size
        )
        return arranged.transpose(0, 2, 1, 3)

    query_heads = rows_by_head(got_query, part_rows)
    grad_heads = rows_by_head(got_grad, part_rows)
    key_heads = rows_by_head(got_pair[..., :band_width], slot_count)
    value_heads = rows_by_head(got_pair[..., band_width:], slot_count)
    score_scale = head_size ** (-0.5)

    def one_head(query_rows, grad_rows, key_rows, value_rows, key_live):
        return attend(query_rows, grad_rows, key_rows, value_rows, key_live, score_scale)

    per_head = jax.vmap(one_head, in_axes=(0, 0, 0, 0, None))
    outputs, d_query, d_key, d_value = jax.vmap(per_head)(
        query_heads, grad_heads, key_heads, value_heads, live_keys
    )

    def back_to_sources(tensor_block, row_count):
        arranged = tensor_block.transpose(0, 2, 1, 3).reshape(
            samples, groups, row_count, band_width
        )
        return arranged.transpose(1, 0, 2, 3)

    query_send = back_to_sources(d_query, part_rows).astype(jnp.bfloat16)
    back_out, back_query = (
        lax.all_to_all(
            back_to_sources(outputs, part_rows), "seq", split_axis=0, concat_axis=0, tiled=True
        ),
        lax.all_to_all(query_send, "seq", split_axis=0, concat_axis=0, tiled=True),
    )
    key_value_grad = jnp.concatenate(
        [back_to_sources(d_key, slot_count), back_to_sources(d_value, slot_count)], axis=3
    )
    back_pair = lax.all_to_all(
        key_value_grad.astype(jnp.bfloat16), "seq", split_axis=0, concat_axis=0, tiled=True
    ).astype(key_value_grad.dtype)

    def from_owners(tensor_block):
        arranged = tensor_block.reshape(head_groups, splits, samples, part_rows, band_width)
        return arranged.transpose(2, 1, 3, 0, 4).reshape(samples, slot_count, model_width)

    attended = from_owners(back_out)
    summed_pair = jnp.sum(
        back_pair.reshape(head_groups, splits, samples, slot_count, 2 * band_width), axis=1
    )
    summed_pair = summed_pair.transpose(1, 2, 0, 3)
    key_grad_rows = (
        summed_pair[..., :band_width].reshape(samples, slot_count, model_width).astype(jnp.bfloat16)
    )
    value_grad_rows = (
        summed_pair[..., band_width:].reshape(samples, slot_count, model_width).astype(jnp.bfloat16)
    )
    d_packed = jnp.concatenate([from_owners(back_query), key_grad_rows, value_grad_rows], axis=2)
    flat_attended = attended.reshape(samples * slot_count, model_width)
    projected = jnp.dot(flat_attended, w_out, preferred_element_type=jnp.float32).reshape(
        samples, slot_count, model_width
    )
    encoded = jnp.where(live_slots[:, :, None], hidden + projected, 0.0).astype(jnp.bfloat16)
    flat_packed = d_packed.reshape(samples * slot_count, 3 * model_width)
    d_normed = jnp.dot(flat_packed, w_qkv.T, preferred_element_type=jnp.float32).reshape(
        samples, slot_count, model_width
    )
    d_hidden = norm_backward(d_normed, gain, unit_rows, inv_std)
    d_patches = jnp.where(
        live_slots[:, :, None], live_grad.astype(jnp.float32) + d_hidden, 0.0
    ).astype(jnp.bfloat16)
    columns = flat_grad
    out_part = lax.psum_scatter(
        jnp.dot(columns.T, flat_attended, preferred_element_type=jnp.float32),
        "seq",
        scatter_dimension=0,
        tiled=True,
    ).T
    my_columns = lax.all_to_all(flat_packed, "seq", split_axis=1, concat_axis=0, tiled=True)
    columns = my_columns
    qkv_part = jnp.dot(
        lax.all_gather(flat_normed, "seq", axis=0, tiled=True).T,
        columns,
        preferred_element_type=jnp.float32,
    )
    qkv_grad, out_grad = lax.psum((qkv_part, out_part), "rep")
    return (encoded, d_patches, qkv_grad, out_grad)


AXES = ("seq", "rep")
MARK = 1024.0
MIB = 1024 * 1024


def line_perm(move, reps):
    pairs = []
    for z in range(4):
        for rep in range(reps):
            x, c = rep // 2, rep % 2
            to_x, to_c, to_z = move(x, c, z)
            pairs.append((z * reps + rep, to_z * reps + 2 * to_x + to_c))
    return pairs


def sine_cosine(phase):
    turns = jnp.floor(phase * np.float32(2.0 / np.pi) + 0.5)
    rest = phase - turns * np.float32(1.5703125)
    rest = rest - turns * np.float32(4.837512969970703125e-4)
    rest = rest - turns * np.float32(7.54978995489188216e-8)
    square = rest * rest
    sine = rest + rest * square * (
        np.float32(-1.6666654611e-1)
        + square * (np.float32(8.3321608736e-3) + square * np.float32(-1.9515295891e-4))
    )
    cosine = (
        1.0
        - 0.5 * square
        + square
        * square
        * (
            np.float32(4.166664568298827e-2)
            + square * (np.float32(-1.388731625493765e-3) + square * np.float32(2.443315711809948e-5))
        )
    )
    quadrant = turns.astype(jnp.int32) & 3
    swap = (quadrant & 1) == 1
    first = jnp.where(swap, cosine, sine)
    second = jnp.where(swap, sine, cosine)
    first = jnp.where(quadrant >= 2, -first, first)
    second = jnp.where((quadrant == 1) | (quadrant == 2), -second, second)
    return first, second


def live_column(count, rows):
    return lax.broadcasted_iota(jnp.int32, (rows, 1), 0) < count


def dot_nn(a, b):
    return jnp.dot(a, b, preferred_element_type=jnp.float32)


def dot_nt(a, b):
    return lax.dot_general(a, b, (((1,), (1,)), ((), ())), preferred_element_type=jnp.float32)


PAR, CORE, LINE, SIDE, KEPT = range(5)


def load_weights(core, first_pair, w_in_hbm, w_out_hbm, wq, wk, wv, wo, sems):
    width = w_out_hbm.shape[0]
    copies = []
    for j in range(wq.shape[1] // 128):
        to = pl.ds(128 * j, 128)
        row = pl.multiple_of(256 * (first_pair + j) + 128 * core, 128)
        pairs = [(w_out_hbm.at[pl.ds(row, 128), :], wo.at[to, :])]
        for t, out in enumerate((wq, wk, wv)):
            at = pl.multiple_of(t * width + row, 128)
            pairs.append((w_in_hbm.at[:, pl.ds(at, 128)], out.at[:, to]))
        copies += [pltpu.make_async_copy(a, b, sems.at[4 * j + i]) for i, (a, b) in enumerate(pairs)]
    for copy in copies:
        copy.start()
    return copies


def norm_kernel(
    place, patch_hbm, cot_hbm, index_hbm, gain_hbm, w_in_hbm, w_out_hbm,
    p0_ref, p1_ref, hidden_ref, wq, wk, wv, wo,
    patch_ref, cot_ref, index_ref, gain_ref, sems, w_sems,
):
    par = place[PAR]
    rows, width = patch_ref.shape[1:]
    quarter = width // 4
    copies = [
        pltpu.make_async_copy(src, dst, sems.at[i])
        for i, (src, dst) in enumerate(
            ((index_hbm, index_ref), (patch_hbm, patch_ref), (gain_hbm, gain_ref), (cot_hbm, cot_ref))
        )
    ]
    for copy in copies:
        copy.start()
    staged = load_weights(place[CORE], 0, w_in_hbm, w_out_hbm, wq, wk, wv, wo, w_sems)
    order = lax.broadcasted_iota(jnp.int32, (1, quarter), 1).astype(jnp.float32)
    freq = jnp.exp(-np.log(np.float32(10000.0)) * order / quarter)
    diagonal = lax.broadcasted_iota(jnp.int32, (rows, rows), 0) == lax.broadcasted_iota(
        jnp.int32, (rows, rows), 1
    )
    copies[0].wait()
    tables = []
    for k in range(2):
        position = index_ref[pl.ds(k ^ par, 1), :]
        grid_row = (position // GRID_COLS).astype(jnp.float32)
        grid_col = (position % GRID_COLS).astype(jnp.float32)
        grid_row = jnp.sum(jnp.where(diagonal, grid_row, 0.0), axis=1, keepdims=True)
        grid_col = jnp.sum(jnp.where(diagonal, grid_col, 0.0), axis=1, keepdims=True)
        pieces = sine_cosine(grid_row * freq) + sine_cosine(grid_col * freq)
        tables.append(jnp.concatenate(pieces, axis=1))
    copies[1].wait()
    copies[2].wait()
    for k, out_ref in enumerate((p0_ref, p1_ref)):
        s = k ^ par
        hidden = patch_ref[s].astype(jnp.float32) + tables[k]
        hidden_ref[k] = hidden
        center = hidden - jnp.mean(hidden, axis=-1, keepdims=True)
        spread = jnp.mean(center * center, axis=-1, keepdims=True)
        normed = center * lax.rsqrt(spread + epsilon) * gain_ref[...]
        live = live_column(place[KEPT + s], rows)
        out_ref[:rows, :] = jnp.where(live, normed, MARK).astype(out_ref.dtype)
    copies[3].wait()
    for k, out_ref in enumerate((p0_ref, p1_ref)):
        s = k ^ par
        live = live_column(place[KEPT + s], rows)
        grad = cot_ref[s]
        out_ref[rows:, :] = jnp.where(live, grad, jnp.zeros_like(grad))
    for copy in staged:
        copy.wait()


def attend_pairs(
    place, payloads, wq, wk, wv, wo, own, oth, keep_t, out_keep, send, norm_s, grad_s, att_s,
):
    block = payloads[0].shape[0] // 2
    rows = 4 * block
    half = 2 * block
    biases = []
    for i, ref in enumerate(payloads):
        at = slice(i * block, (i + 1) * block)
        value = ref[:block, :]
        live = value[:, 0:1].astype(jnp.float32) < MARK
        norm_s[at, :] = jnp.where(live, value, jnp.zeros_like(value))
        grad_s[at, :] = ref[block:, :]
        biases.append(jnp.where(live, 0.0, -1e30))
    bias = jnp.concatenate(biases, axis=0)
    low = lax.broadcasted_iota(jnp.int32, (rows, 128), 1) < 64
    scale = jnp.bfloat16(0.125)
    zero = jnp.zeros((rows, 128), jnp.bfloat16)
    first = place[SIDE] == 0
    count = wq.shape[1] // 128
    normed = norm_s[...]
    queries = dot_nn(normed, wq[...]).astype(jnp.bfloat16)
    keys = dot_nn(normed, wk[...]).astype(jnp.bfloat16)
    values = dot_nn(normed, wv[...]).astype(jnp.bfloat16)
    d_att = dot_nt(grad_s[...], wo[...]).astype(jnp.bfloat16)
    for j in range(count):
        cols = slice(128 * j, 128 * j + 128)
        q = queries[:, cols] * scale
        k = keys[:, cols]
        v = values[:, cols]
        g = d_att[:, cols]
        v_t = v.T
        k_t = (k * scale).T
        att_t, dq_t, dk, dv = [], [], [], []
        for h in range(2):
            mine = low if h == 0 else jnp.logical_not(low)
            scores = dot_nt(k, jnp.where(mine, q, zero)) + bias
            raised = jnp.exp(scores - jnp.max(scores, axis=0, keepdims=True))
            prob = raised * (1.0 / jnp.sum(raised, axis=0, keepdims=True))
            weights = prob.astype(jnp.bfloat16)
            part = slice(64 * h, 64 * h + 64)
            att_t.append(dot_nn(v_t[part], weights))
            dv.append(dot_nn(weights, g))
            d_prob = dot_nt(v, jnp.where(mine, g, zero))
            total = jnp.sum(prob * d_prob, axis=0, keepdims=True)
            d_score = (prob * (d_prob - total)).astype(jnp.bfloat16)
            dq_t.append(dot_nn(k_t[part], d_score))
            dk.append(dot_nn(d_score, q))
        att_pair_t = jnp.concatenate(att_t, axis=0).astype(jnp.bfloat16)
        dq_pair_t = jnp.concatenate(dq_t, axis=0).astype(jnp.bfloat16)
        dk_pair = jnp.where(low, dk[0], dk[1]).astype(jnp.bfloat16)
        dv_pair = jnp.where(low, dv[0], dv[1]).astype(jnp.bfloat16)
        for t, piece in enumerate((dq_pair_t.T, dk_pair, dv_pair, att_pair_t.T)):
            own[t, :, cols] = piece[:half]
            oth[t, :, cols] = piece[half:]
        for t, piece in enumerate((dq_pair_t, dk_pair.T, dv_pair.T)):
            at = slice(64 * j, 64 * j + 64)
            part = slice(rows * t, rows * t + rows)
            keep_t[at, part] = jnp.where(first, piece[:64], piece[64:])
            send[at, part] = jnp.where(first, piece[64:], piece[:64])
        at = slice(64 * j, 64 * j + 64)
        att_s[0, at, :] = jnp.where(first, att_pair_t[:64], att_pair_t[64:])
        att_s[1, at, :] = jnp.where(first, att_pair_t[64:], att_pair_t[:64])
    out_keep[...] = dot_nn(att_s[0], grad_s[...])
    send[:, 3 * rows :] = dot_nn(att_s[1], grad_s[...]).astype(send.dtype)


def attend_first(
    place, p0, p1, p2, p3, wq, wk, wv, wo, w_in_hbm, w_out_hbm,
    own, oth, keep_t, out_keep, send, wq2, wk2, wv2, wo2, norm_s, grad_s, att_s, sems,
):
    copies = load_weights(place[CORE], 2, w_in_hbm, w_out_hbm, wq2, wk2, wv2, wo2, sems)
    attend_pairs(
        place, (p0, p1, p2, p3), wq, wk, wv, wo, own, oth, keep_t, out_keep, send, norm_s, grad_s, att_s
    )
    for copy in copies:
        copy.wait()


def attend_second(place, p0, p1, p2, p3, wq, wk, wv, wo, after, *refs):
    del after
    attend_pairs(place, (p0, p1, p2, p3), wq, wk, wv, wo, *refs)


def in_order(place, own, got):
    pieces = []
    low = place == 0
    for j in range(own.shape[1] // 128):
        a, b = own[:, 128 * j : 128 * j + 128], got[:, 128 * j : 128 * j + 128]
        pieces += [jnp.where(low, a, b), jnp.where(low, b, a)]
    return jnp.concatenate(pieces, axis=1)


def rows_kernel(place, own_a, got_a, own_b, got_b, w_ref, after, before, o0, o1, total):
    del after, before
    step = pl.program_id(0)
    core = place[CORE]
    block = o0.shape[0] // 2

    def rows_of(t):
        return jnp.concatenate([in_order(core, own_a[t], got_a[t]), in_order(core, own_b[t], got_b[t])], axis=1)

    term = dot_nt(rows_of(step), w_ref[...])

    @pl.when(step == 0)
    def _():
        total[...] = term
        att = rows_of(3)
        o0[:block, :] = att[:block]
        o1[:block, :] = att[block:]

    @pl.when(step > 0)
    def _():
        total[...] += term

    @pl.when(step == pl.num_programs(0) - 1)
    def _():
        o0[block:, :] = total[:block].astype(o0.dtype)
        o1[block:, :] = total[block:].astype(o1.dtype)


def return_kernel(place, r0, r1, w_ref, hidden_ref, m0, m1, gain_ref, after, encoded, d_patches):
    del after
    par = place[PAR]
    rows = r0.shape[0] // 2
    for k, (r_ref, m_ref) in enumerate(((r0, m0), (r1, m1))):
        s = k ^ par
        live = live_column(place[KEPT + s], rows)
        hidden = hidden_ref[k]
        projected = dot_nn(r_ref[:rows, :], w_ref[...])
        encoded[s] = jnp.where(live, hidden + projected, 0.0).astype(encoded.dtype)
        center = hidden - jnp.mean(hidden, axis=-1, keepdims=True)
        spread = jnp.mean(center * center, axis=-1, keepdims=True)
        inv_std = lax.rsqrt(spread + epsilon)
        unit = center * inv_std
        d_hidden = norm_backward(r_ref[rows:, :].astype(jnp.float32), gain_ref[...], unit, inv_std)
        value = m_ref[rows:, :].astype(jnp.float32) + d_hidden
        d_patches[s] = jnp.where(live, value, 0.0).astype(d_patches.dtype)


def put_parts(place, total, out_keep, got, keep, send, out_total):
    out_total[...] = out_keep[...] + got[:, got.shape[1] - out_total.shape[1] :].astype(jnp.float32)
    columns = out_total.shape[1] // 4
    tall = out_total.shape[0] // 4
    count = total.shape[0] // 4
    for k in range(4):
        ref, spot = (keep, send)[k % 2], k // 2
        at = pl.multiple_of((place[LINE] ^ k) * count, 64)
        ref[spot, :count, :] = total[pl.ds(at, count), :].astype(ref.dtype)
        at = pl.multiple_of((place[LINE] ^ k) * columns, 128)
        value = out_total[:, pl.ds(at, columns)].astype(ref.dtype)
        for j in range(4):
            ref[spot, count:, columns * j : columns * j + columns] = value[tall * j : tall * j + tall, :]


def piece_of(ref, at, rows):
    t, j = at // 2, at % 2
    return ref[64 * j : 64 * j + 64, rows * t : rows * t + rows]


def weight_first(
    place, keep, out_keep, got, p0, p1, p2, p3, n0, n1,
    part_keep, part_send, tokens, left, total, out_total,
):
    block = p0.shape[0] // 2
    rows = 4 * block
    for i, ref in enumerate((p0, p1, p2, p3)):
        tokens[i * block : (i + 1) * block, :] = ref[:block, :]
    tokens[rows : rows + 2 * block, :] = n0[...]
    tokens[rows + 2 * block :, :] = n1[...]
    for side, ref in enumerate((keep, got)):
        for i, at in enumerate((0, 2, 4, 5)):
            left[side, 64 * i : 64 * i + 64, :] = piece_of(ref, at, rows)
    total[...] = dot_nn(left[0], tokens[:rows, :]) + dot_nn(left[1], tokens[rows:, :])
    put_parts(place, total, out_keep, got, part_keep, part_send, out_total)


def weight_second(
    place, keep_a, got_a, keep_b, out_keep, got_b, p0, p1, p2, p3, n0, n1, after,
    part_keep, part_send, tokens, left, total, out_total,
):
    del after
    block = p0.shape[0] // 2
    rows = 4 * block
    for i, ref in enumerate((p0, p1, p2, p3)):
        tokens[i * block : (i + 1) * block, :] = ref[:block, :]
    tokens[rows : rows + 2 * block, :] = n0[...]
    tokens[rows + 2 * block :, :] = n1[...]
    for side, (a, b) in enumerate(((keep_a, keep_b), (got_a, got_b))):
        for i, (ref, at) in enumerate(
            ((a, 1), (b, 0), (b, 1), (a, 3), (b, 2), (b, 3), (b, 4), (b, 5))
        ):
            left[side, 64 * i : 64 * i + 64, :] = piece_of(ref, at, rows)
    total[...] = dot_nn(left[0], tokens[:rows, :]) + dot_nn(left[1], tokens[rows:, :])
    put_parts(place, total, out_keep, got_b, part_keep, part_send, out_total)


def pair_kernel(keep, got, mine, send):
    mine[...] = keep[0] + got[0].astype(jnp.float32)
    send[...] = (keep[1] + got[1].astype(jnp.float32)).astype(send.dtype)


def sum_kernel(mine, got, *refs):
    out = refs[-1]
    out[...] = (mine[...] + got[...].astype(jnp.float32)).astype(out.dtype)


def finish_kernel(place, a0, a1, a2, a3, b0, b1, b2, b3, wide, narrow):
    core_low, side_low = place[CORE] == 0, place[SIDE] == 0
    slab = place[LINE]
    columns = narrow.shape[1]
    spot = jnp.where(slab == 3, 0, slab)
    spots = (spot, jnp.where(spot == 0, 1, 0), jnp.where(spot == 2, 1, 2))

    def pick(refs, c, x, at, part):
        own, by_x, by_core, by_both = refs
        near = jnp.where(side_low == (x == 0), own[at, part], by_x[at, part])
        far = jnp.where(side_low == (x == 0), by_core[at, part], by_both[at, part])
        return jnp.where(core_low == (c == 0), near, far)

    every = slice(None)
    first, second = (a0, a1, a2, a3), (b0, b1, b2, b3)
    for c in range(2):
        for i, (refs, row) in enumerate(((first, 0), (second, 0), (second, 64))):
            at = slice(row, row + 64)
            both = jnp.concatenate([pick(refs, c, x, at, every) for x in range(2)], axis=0)
            col = pl.multiple_of(128 * (2 * spots[i] + c), 128)
            wide[:, pl.ds(col, 128)] = both.T.astype(wide.dtype)
        for half, (refs, base) in enumerate(((first, 64), (second, 128))):
            for j in range(4):
                at = slice(base, base + 32)
                part = slice(columns * j, columns * j + columns)
                for x in range(2):
                    pair, row = 2 * half + j // 2, 32 * (j % 2)
                    row += 128 * (2 * pair + c) + 64 * x
                    narrow[row : row + 32, :] = pick(refs, c, x, at, part).astype(narrow.dtype)


SMEM_SPEC = pl.BlockSpec(memory_space=pltpu.SMEM)
VMEM_SPEC = pl.BlockSpec(memory_space=pltpu.VMEM)


def struct(shape, dtype=jnp.bfloat16):
    return jax.ShapeDtypeStruct(shape, dtype)


COST = pl.CostEstimate(flops=1000, bytes_accessed=1000, transcendentals=0)


def in_hbm(value):
    return pltpu.with_memory_space_constraint(value, pltpu.HBM)


def call(kernel, args, outs, limit, place=None, scratch=(), specs=None):
    specs = specs or [VMEM_SPEC] * len(args)
    if place is not None:
        args, specs = (place, *args), [SMEM_SPEC] + specs
    single = not isinstance(outs, list)
    return pl.pallas_call(
        kernel,
        in_specs=specs,
        out_specs=VMEM_SPEC if single else [VMEM_SPEC] * len(outs),
        out_shape=outs,
        scratch_shapes=list(scratch),
        compiler_params=pltpu.CompilerParams(vmem_limit_bytes=limit * MIB),
        cost_estimate=COST,
    )(*args)


def chip_shards(patches, kept_index, kept_count, cotangent, w_qkv, w_out, gain):
    bf16, f32 = jnp.bfloat16, jnp.float32
    samples, slots, width = patches.shape
    reps = lax.axis_size("rep")
    rep = lax.axis_index("rep")
    z = lax.axis_index("seq")
    core, x = rep & 1, rep >> 1
    place = jnp.concatenate(
        [jnp.stack([z & 1, core, z, x]).astype(jnp.int32), kept_count.reshape(samples)]
    )
    own_width = width // 2
    quarter = width // 4
    rows = 4 * slots

    def send(value, move):
        return lax.ppermute(value, AXES, line_perm(move, reps))

    def to_core(value):
        return send(value, lambda x, c, z: (x, 1 - c, z))

    def to_x(value):
        return send(value, lambda x, c, z: (1 - x, c, z))

    def to_chip(value, k):
        return send(value, lambda x, c, z: (x, z >> 1, 2 * c + (k ^ (z & 1))))

    def to_rows(value, k, other):
        return send(value, lambda x, c, z: (x, z >> 1, 2 * (c ^ other) + (k ^ (z & 1))))

    def along(value, k):
        return send(value, lambda x, c, z: (x, c, z ^ k))

    gain_row = gain.reshape(1, width)
    pay = struct((2 * slots, width))
    hbm = pl.BlockSpec(memory_space=pl.ANY)
    any_spec = pl.BlockSpec(memory_space=pl.ANY)
    pairs = width // 512
    half_w = [struct((width, 128 * pairs))] * 3 + [struct((128 * pairs, width))]
    *outs, wq, wk, wv, wo = call(
        norm_kernel,
        tuple(in_hbm(v) for v in (patches, cotangent, kept_index, gain_row, w_qkv, w_out)),
        [pay, pay, struct(patches.shape, f32)] + half_w,
        24,
        place,
        scratch=[
            pltpu.VMEM(patches.shape, bf16),
            pltpu.VMEM(patches.shape, bf16),
            pltpu.VMEM(kept_index.shape, jnp.int32),
            pltpu.VMEM(gain_row.shape, f32),
            pltpu.SemaphoreType.DMA((4,)),
            pltpu.SemaphoreType.DMA((4 * pairs,)),
        ],
        specs=[any_spec] * 6,
    )
    *mine, hidden = outs
    got = [to_chip(mine[k], k) for k in range(2)]
    here = got + [to_core(v) for v in got]
    from_x = to_x(jnp.concatenate([v[:slots] for v in got], axis=0))
    there = (from_x, to_core(from_x))

    half_rows = struct((4, 2 * slots, 128 * pairs))
    out_half = (64 * pairs, width)
    half_t = struct((64 * pairs, 3 * rows))
    half_send = struct((64 * pairs, 3 * rows + width))

    def attend(kernel, args, outs=(), scratch=()):
        return call(
            kernel,
            (*here, *args),
            [half_rows] * 2 + [half_t, struct(out_half, f32), half_send] + list(outs),
            32,
            place,
            scratch=[pltpu.VMEM((rows, width), bf16)] * 2
            + [pltpu.VMEM((2, 64 * pairs, rows), bf16)]
            + list(scratch),
            specs=[VMEM_SPEC] * 8 + [any_spec] * (len(args) - 4),
        )

    own_a, oth_a, keep_a, out_keep_a, send_a, *staged = attend(
        attend_first,
        (wq, wk, wv, wo, in_hbm(w_qkv), in_hbm(w_out)),
        half_w,
        [pltpu.SemaphoreType.DMA((4 * pairs,))],
    )
    got_a = to_x(send_a)
    core_a = to_core(oth_a)
    own_b, oth_b, keep_b, out_keep_b, send_b = attend(attend_second, (*staged, from_x))
    got_b = to_x(send_b)
    core_b = to_core(oth_b)

    def parts_of(kernel, args, tall, scratch, after=()):
        return call(
            kernel,
            (*args, *here, *there, *after),
            [struct((2, tall, width), f32), struct((2, tall, width))],
            16,
            place,
            scratch=[pltpu.VMEM((2 * rows, width), bf16)] + scratch + [pltpu.VMEM(out_half, f32)],
            specs=[VMEM_SPEC] * (len(args) + 6) + [any_spec] * len(after),
        )

    def pair_sums(keep, part):
        shape = keep.shape[1:]
        mine, part = call(pair_kernel, (keep, along(part, 1)), [struct(shape, f32), struct(shape)], 8)
        return mine, part, along(part, 2)

    def spread(mine, part, after=()):
        sums = call(
            sum_kernel,
            (mine, part, *after),
            struct(part.shape),
            8,
            specs=[VMEM_SPEC] * 2 + [any_spec] * len(after),
        )
        by_x = to_x(sums)
        return (sums, by_x, to_core(sums), to_core(by_x))

    keep, part = parts_of(
        weight_first,
        (keep_a, out_keep_a, got_a),
        96,
        [pltpu.VMEM((2, 256, rows), bf16), pltpu.VMEM((256, width), f32)],
    )
    first_sum, paired, first_got = pair_sums(keep, part)
    keep, part = parts_of(
        weight_second,
        (keep_a, got_a, keep_b, out_keep_b, got_b),
        160,
        [pltpu.VMEM((2, 512, rows), bf16), pltpu.VMEM((512, width), f32)],
        (paired,),
    )
    started = part
    second_sum, _, second_got = pair_sums(keep, part)
    first = spread(first_sum, first_got)
    back = pl.pallas_call(
        rows_kernel,
        grid_spec=pltpu.PrefetchScalarGridSpec(
            num_scalar_prefetch=1,
            grid=(3,),
            in_specs=[pl.BlockSpec(half_rows.shape, lambda i, p: (0, 0, 0))] * 4
            + [pl.BlockSpec((width, width), lambda i, p: (0, i)), any_spec, any_spec],
            out_specs=[pl.BlockSpec(pay.shape, lambda i, p: (0, 0))] * 2,
            scratch_shapes=[pltpu.VMEM((2 * slots, width), f32)],
        ),
        out_shape=[pay] * 2,
        compiler_params=pltpu.CompilerParams(vmem_limit_bytes=20 * MIB),
        cost_estimate=COST,
    )(place, own_a, core_a, own_b, core_b, in_hbm(w_qkv), started, first[1])
    second = spread(second_sum, second_got, (back[0], *first[1:]))
    back = [to_rows(back[k], k, 0) for k in range(2)]
    qkv_grad, out_grad = call(
        finish_kernel,
        (*first, *second),
        [struct((width, 3 * quarter), f32), struct((width, quarter), f32)],
        12,
        place,
    )
    encoded, d_patches = call(
        return_kernel,
        (*back, w_out, hidden, *mine, gain_row, qkv_grad),
        [struct(patches.shape)] * 2,
        12,
        place,
        specs=[VMEM_SPEC] * 7 + [any_spec],
    )
    return (encoded, d_patches, qkv_grad, out_grad)


def solution(mesh):
    in_specs = (
        P(("grp", "rep"), "seq", None),
        P(("grp", "rep"), "seq"),
        P(("grp", "rep"), "seq"),
        P(("grp", "rep"), "seq", None),
        P(),
        P(),
        P(),
    )
    out_specs = (
        P(("grp", "rep"), "seq", None),
        P(("grp", "rep"), "seq", None),
        P("grp", "seq"),
        P("grp", "seq"),
    )
    chips = mesh.shape["seq"] == 4 and mesh.shape["rep"] % 2 == 0 and HEADS % 8 == 0

    def run(patches, *rest):
        per_device = patches.shape[0] // (mesh.shape["grp"] * mesh.shape["rep"])
        body = chip_shards if chips and per_device == 2 else shards
        inner = jax.shard_map(body, mesh=mesh, in_specs=in_specs, out_specs=out_specs, check_vma=False)
        return inner(patches, *rest)

    return run
```

```python
import functools

import jax
import jax.numpy as jnp
import numpy as np
from jax import lax
from jax.experimental import pallas as pl
from jax.experimental.pallas import tpu as pltpu
from jax.sharding import PartitionSpec as P

HEADS = 16
GRID_COLS = 512


epsilon = 1e-06


def position_table(position, model_width):
    quarter = model_width // 4
    frequency = jnp.exp(-jnp.log(10000.0) * jnp.arange(quarter, dtype=jnp.float32) / quarter)
    grid_row = (position // GRID_COLS).astype(jnp.float32)
    grid_col = (position % GRID_COLS).astype(jnp.float32)
    row_phase = grid_row[..., None] * frequency
    col_phase = grid_col[..., None] * frequency
    return jnp.concatenate(
        [jnp.sin(row_phase), jnp.cos(row_phase), jnp.sin(col_phase), jnp.cos(col_phase)], axis=-1
    )


def normalize(hidden, gain):
    center = hidden - jnp.mean(hidden, axis=-1, keepdims=True)
    spread = jnp.mean(center * center, axis=-1, keepdims=True)
    inv_std = lax.rsqrt(spread + epsilon)
    unit_rows = center * inv_std
    return ((unit_rows * gain).astype(jnp.bfloat16), unit_rows, inv_std)


def norm_backward(d_normed, gain, unit_rows, inv_std):
    scaled = d_normed * gain
    return inv_std * (
        scaled
        - jnp.mean(scaled, axis=-1, keepdims=True)
        - unit_rows * jnp.mean(scaled * unit_rows, axis=-1, keepdims=True)
    )


def head_block(query_rows, grad_rows, key_rows, value_rows, live_keys, score_scale):
    scores = jnp.dot(query_rows, key_rows.T, preferred_element_type=jnp.float32) * score_scale
    scores = jnp.where(live_keys[None, :], scores, -1e30)
    top_score = jnp.max(scores, axis=1, keepdims=True)
    raised = jnp.exp(scores - top_score)
    probability = raised / jnp.sum(raised, axis=1, keepdims=True)
    rounded = probability.astype(jnp.bfloat16)
    attended = jnp.dot(rounded, value_rows, preferred_element_type=jnp.float32).astype(jnp.bfloat16)
    d_value = jnp.dot(rounded.T, grad_rows, preferred_element_type=jnp.float32)
    d_prob = jnp.dot(grad_rows, value_rows.T, preferred_element_type=jnp.float32)
    d_score = (
        probability * (d_prob - jnp.sum(probability * d_prob, axis=1, keepdims=True)) * score_scale
    ).astype(jnp.bfloat16)
    d_query = jnp.dot(d_score, key_rows, preferred_element_type=jnp.float32)
    d_key = jnp.dot(d_score.T, query_rows, preferred_element_type=jnp.float32)
    return (attended, d_query, d_key, d_value)


def attend(query_rows, grad_rows, key_rows, value_rows, live_keys, score_scale):
    row_count = query_rows.shape[0]
    blocks = max(1, row_count // 512)
    while row_count % blocks:
        blocks -= 1
    block_rows = row_count // blocks
    query_blocks = query_rows.reshape(blocks, block_rows, query_rows.shape[1])
    grad_blocks = grad_rows.reshape(blocks, block_rows, grad_rows.shape[1])

    def block_step(carry, pieces):
        key_total, value_total = carry
        attended, d_query, d_key, d_value = head_block(
            pieces[0], pieces[1], key_rows, value_rows, live_keys, score_scale
        )
        return ((key_total + d_key, value_total + d_value), (attended, d_query))

    empty = jnp.zeros(key_rows.shape, jnp.float32)
    (key_total, value_total), (attended, d_query) = lax.scan(
        block_step, (empty, empty), (query_blocks, grad_blocks)
    )
    return (attended.reshape(row_count, -1), d_query.reshape(row_count, -1), key_total, value_total)


def shards(patches, kept_index, kept_count, cotangent, w_qkv, w_out, gain):
    groups = lax.axis_size("seq")
    samples, slot_count, model_width = patches.shape
    head_size = model_width // HEADS
    per_device = max(1, HEADS // groups)
    splits = max(1, groups // HEADS)
    head_groups = groups // splits
    band_width = per_device * head_size
    part_rows = slot_count // splits
    slot_ids = jnp.arange(slot_count, dtype=jnp.int32)
    live_slots = slot_ids[None, :] < kept_count
    hidden = patches.astype(jnp.float32) + position_table(kept_index, model_width)
    normed, unit_rows, inv_std = normalize(hidden, gain)
    flat_normed = normed.reshape(samples * slot_count, model_width)
    packed = jnp.dot(flat_normed, w_qkv, preferred_element_type=jnp.float32).astype(jnp.bfloat16)
    packed = packed.reshape(samples, slot_count, 3 * model_width)
    live_grad = jnp.where(live_slots[:, :, None], cotangent, jnp.zeros_like(cotangent))
    flat_grad = live_grad.reshape(samples * slot_count, model_width)
    d_attended = jnp.dot(flat_grad, w_out.T, preferred_element_type=jnp.float32).astype(
        jnp.bfloat16
    )
    d_attended = d_attended.reshape(samples, slot_count, model_width)

    def to_owners(tensor_block):
        arranged = tensor_block.reshape(samples, splits, part_rows, head_groups, band_width)
        return arranged.transpose(3, 1, 0, 2, 4).reshape(groups, samples, part_rows, band_width)

    key_value_send = jnp.concatenate(
        [
            packed[:, :, model_width : 2 * model_width].reshape(
                samples, slot_count, head_groups, band_width
            ),
            packed[:, :, 2 * model_width :].reshape(samples, slot_count, head_groups, band_width),
        ],
        axis=3,
    )
    key_value_send = key_value_send.transpose(2, 0, 1, 3)
    key_value_send = jnp.broadcast_to(
        key_value_send[:, None], (head_groups, splits, samples, slot_count, 2 * band_width)
    )
    key_value_send = key_value_send.reshape(groups, samples, slot_count, 2 * band_width)
    got_query, got_grad, got_pair = (
        lax.all_to_all(
            to_owners(packed[:, :, :model_width]), "seq", split_axis=0, concat_axis=0, tiled=True
        ),
        lax.all_to_all(to_owners(d_attended), "seq", split_axis=0, concat_axis=0, tiled=True),
        lax.all_to_all(key_value_send, "seq", split_axis=0, concat_axis=0, tiled=True),
    )
    all_counts = lax.all_gather(kept_count, "seq", axis=1, tiled=True)
    live_keys = (slot_ids[None, None, :] < all_counts[:, :, None]).reshape(
        samples, groups * slot_count
    )

    def rows_by_head(tensor_block, row_count):
        arranged = tensor_block.transpose(1, 0, 2, 3).reshape(
            samples, groups * row_count, per_device, head_size
        )
        return arranged.transpose(0, 2, 1, 3)

    query_heads = rows_by_head(got_query, part_rows)
    grad_heads = rows_by_head(got_grad, part_rows)
    key_heads = rows_by_head(got_pair[..., :band_width], slot_count)
    value_heads = rows_by_head(got_pair[..., band_width:], slot_count)
    score_scale = head_size ** (-0.5)

    def one_head(query_rows, grad_rows, key_rows, value_rows, key_live):
        return attend(query_rows, grad_rows, key_rows, value_rows, key_live, score_scale)

    per_head = jax.vmap(one_head, in_axes=(0, 0, 0, 0, None))
    outputs, d_query, d_key, d_value = jax.vmap(per_head)(
        query_heads, grad_heads, key_heads, value_heads, live_keys
    )

    def back_to_sources(tensor_block, row_count):
        arranged = tensor_block.transpose(0, 2, 1, 3).reshape(
            samples, groups, row_count, band_width
        )
        return arranged.transpose(1, 0, 2, 3)

    query_send = back_to_sources(d_query, part_rows).astype(jnp.bfloat16)
    back_out, back_query = (
        lax.all_to_all(
            back_to_sources(outputs, part_rows), "seq", split_axis=0, concat_axis=0, tiled=True
        ),
        lax.all_to_all(query_send, "seq", split_axis=0, concat_axis=0, tiled=True),
    )
    key_value_grad = jnp.concatenate(
        [back_to_sources(d_key, slot_count), back_to_sources(d_value, slot_count)], axis=3
    )
    back_pair = lax.all_to_all(
        key_value_grad.astype(jnp.bfloat16), "seq", split_axis=0, concat_axis=0, tiled=True
    ).astype(key_value_grad.dtype)

    def from_owners(tensor_block):
        arranged = tensor_block.reshape(head_groups, splits, samples, part_rows, band_width)
        return arranged.transpose(2, 1, 3, 0, 4).reshape(samples, slot_count, model_width)

    attended = from_owners(back_out)
    summed_pair = jnp.sum(
        back_pair.reshape(head_groups, splits, samples, slot_count, 2 * band_width), axis=1
    )
    summed_pair = summed_pair.transpose(1, 2, 0, 3)
    key_grad_rows = (
        summed_pair[..., :band_width].reshape(samples, slot_count, model_width).astype(jnp.bfloat16)
    )
    value_grad_rows = (
        summed_pair[..., band_width:].reshape(samples, slot_count, model_width).astype(jnp.bfloat16)
    )
    d_packed = jnp.concatenate([from_owners(back_query), key_grad_rows, value_grad_rows], axis=2)
    flat_attended = attended.reshape(samples * slot_count, model_width)
    projected = jnp.dot(flat_attended, w_out, preferred_element_type=jnp.float32).reshape(
        samples, slot_count, model_width
    )
    encoded = jnp.where(live_slots[:, :, None], hidden + projected, 0.0).astype(jnp.bfloat16)
    flat_packed = d_packed.reshape(samples * slot_count, 3 * model_width)
    d_normed = jnp.dot(flat_packed, w_qkv.T, preferred_element_type=jnp.float32).reshape(
        samples, slot_count, model_width
    )
    d_hidden = norm_backward(d_normed, gain, unit_rows, inv_std)
    d_patches = jnp.where(
        live_slots[:, :, None], live_grad.astype(jnp.float32) + d_hidden, 0.0
    ).astype(jnp.bfloat16)
    columns = flat_grad
    out_part = lax.psum_scatter(
        jnp.dot(columns.T, flat_attended, preferred_element_type=jnp.float32),
        "seq",
        scatter_dimension=0,
        tiled=True,
    ).T
    my_columns = lax.all_to_all(flat_packed, "seq", split_axis=1, concat_axis=0, tiled=True)
    columns = my_columns
    qkv_part = jnp.dot(
        lax.all_gather(flat_normed, "seq", axis=0, tiled=True).T,
        columns,
        preferred_element_type=jnp.float32,
    )
    qkv_grad, out_grad = lax.psum((qkv_part, out_part), "rep")
    return (encoded, d_patches, qkv_grad, out_grad)


AXES = ("seq", "rep")
MARK = 1024.0
MIB = 1024 * 1024


def line_perm(move, reps):
    pairs = []
    for z in range(4):
        for rep in range(reps):
            x, c = rep // 2, rep % 2
            to_x, to_c, to_z = move(x, c, z)
            pairs.append((z * reps + rep, to_z * reps + 2 * to_x + to_c))
    return pairs


def sine_cosine(phase):
    turns = jnp.floor(phase * np.float32(2.0 / np.pi) + 0.5)
    rest = phase - turns * np.float32(1.5703125)
    rest = rest - turns * np.float32(4.837512969970703125e-4)
    rest = rest - turns * np.float32(7.54978995489188216e-8)
    square = rest * rest
    sine = rest + rest * square * (
        np.float32(-1.6666654611e-1)
        + square * (np.float32(8.3321608736e-3) + square * np.float32(-1.9515295891e-4))
    )
    cosine = (
        1.0
        - 0.5 * square
        + square
        * square
        * (
            np.float32(4.166664568298827e-2)
            + square * (np.float32(-1.388731625493765e-3) + square * np.float32(2.443315711809948e-5))
        )
    )
    quadrant = turns.astype(jnp.int32) & 3
    swap = (quadrant & 1) == 1
    first = jnp.where(swap, cosine, sine)
    second = jnp.where(swap, sine, cosine)
    first = jnp.where(quadrant >= 2, -first, first)
    second = jnp.where((quadrant == 1) | (quadrant == 2), -second, second)
    return first, second


def live_column(count, rows):
    return lax.broadcasted_iota(jnp.int32, (rows, 1), 0) < count


def dot_nn(a, b):
    return jnp.dot(a, b, preferred_element_type=jnp.float32)


def dot_nt(a, b):
    return lax.dot_general(a, b, (((1,), (1,)), ((), ())), preferred_element_type=jnp.float32)


PAR, CORE, LINE, SIDE, KEPT = range(5)


def load_weights(core, w_in_hbm, w_out_hbm, wq, wk, wv, wo, sems):
    width = w_out_hbm.shape[0]
    copies = []
    for j in range(wq.shape[1] // 128):
        to = pl.ds(128 * j, 128)
        row = pl.multiple_of(256 * j + 128 * core, 128)
        pairs = [(w_out_hbm.at[pl.ds(row, 128), :], wo.at[to, :])]
        for t, out in enumerate((wq, wk, wv)):
            at = pl.multiple_of(t * width + row, 128)
            pairs.append((w_in_hbm.at[:, pl.ds(at, 128)], out.at[:, to]))
        copies += [pltpu.make_async_copy(a, b, sems.at[4 * j + i]) for i, (a, b) in enumerate(pairs)]
    for copy in copies:
        copy.start()
    return copies


def norm_kernel(
    place, patch_hbm, cot_hbm, index_hbm, gain_hbm, w_in_hbm, w_out_hbm,
    p0_ref, p1_ref, hidden_ref, wq, wk, wv, wo,
    patch_ref, cot_ref, index_ref, gain_ref, sems, w_sems,
):
    par = place[PAR]
    rows, width = patch_ref.shape[1:]
    quarter = width // 4
    copies = [
        pltpu.make_async_copy(src, dst, sems.at[i])
        for i, (src, dst) in enumerate(
            ((index_hbm, index_ref), (patch_hbm, patch_ref), (gain_hbm, gain_ref), (cot_hbm, cot_ref))
        )
    ]
    for copy in copies:
        copy.start()
    staged = load_weights(place[CORE], w_in_hbm, w_out_hbm, wq, wk, wv, wo, w_sems)
    order = lax.broadcasted_iota(jnp.int32, (1, quarter), 1).astype(jnp.float32)
    freq = jnp.exp(-np.log(np.float32(10000.0)) * order / quarter)
    diagonal = lax.broadcasted_iota(jnp.int32, (rows, rows), 0) == lax.broadcasted_iota(
        jnp.int32, (rows, rows), 1
    )
    copies[0].wait()
    tables = []
    for k in range(2):
        position = index_ref[pl.ds(k ^ par, 1), :]
        grid_row = (position // GRID_COLS).astype(jnp.float32)
        grid_col = (position % GRID_COLS).astype(jnp.float32)
        grid_row = jnp.sum(jnp.where(diagonal, grid_row, 0.0), axis=1, keepdims=True)
        grid_col = jnp.sum(jnp.where(diagonal, grid_col, 0.0), axis=1, keepdims=True)
        pieces = sine_cosine(grid_row * freq) + sine_cosine(grid_col * freq)
        tables.append(jnp.concatenate(pieces, axis=1))
    copies[1].wait()
    copies[2].wait()
    for k, out_ref in enumerate((p0_ref, p1_ref)):
        s = k ^ par
        hidden = patch_ref[s].astype(jnp.float32) + tables[k]
        hidden_ref[k] = hidden
        center = hidden - jnp.mean(hidden, axis=-1, keepdims=True)
        spread = jnp.mean(center * center, axis=-1, keepdims=True)
        normed = center * lax.rsqrt(spread + epsilon) * gain_ref[...]
        live = live_column(place[KEPT + s], rows)
        out_ref[:rows, :] = jnp.where(live, normed, MARK).astype(out_ref.dtype)
    copies[3].wait()
    for k, out_ref in enumerate((p0_ref, p1_ref)):
        s = k ^ par
        live = live_column(place[KEPT + s], rows)
        grad = cot_ref[s]
        out_ref[rows:, :] = jnp.where(live, grad, jnp.zeros_like(grad))
    for copy in staged:
        copy.wait()


def attend_pairs(
    place, first_pair, payloads, wq, wk, wv, wo, own, oth, keep_t, out_keep, send, norm_s, grad_s, att_s,
):
    block = payloads[0].shape[0] // 2
    rows = 4 * block
    half = 2 * block
    biases = []
    for i, ref in enumerate(payloads):
        at = slice(i * block, (i + 1) * block)
        value = ref[:block, :]
        live = value[:, 0:1].astype(jnp.float32) < MARK
        norm_s[at, :] = jnp.where(live, value, jnp.zeros_like(value))
        grad_s[at, :] = ref[block:, :]
        biases.append(jnp.where(live, 0.0, -1e30))
    bias = jnp.concatenate(biases, axis=0)
    low = lax.broadcasted_iota(jnp.int32, (rows, 128), 1) < 64
    scale = jnp.bfloat16(0.125)
    zero = jnp.zeros((rows, 128), jnp.bfloat16)
    first = place[SIDE] == 0
    count = own.shape[2] // 128
    here = slice(128 * first_pair, 128 * (first_pair + count))
    normed = norm_s[...]
    queries = dot_nn(normed, wq[:, here]).astype(jnp.bfloat16)
    keys = dot_nn(normed, wk[:, here]).astype(jnp.bfloat16)
    values = dot_nn(normed, wv[:, here]).astype(jnp.bfloat16)
    d_att = dot_nt(grad_s[...], wo[here, :]).astype(jnp.bfloat16)
    for j in range(count):
        cols = slice(128 * j, 128 * j + 128)
        q = queries[:, cols] * scale
        k = keys[:, cols]
        v = values[:, cols]
        g = d_att[:, cols]
        v_t = v.T
        k_t = (k * scale).T
        att_t, dq_t, dk, dv = [], [], [], []
        for h in range(2):
            mine = low if h == 0 else jnp.logical_not(low)
            scores = dot_nt(k, jnp.where(mine, q, zero)) + bias
            raised = jnp.exp(scores - jnp.max(scores, axis=0, keepdims=True))
            prob = raised * (1.0 / jnp.sum(raised, axis=0, keepdims=True))
            weights = prob.astype(jnp.bfloat16)
            part = slice(64 * h, 64 * h + 64)
            att_t.append(dot_nn(v_t[part], weights))
            dv.append(dot_nn(weights, g))
            d_prob = dot_nt(v, jnp.where(mine, g, zero))
            total = jnp.sum(prob * d_prob, axis=0, keepdims=True)
            d_score = (prob * (d_prob - total)).astype(jnp.bfloat16)
            dq_t.append(dot_nn(k_t[part], d_score))
            dk.append(dot_nn(d_score, q))
        att_pair_t = jnp.concatenate(att_t, axis=0).astype(jnp.bfloat16)
        dq_pair_t = jnp.concatenate(dq_t, axis=0).astype(jnp.bfloat16)
        dk_pair = jnp.where(low, dk[0], dk[1]).astype(jnp.bfloat16)
        dv_pair = jnp.where(low, dv[0], dv[1]).astype(jnp.bfloat16)
        for t, piece in enumerate((dq_pair_t.T, dk_pair, dv_pair, att_pair_t.T)):
            own[t, :, cols] = piece[:half]
            oth[t, :, cols] = piece[half:]
        for t, piece in enumerate((dq_pair_t, dk_pair.T, dv_pair.T)):
            at = slice(64 * j, 64 * j + 64)
            part = slice(rows * t, rows * t + rows)
            keep_t[at, part] = jnp.where(first, piece[:64], piece[64:])
            send[at, part] = jnp.where(first, piece[64:], piece[:64])
        at = slice(64 * j, 64 * j + 64)
        att_s[0, at, :] = jnp.where(first, att_pair_t[:64], att_pair_t[64:])
        att_s[1, at, :] = jnp.where(first, att_pair_t[64:], att_pair_t[:64])
    out_keep[...] = dot_nn(att_s[0], grad_s[...])
    send[:, 3 * rows :] = dot_nn(att_s[1], grad_s[...]).astype(send.dtype)


def attend_first(place, p0, p1, p2, p3, *refs):
    attend_pairs(place, 0, (p0, p1, p2, p3), *refs)


def attend_second(place, p0, p1, p2, p3, wq, wk, wv, wo, after, *refs):
    del after
    attend_pairs(place, 2, (p0, p1, p2, p3), wq, wk, wv, wo, *refs)


def in_order(place, own, got):
    pieces = []
    low = place == 0
    for j in range(own.shape[1] // 128):
        a, b = own[:, 128 * j : 128 * j + 128], got[:, 128 * j : 128 * j + 128]
        pieces += [jnp.where(low, a, b), jnp.where(low, b, a)]
    return jnp.concatenate(pieces, axis=1)


def rows_kernel(place, own_a, got_a, own_b, got_b, w_ref, w_out_ref, after, before, o0, o1, total):
    del after, before
    step = pl.program_id(0)
    core = place[CORE]
    block = o0.shape[0] // 2

    def rows_of(t):
        return jnp.concatenate([in_order(core, own_a[t], got_a[t]), in_order(core, own_b[t], got_b[t])], axis=1)

    term = dot_nt(rows_of(step), w_ref[...])

    @pl.when(step == 0)
    def _():
        total[...] = term
        projected = dot_nn(rows_of(3), w_out_ref[...]).astype(o0.dtype)
        o0[:block, :] = projected[:block]
        o1[:block, :] = projected[block:]

    @pl.when(step > 0)
    def _():
        total[...] += term

    @pl.when(step == pl.num_programs(0) - 1)
    def _():
        o0[block:, :] = total[:block].astype(o0.dtype)
        o1[block:, :] = total[block:].astype(o1.dtype)


def return_kernel(place, r0, r1, hidden_ref, m0, m1, gain_ref, after, encoded, d_patches):
    del after
    par = place[PAR]
    rows = r0.shape[0] // 2
    for k, (r_ref, m_ref) in enumerate(((r0, m0), (r1, m1))):
        s = k ^ par
        live = live_column(place[KEPT + s], rows)
        hidden = hidden_ref[k]
        projected = r_ref[:rows, :].astype(jnp.float32)
        encoded[s] = jnp.where(live, hidden + projected, 0.0).astype(encoded.dtype)
        center = hidden - jnp.mean(hidden, axis=-1, keepdims=True)
        spread = jnp.mean(center * center, axis=-1, keepdims=True)
        inv_std = lax.rsqrt(spread + epsilon)
        unit = center * inv_std
        d_hidden = norm_backward(r_ref[rows:, :].astype(jnp.float32), gain_ref[...], unit, inv_std)
        value = m_ref[rows:, :].astype(jnp.float32) + d_hidden
        d_patches[s] = jnp.where(live, value, 0.0).astype(d_patches.dtype)


def put_parts(place, total, out_keep, got, keep, send, out_total):
    out_total[...] = out_keep[...] + got[:, got.shape[1] - out_total.shape[1] :].astype(jnp.float32)
    columns = out_total.shape[1] // 4
    tall = out_total.shape[0] // 4
    count = total.shape[0] // 4
    for k in range(4):
        ref, spot = (keep, send)[k % 2], k // 2
        at = pl.multiple_of((place[LINE] ^ k) * count, 64)
        ref[spot, :count, :] = total[pl.ds(at, count), :].astype(ref.dtype)
        at = pl.multiple_of((place[LINE] ^ k) * columns, 128)
        value = out_total[:, pl.ds(at, columns)].astype(ref.dtype)
        for j in range(4):
            ref[spot, count:, columns * j : columns * j + columns] = value[tall * j : tall * j + tall, :]


def piece_of(ref, at, rows):
    t, j = at // 2, at % 2
    return ref[64 * j : 64 * j + 64, rows * t : rows * t + rows]


def weight_first(
    place, keep, out_keep, got, p0, p1, p2, p3, n0, n1,
    part_keep, part_send, tokens, left, total, out_total,
):
    block = p0.shape[0] // 2
    rows = 4 * block
    for i, ref in enumerate((p0, p1, p2, p3)):
        tokens[i * block : (i + 1) * block, :] = ref[:block, :]
    tokens[rows : rows + 2 * block, :] = n0[...]
    tokens[rows + 2 * block :, :] = n1[...]
    for side, ref in enumerate((keep, got)):
        for i, at in enumerate((0, 2, 4, 5)):
            left[side, 64 * i : 64 * i + 64, :] = piece_of(ref, at, rows)
    total[...] = dot_nn(left[0], tokens[:rows, :]) + dot_nn(left[1], tokens[rows:, :])
    put_parts(place, total, out_keep, got, part_keep, part_send, out_total)


def weight_second(
    place, keep_a, got_a, keep_b, out_keep, got_b, p0, p1, p2, p3, n0, n1, after,
    part_keep, part_send, tokens, left, total, out_total,
):
    del after
    block = p0.shape[0] // 2
    rows = 4 * block
    for i, ref in enumerate((p0, p1, p2, p3)):
        tokens[i * block : (i + 1) * block, :] = ref[:block, :]
    tokens[rows : rows + 2 * block, :] = n0[...]
    tokens[rows + 2 * block :, :] = n1[...]
    for side, (a, b) in enumerate(((keep_a, keep_b), (got_a, got_b))):
        for i, (ref, at) in enumerate(
            ((a, 1), (b, 0), (b, 1), (a, 3), (b, 2), (b, 3), (b, 4), (b, 5))
        ):
            left[side, 64 * i : 64 * i + 64, :] = piece_of(ref, at, rows)
    total[...] = dot_nn(left[0], tokens[:rows, :]) + dot_nn(left[1], tokens[rows:, :])
    put_parts(place, total, out_keep, got_b, part_keep, part_send, out_total)


def pair_kernel(keep, got, mine, send):
    mine[...] = keep[0] + got[0].astype(jnp.float32)
    send[...] = (keep[1] + got[1].astype(jnp.float32)).astype(send.dtype)


def sum_kernel(mine, got, *refs):
    out = refs[-1]
    out[...] = (mine[...] + got[...].astype(jnp.float32)).astype(out.dtype)


def finish_kernel(place, a0, a1, a2, a3, b0, b1, b2, b3, wide, narrow):
    core_low, side_low = place[CORE] == 0, place[SIDE] == 0
    slab = place[LINE]
    columns = narrow.shape[1]
    spot = jnp.where(slab == 3, 0, slab)
    spots = (spot, jnp.where(spot == 0, 1, 0), jnp.where(spot == 2, 1, 2))

    def pick(refs, c, x, at, part):
        own, by_x, by_core, by_both = refs
        near = jnp.where(side_low == (x == 0), own[at, part], by_x[at, part])
        far = jnp.where(side_low == (x == 0), by_core[at, part], by_both[at, part])
        return jnp.where(core_low == (c == 0), near, far)

    every = slice(None)
    first, second = (a0, a1, a2, a3), (b0, b1, b2, b3)
    for c in range(2):
        for i, (refs, row) in enumerate(((first, 0), (second, 0), (second, 64))):
            at = slice(row, row + 64)
            both = jnp.concatenate([pick(refs, c, x, at, every) for x in range(2)], axis=0)
            col = pl.multiple_of(128 * (2 * spots[i] + c), 128)
            wide[:, pl.ds(col, 128)] = both.T.astype(wide.dtype)
        for half, (refs, base) in enumerate(((first, 64), (second, 128))):
            for j in range(4):
                at = slice(base, base + 32)
                part = slice(columns * j, columns * j + columns)
                for x in range(2):
                    pair, row = 2 * half + j // 2, 32 * (j % 2)
                    row += 128 * (2 * pair + c) + 64 * x
                    narrow[row : row + 32, :] = pick(refs, c, x, at, part).astype(narrow.dtype)


SMEM_SPEC = pl.BlockSpec(memory_space=pltpu.SMEM)
VMEM_SPEC = pl.BlockSpec(memory_space=pltpu.VMEM)


def struct(shape, dtype=jnp.bfloat16):
    return jax.ShapeDtypeStruct(shape, dtype)


COST = pl.CostEstimate(flops=1000, bytes_accessed=1000, transcendentals=0)


def in_hbm(value):
    return pltpu.with_memory_space_constraint(value, pltpu.HBM)


def call(kernel, args, outs, limit, place=None, scratch=(), specs=None):
    specs = specs or [VMEM_SPEC] * len(args)
    if place is not None:
        args, specs = (place, *args), [SMEM_SPEC] + specs
    single = not isinstance(outs, list)
    return pl.pallas_call(
        kernel,
        in_specs=specs,
        out_specs=VMEM_SPEC if single else [VMEM_SPEC] * len(outs),
        out_shape=outs,
        scratch_shapes=list(scratch),
        compiler_params=pltpu.CompilerParams(vmem_limit_bytes=limit * MIB),
        cost_estimate=COST,
    )(*args)


def chip_shards(patches, kept_index, kept_count, cotangent, w_qkv, w_out, gain):
    bf16, f32 = jnp.bfloat16, jnp.float32
    samples, slots, width = patches.shape
    reps = lax.axis_size("rep")
    rep = lax.axis_index("rep")
    z = lax.axis_index("seq")
    core, x = rep & 1, rep >> 1
    place = jnp.concatenate(
        [jnp.stack([z & 1, core, z, x]).astype(jnp.int32), kept_count.reshape(samples)]
    )
    own_width = width // 2
    quarter = width // 4
    rows = 4 * slots

    def send(value, move):
        return lax.ppermute(value, AXES, line_perm(move, reps))

    def to_core(value):
        return send(value, lambda x, c, z: (x, 1 - c, z))

    def to_x(value):
        return send(value, lambda x, c, z: (1 - x, c, z))

    def to_chip(value, k):
        return send(value, lambda x, c, z: (x, z >> 1, 2 * c + (k ^ (z & 1))))

    def to_rows(value, k, other):
        return send(value, lambda x, c, z: (x, z >> 1, 2 * (c ^ other) + (k ^ (z & 1))))

    def along(value, k):
        return send(value, lambda x, c, z: (x, c, z ^ k))

    gain_row = gain.reshape(1, width)
    pay = struct((2 * slots, width))
    hbm = pl.BlockSpec(memory_space=pl.ANY)
    any_spec = pl.BlockSpec(memory_space=pl.ANY)
    pairs = width // 512
    own_w = [struct((width, own_width))] * 3 + [struct((own_width, width))]
    *outs, wq, wk, wv, wo = call(
        norm_kernel,
        tuple(in_hbm(v) for v in (patches, cotangent, kept_index, gain_row, w_qkv, w_out)),
        [pay, pay, struct(patches.shape, f32)] + own_w,
        24,
        place,
        scratch=[
            pltpu.VMEM(patches.shape, bf16),
            pltpu.VMEM(patches.shape, bf16),
            pltpu.VMEM(kept_index.shape, jnp.int32),
            pltpu.VMEM(gain_row.shape, f32),
            pltpu.SemaphoreType.DMA((4,)),
            pltpu.SemaphoreType.DMA((8 * pairs,)),
        ],
        specs=[any_spec] * 6,
    )
    *mine, hidden = outs
    got = [to_chip(mine[k], k) for k in range(2)]
    here = got + [to_core(v) for v in got]
    from_x = to_x(jnp.concatenate([v[:slots] for v in got], axis=0))
    there = (from_x, to_core(from_x))

    half_rows = struct((4, 2 * slots, 128 * pairs))
    out_half = (64 * pairs, width)
    half_t = struct((64 * pairs, 3 * rows))
    half_send = struct((64 * pairs, 3 * rows + width))

    staged = (wq, wk, wv, wo)

    def attend(kernel, after):
        return call(
            kernel,
            (*here, *staged, *after),
            [half_rows] * 2 + [half_t, struct(out_half, f32), half_send],
            32,
            place,
            scratch=[pltpu.VMEM((rows, width), bf16)] * 2 + [pltpu.VMEM((2, 64 * pairs, rows), bf16)],
            specs=[VMEM_SPEC] * 8 + [any_spec] * len(after),
        )

    own_a, oth_a, keep_a, out_keep_a, send_a = attend(attend_first, ())
    got_a = to_x(send_a)
    core_a = to_core(oth_a)
    own_b, oth_b, keep_b, out_keep_b, send_b = attend(attend_second, (from_x,))
    got_b = to_x(send_b)
    core_b = to_core(oth_b)

    def parts_of(kernel, args, tall, scratch, after=()):
        return call(
            kernel,
            (*args, *here, *there, *after),
            [struct((2, tall, width), f32), struct((2, tall, width))],
            16,
            place,
            scratch=[pltpu.VMEM((2 * rows, width), bf16)] + scratch + [pltpu.VMEM(out_half, f32)],
            specs=[VMEM_SPEC] * (len(args) + 6) + [any_spec] * len(after),
        )

    def pair_sums(keep, part):
        shape = keep.shape[1:]
        mine, part = call(pair_kernel, (keep, along(part, 1)), [struct(shape, f32), struct(shape)], 8)
        return mine, part, along(part, 2)

    def spread(mine, part, after=()):
        sums = call(
            sum_kernel,
            (mine, part, *after),
            struct(part.shape),
            8,
            specs=[VMEM_SPEC] * 2 + [any_spec] * len(after),
        )
        by_x = to_x(sums)
        return (sums, by_x, to_core(sums), to_core(by_x))

    keep, part = parts_of(
        weight_first,
        (keep_a, out_keep_a, got_a),
        96,
        [pltpu.VMEM((2, 256, rows), bf16), pltpu.VMEM((256, width), f32)],
    )
    first_sum, paired, first_got = pair_sums(keep, part)
    keep, part = parts_of(
        weight_second,
        (keep_a, got_a, keep_b, out_keep_b, got_b),
        160,
        [pltpu.VMEM((2, 512, rows), bf16), pltpu.VMEM((512, width), f32)],
        (paired,),
    )
    started = part
    second_sum, _, second_got = pair_sums(keep, part)
    first = spread(first_sum, first_got)
    whole_w = pl.BlockSpec((width, width), lambda i, p: (0, 0))
    back = pl.pallas_call(
        rows_kernel,
        grid_spec=pltpu.PrefetchScalarGridSpec(
            num_scalar_prefetch=1,
            grid=(3,),
            in_specs=[pl.BlockSpec(half_rows.shape, lambda i, p: (0, 0, 0))] * 4
            + [pl.BlockSpec((width, width), lambda i, p: (0, i)), whole_w, any_spec, any_spec],
            out_specs=[pl.BlockSpec(pay.shape, lambda i, p: (0, 0))] * 2,
            scratch_shapes=[pltpu.VMEM((2 * slots, width), f32)],
        ),
        out_shape=[pay] * 2,
        compiler_params=pltpu.CompilerParams(vmem_limit_bytes=20 * MIB),
        cost_estimate=COST,
    )(place, own_a, core_a, own_b, core_b, in_hbm(w_qkv), in_hbm(w_out), started, first[1])
    second = spread(second_sum, second_got, (back[0], *first[1:]))
    back = [to_rows(back[k], k, 0) for k in range(2)]
    qkv_grad, out_grad = call(
        finish_kernel,
        (*first, *second),
        [struct((width, 3 * quarter), f32), struct((width, quarter), f32)],
        12,
        place,
    )
    encoded, d_patches = call(
        return_kernel,
        (*back, hidden, *mine, gain_row, qkv_grad),
        [struct(patches.shape)] * 2,
        12,
        place,
        specs=[VMEM_SPEC] * 6 + [any_spec],
    )
    return (encoded, d_patches, qkv_grad, out_grad)


def solution(mesh):
    in_specs = (
        P(("grp", "rep"), "seq", None),
        P(("grp", "rep"), "seq"),
        P(("grp", "rep"), "seq"),
        P(("grp", "rep"), "seq", None),
        P(),
        P(),
        P(),
    )
    out_specs = (
        P(("grp", "rep"), "seq", None),
        P(("grp", "rep"), "seq", None),
        P("grp", "seq"),
        P("grp", "seq"),
    )
    chips = mesh.shape["seq"] == 4 and mesh.shape["rep"] % 2 == 0 and HEADS % 8 == 0

    def run(patches, *rest):
        per_device = patches.shape[0] // (mesh.shape["grp"] * mesh.shape["rep"])
        body = chip_shards if chips and per_device == 2 else shards
        inner = jax.shard_map(body, mesh=mesh, in_specs=in_specs, out_specs=out_specs, check_vma=False)
        return inner(patches, *rest)

    return run
```

```python
import functools

import jax
import jax.numpy as jnp
import numpy as np
from jax import lax
from jax.experimental import pallas as pl
from jax.experimental.pallas import tpu as pltpu
from jax.sharding import PartitionSpec as P

HEADS = 16
GRID_COLS = 512


epsilon = 1e-06


def position_table(position, model_width):
    quarter = model_width // 4
    frequency = jnp.exp(-jnp.log(10000.0) * jnp.arange(quarter, dtype=jnp.float32) / quarter)
    grid_row = (position // GRID_COLS).astype(jnp.float32)
    grid_col = (position % GRID_COLS).astype(jnp.float32)
    row_phase = grid_row[..., None] * frequency
    col_phase = grid_col[..., None] * frequency
    return jnp.concatenate(
        [jnp.sin(row_phase), jnp.cos(row_phase), jnp.sin(col_phase), jnp.cos(col_phase)], axis=-1
    )


def normalize(hidden, gain):
    center = hidden - jnp.mean(hidden, axis=-1, keepdims=True)
    spread = jnp.mean(center * center, axis=-1, keepdims=True)
    inv_std = lax.rsqrt(spread + epsilon)
    unit_rows = center * inv_std
    return ((unit_rows * gain).astype(jnp.bfloat16), unit_rows, inv_std)


def norm_backward(d_normed, gain, unit_rows, inv_std):
    scaled = d_normed * gain
    return inv_std * (
        scaled
        - jnp.mean(scaled, axis=-1, keepdims=True)
        - unit_rows * jnp.mean(scaled * unit_rows, axis=-1, keepdims=True)
    )


def head_block(query_rows, grad_rows, key_rows, value_rows, live_keys, score_scale):
    scores = jnp.dot(query_rows, key_rows.T, preferred_element_type=jnp.float32) * score_scale
    scores = jnp.where(live_keys[None, :], scores, -1e30)
    top_score = jnp.max(scores, axis=1, keepdims=True)
    raised = jnp.exp(scores - top_score)
    probability = raised / jnp.sum(raised, axis=1, keepdims=True)
    rounded = probability.astype(jnp.bfloat16)
    attended = jnp.dot(rounded, value_rows, preferred_element_type=jnp.float32).astype(jnp.bfloat16)
    d_value = jnp.dot(rounded.T, grad_rows, preferred_element_type=jnp.float32)
    d_prob = jnp.dot(grad_rows, value_rows.T, preferred_element_type=jnp.float32)
    d_score = (
        probability * (d_prob - jnp.sum(probability * d_prob, axis=1, keepdims=True)) * score_scale
    ).astype(jnp.bfloat16)
    d_query = jnp.dot(d_score, key_rows, preferred_element_type=jnp.float32)
    d_key = jnp.dot(d_score.T, query_rows, preferred_element_type=jnp.float32)
    return (attended, d_query, d_key, d_value)


def attend(query_rows, grad_rows, key_rows, value_rows, live_keys, score_scale):
    row_count = query_rows.shape[0]
    blocks = max(1, row_count // 512)
    while row_count % blocks:
        blocks -= 1
    block_rows = row_count // blocks
    query_blocks = query_rows.reshape(blocks, block_rows, query_rows.shape[1])
    grad_blocks = grad_rows.reshape(blocks, block_rows, grad_rows.shape[1])

    def block_step(carry, pieces):
        key_total, value_total = carry
        attended, d_query, d_key, d_value = head_block(
            pieces[0], pieces[1], key_rows, value_rows, live_keys, score_scale
        )
        return ((key_total + d_key, value_total + d_value), (attended, d_query))

    empty = jnp.zeros(key_rows.shape, jnp.float32)
    (key_total, value_total), (attended, d_query) = lax.scan(
        block_step, (empty, empty), (query_blocks, grad_blocks)
    )
    return (attended.reshape(row_count, -1), d_query.reshape(row_count, -1), key_total, value_total)


def shards(patches, kept_index, kept_count, cotangent, w_qkv, w_out, gain):
    groups = lax.axis_size("seq")
    samples, slot_count, model_width = patches.shape
    head_size = model_width // HEADS
    per_device = max(1, HEADS // groups)
    splits = max(1, groups // HEADS)
    head_groups = groups // splits
    band_width = per_device * head_size
    part_rows = slot_count // splits
    slot_ids = jnp.arange(slot_count, dtype=jnp.int32)
    live_slots = slot_ids[None, :] < kept_count
    hidden = patches.astype(jnp.float32) + position_table(kept_index, model_width)
    normed, unit_rows, inv_std = normalize(hidden, gain)
    flat_normed = normed.reshape(samples * slot_count, model_width)
    packed = jnp.dot(flat_normed, w_qkv, preferred_element_type=jnp.float32).astype(jnp.bfloat16)
    packed = packed.reshape(samples, slot_count, 3 * model_width)
    live_grad = jnp.where(live_slots[:, :, None], cotangent, jnp.zeros_like(cotangent))
    flat_grad = live_grad.reshape(samples * slot_count, model_width)
    d_attended = jnp.dot(flat_grad, w_out.T, preferred_element_type=jnp.float32).astype(
        jnp.bfloat16
    )
    d_attended = d_attended.reshape(samples, slot_count, model_width)

    def to_owners(tensor_block):
        arranged = tensor_block.reshape(samples, splits, part_rows, head_groups, band_width)
        return arranged.transpose(3, 1, 0, 2, 4).reshape(groups, samples, part_rows, band_width)

    key_value_send = jnp.concatenate(
        [
            packed[:, :, model_width : 2 * model_width].reshape(
                samples, slot_count, head_groups, band_width
            ),
            packed[:, :, 2 * model_width :].reshape(samples, slot_count, head_groups, band_width),
        ],
        axis=3,
    )
    key_value_send = key_value_send.transpose(2, 0, 1, 3)
    key_value_send = jnp.broadcast_to(
        key_value_send[:, None], (head_groups, splits, samples, slot_count, 2 * band_width)
    )
    key_value_send = key_value_send.reshape(groups, samples, slot_count, 2 * band_width)
    got_query, got_grad, got_pair = (
        lax.all_to_all(
            to_owners(packed[:, :, :model_width]), "seq", split_axis=0, concat_axis=0, tiled=True
        ),
        lax.all_to_all(to_owners(d_attended), "seq", split_axis=0, concat_axis=0, tiled=True),
        lax.all_to_all(key_value_send, "seq", split_axis=0, concat_axis=0, tiled=True),
    )
    all_counts = lax.all_gather(kept_count, "seq", axis=1, tiled=True)
    live_keys = (slot_ids[None, None, :] < all_counts[:, :, None]).reshape(
        samples, groups * slot_count
    )

    def rows_by_head(tensor_block, row_count):
        arranged = tensor_block.transpose(1, 0, 2, 3).reshape(
            samples, groups * row_count, per_device, head_size
        )
        return arranged.transpose(0, 2, 1, 3)

    query_heads = rows_by_head(got_query, part_rows)
    grad_heads = rows_by_head(got_grad, part_rows)
    key_heads = rows_by_head(got_pair[..., :band_width], slot_count)
    value_heads = rows_by_head(got_pair[..., band_width:], slot_count)
    score_scale = head_size ** (-0.5)

    def one_head(query_rows, grad_rows, key_rows, value_rows, key_live):
        return attend(query_rows, grad_rows, key_rows, value_rows, key_live, score_scale)

    per_head = jax.vmap(one_head, in_axes=(0, 0, 0, 0, None))
    outputs, d_query, d_key, d_value = jax.vmap(per_head)(
        query_heads, grad_heads, key_heads, value_heads, live_keys
    )

    def back_to_sources(tensor_block, row_count):
        arranged = tensor_block.transpose(0, 2, 1, 3).reshape(
            samples, groups, row_count, band_width
        )
        return arranged.transpose(1, 0, 2, 3)

    query_send = back_to_sources(d_query, part_rows).astype(jnp.bfloat16)
    back_out, back_query = (
        lax.all_to_all(
            back_to_sources(outputs, part_rows), "seq", split_axis=0, concat_axis=0, tiled=True
        ),
        lax.all_to_all(query_send, "seq", split_axis=0, concat_axis=0, tiled=True),
    )
    key_value_grad = jnp.concatenate(
        [back_to_sources(d_key, slot_count), back_to_sources(d_value, slot_count)], axis=3
    )
    back_pair = lax.all_to_all(
        key_value_grad.astype(jnp.bfloat16), "seq", split_axis=0, concat_axis=0, tiled=True
    ).astype(key_value_grad.dtype)

    def from_owners(tensor_block):
        arranged = tensor_block.reshape(head_groups, splits, samples, part_rows, band_width)
        return arranged.transpose(2, 1, 3, 0, 4).reshape(samples, slot_count, model_width)

    attended = from_owners(back_out)
    summed_pair = jnp.sum(
        back_pair.reshape(head_groups, splits, samples, slot_count, 2 * band_width), axis=1
    )
    summed_pair = summed_pair.transpose(1, 2, 0, 3)
    key_grad_rows = (
        summed_pair[..., :band_width].reshape(samples, slot_count, model_width).astype(jnp.bfloat16)
    )
    value_grad_rows = (
        summed_pair[..., band_width:].reshape(samples, slot_count, model_width).astype(jnp.bfloat16)
    )
    d_packed = jnp.concatenate([from_owners(back_query), key_grad_rows, value_grad_rows], axis=2)
    flat_attended = attended.reshape(samples * slot_count, model_width)
    projected = jnp.dot(flat_attended, w_out, preferred_element_type=jnp.float32).reshape(
        samples, slot_count, model_width
    )
    encoded = jnp.where(live_slots[:, :, None], hidden + projected, 0.0).astype(jnp.bfloat16)
    flat_packed = d_packed.reshape(samples * slot_count, 3 * model_width)
    d_normed = jnp.dot(flat_packed, w_qkv.T, preferred_element_type=jnp.float32).reshape(
        samples, slot_count, model_width
    )
    d_hidden = norm_backward(d_normed, gain, unit_rows, inv_std)
    d_patches = jnp.where(
        live_slots[:, :, None], live_grad.astype(jnp.float32) + d_hidden, 0.0
    ).astype(jnp.bfloat16)
    columns = flat_grad
    out_part = lax.psum_scatter(
        jnp.dot(columns.T, flat_attended, preferred_element_type=jnp.float32),
        "seq",
        scatter_dimension=0,
        tiled=True,
    ).T
    my_columns = lax.all_to_all(flat_packed, "seq", split_axis=1, concat_axis=0, tiled=True)
    columns = my_columns
    qkv_part = jnp.dot(
        lax.all_gather(flat_normed, "seq", axis=0, tiled=True).T,
        columns,
        preferred_element_type=jnp.float32,
    )
    qkv_grad, out_grad = lax.psum((qkv_part, out_part), "rep")
    return (encoded, d_patches, qkv_grad, out_grad)


AXES = ("seq", "rep")
MARK = 1024.0
MIB = 1024 * 1024


def line_perm(move, reps):
    pairs = []
    for z in range(4):
        for rep in range(reps):
            x, c = rep // 2, rep % 2
            to_x, to_c, to_z = move(x, c, z)
            pairs.append((z * reps + rep, to_z * reps + 2 * to_x + to_c))
    return pairs


def sine_cosine(phase):
    turns = jnp.floor(phase * np.float32(2.0 / np.pi) + 0.5)
    rest = phase - turns * np.float32(1.5703125)
    rest = rest - turns * np.float32(4.837512969970703125e-4)
    rest = rest - turns * np.float32(7.54978995489188216e-8)
    square = rest * rest
    sine = rest + rest * square * (
        np.float32(-1.6666654611e-1)
        + square * (np.float32(8.3321608736e-3) + square * np.float32(-1.9515295891e-4))
    )
    cosine = (
        1.0
        - 0.5 * square
        + square
        * square
        * (
            np.float32(4.166664568298827e-2)
            + square * (np.float32(-1.388731625493765e-3) + square * np.float32(2.443315711809948e-5))
        )
    )
    quadrant = turns.astype(jnp.int32) & 3
    swap = (quadrant & 1) == 1
    first = jnp.where(swap, cosine, sine)
    second = jnp.where(swap, sine, cosine)
    first = jnp.where(quadrant >= 2, -first, first)
    second = jnp.where((quadrant == 1) | (quadrant == 2), -second, second)
    return first, second


def live_column(count, rows):
    return lax.broadcasted_iota(jnp.int32, (rows, 1), 0) < count


def dot_nn(a, b):
    return jnp.dot(a, b, preferred_element_type=jnp.float32)


def dot_nt(a, b):
    return lax.dot_general(a, b, (((1,), (1,)), ((), ())), preferred_element_type=jnp.float32)


PAR, CORE, LINE, SIDE, KEPT = range(5)


def load_weights(core, w_in_hbm, w_out_hbm, wq, wk, wv, wo, sems):
    width = w_out_hbm.shape[0]
    copies = []
    for j in range(wq.shape[1] // 128):
        to = pl.ds(128 * j, 128)
        row = pl.multiple_of(256 * j + 128 * core, 128)
        pairs = [(w_out_hbm.at[pl.ds(row, 128), :], wo.at[to, :])]
        for t, out in enumerate((wq, wk, wv)):
            at = pl.multiple_of(t * width + row, 128)
            pairs.append((w_in_hbm.at[:, pl.ds(at, 128)], out.at[:, to]))
        copies += [pltpu.make_async_copy(a, b, sems.at[4 * j + i]) for i, (a, b) in enumerate(pairs)]
    for copy in copies:
        copy.start()
    return copies


def norm_kernel(
    place, patch_hbm, cot_hbm, index_hbm, gain_hbm, w_in_hbm, w_out_hbm,
    p0_ref, p1_ref, hidden_ref, wq, wk, wv, wo,
    patch_ref, cot_ref, index_ref, gain_ref, sems, w_sems,
):
    par = place[PAR]
    rows, width = patch_ref.shape[1:]
    quarter = width // 4
    copies = [
        pltpu.make_async_copy(src, dst, sems.at[i])
        for i, (src, dst) in enumerate(
            ((index_hbm, index_ref), (patch_hbm, patch_ref), (gain_hbm, gain_ref), (cot_hbm, cot_ref))
        )
    ]
    for copy in copies:
        copy.start()
    staged = load_weights(place[CORE], w_in_hbm, w_out_hbm, wq, wk, wv, wo, w_sems)
    order = lax.broadcasted_iota(jnp.int32, (1, quarter), 1).astype(jnp.float32)
    freq = jnp.exp(-np.log(np.float32(10000.0)) * order / quarter)
    diagonal = lax.broadcasted_iota(jnp.int32, (rows, rows), 0) == lax.broadcasted_iota(
        jnp.int32, (rows, rows), 1
    )
    copies[0].wait()
    tables = []
    for k in range(2):
        position = index_ref[pl.ds(k ^ par, 1), :]
        grid_row = (position // GRID_COLS).astype(jnp.float32)
        grid_col = (position % GRID_COLS).astype(jnp.float32)
        grid_row = jnp.sum(jnp.where(diagonal, grid_row, 0.0), axis=1, keepdims=True)
        grid_col = jnp.sum(jnp.where(diagonal, grid_col, 0.0), axis=1, keepdims=True)
        pieces = sine_cosine(grid_row * freq) + sine_cosine(grid_col * freq)
        tables.append(jnp.concatenate(pieces, axis=1))
    copies[1].wait()
    copies[2].wait()
    for k, out_ref in enumerate((p0_ref, p1_ref)):
        s = k ^ par
        hidden = patch_ref[s].astype(jnp.float32) + tables[k]
        hidden_ref[k] = hidden
        center = hidden - jnp.mean(hidden, axis=-1, keepdims=True)
        spread = jnp.mean(center * center, axis=-1, keepdims=True)
        normed = center * lax.rsqrt(spread + epsilon) * gain_ref[...]
        live = live_column(place[KEPT + s], rows)
        out_ref[:rows, :] = jnp.where(live, normed, MARK).astype(out_ref.dtype)
    copies[3].wait()
    for k, out_ref in enumerate((p0_ref, p1_ref)):
        s = k ^ par
        live = live_column(place[KEPT + s], rows)
        grad = cot_ref[s]
        out_ref[rows:, :] = jnp.where(live, grad, jnp.zeros_like(grad))
    for copy in staged:
        copy.wait()


def attend_pairs(
    place, first_pair, payloads, wq, wk, wv, wo, own, oth, keep_t, out_keep, send, norm_s, grad_s, att_s,
):
    block = payloads[0].shape[0] // 2
    rows = 4 * block
    half = 2 * block
    biases = []
    for i, ref in enumerate(payloads):
        at = slice(i * block, (i + 1) * block)
        value = ref[:block, :]
        live = value[:, 0:1].astype(jnp.float32) < MARK
        norm_s[at, :] = jnp.where(live, value, jnp.zeros_like(value))
        grad_s[at, :] = ref[block:, :]
        biases.append(jnp.where(live, 0.0, -1e30))
    bias = jnp.concatenate(biases, axis=0)
    low = lax.broadcasted_iota(jnp.int32, (rows, 128), 1) < 64
    scale = jnp.bfloat16(0.125)
    zero = jnp.zeros((rows, 128), jnp.bfloat16)
    first = place[SIDE] == 0
    count = own.shape[2] // 128
    here = slice(128 * first_pair, 128 * (first_pair + count))
    normed = norm_s[...]
    queries = dot_nn(normed, wq[:, here]).astype(jnp.bfloat16)
    keys = dot_nn(normed, wk[:, here]).astype(jnp.bfloat16)
    values = dot_nn(normed, wv[:, here]).astype(jnp.bfloat16)
    d_att = dot_nt(grad_s[...], wo[here, :]).astype(jnp.bfloat16)
    for j in range(count):
        cols = slice(128 * j, 128 * j + 128)
        q = queries[:, cols] * scale
        k = keys[:, cols]
        v = values[:, cols]
        g = d_att[:, cols]
        v_t = v.T
        k_t = (k * scale).T
        att_t, dq_t, dk, dv = [], [], [], []
        for h in range(2):
            mine = low if h == 0 else jnp.logical_not(low)
            scores = dot_nt(k, jnp.where(mine, q, zero)) + bias
            raised = jnp.exp(scores - jnp.max(scores, axis=0, keepdims=True))
            prob = raised * (1.0 / jnp.sum(raised, axis=0, keepdims=True))
            weights = prob.astype(jnp.bfloat16)
            part = slice(64 * h, 64 * h + 64)
            att_t.append(dot_nn(v_t[part], weights))
            dv.append(dot_nn(weights, g))
            d_prob = dot_nt(v, jnp.where(mine, g, zero))
            total = jnp.sum(prob * d_prob, axis=0, keepdims=True)
            d_score = (prob * (d_prob - total)).astype(jnp.bfloat16)
            dq_t.append(dot_nn(k_t[part], d_score))
            dk.append(dot_nn(d_score, q))
        att_pair_t = jnp.concatenate(att_t, axis=0).astype(jnp.bfloat16)
        dq_pair_t = jnp.concatenate(dq_t, axis=0).astype(jnp.bfloat16)
        dk_pair = jnp.where(low, dk[0], dk[1]).astype(jnp.bfloat16)
        dv_pair = jnp.where(low, dv[0], dv[1]).astype(jnp.bfloat16)
        for t, piece in enumerate((dq_pair_t.T, dk_pair, dv_pair, att_pair_t.T)):
            own[t, :, cols] = piece[:half]
            oth[t, :, cols] = piece[half:]
        for t, piece in enumerate((dq_pair_t, dk_pair.T, dv_pair.T)):
            at = slice(64 * j, 64 * j + 64)
            part = slice(rows * t, rows * t + rows)
            keep_t[at, part] = jnp.where(first, piece[:64], piece[64:])
            send[at, part] = jnp.where(first, piece[64:], piece[:64])
        at = slice(64 * j, 64 * j + 64)
        att_s[0, at, :] = jnp.where(first, att_pair_t[:64], att_pair_t[64:])
        att_s[1, at, :] = jnp.where(first, att_pair_t[64:], att_pair_t[:64])
    out_keep[...] = dot_nn(att_s[0], grad_s[...])
    send[:, 3 * rows :] = dot_nn(att_s[1], grad_s[...]).astype(send.dtype)


def attend_first(place, p0, p1, p2, p3, *refs):
    attend_pairs(place, 0, (p0, p1, p2, p3), *refs)


def attend_second(place, p0, p1, p2, p3, wq, wk, wv, wo, after, *refs):
    del after
    attend_pairs(place, 2, (p0, p1, p2, p3), wq, wk, wv, wo, *refs)


def in_order(place, own, got):
    pieces = []
    low = place == 0
    for j in range(own.shape[1] // 128):
        a, b = own[:, 128 * j : 128 * j + 128], got[:, 128 * j : 128 * j + 128]
        pieces += [jnp.where(low, a, b), jnp.where(low, b, a)]
    return jnp.concatenate(pieces, axis=1)


def rows_kernel(place, own_a, got_a, own_b, got_b, w_ref, w_out_ref, after, before, o0, o1, total):
    del after, before
    step = pl.program_id(0)
    core = place[CORE]
    block = o0.shape[0] // 2

    def rows_of(t):
        return jnp.concatenate([in_order(core, own_a[t], got_a[t]), in_order(core, own_b[t], got_b[t])], axis=1)

    term = dot_nt(rows_of(step), w_ref[...])

    @pl.when(step == 0)
    def _():
        total[...] = term
        projected = dot_nn(rows_of(3), w_out_ref[...]).astype(o0.dtype)
        o0[:block, :] = projected[:block]
        o1[:block, :] = projected[block:]

    @pl.when(step > 0)
    def _():
        total[...] += term

    @pl.when(step == pl.num_programs(0) - 1)
    def _():
        o0[block:, :] = total[:block].astype(o0.dtype)
        o1[block:, :] = total[block:].astype(o1.dtype)


def return_kernel(place, r0, r1, hidden_ref, m0, m1, gain_ref, after, encoded, d_patches):
    del after
    par = place[PAR]
    rows = r0.shape[0] // 2
    for k, (r_ref, m_ref) in enumerate(((r0, m0), (r1, m1))):
        s = k ^ par
        live = live_column(place[KEPT + s], rows)
        hidden = hidden_ref[k]
        projected = r_ref[:rows, :].astype(jnp.float32)
        encoded[s] = jnp.where(live, hidden + projected, 0.0).astype(encoded.dtype)
        center = hidden - jnp.mean(hidden, axis=-1, keepdims=True)
        spread = jnp.mean(center * center, axis=-1, keepdims=True)
        inv_std = lax.rsqrt(spread + epsilon)
        unit = center * inv_std
        d_hidden = norm_backward(r_ref[rows:, :].astype(jnp.float32), gain_ref[...], unit, inv_std)
        value = m_ref[rows:, :].astype(jnp.float32) + d_hidden
        d_patches[s] = jnp.where(live, value, 0.0).astype(d_patches.dtype)


def put_parts(place, total, out_keep, got, keep, send, out_total):
    out_total[...] = out_keep[...] + got[:, got.shape[1] - out_total.shape[1] :].astype(jnp.float32)
    columns = out_total.shape[1] // 4
    tall = out_total.shape[0] // 4
    count = total.shape[0] // 4
    for k in range(4):
        ref, spot = (keep, send)[k % 2], k // 2
        at = pl.multiple_of((place[LINE] ^ k) * count, 64)
        ref[spot, :count, :] = total[pl.ds(at, count), :].astype(ref.dtype)
        at = pl.multiple_of((place[LINE] ^ k) * columns, 128)
        value = out_total[:, pl.ds(at, columns)].astype(ref.dtype)
        for j in range(4):
            ref[spot, count:, columns * j : columns * j + columns] = value[tall * j : tall * j + tall, :]


def piece_of(ref, at, rows):
    t, j = at // 2, at % 2
    return ref[64 * j : 64 * j + 64, rows * t : rows * t + rows]


def weight_first(
    place, keep, out_keep, got, p0, p1, p2, p3, n0, n1,
    part_keep, part_send, tokens, left, total, out_total,
):
    block = p0.shape[0] // 2
    rows = 4 * block
    for i, ref in enumerate((p0, p1, p2, p3)):
        tokens[i * block : (i + 1) * block, :] = ref[:block, :]
    tokens[rows : rows + 2 * block, :] = n0[...]
    tokens[rows + 2 * block :, :] = n1[...]
    for side, ref in enumerate((keep, got)):
        for i, at in enumerate((0, 2, 4, 5)):
            left[side, 64 * i : 64 * i + 64, :] = piece_of(ref, at, rows)
    total[...] = dot_nn(left[0], tokens[:rows, :]) + dot_nn(left[1], tokens[rows:, :])
    put_parts(place, total, out_keep, got, part_keep, part_send, out_total)


def weight_second(
    place, keep_a, got_a, keep_b, out_keep, got_b, p0, p1, p2, p3, n0, n1, after,
    part_keep, part_send, tokens, left, total, out_total,
):
    del after
    block = p0.shape[0] // 2
    rows = 4 * block
    for i, ref in enumerate((p0, p1, p2, p3)):
        tokens[i * block : (i + 1) * block, :] = ref[:block, :]
    tokens[rows : rows + 2 * block, :] = n0[...]
    tokens[rows + 2 * block :, :] = n1[...]
    for side, (a, b) in enumerate(((keep_a, keep_b), (got_a, got_b))):
        for i, (ref, at) in enumerate(
            ((a, 1), (b, 0), (b, 1), (a, 3), (b, 2), (b, 3), (b, 4), (b, 5))
        ):
            left[side, 64 * i : 64 * i + 64, :] = piece_of(ref, at, rows)
    total[...] = dot_nn(left[0], tokens[:rows, :]) + dot_nn(left[1], tokens[rows:, :])
    put_parts(place, total, out_keep, got_b, part_keep, part_send, out_total)


def pair_kernel(keep, got, mine, send):
    mine[...] = keep[0] + got[0].astype(jnp.float32)
    send[...] = (keep[1] + got[1].astype(jnp.float32)).astype(send.dtype)


def sum_kernel(mine, got, *refs):
    out = refs[-1]
    out[...] = (mine[...] + got[...].astype(jnp.float32)).astype(out.dtype)


def finish_kernel(place, a0, a1, a2, a3, b0, b1, b2, b3, wide, narrow):
    core_low, side_low = place[CORE] == 0, place[SIDE] == 0
    slab = place[LINE]
    columns = narrow.shape[1]
    spot = jnp.where(slab == 3, 0, slab)
    spots = (spot, jnp.where(spot == 0, 1, 0), jnp.where(spot == 2, 1, 2))

    def pick(refs, c, x, at, part):
        own, by_x, by_core, by_both = refs
        near = jnp.where(side_low == (x == 0), own[at, part], by_x[at, part])
        far = jnp.where(side_low == (x == 0), by_core[at, part], by_both[at, part])
        return jnp.where(core_low == (c == 0), near, far)

    every = slice(None)
    first, second = (a0, a1, a2, a3), (b0, b1, b2, b3)
    for c in range(2):
        for i, (refs, row) in enumerate(((first, 0), (second, 0), (second, 64))):
            at = slice(row, row + 64)
            both = jnp.concatenate([pick(refs, c, x, at, every) for x in range(2)], axis=0)
            col = pl.multiple_of(128 * (2 * spots[i] + c), 128)
            wide[:, pl.ds(col, 128)] = both.T.astype(wide.dtype)
        for half, (refs, base) in enumerate(((first, 64), (second, 128))):
            for j in range(4):
                at = slice(base, base + 32)
                part = slice(columns * j, columns * j + columns)
                for x in range(2):
                    pair, row = 2 * half + j // 2, 32 * (j % 2)
                    row += 128 * (2 * pair + c) + 64 * x
                    narrow[row : row + 32, :] = pick(refs, c, x, at, part).astype(narrow.dtype)


SMEM_SPEC = pl.BlockSpec(memory_space=pltpu.SMEM)
VMEM_SPEC = pl.BlockSpec(memory_space=pltpu.VMEM)


def struct(shape, dtype=jnp.bfloat16):
    return jax.ShapeDtypeStruct(shape, dtype)


COST = pl.CostEstimate(flops=1000, bytes_accessed=1000, transcendentals=0)


def in_hbm(value):
    return pltpu.with_memory_space_constraint(value, pltpu.HBM)


def call(kernel, args, outs, limit, place=None, scratch=(), specs=None):
    specs = specs or [VMEM_SPEC] * len(args)
    if place is not None:
        args, specs = (place, *args), [SMEM_SPEC] + specs
    single = not isinstance(outs, list)
    return pl.pallas_call(
        kernel,
        in_specs=specs,
        out_specs=VMEM_SPEC if single else [VMEM_SPEC] * len(outs),
        out_shape=outs,
        scratch_shapes=list(scratch),
        compiler_params=pltpu.CompilerParams(vmem_limit_bytes=limit * MIB),
        cost_estimate=COST,
    )(*args)


def chip_shards(patches, kept_index, kept_count, cotangent, w_qkv, w_out, gain):
    bf16, f32 = jnp.bfloat16, jnp.float32
    samples, slots, width = patches.shape
    reps = lax.axis_size("rep")
    rep = lax.axis_index("rep")
    z = lax.axis_index("seq")
    core, x = rep & 1, rep >> 1
    place = jnp.concatenate(
        [jnp.stack([z & 1, core, z, x]).astype(jnp.int32), kept_count.reshape(samples)]
    )
    own_width = width // 2
    quarter = width // 4
    rows = 4 * slots

    def send(value, move):
        return lax.ppermute(value, AXES, line_perm(move, reps))

    def to_core(value):
        return send(value, lambda x, c, z: (x, 1 - c, z))

    def to_x(value):
        return send(value, lambda x, c, z: (1 - x, c, z))

    def to_chip(value, k):
        return send(value, lambda x, c, z: (x, z >> 1, 2 * c + (k ^ (z & 1))))

    def to_rows(value, k, other):
        return send(value, lambda x, c, z: (x, z >> 1, 2 * (c ^ other) + (k ^ (z & 1))))

    def along(value, k):
        return send(value, lambda x, c, z: (x, c, z ^ k))

    gain_row = gain.reshape(1, width)
    pay = struct((2 * slots, width))
    hbm = pl.BlockSpec(memory_space=pl.ANY)
    any_spec = pl.BlockSpec(memory_space=pl.ANY)
    pairs = width // 512
    own_w = [struct((width, own_width))] * 3 + [struct((own_width, width))]
    *outs, wq, wk, wv, wo = call(
        norm_kernel,
        tuple(in_hbm(v) for v in (patches, cotangent, kept_index, gain_row, w_qkv, w_out)),
        [pay, pay, struct(patches.shape, f32)] + own_w,
        24,
        place,
        scratch=[
            pltpu.VMEM(patches.shape, bf16),
            pltpu.VMEM(patches.shape, bf16),
            pltpu.VMEM(kept_index.shape, jnp.int32),
            pltpu.VMEM(gain_row.shape, f32),
            pltpu.SemaphoreType.DMA((4,)),
            pltpu.SemaphoreType.DMA((8 * pairs,)),
        ],
        specs=[any_spec] * 6,
    )
    *mine, hidden = outs
    got = [to_chip(mine[k], k) for k in range(2)]
    here = got + [to_core(v) for v in got]
    from_x = to_x(jnp.concatenate([v[:slots] for v in got], axis=0))
    there = (from_x, to_core(from_x))

    half_rows = struct((4, 2 * slots, 128 * pairs))
    out_half = (64 * pairs, width)
    half_t = struct((64 * pairs, 3 * rows))
    half_send = struct((64 * pairs, 3 * rows + width))

    staged = (wq, wk, wv, wo)

    def attend(kernel, after):
        return call(
            kernel,
            (*here, *staged, *after),
            [half_rows] * 2 + [half_t, struct(out_half, f32), half_send],
            32,
            place,
            scratch=[pltpu.VMEM((rows, width), bf16)] * 2 + [pltpu.VMEM((2, 64 * pairs, rows), bf16)],
            specs=[VMEM_SPEC] * 8 + [any_spec] * len(after),
        )

    own_a, oth_a, keep_a, out_keep_a, send_a = attend(attend_first, ())
    got_a = to_x(send_a)
    core_a = to_core(oth_a)
    own_b, oth_b, keep_b, out_keep_b, send_b = attend(attend_second, (from_x,))
    got_b = to_x(send_b)
    core_b = to_core(oth_b)

    def parts_of(kernel, args, tall, scratch, after=()):
        return call(
            kernel,
            (*args, *here, *there, *after),
            [struct((2, tall, width), f32), struct((2, tall, width))],
            16,
            place,
            scratch=[pltpu.VMEM((2 * rows, width), bf16)] + scratch + [pltpu.VMEM(out_half, f32)],
            specs=[VMEM_SPEC] * (len(args) + 6) + [any_spec] * len(after),
        )

    def pair_sums(keep, part):
        shape = keep.shape[1:]
        mine, part = call(pair_kernel, (keep, along(part, 1)), [struct(shape, f32), struct(shape)], 8)
        return mine, part, along(part, 2)

    def spread(mine, part, after=()):
        sums = call(
            sum_kernel,
            (mine, part, *after),
            struct(part.shape),
            8,
            specs=[VMEM_SPEC] * 2 + [any_spec] * len(after),
        )
        by_x = to_x(sums)
        return (sums, by_x, to_core(sums), to_core(by_x))

    keep, part = parts_of(
        weight_first,
        (keep_a, out_keep_a, got_a),
        96,
        [pltpu.VMEM((2, 256, rows), bf16), pltpu.VMEM((256, width), f32)],
    )
    first_sum, paired, first_got = pair_sums(keep, part)
    keep, part = parts_of(
        weight_second,
        (keep_a, got_a, keep_b, out_keep_b, got_b),
        160,
        [pltpu.VMEM((2, 512, rows), bf16), pltpu.VMEM((512, width), f32)],
        (paired,),
    )
    started = part
    second_sum, _, second_got = pair_sums(keep, part)
    first = spread(first_sum, first_got)
    whole_w = pl.BlockSpec((width, width), lambda i, p: (0, 0))
    back = pl.pallas_call(
        rows_kernel,
        grid_spec=pltpu.PrefetchScalarGridSpec(
            num_scalar_prefetch=1,
            grid=(3,),
            in_specs=[pl.BlockSpec(half_rows.shape, lambda i, p: (0, 0, 0))] * 4
            + [pl.BlockSpec((width, width), lambda i, p: (0, i)), whole_w, any_spec, any_spec],
            out_specs=[pl.BlockSpec(pay.shape, lambda i, p: (0, 0))] * 2,
            scratch_shapes=[pltpu.VMEM((2 * slots, width), f32)],
        ),
        out_shape=[pay] * 2,
        compiler_params=pltpu.CompilerParams(vmem_limit_bytes=20 * MIB),
        cost_estimate=COST,
    )(place, own_a, core_a, own_b, core_b, in_hbm(w_qkv), in_hbm(w_out), started, first[1])
    second = spread(second_sum, second_got, (back[0], *first[1:]))
    back = [to_rows(back[k], k, 0) for k in range(2)]
    qkv_grad, out_grad = call(
        finish_kernel,
        (*first, *second),
        [struct((width, 3 * quarter), f32), struct((width, quarter), f32)],
        12,
        place,
    )
    encoded, d_patches = call(
        return_kernel,
        (*back, hidden, *mine, gain_row, in_hbm(qkv_grad)),
        [struct(patches.shape)] * 2,
        12,
        place,
        specs=[VMEM_SPEC] * 6 + [any_spec],
    )
    return (encoded, d_patches, qkv_grad, out_grad)


def solution(mesh):
    in_specs = (
        P(("grp", "rep"), "seq", None),
        P(("grp", "rep"), "seq"),
        P(("grp", "rep"), "seq"),
        P(("grp", "rep"), "seq", None),
        P(),
        P(),
        P(),
    )
    out_specs = (
        P(("grp", "rep"), "seq", None),
        P(("grp", "rep"), "seq", None),
        P("grp", "seq"),
        P("grp", "seq"),
    )
    chips = mesh.shape["seq"] == 4 and mesh.shape["rep"] % 2 == 0 and HEADS % 8 == 0

    def run(patches, *rest):
        per_device = patches.shape[0] // (mesh.shape["grp"] * mesh.shape["rep"])
        body = chip_shards if chips and per_device == 2 else shards
        inner = jax.shard_map(body, mesh=mesh, in_specs=in_specs, out_specs=out_specs, check_vma=False)
        return inner(patches, *rest)

    return run
```

```python
import functools

import jax
import jax.numpy as jnp
import numpy as np
from jax import lax
from jax.experimental import pallas as pl
from jax.experimental.pallas import tpu as pltpu
from jax.sharding import PartitionSpec as P

HEADS = 16
GRID_COLS = 512


epsilon = 1e-06


def position_table(position, model_width):
    quarter = model_width // 4
    frequency = jnp.exp(-jnp.log(10000.0) * jnp.arange(quarter, dtype=jnp.float32) / quarter)
    grid_row = (position // GRID_COLS).astype(jnp.float32)
    grid_col = (position % GRID_COLS).astype(jnp.float32)
    row_phase = grid_row[..., None] * frequency
    col_phase = grid_col[..., None] * frequency
    return jnp.concatenate(
        [jnp.sin(row_phase), jnp.cos(row_phase), jnp.sin(col_phase), jnp.cos(col_phase)], axis=-1
    )


def normalize(hidden, gain):
    center = hidden - jnp.mean(hidden, axis=-1, keepdims=True)
    spread = jnp.mean(center * center, axis=-1, keepdims=True)
    inv_std = lax.rsqrt(spread + epsilon)
    unit_rows = center * inv_std
    return ((unit_rows * gain).astype(jnp.bfloat16), unit_rows, inv_std)


def norm_backward(d_normed, gain, unit_rows, inv_std):
    scaled = d_normed * gain
    return inv_std * (
        scaled
        - jnp.mean(scaled, axis=-1, keepdims=True)
        - unit_rows * jnp.mean(scaled * unit_rows, axis=-1, keepdims=True)
    )


def head_block(query_rows, grad_rows, key_rows, value_rows, live_keys, score_scale):
    scores = jnp.dot(query_rows, key_rows.T, preferred_element_type=jnp.float32) * score_scale
    scores = jnp.where(live_keys[None, :], scores, -1e30)
    top_score = jnp.max(scores, axis=1, keepdims=True)
    raised = jnp.exp(scores - top_score)
    probability = raised / jnp.sum(raised, axis=1, keepdims=True)
    rounded = probability.astype(jnp.bfloat16)
    attended = jnp.dot(rounded, value_rows, preferred_element_type=jnp.float32).astype(jnp.bfloat16)
    d_value = jnp.dot(rounded.T, grad_rows, preferred_element_type=jnp.float32)
    d_prob = jnp.dot(grad_rows, value_rows.T, preferred_element_type=jnp.float32)
    d_score = (
        probability * (d_prob - jnp.sum(probability * d_prob, axis=1, keepdims=True)) * score_scale
    ).astype(jnp.bfloat16)
    d_query = jnp.dot(d_score, key_rows, preferred_element_type=jnp.float32)
    d_key = jnp.dot(d_score.T, query_rows, preferred_element_type=jnp.float32)
    return (attended, d_query, d_key, d_value)


def attend(query_rows, grad_rows, key_rows, value_rows, live_keys, score_scale):
    row_count = query_rows.shape[0]
    blocks = max(1, row_count // 512)
    while row_count % blocks:
        blocks -= 1
    block_rows = row_count // blocks
    query_blocks = query_rows.reshape(blocks, block_rows, query_rows.shape[1])
    grad_blocks = grad_rows.reshape(blocks, block_rows, grad_rows.shape[1])

    def block_step(carry, pieces):
        key_total, value_total = carry
        attended, d_query, d_key, d_value = head_block(
            pieces[0], pieces[1], key_rows, value_rows, live_keys, score_scale
        )
        return ((key_total + d_key, value_total + d_value), (attended, d_query))

    empty = jnp.zeros(key_rows.shape, jnp.float32)
    (key_total, value_total), (attended, d_query) = lax.scan(
        block_step, (empty, empty), (query_blocks, grad_blocks)
    )
    return (attended.reshape(row_count, -1), d_query.reshape(row_count, -1), key_total, value_total)


def shards(patches, kept_index, kept_count, cotangent, w_qkv, w_out, gain):
    groups = lax.axis_size("seq")
    samples, slot_count, model_width = patches.shape
    head_size = model_width // HEADS
    per_device = max(1, HEADS // groups)
    splits = max(1, groups // HEADS)
    head_groups = groups // splits
    band_width = per_device * head_size
    part_rows = slot_count // splits
    slot_ids = jnp.arange(slot_count, dtype=jnp.int32)
    live_slots = slot_ids[None, :] < kept_count
    hidden = patches.astype(jnp.float32) + position_table(kept_index, model_width)
    normed, unit_rows, inv_std = normalize(hidden, gain)
    flat_normed = normed.reshape(samples * slot_count, model_width)
    packed = jnp.dot(flat_normed, w_qkv, preferred_element_type=jnp.float32).astype(jnp.bfloat16)
    packed = packed.reshape(samples, slot_count, 3 * model_width)
    live_grad = jnp.where(live_slots[:, :, None], cotangent, jnp.zeros_like(cotangent))
    flat_grad = live_grad.reshape(samples * slot_count, model_width)
    d_attended = jnp.dot(flat_grad, w_out.T, preferred_element_type=jnp.float32).astype(
        jnp.bfloat16
    )
    d_attended = d_attended.reshape(samples, slot_count, model_width)

    def to_owners(tensor_block):
        arranged = tensor_block.reshape(samples, splits, part_rows, head_groups, band_width)
        return arranged.transpose(3, 1, 0, 2, 4).reshape(groups, samples, part_rows, band_width)

    key_value_send = jnp.concatenate(
        [
            packed[:, :, model_width : 2 * model_width].reshape(
                samples, slot_count, head_groups, band_width
            ),
            packed[:, :, 2 * model_width :].reshape(samples, slot_count, head_groups, band_width),
        ],
        axis=3,
    )
    key_value_send = key_value_send.transpose(2, 0, 1, 3)
    key_value_send = jnp.broadcast_to(
        key_value_send[:, None], (head_groups, splits, samples, slot_count, 2 * band_width)
    )
    key_value_send = key_value_send.reshape(groups, samples, slot_count, 2 * band_width)
    got_query, got_grad, got_pair = (
        lax.all_to_all(
            to_owners(packed[:, :, :model_width]), "seq", split_axis=0, concat_axis=0, tiled=True
        ),
        lax.all_to_all(to_owners(d_attended), "seq", split_axis=0, concat_axis=0, tiled=True),
        lax.all_to_all(key_value_send, "seq", split_axis=0, concat_axis=0, tiled=True),
    )
    all_counts = lax.all_gather(kept_count, "seq", axis=1, tiled=True)
    live_keys = (slot_ids[None, None, :] < all_counts[:, :, None]).reshape(
        samples, groups * slot_count
    )

    def rows_by_head(tensor_block, row_count):
        arranged = tensor_block.transpose(1, 0, 2, 3).reshape(
            samples, groups * row_count, per_device, head_size
        )
        return arranged.transpose(0, 2, 1, 3)

    query_heads = rows_by_head(got_query, part_rows)
    grad_heads = rows_by_head(got_grad, part_rows)
    key_heads = rows_by_head(got_pair[..., :band_width], slot_count)
    value_heads = rows_by_head(got_pair[..., band_width:], slot_count)
    score_scale = head_size ** (-0.5)

    def one_head(query_rows, grad_rows, key_rows, value_rows, key_live):
        return attend(query_rows, grad_rows, key_rows, value_rows, key_live, score_scale)

    per_head = jax.vmap(one_head, in_axes=(0, 0, 0, 0, None))
    outputs, d_query, d_key, d_value = jax.vmap(per_head)(
        query_heads, grad_heads, key_heads, value_heads, live_keys
    )

    def back_to_sources(tensor_block, row_count):
        arranged = tensor_block.transpose(0, 2, 1, 3).reshape(
            samples, groups, row_count, band_width
        )
        return arranged.transpose(1, 0, 2, 3)

    query_send = back_to_sources(d_query, part_rows).astype(jnp.bfloat16)
    back_out, back_query = (
        lax.all_to_all(
            back_to_sources(outputs, part_rows), "seq", split_axis=0, concat_axis=0, tiled=True
        ),
        lax.all_to_all(query_send, "seq", split_axis=0, concat_axis=0, tiled=True),
    )
    key_value_grad = jnp.concatenate(
        [back_to_sources(d_key, slot_count), back_to_sources(d_value, slot_count)], axis=3
    )
    back_pair = lax.all_to_all(
        key_value_grad.astype(jnp.bfloat16), "seq", split_axis=0, concat_axis=0, tiled=True
    ).astype(key_value_grad.dtype)

    def from_owners(tensor_block):
        arranged = tensor_block.reshape(head_groups, splits, samples, part_rows, band_width)
        return arranged.transpose(2, 1, 3, 0, 4).reshape(samples, slot_count, model_width)

    attended = from_owners(back_out)
    summed_pair = jnp.sum(
        back_pair.reshape(head_groups, splits, samples, slot_count, 2 * band_width), axis=1
    )
    summed_pair = summed_pair.transpose(1, 2, 0, 3)
    key_grad_rows = (
        summed_pair[..., :band_width].reshape(samples, slot_count, model_width).astype(jnp.bfloat16)
    )
    value_grad_rows = (
        summed_pair[..., band_width:].reshape(samples, slot_count, model_width).astype(jnp.bfloat16)
    )
    d_packed = jnp.concatenate([from_owners(back_query), key_grad_rows, value_grad_rows], axis=2)
    flat_attended = attended.reshape(samples * slot_count, model_width)
    projected = jnp.dot(flat_attended, w_out, preferred_element_type=jnp.float32).reshape(
        samples, slot_count, model_width
    )
    encoded = jnp.where(live_slots[:, :, None], hidden + projected, 0.0).astype(jnp.bfloat16)
    flat_packed = d_packed.reshape(samples * slot_count, 3 * model_width)
    d_normed = jnp.dot(flat_packed, w_qkv.T, preferred_element_type=jnp.float32).reshape(
        samples, slot_count, model_width
    )
    d_hidden = norm_backward(d_normed, gain, unit_rows, inv_std)
    d_patches = jnp.where(
        live_slots[:, :, None], live_grad.astype(jnp.float32) + d_hidden, 0.0
    ).astype(jnp.bfloat16)
    columns = flat_grad
    out_part = lax.psum_scatter(
        jnp.dot(columns.T, flat_attended, preferred_element_type=jnp.float32),
        "seq",
        scatter_dimension=0,
        tiled=True,
    ).T
    my_columns = lax.all_to_all(flat_packed, "seq", split_axis=1, concat_axis=0, tiled=True)
    columns = my_columns
    qkv_part = jnp.dot(
        lax.all_gather(flat_normed, "seq", axis=0, tiled=True).T,
        columns,
        preferred_element_type=jnp.float32,
    )
    qkv_grad, out_grad = lax.psum((qkv_part, out_part), "rep")
    return (encoded, d_patches, qkv_grad, out_grad)


AXES = ("seq", "rep")
MARK = 1024.0
MIB = 1024 * 1024


def line_perm(move, reps):
    pairs = []
    for z in range(4):
        for rep in range(reps):
            x, c = rep // 2, rep % 2
            to_x, to_c, to_z = move(x, c, z)
            pairs.append((z * reps + rep, to_z * reps + 2 * to_x + to_c))
    return pairs


def sine_cosine(phase):
    turns = jnp.floor(phase * np.float32(2.0 / np.pi) + 0.5)
    rest = phase - turns * np.float32(1.5703125)
    rest = rest - turns * np.float32(4.837512969970703125e-4)
    rest = rest - turns * np.float32(7.54978995489188216e-8)
    square = rest * rest
    sine = rest + rest * square * (
        np.float32(-1.6666654611e-1)
        + square * (np.float32(8.3321608736e-3) + square * np.float32(-1.9515295891e-4))
    )
    cosine = (
        1.0
        - 0.5 * square
        + square
        * square
        * (
            np.float32(4.166664568298827e-2)
            + square * (np.float32(-1.388731625493765e-3) + square * np.float32(2.443315711809948e-5))
        )
    )
    quadrant = turns.astype(jnp.int32) & 3
    swap = (quadrant & 1) == 1
    first = jnp.where(swap, cosine, sine)
    second = jnp.where(swap, sine, cosine)
    first = jnp.where(quadrant >= 2, -first, first)
    second = jnp.where((quadrant == 1) | (quadrant == 2), -second, second)
    return first, second


def live_column(count, rows):
    return lax.broadcasted_iota(jnp.int32, (rows, 1), 0) < count


def dot_nn(a, b):
    return jnp.dot(a, b, preferred_element_type=jnp.float32)


def dot_nt(a, b):
    return lax.dot_general(a, b, (((1,), (1,)), ((), ())), preferred_element_type=jnp.float32)


PAR, CORE, LINE, SIDE, KEPT = range(5)


def load_weights(core, w_in_hbm, w_out_hbm, wq, wk, wv, wo, sems):
    width = w_out_hbm.shape[0]
    copies = []
    for j in range(wq.shape[1] // 128):
        to = pl.ds(128 * j, 128)
        row = pl.multiple_of(256 * j + 128 * core, 128)
        pairs = [(w_out_hbm.at[pl.ds(row, 128), :], wo.at[to, :])]
        for t, out in enumerate((wq, wk, wv)):
            at = pl.multiple_of(t * width + row, 128)
            pairs.append((w_in_hbm.at[:, pl.ds(at, 128)], out.at[:, to]))
        copies += [pltpu.make_async_copy(a, b, sems.at[4 * j + i]) for i, (a, b) in enumerate(pairs)]
    for copy in copies:
        copy.start()
    return copies


def norm_block(
    k, place, patch_hbm, cot_hbm, index_hbm, gain_hbm, out_ref, hidden_ref,
    patch_ref, cot_ref, index_ref, gain_ref, sems,
):
    s = k ^ place[PAR]
    rows, width = patch_ref.shape
    quarter = width // 4
    copies = [
        pltpu.make_async_copy(src, dst, sems.at[i])
        for i, (src, dst) in enumerate(
            (
                (index_hbm, index_ref),
                (patch_hbm.at[s], patch_ref),
                (gain_hbm, gain_ref),
                (cot_hbm.at[s], cot_ref),
            )
        )
    ]
    for copy in copies:
        copy.start()
    order = lax.broadcasted_iota(jnp.int32, (1, quarter), 1).astype(jnp.float32)
    freq = jnp.exp(-np.log(np.float32(10000.0)) * order / quarter)
    diagonal = lax.broadcasted_iota(jnp.int32, (rows, rows), 0) == lax.broadcasted_iota(
        jnp.int32, (rows, rows), 1
    )
    copies[0].wait()
    position = index_ref[pl.ds(s, 1), :]
    grid_row = (position // GRID_COLS).astype(jnp.float32)
    grid_col = (position % GRID_COLS).astype(jnp.float32)
    grid_row = jnp.sum(jnp.where(diagonal, grid_row, 0.0), axis=1, keepdims=True)
    grid_col = jnp.sum(jnp.where(diagonal, grid_col, 0.0), axis=1, keepdims=True)
    table = jnp.concatenate(sine_cosine(grid_row * freq) + sine_cosine(grid_col * freq), axis=1)
    copies[1].wait()
    copies[2].wait()
    hidden = patch_ref[...].astype(jnp.float32) + table
    hidden_ref[...] = hidden
    center = hidden - jnp.mean(hidden, axis=-1, keepdims=True)
    spread = jnp.mean(center * center, axis=-1, keepdims=True)
    normed = center * lax.rsqrt(spread + epsilon) * gain_ref[...]
    live = live_column(place[KEPT + s], rows)
    out_ref[:rows, :] = jnp.where(live, normed, MARK).astype(out_ref.dtype)
    copies[3].wait()
    grad = cot_ref[...]
    out_ref[rows:, :] = jnp.where(live, grad, jnp.zeros_like(grad))


def norm_first(place, patch_hbm, cot_hbm, index_hbm, gain_hbm, *refs):
    norm_block(0, place, patch_hbm, cot_hbm, index_hbm, gain_hbm, *refs)


def norm_second(
    place, patch_hbm, cot_hbm, index_hbm, gain_hbm, w_in_hbm, w_out_hbm, after,
    out_ref, hidden_ref, wq, wk, wv, wo, *refs,
):
    del after
    staged = load_weights(place[CORE], w_in_hbm, w_out_hbm, wq, wk, wv, wo, refs[-1])
    norm_block(1, place, patch_hbm, cot_hbm, index_hbm, gain_hbm, out_ref, hidden_ref, *refs[:-1])
    for copy in staged:
        copy.wait()


def attend_pairs(
    place, first_pair, payloads, wq, wk, wv, wo, own, oth, keep_t, out_keep, send, norm_s, grad_s, att_s,
):
    block = payloads[0].shape[0] // 2
    rows = 4 * block
    half = 2 * block
    biases = []
    for i, ref in enumerate(payloads):
        at = slice(i * block, (i + 1) * block)
        value = ref[:block, :]
        live = value[:, 0:1].astype(jnp.float32) < MARK
        norm_s[at, :] = jnp.where(live, value, jnp.zeros_like(value))
        grad_s[at, :] = ref[block:, :]
        biases.append(jnp.where(live, 0.0, -1e30))
    bias = jnp.concatenate(biases, axis=0)
    low = lax.broadcasted_iota(jnp.int32, (rows, 128), 1) < 64
    scale = jnp.bfloat16(0.125)
    zero = jnp.zeros((rows, 128), jnp.bfloat16)
    first = place[SIDE] == 0
    count = own.shape[2] // 128
    here = slice(128 * first_pair, 128 * (first_pair + count))
    normed = norm_s[...]
    queries = dot_nn(normed, wq[:, here]).astype(jnp.bfloat16)
    keys = dot_nn(normed, wk[:, here]).astype(jnp.bfloat16)
    values = dot_nn(normed, wv[:, here]).astype(jnp.bfloat16)
    d_att = dot_nt(grad_s[...], wo[here, :]).astype(jnp.bfloat16)
    for j in range(count):
        cols = slice(128 * j, 128 * j + 128)
        q = queries[:, cols] * scale
        k = keys[:, cols]
        v = values[:, cols]
        g = d_att[:, cols]
        v_t = v.T
        k_t = (k * scale).T
        att_t, dq_t, dk, dv = [], [], [], []
        for h in range(2):
            mine = low if h == 0 else jnp.logical_not(low)
            scores = dot_nt(k, jnp.where(mine, q, zero)) + bias
            raised = jnp.exp(scores - jnp.max(scores, axis=0, keepdims=True))
            prob = raised * (1.0 / jnp.sum(raised, axis=0, keepdims=True))
            weights = prob.astype(jnp.bfloat16)
            part = slice(64 * h, 64 * h + 64)
            att_t.append(dot_nn(v_t[part], weights))
            dv.append(dot_nn(weights, g))
            d_prob = dot_nt(v, jnp.where(mine, g, zero))
            total = jnp.sum(prob * d_prob, axis=0, keepdims=True)
            d_score = (prob * (d_prob - total)).astype(jnp.bfloat16)
            dq_t.append(dot_nn(k_t[part], d_score))
            dk.append(dot_nn(d_score, q))
        att_pair_t = jnp.concatenate(att_t, axis=0).astype(jnp.bfloat16)
        dq_pair_t = jnp.concatenate(dq_t, axis=0).astype(jnp.bfloat16)
        dk_pair = jnp.where(low, dk[0], dk[1]).astype(jnp.bfloat16)
        dv_pair = jnp.where(low, dv[0], dv[1]).astype(jnp.bfloat16)
        for t, piece in enumerate((dq_pair_t.T, dk_pair, dv_pair, att_pair_t.T)):
            own[t, :, cols] = piece[:half]
            oth[t, :, cols] = piece[half:]
        for t, piece in enumerate((dq_pair_t, dk_pair.T, dv_pair.T)):
            at = slice(64 * j, 64 * j + 64)
            part = slice(rows * t, rows * t + rows)
            keep_t[at, part] = jnp.where(first, piece[:64], piece[64:])
            send[at, part] = jnp.where(first, piece[64:], piece[:64])
        at = slice(64 * j, 64 * j + 64)
        att_s[0, at, :] = jnp.where(first, att_pair_t[:64], att_pair_t[64:])
        att_s[1, at, :] = jnp.where(first, att_pair_t[64:], att_pair_t[:64])
    out_keep[...] = dot_nn(att_s[0], grad_s[...])
    send[:, 3 * rows :] = dot_nn(att_s[1], grad_s[...]).astype(send.dtype)


def attend_first(place, p0, p1, p2, p3, *refs):
    attend_pairs(place, 0, (p0, p1, p2, p3), *refs)


def attend_second(place, p0, p1, p2, p3, wq, wk, wv, wo, after, *refs):
    del after
    attend_pairs(place, 2, (p0, p1, p2, p3), wq, wk, wv, wo, *refs)


def in_order(place, own, got):
    pieces = []
    low = place == 0
    for j in range(own.shape[1] // 128):
        a, b = own[:, 128 * j : 128 * j + 128], got[:, 128 * j : 128 * j + 128]
        pieces += [jnp.where(low, a, b), jnp.where(low, b, a)]
    return jnp.concatenate(pieces, axis=1)


def rows_kernel(place, own_a, got_a, own_b, got_b, w_ref, w_out_ref, after, before, o0, o1, total):
    del after, before
    step = pl.program_id(0)
    core = place[CORE]
    block = o0.shape[0] // 2

    def rows_of(t):
        return jnp.concatenate([in_order(core, own_a[t], got_a[t]), in_order(core, own_b[t], got_b[t])], axis=1)

    term = dot_nt(rows_of(step), w_ref[...])

    @pl.when(step == 0)
    def _():
        total[...] = term
        projected = dot_nn(rows_of(3), w_out_ref[...]).astype(o0.dtype)
        o0[:block, :] = projected[:block]
        o1[:block, :] = projected[block:]

    @pl.when(step > 0)
    def _():
        total[...] += term

    @pl.when(step == pl.num_programs(0) - 1)
    def _():
        o0[block:, :] = total[:block].astype(o0.dtype)
        o1[block:, :] = total[block:].astype(o1.dtype)


def return_kernel(place, r0, r1, h0, h1, m0, m1, gain_ref, after, encoded, d_patches):
    del after
    par = place[PAR]
    rows = r0.shape[0] // 2
    for k, (r_ref, m_ref, hidden_ref) in enumerate(((r0, m0, h0), (r1, m1, h1))):
        s = k ^ par
        live = live_column(place[KEPT + s], rows)
        hidden = hidden_ref[...]
        projected = r_ref[:rows, :].astype(jnp.float32)
        encoded[s] = jnp.where(live, hidden + projected, 0.0).astype(encoded.dtype)
        center = hidden - jnp.mean(hidden, axis=-1, keepdims=True)
        spread = jnp.mean(center * center, axis=-1, keepdims=True)
        inv_std = lax.rsqrt(spread + epsilon)
        unit = center * inv_std
        d_hidden = norm_backward(r_ref[rows:, :].astype(jnp.float32), gain_ref[...], unit, inv_std)
        value = m_ref[rows:, :].astype(jnp.float32) + d_hidden
        d_patches[s] = jnp.where(live, value, 0.0).astype(d_patches.dtype)


def put_parts(place, total, out_keep, got, keep, send, out_total):
    out_total[...] = out_keep[...] + got[:, got.shape[1] - out_total.shape[1] :].astype(jnp.float32)
    columns = out_total.shape[1] // 4
    tall = out_total.shape[0] // 4
    count = total.shape[0] // 4
    for k in range(4):
        ref, spot = (keep, send)[k % 2], k // 2
        at = pl.multiple_of((place[LINE] ^ k) * count, 64)
        ref[spot, :count, :] = total[pl.ds(at, count), :].astype(ref.dtype)
        at = pl.multiple_of((place[LINE] ^ k) * columns, 128)
        value = out_total[:, pl.ds(at, columns)].astype(ref.dtype)
        for j in range(4):
            ref[spot, count:, columns * j : columns * j + columns] = value[tall * j : tall * j + tall, :]


def piece_of(ref, at, rows):
    t, j = at // 2, at % 2
    return ref[64 * j : 64 * j + 64, rows * t : rows * t + rows]


def weight_first(
    place, keep, out_keep, got, p0, p1, p2, p3, n0, n1,
    part_keep, part_send, tokens, left, total, out_total,
):
    block = p0.shape[0] // 2
    rows = 4 * block
    for i, ref in enumerate((p0, p1, p2, p3)):
        tokens[i * block : (i + 1) * block, :] = ref[:block, :]
    tokens[rows : rows + 2 * block, :] = n0[...]
    tokens[rows + 2 * block :, :] = n1[...]
    for side, ref in enumerate((keep, got)):
        for i, at in enumerate((0, 2, 4, 5)):
            left[side, 64 * i : 64 * i + 64, :] = piece_of(ref, at, rows)
    total[...] = dot_nn(left[0], tokens[:rows, :]) + dot_nn(left[1], tokens[rows:, :])
    put_parts(place, total, out_keep, got, part_keep, part_send, out_total)


def weight_second(
    place, keep_a, got_a, keep_b, out_keep, got_b, p0, p1, p2, p3, n0, n1, after,
    part_keep, part_send, tokens, left, total, out_total,
):
    del after
    block = p0.shape[0] // 2
    rows = 4 * block
    for i, ref in enumerate((p0, p1, p2, p3)):
        tokens[i * block : (i + 1) * block, :] = ref[:block, :]
    tokens[rows : rows + 2 * block, :] = n0[...]
    tokens[rows + 2 * block :, :] = n1[...]
    for side, (a, b) in enumerate(((keep_a, keep_b), (got_a, got_b))):
        for i, (ref, at) in enumerate(
            ((a, 1), (b, 0), (b, 1), (a, 3), (b, 2), (b, 3), (b, 4), (b, 5))
        ):
            left[side, 64 * i : 64 * i + 64, :] = piece_of(ref, at, rows)
    total[...] = dot_nn(left[0], tokens[:rows, :]) + dot_nn(left[1], tokens[rows:, :])
    put_parts(place, total, out_keep, got_b, part_keep, part_send, out_total)


def pair_kernel(keep, got, mine, send):
    mine[...] = keep[0] + got[0].astype(jnp.float32)
    send[...] = (keep[1] + got[1].astype(jnp.float32)).astype(send.dtype)


def sum_kernel(mine, got, *refs):
    out = refs[-1]
    out[...] = (mine[...] + got[...].astype(jnp.float32)).astype(out.dtype)


def finish_kernel(place, a0, a1, a2, a3, b0, b1, b2, b3, wide, narrow):
    core_low, side_low = place[CORE] == 0, place[SIDE] == 0
    slab = place[LINE]
    columns = narrow.shape[1]
    spot = jnp.where(slab == 3, 0, slab)
    spots = (spot, jnp.where(spot == 0, 1, 0), jnp.where(spot == 2, 1, 2))

    def pick(refs, c, x, at, part):
        own, by_x, by_core, by_both = refs
        near = jnp.where(side_low == (x == 0), own[at, part], by_x[at, part])
        far = jnp.where(side_low == (x == 0), by_core[at, part], by_both[at, part])
        return jnp.where(core_low == (c == 0), near, far)

    every = slice(None)
    first, second = (a0, a1, a2, a3), (b0, b1, b2, b3)
    for c in range(2):
        for i, (refs, row) in enumerate(((first, 0), (second, 0), (second, 64))):
            at = slice(row, row + 64)
            both = jnp.concatenate([pick(refs, c, x, at, every) for x in range(2)], axis=0)
            col = pl.multiple_of(128 * (2 * spots[i] + c), 128)
            wide[:, pl.ds(col, 128)] = both.T.astype(wide.dtype)
        for half, (refs, base) in enumerate(((first, 64), (second, 128))):
            for j in range(4):
                at = slice(base, base + 32)
                part = slice(columns * j, columns * j + columns)
                for x in range(2):
                    pair, row = 2 * half + j // 2, 32 * (j % 2)
                    row += 128 * (2 * pair + c) + 64 * x
                    narrow[row : row + 32, :] = pick(refs, c, x, at, part).astype(narrow.dtype)


SMEM_SPEC = pl.BlockSpec(memory_space=pltpu.SMEM)
VMEM_SPEC = pl.BlockSpec(memory_space=pltpu.VMEM)


def struct(shape, dtype=jnp.bfloat16):
    return jax.ShapeDtypeStruct(shape, dtype)


COST = pl.CostEstimate(flops=1000, bytes_accessed=1000, transcendentals=0)


def in_hbm(value):
    return pltpu.with_memory_space_constraint(value, pltpu.HBM)


def call(kernel, args, outs, limit, place=None, scratch=(), specs=None):
    specs = specs or [VMEM_SPEC] * len(args)
    if place is not None:
        args, specs = (place, *args), [SMEM_SPEC] + specs
    single = not isinstance(outs, list)
    return pl.pallas_call(
        kernel,
        in_specs=specs,
        out_specs=VMEM_SPEC if single else [VMEM_SPEC] * len(outs),
        out_shape=outs,
        scratch_shapes=list(scratch),
        compiler_params=pltpu.CompilerParams(vmem_limit_bytes=limit * MIB),
        cost_estimate=COST,
    )(*args)


def chip_shards(patches, kept_index, kept_count, cotangent, w_qkv, w_out, gain):
    bf16, f32 = jnp.bfloat16, jnp.float32
    samples, slots, width = patches.shape
    reps = lax.axis_size("rep")
    rep = lax.axis_index("rep")
    z = lax.axis_index("seq")
    core, x = rep & 1, rep >> 1
    place = jnp.concatenate(
        [jnp.stack([z & 1, core, z, x]).astype(jnp.int32), kept_count.reshape(samples)]
    )
    own_width = width // 2
    quarter = width // 4
    rows = 4 * slots

    def send(value, move):
        return lax.ppermute(value, AXES, line_perm(move, reps))

    def to_core(value):
        return send(value, lambda x, c, z: (x, 1 - c, z))

    def to_x(value):
        return send(value, lambda x, c, z: (1 - x, c, z))

    def to_chip(value, k):
        return send(value, lambda x, c, z: (x, z >> 1, 2 * c + (k ^ (z & 1))))

    def to_rows(value, k, other):
        return send(value, lambda x, c, z: (x, z >> 1, 2 * (c ^ other) + (k ^ (z & 1))))

    def along(value, k):
        return send(value, lambda x, c, z: (x, c, z ^ k))

    gain_row = gain.reshape(1, width)
    pay = struct((2 * slots, width))
    hbm = pl.BlockSpec(memory_space=pl.ANY)
    any_spec = pl.BlockSpec(memory_space=pl.ANY)
    pairs = width // 512
    own_w = [struct((width, own_width))] * 3 + [struct((own_width, width))]
    rows_in = tuple(in_hbm(v) for v in (patches, cotangent, kept_index, gain_row))
    held = struct((slots, width), f32)
    scratch = [
        pltpu.VMEM((slots, width), bf16),
        pltpu.VMEM((slots, width), bf16),
        pltpu.VMEM(kept_index.shape, jnp.int32),
        pltpu.VMEM(gain_row.shape, f32),
        pltpu.SemaphoreType.DMA((4,)),
    ]
    first_in, first_hidden = call(
        norm_first, rows_in, [pay, held], 24, place, scratch=scratch, specs=[any_spec] * 4
    )
    second_in, second_hidden, wq, wk, wv, wo = call(
        norm_second,
        (*rows_in, in_hbm(w_qkv), in_hbm(w_out), first_in),
        [pay, held] + own_w,
        24,
        place,
        scratch=scratch + [pltpu.SemaphoreType.DMA((8 * pairs,))],
        specs=[any_spec] * 7,
    )
    mine = (first_in, second_in)
    got = [to_chip(mine[k], k) for k in range(2)]
    here = got + [to_core(v) for v in got]
    from_x = to_x(jnp.concatenate([v[:slots] for v in got], axis=0))
    there = (from_x, to_core(from_x))

    half_rows = struct((4, 2 * slots, 128 * pairs))
    out_half = (64 * pairs, width)
    half_t = struct((64 * pairs, 3 * rows))
    half_send = struct((64 * pairs, 3 * rows + width))

    staged = (wq, wk, wv, wo)

    def attend(kernel, after):
        return call(
            kernel,
            (*here, *staged, *after),
            [half_rows] * 2 + [half_t, struct(out_half, f32), half_send],
            32,
            place,
            scratch=[pltpu.VMEM((rows, width), bf16)] * 2 + [pltpu.VMEM((2, 64 * pairs, rows), bf16)],
            specs=[VMEM_SPEC] * 8 + [any_spec] * len(after),
        )

    own_a, oth_a, keep_a, out_keep_a, send_a = attend(attend_first, ())
    got_a = to_x(send_a)
    core_a = to_core(oth_a)
    own_b, oth_b, keep_b, out_keep_b, send_b = attend(attend_second, (from_x,))
    got_b = to_x(send_b)
    core_b = to_core(oth_b)

    def parts_of(kernel, args, tall, scratch, after=()):
        return call(
            kernel,
            (*args, *here, *there, *after),
            [struct((2, tall, width), f32), struct((2, tall, width))],
            16,
            place,
            scratch=[pltpu.VMEM((2 * rows, width), bf16)] + scratch + [pltpu.VMEM(out_half, f32)],
            specs=[VMEM_SPEC] * (len(args) + 6) + [any_spec] * len(after),
        )

    def pair_sums(keep, part):
        shape = keep.shape[1:]
        mine, part = call(pair_kernel, (keep, along(part, 1)), [struct(shape, f32), struct(shape)], 8)
        return mine, part, along(part, 2)

    def spread(mine, part, after=()):
        sums = call(
            sum_kernel,
            (mine, part, *after),
            struct(part.shape),
            8,
            specs=[VMEM_SPEC] * 2 + [any_spec] * len(after),
        )
        by_x = to_x(sums)
        return (sums, by_x, to_core(sums), to_core(by_x))

    keep, part = parts_of(
        weight_first,
        (keep_a, out_keep_a, got_a),
        96,
        [pltpu.VMEM((2, 256, rows), bf16), pltpu.VMEM((256, width), f32)],
    )
    first_sum, paired, first_got = pair_sums(keep, part)
    keep, part = parts_of(
        weight_second,
        (keep_a, got_a, keep_b, out_keep_b, got_b),
        160,
        [pltpu.VMEM((2, 512, rows), bf16), pltpu.VMEM((512, width), f32)],
        (paired,),
    )
    started = part
    second_sum, _, second_got = pair_sums(keep, part)
    first = spread(first_sum, first_got)
    whole_w = pl.BlockSpec((width, width), lambda i, p: (0, 0))
    back = pl.pallas_call(
        rows_kernel,
        grid_spec=pltpu.PrefetchScalarGridSpec(
            num_scalar_prefetch=1,
            grid=(3,),
            in_specs=[pl.BlockSpec(half_rows.shape, lambda i, p: (0, 0, 0))] * 4
            + [pl.BlockSpec((width, width), lambda i, p: (0, i)), whole_w, any_spec, any_spec],
            out_specs=[pl.BlockSpec(pay.shape, lambda i, p: (0, 0))] * 2,
            scratch_shapes=[pltpu.VMEM((2 * slots, width), f32)],
        ),
        out_shape=[pay] * 2,
        compiler_params=pltpu.CompilerParams(vmem_limit_bytes=20 * MIB),
        cost_estimate=COST,
    )(place, own_a, core_a, own_b, core_b, in_hbm(w_qkv), in_hbm(w_out), started, first[1])
    second = spread(second_sum, second_got, (back[0], *first[1:]))
    back = [to_rows(back[k], k, 0) for k in range(2)]
    qkv_grad, out_grad = call(
        finish_kernel,
        (*first, *second),
        [struct((width, 3 * quarter), f32), struct((width, quarter), f32)],
        12,
        place,
    )
    encoded, d_patches = call(
        return_kernel,
        (*back, first_hidden, second_hidden, *mine, gain_row, in_hbm(qkv_grad)),
        [struct(patches.shape)] * 2,
        12,
        place,
        specs=[VMEM_SPEC] * 7 + [any_spec],
    )
    return (encoded, d_patches, qkv_grad, out_grad)


def solution(mesh):
    in_specs = (
        P(("grp", "rep"), "seq", None),
        P(("grp", "rep"), "seq"),
        P(("grp", "rep"), "seq"),
        P(("grp", "rep"), "seq", None),
        P(),
        P(),
        P(),
    )
    out_specs = (
        P(("grp", "rep"), "seq", None),
        P(("grp", "rep"), "seq", None),
        P("grp", "seq"),
        P("grp", "seq"),
    )
    chips = mesh.shape["seq"] == 4 and mesh.shape["rep"] % 2 == 0 and HEADS % 8 == 0

    def run(patches, *rest):
        per_device = patches.shape[0] // (mesh.shape["grp"] * mesh.shape["rep"])
        body = chip_shards if chips and per_device == 2 else shards
        inner = jax.shard_map(body, mesh=mesh, in_specs=in_specs, out_specs=out_specs, check_vma=False)
        return inner(patches, *rest)

    return run
```

```python
import functools

import jax
import jax.numpy as jnp
import numpy as np
from jax import lax
from jax.experimental import pallas as pl
from jax.experimental.pallas import tpu as pltpu
from jax.sharding import PartitionSpec as P

HEADS = 16
GRID_COLS = 512


epsilon = 1e-06


def position_table(position, model_width):
    quarter = model_width // 4
    frequency = jnp.exp(-jnp.log(10000.0) * jnp.arange(quarter, dtype=jnp.float32) / quarter)
    grid_row = (position // GRID_COLS).astype(jnp.float32)
    grid_col = (position % GRID_COLS).astype(jnp.float32)
    row_phase = grid_row[..., None] * frequency
    col_phase = grid_col[..., None] * frequency
    return jnp.concatenate(
        [jnp.sin(row_phase), jnp.cos(row_phase), jnp.sin(col_phase), jnp.cos(col_phase)], axis=-1
    )


def normalize(hidden, gain):
    center = hidden - jnp.mean(hidden, axis=-1, keepdims=True)
    spread = jnp.mean(center * center, axis=-1, keepdims=True)
    inv_std = lax.rsqrt(spread + epsilon)
    unit_rows = center * inv_std
    return ((unit_rows * gain).astype(jnp.bfloat16), unit_rows, inv_std)


def norm_backward(d_normed, gain, unit_rows, inv_std):
    scaled = d_normed * gain
    return inv_std * (
        scaled
        - jnp.mean(scaled, axis=-1, keepdims=True)
        - unit_rows * jnp.mean(scaled * unit_rows, axis=-1, keepdims=True)
    )


def head_block(query_rows, grad_rows, key_rows, value_rows, live_keys, score_scale):
    scores = jnp.dot(query_rows, key_rows.T, preferred_element_type=jnp.float32) * score_scale
    scores = jnp.where(live_keys[None, :], scores, -1e30)
    top_score = jnp.max(scores, axis=1, keepdims=True)
    raised = jnp.exp(scores - top_score)
    probability = raised / jnp.sum(raised, axis=1, keepdims=True)
    rounded = probability.astype(jnp.bfloat16)
    attended = jnp.dot(rounded, value_rows, preferred_element_type=jnp.float32).astype(jnp.bfloat16)
    d_value = jnp.dot(rounded.T, grad_rows, preferred_element_type=jnp.float32)
    d_prob = jnp.dot(grad_rows, value_rows.T, preferred_element_type=jnp.float32)
    d_score = (
        probability * (d_prob - jnp.sum(probability * d_prob, axis=1, keepdims=True)) * score_scale
    ).astype(jnp.bfloat16)
    d_query = jnp.dot(d_score, key_rows, preferred_element_type=jnp.float32)
    d_key = jnp.dot(d_score.T, query_rows, preferred_element_type=jnp.float32)
    return (attended, d_query, d_key, d_value)


def attend(query_rows, grad_rows, key_rows, value_rows, live_keys, score_scale):
    row_count = query_rows.shape[0]
    blocks = max(1, row_count // 512)
    while row_count % blocks:
        blocks -= 1
    block_rows = row_count // blocks
    query_blocks = query_rows.reshape(blocks, block_rows, query_rows.shape[1])
    grad_blocks = grad_rows.reshape(blocks, block_rows, grad_rows.shape[1])

    def block_step(carry, pieces):
        key_total, value_total = carry
        attended, d_query, d_key, d_value = head_block(
            pieces[0], pieces[1], key_rows, value_rows, live_keys, score_scale
        )
        return ((key_total + d_key, value_total + d_value), (attended, d_query))

    empty = jnp.zeros(key_rows.shape, jnp.float32)
    (key_total, value_total), (attended, d_query) = lax.scan(
        block_step, (empty, empty), (query_blocks, grad_blocks)
    )
    return (attended.reshape(row_count, -1), d_query.reshape(row_count, -1), key_total, value_total)


def shards(patches, kept_index, kept_count, cotangent, w_qkv, w_out, gain):
    groups = lax.axis_size("seq")
    samples, slot_count, model_width = patches.shape
    head_size = model_width // HEADS
    per_device = max(1, HEADS // groups)
    splits = max(1, groups // HEADS)
    head_groups = groups // splits
    band_width = per_device * head_size
    part_rows = slot_count // splits
    slot_ids = jnp.arange(slot_count, dtype=jnp.int32)
    live_slots = slot_ids[None, :] < kept_count
    hidden = patches.astype(jnp.float32) + position_table(kept_index, model_width)
    normed, unit_rows, inv_std = normalize(hidden, gain)
    flat_normed = normed.reshape(samples * slot_count, model_width)
    packed = jnp.dot(flat_normed, w_qkv, preferred_element_type=jnp.float32).astype(jnp.bfloat16)
    packed = packed.reshape(samples, slot_count, 3 * model_width)
    live_grad = jnp.where(live_slots[:, :, None], cotangent, jnp.zeros_like(cotangent))
    flat_grad = live_grad.reshape(samples * slot_count, model_width)
    d_attended = jnp.dot(flat_grad, w_out.T, preferred_element_type=jnp.float32).astype(
        jnp.bfloat16
    )
    d_attended = d_attended.reshape(samples, slot_count, model_width)

    def to_owners(tensor_block):
        arranged = tensor_block.reshape(samples, splits, part_rows, head_groups, band_width)
        return arranged.transpose(3, 1, 0, 2, 4).reshape(groups, samples, part_rows, band_width)

    key_value_send = jnp.concatenate(
        [
            packed[:, :, model_width : 2 * model_width].reshape(
                samples, slot_count, head_groups, band_width
            ),
            packed[:, :, 2 * model_width :].reshape(samples, slot_count, head_groups, band_width),
        ],
        axis=3,
    )
    key_value_send = key_value_send.transpose(2, 0, 1, 3)
    key_value_send = jnp.broadcast_to(
        key_value_send[:, None], (head_groups, splits, samples, slot_count, 2 * band_width)
    )
    key_value_send = key_value_send.reshape(groups, samples, slot_count, 2 * band_width)
    got_query, got_grad, got_pair = (
        lax.all_to_all(
            to_owners(packed[:, :, :model_width]), "seq", split_axis=0, concat_axis=0, tiled=True
        ),
        lax.all_to_all(to_owners(d_attended), "seq", split_axis=0, concat_axis=0, tiled=True),
        lax.all_to_all(key_value_send, "seq", split_axis=0, concat_axis=0, tiled=True),
    )
    all_counts = lax.all_gather(kept_count, "seq", axis=1, tiled=True)
    live_keys = (slot_ids[None, None, :] < all_counts[:, :, None]).reshape(
        samples, groups * slot_count
    )

    def rows_by_head(tensor_block, row_count):
        arranged = tensor_block.transpose(1, 0, 2, 3).reshape(
            samples, groups * row_count, per_device, head_size
        )
        return arranged.transpose(0, 2, 1, 3)

    query_heads = rows_by_head(got_query, part_rows)
    grad_heads = rows_by_head(got_grad, part_rows)
    key_heads = rows_by_head(got_pair[..., :band_width], slot_count)
    value_heads = rows_by_head(got_pair[..., band_width:], slot_count)
    score_scale = head_size ** (-0.5)

    def one_head(query_rows, grad_rows, key_rows, value_rows, key_live):
        return attend(query_rows, grad_rows, key_rows, value_rows, key_live, score_scale)

    per_head = jax.vmap(one_head, in_axes=(0, 0, 0, 0, None))
    outputs, d_query, d_key, d_value = jax.vmap(per_head)(
        query_heads, grad_heads, key_heads, value_heads, live_keys
    )

    def back_to_sources(tensor_block, row_count):
        arranged = tensor_block.transpose(0, 2, 1, 3).reshape(
            samples, groups, row_count, band_width
        )
        return arranged.transpose(1, 0, 2, 3)

    query_send = back_to_sources(d_query, part_rows).astype(jnp.bfloat16)
    back_out, back_query = (
        lax.all_to_all(
            back_to_sources(outputs, part_rows), "seq", split_axis=0, concat_axis=0, tiled=True
        ),
        lax.all_to_all(query_send, "seq", split_axis=0, concat_axis=0, tiled=True),
    )
    key_value_grad = jnp.concatenate(
        [back_to_sources(d_key, slot_count), back_to_sources(d_value, slot_count)], axis=3
    )
    back_pair = lax.all_to_all(
        key_value_grad.astype(jnp.bfloat16), "seq", split_axis=0, concat_axis=0, tiled=True
    ).astype(key_value_grad.dtype)

    def from_owners(tensor_block):
        arranged = tensor_block.reshape(head_groups, splits, samples, part_rows, band_width)
        return arranged.transpose(2, 1, 3, 0, 4).reshape(samples, slot_count, model_width)

    attended = from_owners(back_out)
    summed_pair = jnp.sum(
        back_pair.reshape(head_groups, splits, samples, slot_count, 2 * band_width), axis=1
    )
    summed_pair = summed_pair.transpose(1, 2, 0, 3)
    key_grad_rows = (
        summed_pair[..., :band_width].reshape(samples, slot_count, model_width).astype(jnp.bfloat16)
    )
    value_grad_rows = (
        summed_pair[..., band_width:].reshape(samples, slot_count, model_width).astype(jnp.bfloat16)
    )
    d_packed = jnp.concatenate([from_owners(back_query), key_grad_rows, value_grad_rows], axis=2)
    flat_attended = attended.reshape(samples * slot_count, model_width)
    projected = jnp.dot(flat_attended, w_out, preferred_element_type=jnp.float32).reshape(
        samples, slot_count, model_width
    )
    encoded = jnp.where(live_slots[:, :, None], hidden + projected, 0.0).astype(jnp.bfloat16)
    flat_packed = d_packed.reshape(samples * slot_count, 3 * model_width)
    d_normed = jnp.dot(flat_packed, w_qkv.T, preferred_element_type=jnp.float32).reshape(
        samples, slot_count, model_width
    )
    d_hidden = norm_backward(d_normed, gain, unit_rows, inv_std)
    d_patches = jnp.where(
        live_slots[:, :, None], live_grad.astype(jnp.float32) + d_hidden, 0.0
    ).astype(jnp.bfloat16)
    columns = flat_grad
    out_part = lax.psum_scatter(
        jnp.dot(columns.T, flat_attended, preferred_element_type=jnp.float32),
        "seq",
        scatter_dimension=0,
        tiled=True,
    ).T
    my_columns = lax.all_to_all(flat_packed, "seq", split_axis=1, concat_axis=0, tiled=True)
    columns = my_columns
    qkv_part = jnp.dot(
        lax.all_gather(flat_normed, "seq", axis=0, tiled=True).T,
        columns,
        preferred_element_type=jnp.float32,
    )
    qkv_grad, out_grad = lax.psum((qkv_part, out_part), "rep")
    return (encoded, d_patches, qkv_grad, out_grad)


AXES = ("seq", "rep")
MARK = 1024.0
MIB = 1024 * 1024


def line_perm(move, reps):
    pairs = []
    for z in range(4):
        for rep in range(reps):
            x, c = rep // 2, rep % 2
            to_x, to_c, to_z = move(x, c, z)
            pairs.append((z * reps + rep, to_z * reps + 2 * to_x + to_c))
    return pairs


def sine_cosine(phase):
    turns = jnp.floor(phase * np.float32(2.0 / np.pi) + 0.5)
    rest = phase - turns * np.float32(1.5703125)
    rest = rest - turns * np.float32(4.837512969970703125e-4)
    rest = rest - turns * np.float32(7.54978995489188216e-8)
    square = rest * rest
    sine = rest + rest * square * (
        np.float32(-1.6666654611e-1)
        + square * (np.float32(8.3321608736e-3) + square * np.float32(-1.9515295891e-4))
    )
    cosine = (
        1.0
        - 0.5 * square
        + square
        * square
        * (
            np.float32(4.166664568298827e-2)
            + square * (np.float32(-1.388731625493765e-3) + square * np.float32(2.443315711809948e-5))
        )
    )
    quadrant = turns.astype(jnp.int32) & 3
    swap = (quadrant & 1) == 1
    first = jnp.where(swap, cosine, sine)
    second = jnp.where(swap, sine, cosine)
    first = jnp.where(quadrant >= 2, -first, first)
    second = jnp.where((quadrant == 1) | (quadrant == 2), -second, second)
    return first, second


def live_column(count, rows):
    return lax.broadcasted_iota(jnp.int32, (rows, 1), 0) < count


def dot_nn(a, b):
    return jnp.dot(a, b, preferred_element_type=jnp.float32)


def dot_nt(a, b):
    return lax.dot_general(a, b, (((1,), (1,)), ((), ())), preferred_element_type=jnp.float32)


PAR, CORE, LINE, SIDE, KEPT = range(5)


def load_weights(core, w_in_hbm, w_out_hbm, wq, wk, wv, wo, sems):
    width = w_out_hbm.shape[0]
    copies = []
    for j in range(wq.shape[1] // 128):
        to = pl.ds(128 * j, 128)
        row = pl.multiple_of(256 * j + 128 * core, 128)
        pairs = [(w_out_hbm.at[pl.ds(row, 128), :], wo.at[to, :])]
        for t, out in enumerate((wq, wk, wv)):
            at = pl.multiple_of(t * width + row, 128)
            pairs.append((w_in_hbm.at[:, pl.ds(at, 128)], out.at[:, to]))
        copies += [pltpu.make_async_copy(a, b, sems.at[4 * j + i]) for i, (a, b) in enumerate(pairs)]
    for copy in copies:
        copy.start()
    return copies


def norm_block(
    k, place, patch_hbm, cot_hbm, index_hbm, gain_hbm, out_ref, hidden_ref, unit_ref, inv_ref,
    patch_ref, cot_ref, index_ref, gain_ref, sems,
):
    s = k ^ place[PAR]
    rows, width = patch_ref.shape
    quarter = width // 4
    copies = [
        pltpu.make_async_copy(src, dst, sems.at[i])
        for i, (src, dst) in enumerate(
            (
                (index_hbm, index_ref),
                (patch_hbm.at[s], patch_ref),
                (gain_hbm, gain_ref),
                (cot_hbm.at[s], cot_ref),
            )
        )
    ]
    for copy in copies:
        copy.start()
    order = lax.broadcasted_iota(jnp.int32, (1, quarter), 1).astype(jnp.float32)
    freq = jnp.exp(-np.log(np.float32(10000.0)) * order / quarter)
    diagonal = lax.broadcasted_iota(jnp.int32, (rows, rows), 0) == lax.broadcasted_iota(
        jnp.int32, (rows, rows), 1
    )
    copies[0].wait()
    position = index_ref[pl.ds(s, 1), :]
    grid_row = (position // GRID_COLS).astype(jnp.float32)
    grid_col = (position % GRID_COLS).astype(jnp.float32)
    grid_row = jnp.sum(jnp.where(diagonal, grid_row, 0.0), axis=1, keepdims=True)
    grid_col = jnp.sum(jnp.where(diagonal, grid_col, 0.0), axis=1, keepdims=True)
    table = jnp.concatenate(sine_cosine(grid_row * freq) + sine_cosine(grid_col * freq), axis=1)
    copies[1].wait()
    copies[2].wait()
    hidden = patch_ref[...].astype(jnp.float32) + table
    hidden_ref[...] = hidden
    center = hidden - jnp.mean(hidden, axis=-1, keepdims=True)
    spread = jnp.mean(center * center, axis=-1, keepdims=True)
    inv_std = lax.rsqrt(spread + epsilon)
    unit = center * inv_std
    unit_ref[...] = unit
    inv_ref[...] = inv_std + jnp.zeros(inv_ref.shape, jnp.float32)
    normed = unit * gain_ref[...]
    live = live_column(place[KEPT + s], rows)
    out_ref[:rows, :] = jnp.where(live, normed, MARK).astype(out_ref.dtype)
    copies[3].wait()
    grad = cot_ref[...]
    out_ref[rows:, :] = jnp.where(live, grad, jnp.zeros_like(grad))


def norm_first(place, patch_hbm, cot_hbm, index_hbm, gain_hbm, *refs):
    norm_block(0, place, patch_hbm, cot_hbm, index_hbm, gain_hbm, *refs)


def norm_second(
    place, patch_hbm, cot_hbm, index_hbm, gain_hbm, w_in_hbm, w_out_hbm, after,
    out_ref, hidden_ref, unit_ref, inv_ref, wq, wk, wv, wo, *refs,
):
    del after
    staged = load_weights(place[CORE], w_in_hbm, w_out_hbm, wq, wk, wv, wo, refs[-1])
    norm_block(1, place, patch_hbm, cot_hbm, index_hbm, gain_hbm, out_ref, hidden_ref, unit_ref, inv_ref, *refs[:-1])
    for copy in staged:
        copy.wait()


def attend_pairs(
    place, first_pair, payloads, wq, wk, wv, wo, own, oth, keep_t, out_keep, send, norm_s, grad_s, att_s,
):
    block = payloads[0].shape[0] // 2
    rows = 4 * block
    half = 2 * block
    biases = []
    for i, ref in enumerate(payloads):
        at = slice(i * block, (i + 1) * block)
        value = ref[:block, :]
        live = value[:, 0:1].astype(jnp.float32) < MARK
        norm_s[at, :] = jnp.where(live, value, jnp.zeros_like(value))
        grad_s[at, :] = ref[block:, :]
        biases.append(jnp.where(live, 0.0, -1e30))
    bias = jnp.concatenate(biases, axis=0)
    low = lax.broadcasted_iota(jnp.int32, (rows, 128), 1) < 64
    scale = jnp.bfloat16(0.125)
    zero = jnp.zeros((rows, 128), jnp.bfloat16)
    first = place[SIDE] == 0
    count = own.shape[2] // 128
    here = slice(128 * first_pair, 128 * (first_pair + count))
    normed = norm_s[...]
    queries = dot_nn(normed, wq[:, here]).astype(jnp.bfloat16)
    keys = dot_nn(normed, wk[:, here]).astype(jnp.bfloat16)
    values = dot_nn(normed, wv[:, here]).astype(jnp.bfloat16)
    d_att = dot_nt(grad_s[...], wo[here, :]).astype(jnp.bfloat16)
    for j in range(count):
        cols = slice(128 * j, 128 * j + 128)
        q = queries[:, cols] * scale
        k = keys[:, cols]
        v = values[:, cols]
        g = d_att[:, cols]
        v_t = v.T
        k_t = (k * scale).T
        att_t, dq_t, dk, dv = [], [], [], []
        for h in range(2):
            mine = low if h == 0 else jnp.logical_not(low)
            scores = dot_nt(k, jnp.where(mine, q, zero)) + bias
            raised = jnp.exp(scores - jnp.max(scores, axis=0, keepdims=True))
            prob = raised * (1.0 / jnp.sum(raised, axis=0, keepdims=True))
            weights = prob.astype(jnp.bfloat16)
            part = slice(64 * h, 64 * h + 64)
            att_t.append(dot_nn(v_t[part], weights))
            dv.append(dot_nn(weights, g))
            d_prob = dot_nt(v, jnp.where(mine, g, zero))
            total = jnp.sum(prob * d_prob, axis=0, keepdims=True)
            d_score = (prob * (d_prob - total)).astype(jnp.bfloat16)
            dq_t.append(dot_nn(k_t[part], d_score))
            dk.append(dot_nn(d_score, q))
        att_pair_t = jnp.concatenate(att_t, axis=0).astype(jnp.bfloat16)
        dq_pair_t = jnp.concatenate(dq_t, axis=0).astype(jnp.bfloat16)
        dk_pair = jnp.where(low, dk[0], dk[1]).astype(jnp.bfloat16)
        dv_pair = jnp.where(low, dv[0], dv[1]).astype(jnp.bfloat16)
        for t, piece in enumerate((dq_pair_t.T, dk_pair, dv_pair, att_pair_t.T)):
            own[t, :, cols] = piece[:half]
            oth[t, :, cols] = piece[half:]
        for t, piece in enumerate((dq_pair_t, dk_pair.T, dv_pair.T)):
            at = slice(64 * j, 64 * j + 64)
            part = slice(rows * t, rows * t + rows)
            keep_t[at, part] = jnp.where(first, piece[:64], piece[64:])
            send[at, part] = jnp.where(first, piece[64:], piece[:64])
        at = slice(64 * j, 64 * j + 64)
        att_s[0, at, :] = jnp.where(first, att_pair_t[:64], att_pair_t[64:])
        att_s[1, at, :] = jnp.where(first, att_pair_t[64:], att_pair_t[:64])
    out_keep[...] = dot_nn(att_s[0], grad_s[...])
    send[:, 3 * rows :] = dot_nn(att_s[1], grad_s[...]).astype(send.dtype)


def attend_first(place, p0, p1, p2, p3, *refs):
    attend_pairs(place, 0, (p0, p1, p2, p3), *refs)


def pieces_of(refs, rows):
    pieces = []
    for ref, at in refs:
        t, j = at // 2, at % 2
        pieces.append(ref[64 * j : 64 * j + 64, rows * t : rows * t + rows])
    return jnp.concatenate(pieces, axis=0)


def first_pieces(a, rows):
    return pieces_of(((a, 0), (a, 2), (a, 4), (a, 5)), rows)


def second_pieces(a, b, rows):
    return pieces_of(((a, 1), (b, 0), (b, 1), (a, 3), (b, 2), (b, 3), (b, 4), (b, 5)), rows)


def attend_second(
    place, p0, p1, p2, p3, wq, wk, wv, wo, keep_a, after,
    own, oth, own_first, own_second, out_keep, send, keep_b, norm_s, grad_s, att_s,
):
    del after
    attend_pairs(
        place, 2, (p0, p1, p2, p3), wq, wk, wv, wo, own, oth, keep_b, out_keep, send, norm_s, grad_s, att_s
    )
    rows = norm_s.shape[0]
    own_first[...] = dot_nn(first_pieces(keep_a, rows), norm_s[...])
    own_second[...] = dot_nn(second_pieces(keep_a, keep_b, rows), norm_s[...])


def in_order(place, own, got):
    pieces = []
    low = place == 0
    for j in range(own.shape[1] // 128):
        a, b = own[:, 128 * j : 128 * j + 128], got[:, 128 * j : 128 * j + 128]
        pieces += [jnp.where(low, a, b), jnp.where(low, b, a)]
    return jnp.concatenate(pieces, axis=1)


def rows_kernel(place, own_a, got_a, own_b, got_b, w_ref, w_out_ref, after, before, o0, o1, total):
    del after, before
    step = pl.program_id(0)
    core = place[CORE]
    block = o0.shape[0] // 2

    def rows_of(t):
        return jnp.concatenate([in_order(core, own_a[t], got_a[t]), in_order(core, own_b[t], got_b[t])], axis=1)

    term = dot_nt(rows_of(step), w_ref[...])

    @pl.when(step == 0)
    def _():
        total[...] = term
        projected = dot_nn(rows_of(3), w_out_ref[...]).astype(o0.dtype)
        o0[:block, :] = projected[:block]
        o1[:block, :] = projected[block:]

    @pl.when(step > 0)
    def _():
        total[...] += term

    @pl.when(step == pl.num_programs(0) - 1)
    def _():
        o0[block:, :] = total[:block].astype(o0.dtype)
        o1[block:, :] = total[block:].astype(o1.dtype)


def return_kernel(place, r0, r1, h0, u0, i0, h1, u1, i1, m0, m1, gain_ref, after, encoded, d_patches):
    del after
    rows = r0.shape[0] // 2
    for k, (r_ref, hidden, unit, inv_std, m_ref) in enumerate(((r0, h0, u0, i0, m0), (r1, h1, u1, i1, m1))):
        s = k ^ place[PAR]
        live = live_column(place[KEPT + s], rows)
        projected = r_ref[:rows, :].astype(jnp.float32)
        encoded[s] = jnp.where(live, hidden[...] + projected, 0.0).astype(encoded.dtype)
        d_normed = r_ref[rows:, :].astype(jnp.float32)
        d_hidden = norm_backward(d_normed, gain_ref[...], unit[...], inv_std[:, 0:1])
        value = m_ref[rows:, :].astype(jnp.float32) + d_hidden
        d_patches[s] = jnp.where(live, value, 0.0).astype(d_patches.dtype)


def put_parts(place, total, out_keep, got, keep, send, out_total):
    out_total[...] = out_keep[...] + got[:, got.shape[1] - out_total.shape[1] :].astype(jnp.float32)
    columns = out_total.shape[1] // 4
    tall = out_total.shape[0] // 4
    count = total.shape[0] // 4
    for k in range(4):
        ref, spot = (keep, send)[k % 2], k // 2
        at = pl.multiple_of((place[LINE] ^ k) * count, 64)
        ref[spot, :count, :] = total[pl.ds(at, count), :].astype(ref.dtype)
        at = pl.multiple_of((place[LINE] ^ k) * columns, 128)
        value = out_total[:, pl.ds(at, columns)].astype(ref.dtype)
        for j in range(4):
            ref[spot, count:, columns * j : columns * j + columns] = value[tall * j : tall * j + tall, :]


def weight_first(place, own, out_keep, got, n0, n1, part_keep, part_send, tokens, total, out_total):
    half, rows = n0.shape[0], 2 * n0.shape[0]
    tokens[:half, :] = n0[...]
    tokens[half:, :] = n1[...]
    total[...] = own[...] + dot_nn(first_pieces(got, rows), tokens[...])
    put_parts(place, total, out_keep, got, part_keep, part_send, out_total)


def weight_second(
    place, own, out_keep, got_a, got_b, n0, n1, after, part_keep, part_send, tokens, total, out_total
):
    del after
    half, rows = n0.shape[0], 2 * n0.shape[0]
    tokens[:half, :] = n0[...]
    tokens[half:, :] = n1[...]
    total[...] = own[...] + dot_nn(second_pieces(got_a, got_b, rows), tokens[...])
    put_parts(place, total, out_keep, got_b, part_keep, part_send, out_total)


def pair_kernel(keep, got, mine, send):
    mine[...] = keep[0] + got[0].astype(jnp.float32)
    send[...] = (keep[1] + got[1].astype(jnp.float32)).astype(send.dtype)


def sum_kernel(mine, got, *refs):
    out = refs[-1]
    out[...] = (mine[...] + got[...].astype(jnp.float32)).astype(out.dtype)


def finish_kernel(place, a0, a1, a2, a3, b0, b1, b2, b3, wide, narrow):
    core_low, side_low = place[CORE] == 0, place[SIDE] == 0
    slab = place[LINE]
    columns = narrow.shape[1]
    spot = jnp.where(slab == 3, 0, slab)
    spots = (spot, jnp.where(spot == 0, 1, 0), jnp.where(spot == 2, 1, 2))

    def pick(refs, c, x, at, part):
        own, by_x, by_core, by_both = refs
        near = jnp.where(side_low == (x == 0), own[at, part], by_x[at, part])
        far = jnp.where(side_low == (x == 0), by_core[at, part], by_both[at, part])
        return jnp.where(core_low == (c == 0), near, far)

    every = slice(None)
    first, second = (a0, a1, a2, a3), (b0, b1, b2, b3)
    for c in range(2):
        for i, (refs, row) in enumerate(((first, 0), (second, 0), (second, 64))):
            at = slice(row, row + 64)
            both = jnp.concatenate([pick(refs, c, x, at, every) for x in range(2)], axis=0)
            col = pl.multiple_of(128 * (2 * spots[i] + c), 128)
            wide[:, pl.ds(col, 128)] = both.T.astype(wide.dtype)
        for half, (refs, base) in enumerate(((first, 64), (second, 128))):
            for j in range(4):
                at = slice(base, base + 32)
                part = slice(columns * j, columns * j + columns)
                for x in range(2):
                    pair, row = 2 * half + j // 2, 32 * (j % 2)
                    row += 128 * (2 * pair + c) + 64 * x
                    narrow[row : row + 32, :] = pick(refs, c, x, at, part).astype(narrow.dtype)


SMEM_SPEC = pl.BlockSpec(memory_space=pltpu.SMEM)
VMEM_SPEC = pl.BlockSpec(memory_space=pltpu.VMEM)


def struct(shape, dtype=jnp.bfloat16):
    return jax.ShapeDtypeStruct(shape, dtype)


COST = pl.CostEstimate(flops=1000, bytes_accessed=1000, transcendentals=0)


def in_hbm(value):
    return pltpu.with_memory_space_constraint(value, pltpu.HBM)


def call(kernel, args, outs, limit, place=None, scratch=(), specs=None):
    specs = specs or [VMEM_SPEC] * len(args)
    if place is not None:
        args, specs = (place, *args), [SMEM_SPEC] + specs
    single = not isinstance(outs, list)
    return pl.pallas_call(
        kernel,
        in_specs=specs,
        out_specs=VMEM_SPEC if single else [VMEM_SPEC] * len(outs),
        out_shape=outs,
        scratch_shapes=list(scratch),
        compiler_params=pltpu.CompilerParams(vmem_limit_bytes=limit * MIB),
        cost_estimate=COST,
    )(*args)


def chip_shards(patches, kept_index, kept_count, cotangent, w_qkv, w_out, gain):
    bf16, f32 = jnp.bfloat16, jnp.float32
    samples, slots, width = patches.shape
    reps = lax.axis_size("rep")
    rep = lax.axis_index("rep")
    z = lax.axis_index("seq")
    core, x = rep & 1, rep >> 1
    place = jnp.concatenate(
        [jnp.stack([z & 1, core, z, x]).astype(jnp.int32), kept_count.reshape(samples)]
    )
    own_width = width // 2
    quarter = width // 4
    rows = 4 * slots

    def send(value, move):
        return lax.ppermute(value, AXES, line_perm(move, reps))

    def to_core(value):
        return send(value, lambda x, c, z: (x, 1 - c, z))

    def to_x(value):
        return send(value, lambda x, c, z: (1 - x, c, z))

    def to_chip(value, k):
        return send(value, lambda x, c, z: (x, z >> 1, 2 * c + (k ^ (z & 1))))

    def to_rows(value, k, other):
        return send(value, lambda x, c, z: (x, z >> 1, 2 * (c ^ other) + (k ^ (z & 1))))

    def along(value, k):
        return send(value, lambda x, c, z: (x, c, z ^ k))

    gain_row = gain.reshape(1, width)
    pay = struct((2 * slots, width))
    hbm = pl.BlockSpec(memory_space=pl.ANY)
    any_spec = pl.BlockSpec(memory_space=pl.ANY)
    pairs = width // 512
    own_w = [struct((width, own_width))] * 3 + [struct((own_width, width))]
    rows_in = tuple(in_hbm(v) for v in (patches, cotangent, kept_index, gain_row))
    held = struct((slots, width), f32)
    scratch = [
        pltpu.VMEM((slots, width), bf16),
        pltpu.VMEM((slots, width), bf16),
        pltpu.VMEM(kept_index.shape, jnp.int32),
        pltpu.VMEM(gain_row.shape, f32),
        pltpu.SemaphoreType.DMA((4,)),
    ]
    kept = [held, held, struct((slots, 128), f32)]
    first_in, *first_kept = call(
        norm_first, rows_in, [pay] + kept, 24, place, scratch=scratch, specs=[any_spec] * 4
    )
    second_in, *second_kept, wq, wk, wv, wo = call(
        norm_second,
        (*rows_in, in_hbm(w_qkv), in_hbm(w_out), first_in),
        [pay] + kept + own_w,
        24,
        place,
        scratch=scratch + [pltpu.SemaphoreType.DMA((8 * pairs,))],
        specs=[any_spec] * 7,
    )
    mine = (first_in, second_in)
    got = [to_chip(mine[k], k) for k in range(2)]
    here = got + [to_core(v) for v in got]
    from_x = to_x(jnp.concatenate([v[:slots] for v in got], axis=0))
    there = (from_x, to_core(from_x))

    half_rows = struct((4, 2 * slots, 128 * pairs))
    out_half = (64 * pairs, width)
    half_t = struct((64 * pairs, 3 * rows))
    half_send = struct((64 * pairs, 3 * rows + width))

    staged = (wq, wk, wv, wo)

    def attend(kernel, args, outs, scratch):
        return call(
            kernel,
            (*here, *staged, *args),
            outs,
            32,
            place,
            scratch=scratch
            + [pltpu.VMEM((rows, width), bf16)] * 2
            + [pltpu.VMEM((2, 64 * pairs, rows), bf16)],
            specs=[VMEM_SPEC] * (8 + len(args[:1])) + [any_spec] * len(args[1:]),
        )

    out_own = struct(out_half, f32)
    own_a, oth_a, keep_a, out_keep_a, send_a = attend(
        attend_first, (), [half_rows] * 2 + [half_t, out_own, half_send], []
    )
    got_a = to_x(send_a)
    core_a = to_core(oth_a)
    own_b, oth_b, own_first, own_second, out_keep_b, send_b = attend(
        attend_second,
        (keep_a, from_x),
        [half_rows] * 2 + [struct((width // 4, width), f32), struct((width // 2, width), f32), out_own, half_send],
        [pltpu.VMEM(half_t.shape, bf16)],
    )
    got_b = to_x(send_b)
    core_b = to_core(oth_b)

    def parts_of(kernel, args, tall, scratch, after=()):
        return call(
            kernel,
            (*args, *there, *after),
            [struct((2, tall, width), f32), struct((2, tall, width))],
            16,
            place,
            scratch=[pltpu.VMEM((rows, width), bf16)] + scratch + [pltpu.VMEM(out_half, f32)],
            specs=[VMEM_SPEC] * (len(args) + 2) + [any_spec] * len(after),
        )

    def pair_sums(keep, part):
        shape = keep.shape[1:]
        mine, part = call(pair_kernel, (keep, along(part, 1)), [struct(shape, f32), struct(shape)], 8)
        return mine, part, along(part, 2)

    def spread(mine, part, after=()):
        sums = call(
            sum_kernel,
            (mine, part, *after),
            struct(part.shape),
            8,
            specs=[VMEM_SPEC] * 2 + [any_spec] * len(after),
        )
        by_x = to_x(sums)
        return (sums, by_x, to_core(sums), to_core(by_x))

    keep, part = parts_of(
        weight_first,
        (own_first, out_keep_a, got_a),
        96,
        [pltpu.VMEM((256, width), f32)],
    )
    first_sum, paired, first_got = pair_sums(keep, part)
    keep, part = parts_of(
        weight_second,
        (own_second, out_keep_b, got_a, got_b),
        160,
        [pltpu.VMEM((512, width), f32)],
        (paired,),
    )
    started = part
    second_sum, _, second_got = pair_sums(keep, part)
    first = spread(first_sum, first_got)
    whole_w = pl.BlockSpec((width, width), lambda i, p: (0, 0))
    back = pl.pallas_call(
        rows_kernel,
        grid_spec=pltpu.PrefetchScalarGridSpec(
            num_scalar_prefetch=1,
            grid=(3,),
            in_specs=[pl.BlockSpec(half_rows.shape, lambda i, p: (0, 0, 0))] * 4
            + [pl.BlockSpec((width, width), lambda i, p: (0, i)), whole_w, any_spec, any_spec],
            out_specs=[pl.BlockSpec(pay.shape, lambda i, p: (0, 0))] * 2,
            scratch_shapes=[pltpu.VMEM((2 * slots, width), f32)],
        ),
        out_shape=[pay] * 2,
        compiler_params=pltpu.CompilerParams(vmem_limit_bytes=20 * MIB),
        cost_estimate=COST,
    )(place, own_a, core_a, own_b, core_b, in_hbm(w_qkv), in_hbm(w_out), started, first[1])
    second = spread(second_sum, second_got, (back[0], *first[1:]))
    back = [to_rows(back[k], k, 0) for k in range(2)]
    qkv_grad, out_grad = call(
        finish_kernel,
        (*first, *second),
        [struct((width, 3 * quarter), f32), struct((width, quarter), f32)],
        12,
        place,
    )
    encoded, d_patches = call(
        return_kernel,
        (*back, *first_kept, *second_kept, *mine, gain_row, in_hbm(qkv_grad)),
        [struct(patches.shape)] * 2,
        12,
        place,
        specs=[VMEM_SPEC] * 11 + [any_spec],
    )
    return (encoded, d_patches, qkv_grad, out_grad)


def solution(mesh):
    in_specs = (
        P(("grp", "rep"), "seq", None),
        P(("grp", "rep"), "seq"),
        P(("grp", "rep"), "seq"),
        P(("grp", "rep"), "seq", None),
        P(),
        P(),
        P(),
    )
    out_specs = (
        P(("grp", "rep"), "seq", None),
        P(("grp", "rep"), "seq", None),
        P("grp", "seq"),
        P("grp", "seq"),
    )
    chips = mesh.shape["seq"] == 4 and mesh.shape["rep"] % 2 == 0 and HEADS % 8 == 0

    def run(patches, *rest):
        per_device = patches.shape[0] // (mesh.shape["grp"] * mesh.shape["rep"])
        body = chip_shards if chips and per_device == 2 else shards
        inner = jax.shard_map(body, mesh=mesh, in_specs=in_specs, out_specs=out_specs, check_vma=False)
        return inner(patches, *rest)

    return run
```

```python
import functools

import jax
import jax.numpy as jnp
import numpy as np
from jax import lax
from jax.experimental import pallas as pl
from jax.experimental.pallas import tpu as pltpu
from jax.sharding import PartitionSpec as P

HEADS = 16
GRID_COLS = 512


epsilon = 1e-06


def position_table(position, model_width):
    quarter = model_width // 4
    frequency = jnp.exp(-jnp.log(10000.0) * jnp.arange(quarter, dtype=jnp.float32) / quarter)
    grid_row = (position // GRID_COLS).astype(jnp.float32)
    grid_col = (position % GRID_COLS).astype(jnp.float32)
    row_phase = grid_row[..., None] * frequency
    col_phase = grid_col[..., None] * frequency
    return jnp.concatenate(
        [jnp.sin(row_phase), jnp.cos(row_phase), jnp.sin(col_phase), jnp.cos(col_phase)], axis=-1
    )


def normalize(hidden, gain):
    center = hidden - jnp.mean(hidden, axis=-1, keepdims=True)
    spread = jnp.mean(center * center, axis=-1, keepdims=True)
    inv_std = lax.rsqrt(spread + epsilon)
    unit_rows = center * inv_std
    return ((unit_rows * gain).astype(jnp.bfloat16), unit_rows, inv_std)


def norm_backward(d_normed, gain, unit_rows, inv_std):
    scaled = d_normed * gain
    return inv_std * (
        scaled
        - jnp.mean(scaled, axis=-1, keepdims=True)
        - unit_rows * jnp.mean(scaled * unit_rows, axis=-1, keepdims=True)
    )


def head_block(query_rows, grad_rows, key_rows, value_rows, live_keys, score_scale):
    scores = jnp.dot(query_rows, key_rows.T, preferred_element_type=jnp.float32) * score_scale
    scores = jnp.where(live_keys[None, :], scores, -1e30)
    top_score = jnp.max(scores, axis=1, keepdims=True)
    raised = jnp.exp(scores - top_score)
    probability = raised / jnp.sum(raised, axis=1, keepdims=True)
    rounded = probability.astype(jnp.bfloat16)
    attended = jnp.dot(rounded, value_rows, preferred_element_type=jnp.float32).astype(jnp.bfloat16)
    d_value = jnp.dot(rounded.T, grad_rows, preferred_element_type=jnp.float32)
    d_prob = jnp.dot(grad_rows, value_rows.T, preferred_element_type=jnp.float32)
    d_score = (
        probability * (d_prob - jnp.sum(probability * d_prob, axis=1, keepdims=True)) * score_scale
    ).astype(jnp.bfloat16)
    d_query = jnp.dot(d_score, key_rows, preferred_element_type=jnp.float32)
    d_key = jnp.dot(d_score.T, query_rows, preferred_element_type=jnp.float32)
    return (attended, d_query, d_key, d_value)


def attend(query_rows, grad_rows, key_rows, value_rows, live_keys, score_scale):
    row_count = query_rows.shape[0]
    blocks = max(1, row_count // 512)
    while row_count % blocks:
        blocks -= 1
    block_rows = row_count // blocks
    query_blocks = query_rows.reshape(blocks, block_rows, query_rows.shape[1])
    grad_blocks = grad_rows.reshape(blocks, block_rows, grad_rows.shape[1])

    def block_step(carry, pieces):
        key_total, value_total = carry
        attended, d_query, d_key, d_value = head_block(
            pieces[0], pieces[1], key_rows, value_rows, live_keys, score_scale
        )
        return ((key_total + d_key, value_total + d_value), (attended, d_query))

    empty = jnp.zeros(key_rows.shape, jnp.float32)
    (key_total, value_total), (attended, d_query) = lax.scan(
        block_step, (empty, empty), (query_blocks, grad_blocks)
    )
    return (attended.reshape(row_count, -1), d_query.reshape(row_count, -1), key_total, value_total)


def shards(patches, kept_index, kept_count, cotangent, w_qkv, w_out, gain):
    groups = lax.axis_size("seq")
    samples, slot_count, model_width = patches.shape
    head_size = model_width // HEADS
    per_device = max(1, HEADS // groups)
    splits = max(1, groups // HEADS)
    head_groups = groups // splits
    band_width = per_device * head_size
    part_rows = slot_count // splits
    slot_ids = jnp.arange(slot_count, dtype=jnp.int32)
    live_slots = slot_ids[None, :] < kept_count
    hidden = patches.astype(jnp.float32) + position_table(kept_index, model_width)
    normed, unit_rows, inv_std = normalize(hidden, gain)
    flat_normed = normed.reshape(samples * slot_count, model_width)
    packed = jnp.dot(flat_normed, w_qkv, preferred_element_type=jnp.float32).astype(jnp.bfloat16)
    packed = packed.reshape(samples, slot_count, 3 * model_width)
    live_grad = jnp.where(live_slots[:, :, None], cotangent, jnp.zeros_like(cotangent))
    flat_grad = live_grad.reshape(samples * slot_count, model_width)
    d_attended = jnp.dot(flat_grad, w_out.T, preferred_element_type=jnp.float32).astype(
        jnp.bfloat16
    )
    d_attended = d_attended.reshape(samples, slot_count, model_width)

    def to_owners(tensor_block):
        arranged = tensor_block.reshape(samples, splits, part_rows, head_groups, band_width)
        return arranged.transpose(3, 1, 0, 2, 4).reshape(groups, samples, part_rows, band_width)

    key_value_send = jnp.concatenate(
        [
            packed[:, :, model_width : 2 * model_width].reshape(
                samples, slot_count, head_groups, band_width
            ),
            packed[:, :, 2 * model_width :].reshape(samples, slot_count, head_groups, band_width),
        ],
        axis=3,
    )
    key_value_send = key_value_send.transpose(2, 0, 1, 3)
    key_value_send = jnp.broadcast_to(
        key_value_send[:, None], (head_groups, splits, samples, slot_count, 2 * band_width)
    )
    key_value_send = key_value_send.reshape(groups, samples, slot_count, 2 * band_width)
    got_query, got_grad, got_pair = (
        lax.all_to_all(
            to_owners(packed[:, :, :model_width]), "seq", split_axis=0, concat_axis=0, tiled=True
        ),
        lax.all_to_all(to_owners(d_attended), "seq", split_axis=0, concat_axis=0, tiled=True),
        lax.all_to_all(key_value_send, "seq", split_axis=0, concat_axis=0, tiled=True),
    )
    all_counts = lax.all_gather(kept_count, "seq", axis=1, tiled=True)
    live_keys = (slot_ids[None, None, :] < all_counts[:, :, None]).reshape(
        samples, groups * slot_count
    )

    def rows_by_head(tensor_block, row_count):
        arranged = tensor_block.transpose(1, 0, 2, 3).reshape(
            samples, groups * row_count, per_device, head_size
        )
        return arranged.transpose(0, 2, 1, 3)

    query_heads = rows_by_head(got_query, part_rows)
    grad_heads = rows_by_head(got_grad, part_rows)
    key_heads = rows_by_head(got_pair[..., :band_width], slot_count)
    value_heads = rows_by_head(got_pair[..., band_width:], slot_count)
    score_scale = head_size ** (-0.5)

    def one_head(query_rows, grad_rows, key_rows, value_rows, key_live):
        return attend(query_rows, grad_rows, key_rows, value_rows, key_live, score_scale)

    per_head = jax.vmap(one_head, in_axes=(0, 0, 0, 0, None))
    outputs, d_query, d_key, d_value = jax.vmap(per_head)(
        query_heads, grad_heads, key_heads, value_heads, live_keys
    )

    def back_to_sources(tensor_block, row_count):
        arranged = tensor_block.transpose(0, 2, 1, 3).reshape(
            samples, groups, row_count, band_width
        )
        return arranged.transpose(1, 0, 2, 3)

    query_send = back_to_sources(d_query, part_rows).astype(jnp.bfloat16)
    back_out, back_query = (
        lax.all_to_all(
            back_to_sources(outputs, part_rows), "seq", split_axis=0, concat_axis=0, tiled=True
        ),
        lax.all_to_all(query_send, "seq", split_axis=0, concat_axis=0, tiled=True),
    )
    key_value_grad = jnp.concatenate(
        [back_to_sources(d_key, slot_count), back_to_sources(d_value, slot_count)], axis=3
    )
    back_pair = lax.all_to_all(
        key_value_grad.astype(jnp.bfloat16), "seq", split_axis=0, concat_axis=0, tiled=True
    ).astype(key_value_grad.dtype)

    def from_owners(tensor_block):
        arranged = tensor_block.reshape(head_groups, splits, samples, part_rows, band_width)
        return arranged.transpose(2, 1, 3, 0, 4).reshape(samples, slot_count, model_width)

    attended = from_owners(back_out)
    summed_pair = jnp.sum(
        back_pair.reshape(head_groups, splits, samples, slot_count, 2 * band_width), axis=1
    )
    summed_pair = summed_pair.transpose(1, 2, 0, 3)
    key_grad_rows = (
        summed_pair[..., :band_width].reshape(samples, slot_count, model_width).astype(jnp.bfloat16)
    )
    value_grad_rows = (
        summed_pair[..., band_width:].reshape(samples, slot_count, model_width).astype(jnp.bfloat16)
    )
    d_packed = jnp.concatenate([from_owners(back_query), key_grad_rows, value_grad_rows], axis=2)
    flat_attended = attended.reshape(samples * slot_count, model_width)
    projected = jnp.dot(flat_attended, w_out, preferred_element_type=jnp.float32).reshape(
        samples, slot_count, model_width
    )
    encoded = jnp.where(live_slots[:, :, None], hidden + projected, 0.0).astype(jnp.bfloat16)
    flat_packed = d_packed.reshape(samples * slot_count, 3 * model_width)
    d_normed = jnp.dot(flat_packed, w_qkv.T, preferred_element_type=jnp.float32).reshape(
        samples, slot_count, model_width
    )
    d_hidden = norm_backward(d_normed, gain, unit_rows, inv_std)
    d_patches = jnp.where(
        live_slots[:, :, None], live_grad.astype(jnp.float32) + d_hidden, 0.0
    ).astype(jnp.bfloat16)
    columns = flat_grad
    out_part = lax.psum_scatter(
        jnp.dot(columns.T, flat_attended, preferred_element_type=jnp.float32),
        "seq",
        scatter_dimension=0,
        tiled=True,
    ).T
    my_columns = lax.all_to_all(flat_packed, "seq", split_axis=1, concat_axis=0, tiled=True)
    columns = my_columns
    qkv_part = jnp.dot(
        lax.all_gather(flat_normed, "seq", axis=0, tiled=True).T,
        columns,
        preferred_element_type=jnp.float32,
    )
    qkv_grad, out_grad = lax.psum((qkv_part, out_part), "rep")
    return (encoded, d_patches, qkv_grad, out_grad)


AXES = ("seq", "rep")
MARK = 1024.0
MIB = 1024 * 1024


def line_perm(move, reps):
    pairs = []
    for z in range(4):
        for rep in range(reps):
            x, c = rep // 2, rep % 2
            to_x, to_c, to_z = move(x, c, z)
            pairs.append((z * reps + rep, to_z * reps + 2 * to_x + to_c))
    return pairs


def sine_cosine(phase):
    turns = jnp.floor(phase * np.float32(2.0 / np.pi) + 0.5)
    rest = phase - turns * np.float32(1.5703125)
    rest = rest - turns * np.float32(4.837512969970703125e-4)
    rest = rest - turns * np.float32(7.54978995489188216e-8)
    square = rest * rest
    sine = rest + rest * square * (
        np.float32(-1.6666654611e-1)
        + square * (np.float32(8.3321608736e-3) + square * np.float32(-1.9515295891e-4))
    )
    cosine = (
        1.0
        - 0.5 * square
        + square
        * square
        * (
            np.float32(4.166664568298827e-2)
            + square * (np.float32(-1.388731625493765e-3) + square * np.float32(2.443315711809948e-5))
        )
    )
    quadrant = turns.astype(jnp.int32) & 3
    swap = (quadrant & 1) == 1
    first = jnp.where(swap, cosine, sine)
    second = jnp.where(swap, sine, cosine)
    first = jnp.where(quadrant >= 2, -first, first)
    second = jnp.where((quadrant == 1) | (quadrant == 2), -second, second)
    return first, second


def live_column(count, rows):
    return lax.broadcasted_iota(jnp.int32, (rows, 1), 0) < count


def dot_nn(a, b):
    return jnp.dot(a, b, preferred_element_type=jnp.float32)


def dot_nt(a, b):
    return lax.dot_general(a, b, (((1,), (1,)), ((), ())), preferred_element_type=jnp.float32)


PAR, CORE, LINE, SIDE, KEPT = range(5)


def load_weights(core, w_in_hbm, w_out_hbm, wq, wk, wv, wo, sems):
    width = w_out_hbm.shape[0]
    copies = []
    for j in range(wq.shape[1] // 128):
        to = pl.ds(128 * j, 128)
        row = pl.multiple_of(256 * j + 128 * core, 128)
        pairs = [(w_out_hbm.at[pl.ds(row, 128), :], wo.at[to, :])]
        for t, out in enumerate((wq, wk, wv)):
            at = pl.multiple_of(t * width + row, 128)
            pairs.append((w_in_hbm.at[:, pl.ds(at, 128)], out.at[:, to]))
        copies += [pltpu.make_async_copy(a, b, sems.at[4 * j + i]) for i, (a, b) in enumerate(pairs)]
    for copy in copies:
        copy.start()
    return copies


def norm_block(
    k, place, patch_hbm, cot_hbm, index_hbm, gain_hbm, out_ref, hidden_ref,
    patch_ref, cot_ref, index_ref, gain_ref, sems,
):
    s = k ^ place[PAR]
    rows, width = patch_ref.shape
    quarter = width // 4
    copies = [
        pltpu.make_async_copy(src, dst, sems.at[i])
        for i, (src, dst) in enumerate(
            (
                (index_hbm, index_ref),
                (patch_hbm.at[s], patch_ref),
                (gain_hbm, gain_ref),
                (cot_hbm.at[s], cot_ref),
            )
        )
    ]
    for copy in copies:
        copy.start()
    order = lax.broadcasted_iota(jnp.int32, (1, quarter), 1).astype(jnp.float32)
    freq = jnp.exp(-np.log(np.float32(10000.0)) * order / quarter)
    diagonal = lax.broadcasted_iota(jnp.int32, (rows, rows), 0) == lax.broadcasted_iota(
        jnp.int32, (rows, rows), 1
    )
    copies[0].wait()
    position = index_ref[pl.ds(s, 1), :]
    grid_row = (position // GRID_COLS).astype(jnp.float32)
    grid_col = (position % GRID_COLS).astype(jnp.float32)
    grid_row = jnp.sum(jnp.where(diagonal, grid_row, 0.0), axis=1, keepdims=True)
    grid_col = jnp.sum(jnp.where(diagonal, grid_col, 0.0), axis=1, keepdims=True)
    table = jnp.concatenate(sine_cosine(grid_row * freq) + sine_cosine(grid_col * freq), axis=1)
    copies[1].wait()
    copies[2].wait()
    hidden = patch_ref[...].astype(jnp.float32) + table
    hidden_ref[...] = hidden
    center = hidden - jnp.mean(hidden, axis=-1, keepdims=True)
    spread = jnp.mean(center * center, axis=-1, keepdims=True)
    normed = center * lax.rsqrt(spread + epsilon) * gain_ref[...]
    live = live_column(place[KEPT + s], rows)
    out_ref[:rows, :] = jnp.where(live, normed, MARK).astype(out_ref.dtype)
    copies[3].wait()
    grad = cot_ref[...]
    out_ref[rows:, :] = jnp.where(live, grad, jnp.zeros_like(grad))


def norm_first(place, patch_hbm, cot_hbm, index_hbm, gain_hbm, *refs):
    norm_block(0, place, patch_hbm, cot_hbm, index_hbm, gain_hbm, *refs)


def norm_second(
    place, patch_hbm, cot_hbm, index_hbm, gain_hbm, w_in_hbm, w_out_hbm, after,
    out_ref, hidden_ref, wq, wk, wv, wo, *refs,
):
    del after
    staged = load_weights(place[CORE], w_in_hbm, w_out_hbm, wq, wk, wv, wo, refs[-1])
    norm_block(1, place, patch_hbm, cot_hbm, index_hbm, gain_hbm, out_ref, hidden_ref, *refs[:-1])
    for copy in staged:
        copy.wait()


def attend_pairs(
    place, first_pair, payloads, wq, wk, wv, wo, own, oth, keep_t, out_keep, send, norm_s, grad_s, att_s,
):
    block = payloads[0].shape[0] // 2
    rows = 4 * block
    half = 2 * block
    biases = []
    for i, ref in enumerate(payloads):
        at = slice(i * block, (i + 1) * block)
        value = ref[:block, :]
        live = value[:, 0:1].astype(jnp.float32) < MARK
        norm_s[at, :] = jnp.where(live, value, jnp.zeros_like(value))
        grad_s[at, :] = ref[block:, :]
        biases.append(jnp.where(live, 0.0, -1e30))
    bias = jnp.concatenate(biases, axis=0)
    low = lax.broadcasted_iota(jnp.int32, (rows, 128), 1) < 64
    scale = jnp.bfloat16(0.125)
    zero = jnp.zeros((rows, 128), jnp.bfloat16)
    first = place[SIDE] == 0
    count = own.shape[2] // 128
    here = slice(128 * first_pair, 128 * (first_pair + count))
    normed = norm_s[...]
    queries = dot_nn(normed, wq[:, here]).astype(jnp.bfloat16)
    keys = dot_nn(normed, wk[:, here]).astype(jnp.bfloat16)
    values = dot_nn(normed, wv[:, here]).astype(jnp.bfloat16)
    d_att = dot_nt(grad_s[...], wo[here, :]).astype(jnp.bfloat16)
    for j in range(count):
        cols = slice(128 * j, 128 * j + 128)
        q = queries[:, cols] * scale
        k = keys[:, cols]
        v = values[:, cols]
        g = d_att[:, cols]
        v_t = v.T
        k_t = (k * scale).T
        att_t, dq_t, dk, dv = [], [], [], []
        for h in range(2):
            mine = low if h == 0 else jnp.logical_not(low)
            scores = dot_nt(k, jnp.where(mine, q, zero)) + bias
            raised = jnp.exp(scores - jnp.max(scores, axis=0, keepdims=True))
            prob = raised * (1.0 / jnp.sum(raised, axis=0, keepdims=True))
            weights = prob.astype(jnp.bfloat16)
            part = slice(64 * h, 64 * h + 64)
            att_t.append(dot_nn(v_t[part], weights))
            dv.append(dot_nn(weights, g))
            d_prob = dot_nt(v, jnp.where(mine, g, zero))
            total = jnp.sum(prob * d_prob, axis=0, keepdims=True)
            d_score = (prob * (d_prob - total)).astype(jnp.bfloat16)
            dq_t.append(dot_nn(k_t[part], d_score))
            dk.append(dot_nn(d_score, q))
        att_pair_t = jnp.concatenate(att_t, axis=0).astype(jnp.bfloat16)
        dq_pair_t = jnp.concatenate(dq_t, axis=0).astype(jnp.bfloat16)
        dk_pair = jnp.where(low, dk[0], dk[1]).astype(jnp.bfloat16)
        dv_pair = jnp.where(low, dv[0], dv[1]).astype(jnp.bfloat16)
        for t, piece in enumerate((dq_pair_t.T, dk_pair, dv_pair, att_pair_t.T)):
            own[t, :, cols] = piece[:half]
            oth[t, :, cols] = piece[half:]
        for t, piece in enumerate((dq_pair_t, dk_pair.T, dv_pair.T)):
            at = slice(64 * j, 64 * j + 64)
            part = slice(rows * t, rows * t + rows)
            keep_t[at, part] = jnp.where(first, piece[:64], piece[64:])
            send[at, part] = jnp.where(first, piece[64:], piece[:64])
        at = slice(64 * j, 64 * j + 64)
        att_s[0, at, :] = jnp.where(first, att_pair_t[:64], att_pair_t[64:])
        att_s[1, at, :] = jnp.where(first, att_pair_t[64:], att_pair_t[:64])
    out_keep[...] = dot_nn(att_s[0], grad_s[...])
    send[:, 3 * rows :] = dot_nn(att_s[1], grad_s[...]).astype(send.dtype)


def pieces_of(refs, rows):
    pieces = []
    for ref, at in refs:
        t, j = at // 2, at % 2
        pieces.append(ref[64 * j : 64 * j + 64, rows * t : rows * t + rows])
    return jnp.concatenate(pieces, axis=0)


def first_pieces(a, rows):
    return pieces_of(((a, 0), (a, 2), (a, 4), (a, 5)), rows)


def second_pieces(a, b, rows):
    return pieces_of(((a, 1), (b, 0), (b, 1), (a, 3), (b, 2), (b, 3), (b, 4), (b, 5)), rows)


def block_rows(refs):
    return jnp.concatenate([ref[64 * at : 64 * at + 64, :] for ref, at in refs], axis=0)


def attend_half(
    first_pair, place, p0, p1, p2, p3, wq, wk, wv, wo,
    own, oth, own_part, out_keep, send, keep, norm_s, grad_s, att_s,
):
    attend_pairs(
        place, first_pair, (p0, p1, p2, p3), wq, wk, wv, wo,
        own, oth, keep, out_keep, send, norm_s, grad_s, att_s,
    )
    rows = norm_s.shape[0]
    own_part[...] = dot_nn(pieces_of([(keep, at) for at in range(6)], rows), norm_s[...])


def attend_first(place, *refs):
    attend_half(0, place, *refs)


def attend_second(place, p0, p1, p2, p3, wq, wk, wv, wo, after, *refs):
    del after
    attend_half(2, place, p0, p1, p2, p3, wq, wk, wv, wo, *refs)


def in_order(place, own, got):
    pieces = []
    low = place == 0
    for j in range(own.shape[1] // 128):
        a, b = own[:, 128 * j : 128 * j + 128], got[:, 128 * j : 128 * j + 128]
        pieces += [jnp.where(low, a, b), jnp.where(low, b, a)]
    return jnp.concatenate(pieces, axis=1)


def rows_kernel(place, own_a, got_a, own_b, got_b, w_ref, w_out_ref, after, before, o0, o1, total):
    del after, before
    step = pl.program_id(0)
    core = place[CORE]
    block = o0.shape[0] // 2

    def rows_of(t):
        return jnp.concatenate([in_order(core, own_a[t], got_a[t]), in_order(core, own_b[t], got_b[t])], axis=1)

    term = dot_nt(rows_of(step), w_ref[...])

    @pl.when(step == 0)
    def _():
        total[...] = term
        projected = dot_nn(rows_of(3), w_out_ref[...]).astype(o0.dtype)
        o0[:block, :] = projected[:block]
        o1[:block, :] = projected[block:]

    @pl.when(step > 0)
    def _():
        total[...] += term

    @pl.when(step == pl.num_programs(0) - 1)
    def _():
        o0[block:, :] = total[:block].astype(o0.dtype)
        o1[block:, :] = total[block:].astype(o1.dtype)


def return_kernel(place, r0, r1, h0, h1, m0, m1, gain_ref, after, encoded, d_patches):
    del after
    par = place[PAR]
    rows = r0.shape[0] // 2
    for k, (r_ref, m_ref, hidden_ref) in enumerate(((r0, m0, h0), (r1, m1, h1))):
        s = k ^ par
        live = live_column(place[KEPT + s], rows)
        hidden = hidden_ref[...]
        projected = r_ref[:rows, :].astype(jnp.float32)
        encoded[s] = jnp.where(live, hidden + projected, 0.0).astype(encoded.dtype)
        center = hidden - jnp.mean(hidden, axis=-1, keepdims=True)
        spread = jnp.mean(center * center, axis=-1, keepdims=True)
        inv_std = lax.rsqrt(spread + epsilon)
        unit = center * inv_std
        d_hidden = norm_backward(r_ref[rows:, :].astype(jnp.float32), gain_ref[...], unit, inv_std)
        value = m_ref[rows:, :].astype(jnp.float32) + d_hidden
        d_patches[s] = jnp.where(live, value, 0.0).astype(d_patches.dtype)


def put_parts(place, total, out_keep, got, keep, send, out_total):
    out_total[...] = out_keep[...] + got[:, got.shape[1] - out_total.shape[1] :].astype(jnp.float32)
    columns = out_total.shape[1] // 4
    tall = out_total.shape[0] // 4
    count = total.shape[0] // 4
    for k in range(4):
        ref, spot = (keep, send)[k % 2], k // 2
        at = pl.multiple_of((place[LINE] ^ k) * count, 64)
        ref[spot, :count, :] = total[pl.ds(at, count), :].astype(ref.dtype)
        at = pl.multiple_of((place[LINE] ^ k) * columns, 128)
        value = out_total[:, pl.ds(at, columns)].astype(ref.dtype)
        for j in range(4):
            ref[spot, count:, columns * j : columns * j + columns] = value[tall * j : tall * j + tall, :]


def weight_first(place, own, out_keep, got, n0, n1, *refs):
    part_keep, part_send, tokens, total, out_total = refs[-5:]
    half, rows = n0.shape[0], 2 * n0.shape[0]
    tokens[:half, :] = n0[...]
    tokens[half:, :] = n1[...]
    mine = block_rows(((own, 0), (own, 2), (own, 4), (own, 5)))
    total[...] = mine + dot_nn(first_pieces(got, rows), tokens[...])
    put_parts(place, total, out_keep, got, part_keep, part_send, out_total)


def weight_second(place, a, b, out_keep, got_a, got_b, n0, n1, *refs):
    part_keep, part_send, tokens, total, out_total = refs[-5:]
    half, rows = n0.shape[0], 2 * n0.shape[0]
    tokens[:half, :] = n0[...]
    tokens[half:, :] = n1[...]
    mine = block_rows(((a, 1), (b, 0), (b, 1), (a, 3), (b, 2), (b, 3), (b, 4), (b, 5)))
    total[...] = mine + dot_nn(second_pieces(got_a, got_b, rows), tokens[...])
    put_parts(place, total, out_keep, got_b, part_keep, part_send, out_total)


def pair_kernel(keep, got, mine, send):
    mine[...] = keep[0] + got[0].astype(jnp.float32)
    send[...] = (keep[1] + got[1].astype(jnp.float32)).astype(send.dtype)


def sum_kernel(mine, got, *refs):
    out = refs[-1]
    out[...] = (mine[...] + got[...].astype(jnp.float32)).astype(out.dtype)


def finish_kernel(place, a0, a1, a2, a3, b0, b1, b2, b3, wide, narrow):
    core_low, side_low = place[CORE] == 0, place[SIDE] == 0
    slab = place[LINE]
    columns = narrow.shape[1]
    spot = jnp.where(slab == 3, 0, slab)
    spots = (spot, jnp.where(spot == 0, 1, 0), jnp.where(spot == 2, 1, 2))

    def pick(refs, c, x, at, part):
        own, by_x, by_core, by_both = refs
        near = jnp.where(side_low == (x == 0), own[at, part], by_x[at, part])
        far = jnp.where(side_low == (x == 0), by_core[at, part], by_both[at, part])
        return jnp.where(core_low == (c == 0), near, far)

    every = slice(None)
    first, second = (a0, a1, a2, a3), (b0, b1, b2, b3)
    for c in range(2):
        for i, (refs, row) in enumerate(((first, 0), (second, 0), (second, 64))):
            at = slice(row, row + 64)
            both = jnp.concatenate([pick(refs, c, x, at, every) for x in range(2)], axis=0)
            col = pl.multiple_of(128 * (2 * spots[i] + c), 128)
            wide[:, pl.ds(col, 128)] = both.T.astype(wide.dtype)
        for half, (refs, base) in enumerate(((first, 64), (second, 128))):
            for j in range(4):
                at = slice(base, base + 32)
                part = slice(columns * j, columns * j + columns)
                for x in range(2):
                    pair, row = 2 * half + j // 2, 32 * (j % 2)
                    row += 128 * (2 * pair + c) + 64 * x
                    narrow[row : row + 32, :] = pick(refs, c, x, at, part).astype(narrow.dtype)


SMEM_SPEC = pl.BlockSpec(memory_space=pltpu.SMEM)
VMEM_SPEC = pl.BlockSpec(memory_space=pltpu.VMEM)


def struct(shape, dtype=jnp.bfloat16):
    return jax.ShapeDtypeStruct(shape, dtype)


COST = pl.CostEstimate(flops=1000, bytes_accessed=1000, transcendentals=0)


def in_hbm(value):
    return pltpu.with_memory_space_constraint(value, pltpu.HBM)


def call(kernel, args, outs, limit, place=None, scratch=(), specs=None):
    specs = specs or [VMEM_SPEC] * len(args)
    if place is not None:
        args, specs = (place, *args), [SMEM_SPEC] + specs
    single = not isinstance(outs, list)
    return pl.pallas_call(
        kernel,
        in_specs=specs,
        out_specs=VMEM_SPEC if single else [VMEM_SPEC] * len(outs),
        out_shape=outs,
        scratch_shapes=list(scratch),
        compiler_params=pltpu.CompilerParams(vmem_limit_bytes=limit * MIB),
        cost_estimate=COST,
    )(*args)


def chip_shards(patches, kept_index, kept_count, cotangent, w_qkv, w_out, gain):
    bf16, f32 = jnp.bfloat16, jnp.float32
    samples, slots, width = patches.shape
    reps = lax.axis_size("rep")
    rep = lax.axis_index("rep")
    z = lax.axis_index("seq")
    core, x = rep & 1, rep >> 1
    place = jnp.concatenate(
        [jnp.stack([z & 1, core, z, x]).astype(jnp.int32), kept_count.reshape(samples)]
    )
    own_width = width // 2
    quarter = width // 4
    rows = 4 * slots

    def send(value, move):
        return lax.ppermute(value, AXES, line_perm(move, reps))

    def to_core(value):
        return send(value, lambda x, c, z: (x, 1 - c, z))

    def to_x(value):
        return send(value, lambda x, c, z: (1 - x, c, z))

    def to_chip(value, k):
        return send(value, lambda x, c, z: (x, z >> 1, 2 * c + (k ^ (z & 1))))

    def to_rows(value, k, other):
        return send(value, lambda x, c, z: (x, z >> 1, 2 * (c ^ other) + (k ^ (z & 1))))

    def along(value, k):
        return send(value, lambda x, c, z: (x, c, z ^ k))

    gain_row = gain.reshape(1, width)
    pay = struct((2 * slots, width))
    hbm = pl.BlockSpec(memory_space=pl.ANY)
    any_spec = pl.BlockSpec(memory_space=pl.ANY)
    pairs = width // 512
    own_w = [struct((width, own_width))] * 3 + [struct((own_width, width))]
    rows_in = tuple(in_hbm(v) for v in (patches, cotangent, kept_index, gain_row))
    held = struct((slots, width), f32)
    scratch = [
        pltpu.VMEM((slots, width), bf16),
        pltpu.VMEM((slots, width), bf16),
        pltpu.VMEM(kept_index.shape, jnp.int32),
        pltpu.VMEM(gain_row.shape, f32),
        pltpu.SemaphoreType.DMA((4,)),
    ]
    first_in, first_hidden = call(
        norm_first, rows_in, [pay, held], 24, place, scratch=scratch, specs=[any_spec] * 4
    )
    second_in, second_hidden, wq, wk, wv, wo = call(
        norm_second,
        (*rows_in, in_hbm(w_qkv), in_hbm(w_out), first_in),
        [pay, held] + own_w,
        24,
        place,
        scratch=scratch + [pltpu.SemaphoreType.DMA((8 * pairs,))],
        specs=[any_spec] * 7,
    )
    mine = (first_in, second_in)
    got = [to_chip(mine[k], k) for k in range(2)]
    here = got + [to_core(v) for v in got]
    from_x = to_x(jnp.concatenate([v[:slots] for v in got], axis=0))
    there = (from_x, to_core(from_x))

    half_rows = struct((4, 2 * slots, 128 * pairs))
    out_half = (64 * pairs, width)
    half_t = struct((64 * pairs, 3 * rows))
    half_send = struct((64 * pairs, 3 * rows + width))

    staged = (wq, wk, wv, wo)

    out_own = struct(out_half, f32)

    def attend(kernel, after):
        return call(
            kernel,
            (*here, *staged, *after),
            [half_rows] * 2 + [struct((192 * pairs, width), f32), out_own, half_send],
            32,
            place,
            scratch=[pltpu.VMEM(half_t.shape, bf16)]
            + [pltpu.VMEM((rows, width), bf16)] * 2
            + [pltpu.VMEM((2, 64 * pairs, rows), bf16)],
            specs=[VMEM_SPEC] * 8 + [any_spec] * len(after),
        )

    own_a, oth_a, part_a, out_keep_a, send_a = attend(attend_first, ())
    got_a = to_x(send_a)
    core_a = to_core(oth_a)
    own_b, oth_b, part_b, out_keep_b, send_b = attend(attend_second, (from_x,))
    got_b = to_x(send_b)
    core_b = to_core(oth_b)

    def parts_of(kernel, args, tall, scratch, after=()):
        return call(
            kernel,
            (*args, *there, *after, *here),
            [struct((2, tall, width), f32), struct((2, tall, width))],
            16,
            place,
            scratch=[pltpu.VMEM((rows, width), bf16)] + scratch + [pltpu.VMEM(out_half, f32)],
            specs=[VMEM_SPEC] * (len(args) + 2) + [any_spec] * (len(after) + 4),
        )

    def pair_sums(keep, part):
        shape = keep.shape[1:]
        mine, part = call(pair_kernel, (keep, along(part, 1)), [struct(shape, f32), struct(shape)], 8)
        return mine, part, along(part, 2)

    def spread(mine, part, after=()):
        sums = call(
            sum_kernel,
            (mine, part, *after),
            struct(part.shape),
            8,
            specs=[VMEM_SPEC] * 2 + [any_spec] * len(after),
        )
        by_x = to_x(sums)
        return (sums, by_x, to_core(sums), to_core(by_x))

    keep, part = parts_of(
        weight_first,
        (part_a, out_keep_a, got_a),
        96,
        [pltpu.VMEM((256, width), f32)],
    )
    first_sum, paired, first_got = pair_sums(keep, part)
    keep, part = parts_of(
        weight_second,
        (part_a, part_b, out_keep_b, got_a, got_b),
        160,
        [pltpu.VMEM((512, width), f32)],
        (paired,),
    )
    started = part
    second_sum, _, second_got = pair_sums(keep, part)
    first = spread(first_sum, first_got)
    whole_w = pl.BlockSpec((width, width), lambda i, p: (0, 0))
    back = pl.pallas_call(
        rows_kernel,
        grid_spec=pltpu.PrefetchScalarGridSpec(
            num_scalar_prefetch=1,
            grid=(3,),
            in_specs=[pl.BlockSpec(half_rows.shape, lambda i, p: (0, 0, 0))] * 4
            + [pl.BlockSpec((width, width), lambda i, p: (0, i)), whole_w, any_spec, any_spec],
            out_specs=[pl.BlockSpec(pay.shape, lambda i, p: (0, 0))] * 2,
            scratch_shapes=[pltpu.VMEM((2 * slots, width), f32)],
        ),
        out_shape=[pay] * 2,
        compiler_params=pltpu.CompilerParams(vmem_limit_bytes=20 * MIB),
        cost_estimate=COST,
    )(place, own_a, core_a, own_b, core_b, in_hbm(w_qkv), in_hbm(w_out), started, first[1])
    second = spread(second_sum, second_got, (back[0], *first[1:]))
    back = [to_rows(back[k], k, 0) for k in range(2)]
    qkv_grad, out_grad = call(
        finish_kernel,
        (*first, *second),
        [struct((width, 3 * quarter), f32), struct((width, quarter), f32)],
        12,
        place,
    )
    encoded, d_patches = call(
        return_kernel,
        (*back, first_hidden, second_hidden, *mine, gain_row, in_hbm(qkv_grad)),
        [struct(patches.shape)] * 2,
        12,
        place,
        specs=[VMEM_SPEC] * 7 + [any_spec],
    )
    return (encoded, d_patches, qkv_grad, out_grad)


def solution(mesh):
    in_specs = (
        P(("grp", "rep"), "seq", None),
        P(("grp", "rep"), "seq"),
        P(("grp", "rep"), "seq"),
        P(("grp", "rep"), "seq", None),
        P(),
        P(),
        P(),
    )
    out_specs = (
        P(("grp", "rep"), "seq", None),
        P(("grp", "rep"), "seq", None),
        P("grp", "seq"),
        P("grp", "seq"),
    )
    chips = mesh.shape["seq"] == 4 and mesh.shape["rep"] % 2 == 0 and HEADS % 8 == 0

    def run(patches, *rest):
        per_device = patches.shape[0] // (mesh.shape["grp"] * mesh.shape["rep"])
        body = chip_shards if chips and per_device == 2 else shards
        inner = jax.shard_map(body, mesh=mesh, in_specs=in_specs, out_specs=out_specs, check_vma=False)
        return inner(patches, *rest)

    return run
```
